32 devices in a mesh: ctx: 8 (over y, x, core), tp: 4 (over z).
Axes of the slice: x: 2, y: 2, z: 4, core: 2. Of those that a mesh axis runs over, the one named last changes fastest.
Arguments:
- layer_in: bfloat16 [8192, 2048], P(('ctx', 'tp')), may hold values from -6 to 6
- norm_gain: float32 [2, 2048], replicated, may hold values from 0.1 to 1.9
- norm_bias: float32 [2, 2048], replicated, may hold values from -3 to 3
- w_qkv: bfloat16 [2048, 3, 2048], P(None, None, 'tp'), may hold values from -0.125 to 0.125
- b_qkv: float32 [3, 2048], P(None, 'tp'), may hold values from -3 to 3
- w_out: bfloat16 [2048, 2048], P('tp'), may hold values from -1.5 to 1.5
- w_gate_up: bfloat16 [2048, 2, 5632], P(None, None, 'tp'), may hold values from -0.125 to 0.125
- w_down: bfloat16 [5632, 2048], P('tp'), may hold values from -0.21875 to 0.21875
- cotangent: bfloat16 [8192, 2048], P(('ctx', 'tp')), may hold values from -6 to 6
- block_table: int32 [8, 2], replicated, may hold values from 0 to 15, as said below
- seq_ids: int32 [16], replicated, may hold values from 0 to 2, never falling along the last dimension, each value on 1 to 12 neighbouring positions
Outputs:
- layer_out: bfloat16 [8192, 2048], P(('ctx', 'tp'))
- grad_input: bfloat16 [8192, 2048], P(('ctx', 'tp'))
- grad_norm_gain: float32 [2, 2048], replicated
- grad_norm_bias: float32 [2, 2048], replicated
- grad_qkv: float32 [2048, 3, 2048], P(None, None, 'tp')
- grad_qkv_bias: float32 [3, 2048], P(None, 'tp')
- grad_out_proj: float32 [2048, 2048], P('tp')
- grad_gate_up: float32 [2048, 2, 5632], P(None, None, 'tp')
- grad_down: float32 [5632, 2048], P('tp')
The draws below stay inside these ranges and needn't reach their ends.
Inputs may be any that keep to these rules, and one draw needn't show every extreme that they name: `block_table`: row c holds a natural block number n and its mirror 2 * 8 - 1 - n; every block number appears once. `seq_ids`: never falling; three sequences, the longest exactly 12 blocks.
All inputs are finite; a program needn't handle non-finite values.
Results may differ from the reference program's by a relative error of at most 0.034.
Values may be sent and summed in bfloat16 or wider, within the bound.
A program may use at most 320 MiB of HBM per device.

```python
import math
import jax
import jax.numpy as jnp
import numpy as np
from jax import lax

D = 2048
HEADS = 32
HEAD = 64
FF = 5632
ROT = 16
BLK = 512
NBLOCKS = 16
TOKENS = 8192


def draw_block_table(key, part):
    key = jax.random.fold_in(key, 11)
    ordering = jax.random.permutation(key, NBLOCKS // 2).astype(jnp.int32)
    return jnp.stack([ordering, NBLOCKS - 1 - ordering], axis=1).astype(jnp.int32)


def levels(rng, dims, cuts, least, high):
    factor_of = 1.0
    for position, shards_of in cuts:
        draws = jax.random.uniform(jax.random.fold_in(jax.random.fold_in(rng, 6), position), (shards_of,), jnp.float32, least / len(cuts), high / len(cuts))
        factor_of = factor_of * jnp.repeat(jnp.exp(draws), dims[position] // shards_of).reshape((-1,) + (1,) * (len(dims) - 1 - position))
    return factor_of


def split_up(number_of, total, bound, slope):
    portions = [(1 << 20) // math.isqrt(grade ** slope) + 1 for grade in range(2, number_of + 1)]
    spare, given = total - bound - (number_of - 1), [1] * (number_of - 1)
    while spare > 0:
        candidates = [i for i in range(number_of - 1) if given[i] < bound]
        whole, budget = sum([portions[i] for i in candidates]), spare
        for i in candidates:
            more = min(bound - given[i], max(1, budget * portions[i] // whole), spare)
            given[i] = given[i] + more
            spare = spare - more
    return np.array([bound] + given)


def ragged_sizes(key, amount, total, most, slope):
    if amount == 2:
        one = jax.random.randint(key, (), max(1, total - most), min(most, total - 1) + 1)
        return jnp.stack([one, total - one])
    lengths = jnp.asarray(split_up(amount, total, most, slope), jnp.int32)
    twos = (amount - 1) // 2
    donor, receiver = lengths[1:1 + 2 * twos:2], lengths[2:2 + 2 * twos:2]
    margin = jnp.minimum(donor - 1, most - receiver)
    moved = jax.random.randint(jax.random.fold_in(key, 1), (twos,), 0, 1 << 20) % (margin + 1)
    lengths = lengths.at[1:1 + 2 * twos:2].set(donor - moved).at[2:2 + 2 * twos:2].set(receiver + moved)
    return lengths[jax.random.permutation(jax.random.fold_in(key, 2), amount)]


def gaussian(rng, dims, width, reach, shards=(), kind=jnp.bfloat16):
    entries = width * jax.random.normal(rng, dims, jnp.float32)
    if shards:
        entries = entries * levels(rng, dims, shards, -0.22, 0.18)
    return jnp.clip(entries, -reach, reach).astype(kind)


def setup_inputs(seed: int = 0) -> dict:
    splits = jax.random.split(jax.random.key(seed), 12)
    layer_in = gaussian(splits[0], (TOKENS, D), 1.0, 6.0, ((0, 32),))
    norm_gain = jnp.clip(1.0 + 0.18 * jax.random.normal(splits[1], (2, D), jnp.float32), 0.1, 1.9)
    norm_bias = gaussian(splits[2], (2, D), 0.5, 3.0, (), jnp.float32)
    w_qkv = gaussian(splits[3], (D, 3, D), D ** -0.5, 0.125, ((2, 4),))
    b_qkv = gaussian(splits[4], (3, D), 0.5, 3.0, ((1, 4),), jnp.float32)
    w_out = gaussian(splits[5], (D, D), (D // 128) ** -0.5, 1.5, ((0, 4),))
    w_gate_up = gaussian(splits[6], (D, 2, FF), D ** -0.5, 0.125, ((2, 4),))
    w_down = gaussian(splits[7], (FF, D), (FF // 8) ** -0.5, 0.21875, ((0, 4),))
    cotangent = gaussian(splits[8], (TOKENS, D), 1.0, 6.0, ((0, 32),))
    block_table = draw_block_table(jax.random.fold_in(splits[11], 71), 0)
    seq_ids = jnp.searchsorted(jnp.cumsum(ragged_sizes(splits[10], 3, NBLOCKS, NBLOCKS - 4, 0)), jnp.arange(NBLOCKS), side="right").astype(jnp.int32)
    return {"layer_in": layer_in, "norm_gain": norm_gain, "norm_bias": norm_bias, "w_qkv": w_qkv, "b_qkv": b_qkv, "w_out": w_out, "w_gate_up": w_gate_up, "w_down": w_down, "cotangent": cotangent, "block_table": block_table, "seq_ids": seq_ids}


highest = lax.Precision.HIGHEST
epsilon = 1e-05
neg_large = -1e+30

@jax.custom_vjp
def low(v):
    return lax.optimization_barrier(v.astype(jnp.bfloat16)).astype(jnp.float32)

@jax.custom_vjp
def low_back(v):
    return v

def low_keep(v):
    return (low(v), None)

def low_pass(kept, grad):
    return (grad,)

def back_keep(v):
    return (v, None)

def back_low(kept, grad):
    return (low(grad),)
low.defvjp(low_keep, low_pass)
low_back.defvjp(back_keep, back_low)

def layer_norm(row_data, norm_scale, norm_shift):
    center = row_data - lax.optimization_barrier(jnp.mean(row_data, axis=1, keepdims=True))
    return center * lax.rsqrt(lax.optimization_barrier(jnp.mean(center * center, axis=1, keepdims=True)) + epsilon) * norm_scale + norm_shift

def rotate(tensor, places):
    half_rot = ROT // 2
    frequency = 10000.0 ** (-2.0 * jnp.arange(half_rot, dtype=jnp.float32) / ROT)
    angles = places.astype(jnp.float32)[:, None] * frequency[None, :]
    cosine = jnp.cos(angles)[:, None, :]
    sines = jnp.sin(angles)[:, None, :]
    leading = tensor[..., :half_rot]
    trailing = tensor[..., half_rot:ROT]
    return jnp.concatenate([leading * cosine - trailing * sines, trailing * cosine + leading * sines, tensor[..., ROT:]], axis=-1)

def forward(inputs, norm_scale, norm_shift, qkv_weight, qkv_bias, out_weight, gate_up_weight, down_weight, places, sequence):
    normed_one = low(layer_norm(inputs, norm_scale[0], norm_shift[0]))
    projected = low_back(jnp.einsum('rd,dcf->rcf', normed_one, qkv_weight, precision=highest) + qkv_bias[None])
    queries = low(rotate(projected[:, 0].reshape(TOKENS, HEADS, HEAD), places))
    key_rows = low(rotate(projected[:, 1].reshape(TOKENS, HEADS, HEAD), places))
    values = low(projected[:, 2].reshape(TOKENS, HEADS, HEAD))
    stride = math.gcd(TOKENS, 512)

    def attend(first_row):
        query_part = lax.dynamic_slice_in_dim(queries, first_row, stride, 0)
        part_places = lax.dynamic_slice_in_dim(places, first_row, stride, 0)
        part_seq = lax.dynamic_slice_in_dim(sequence, first_row, stride, 0)
        raw_scores = low_back(jnp.einsum('qhe,khe->qhk', query_part, key_rows, precision=highest))
        allowed = ((part_seq[:, None] == sequence[None, :]) & (places[None, :] <= part_places[:, None]))[:, None, :]
        scores = jnp.where(allowed, raw_scores * HEAD ** (-0.5), neg_large)
        maxima = lax.optimization_barrier(jnp.max(scores, axis=2, keepdims=True))
        weights = jnp.exp(scores - maxima)
        probabilities = low(weights / lax.optimization_barrier(jnp.sum(weights, axis=2, keepdims=True)))
        return jnp.einsum('qhk,khe->qhe', probabilities, values, precision=highest)
    starts = jnp.arange(TOKENS // stride, dtype=jnp.int32) * stride
    attended = lax.map(jax.checkpoint(attend), starts).reshape(TOKENS, HEADS * HEAD)
    attended = low_back(low(attended))
    middle = inputs + low_back(jnp.dot(attended, out_weight, precision=highest))
    normed_two = low(layer_norm(middle, norm_scale[1], norm_shift[1]))
    gate_up = low_back(jnp.einsum('rd,dcf->rcf', normed_two, gate_up_weight, precision=highest))
    hidden = low(jax.nn.silu(gate_up[:, 0]) * gate_up[:, 1])
    return middle + jnp.dot(hidden, down_weight, precision=highest)

def reference(layer_in, norm_gain, norm_bias, w_qkv, b_qkv, w_out, w_gate_up, w_down, cotangent, block_table, seq_ids):
    row_ids = jnp.arange(TOKENS, dtype=jnp.int32)
    natural = block_table.reshape(-1)[row_ids // BLK].astype(jnp.int32)
    places = (natural * BLK + row_ids % BLK).astype(jnp.int32)
    sequence = seq_ids[natural].astype(jnp.int32)

    def run(inputs, norm_scale, norm_shift, qkv_weight, qkv_bias, out_weight, gate_up_weight, down_weight):
        return forward(inputs, norm_scale, norm_shift, qkv_weight, qkv_bias, out_weight, gate_up_weight, down_weight, places, sequence)
    result, pullback = jax.vjp(run, layer_in.astype(jnp.float32), norm_gain.astype(jnp.float32), norm_bias.astype(jnp.float32), w_qkv.astype(jnp.float32), b_qkv.astype(jnp.float32), w_out.astype(jnp.float32), w_gate_up.astype(jnp.float32), w_down.astype(jnp.float32))
    gradients = pullback(cotangent.astype(jnp.float32))
    return (result.astype(jnp.bfloat16), gradients[0].astype(jnp.bfloat16), gradients[1], gradients[2], gradients[3], gradients[4], gradients[5], gradients[6], gradients[7])
```

```python
import math

import jax
import jax.numpy as jnp
from jax import lax
from jax.experimental import pallas as pl
from jax.experimental.pallas import tpu as pltpu
from jax.sharding import PartitionSpec as P

HEAD = 64
ROT = 16
BLK = 512
EXTRA = 16

epsilon = 1e-05
neg_large = -1e30
bf16 = jnp.bfloat16
f32 = jnp.float32


def dot(left, right, left_dim, right_dim):
    return lax.dot_general(
        left, right, (((left_dim,), (right_dim,)), ((), ())), preferred_element_type=f32
    )


def causal_keep():
    return lax.broadcasted_iota(jnp.int32, (BLK, BLK), 0) <= lax.broadcasted_iota(
        jnp.int32, (BLK, BLK), 1
    )


def turn(tile):
    return tile.astype(f32).T.astype(bf16)


def attention_forward(order, qkv):
    blocks = qkv.shape[0]

    def kernel(order, qkv, out, logsum, keys, values):
        row = lax.broadcasted_iota(jnp.int32, (EXTRA, BLK), 0)
        ones = jnp.where(row == 0, 1.0, 0.0).astype(bf16)

        def prepare(place, carry):
            keys[place] = turn(qkv[place, HEAD : 2 * HEAD, :])
            values[place, 0:HEAD, :] = qkv[place, 2 * HEAD : 3 * HEAD, :]
            values[place, HEAD : HEAD + EXTRA, :] = ones
            return carry

        lax.fori_loop(0, blocks, prepare, 0)
        keep = causal_keep()

        def query_block(i, carry):
            place = order[i]
            query = qkv[place, 0:HEAD, :] * jnp.asarray(HEAD**-0.5, bf16)

            def step(j, state, masked):
                maxima, summed = state
                other = order[j]
                scores = dot(keys[other], query, 1, 0)
                if masked:
                    scores = jnp.where(keep, scores, neg_large)
                new_maxima = jnp.maximum(maxima, jnp.max(scores, axis=0, keepdims=True))
                weights = jnp.exp(scores - new_maxima).astype(bf16)
                summed = summed * jnp.exp(maxima - new_maxima) + dot(values[other], weights, 1, 0)
                return new_maxima, summed

            state = (jnp.full((1, BLK), neg_large, f32), jnp.zeros((HEAD + EXTRA, BLK), f32))
            state = lax.fori_loop(order[blocks + i], i, lambda j, s: step(j, s, False), state)
            maxima, summed = step(i, state, True)
            totals = summed[HEAD : HEAD + 1]
            out[place] = (summed[0:HEAD] / totals).astype(bf16)
            logsum[place] = maxima + jnp.log(totals)
            return carry

        lax.fori_loop(0, blocks, query_block, 0)

    vmem = pl.BlockSpec(memory_space=pltpu.VMEM)
    return pl.pallas_call(
        kernel,
        out_shape=(
            jax.ShapeDtypeStruct((blocks, HEAD, BLK), bf16),
            jax.ShapeDtypeStruct((blocks, 1, BLK), f32),
        ),
        in_specs=[pl.BlockSpec(memory_space=pltpu.SMEM), vmem],
        out_specs=(vmem, vmem),
        scratch_shapes=[
            pltpu.VMEM((blocks, BLK, HEAD), bf16),
            pltpu.VMEM((blocks, HEAD + EXTRA, BLK), bf16),
        ],
        compiler_params=pltpu.CompilerParams(vmem_limit_bytes=48 * 2**20),
        cost_estimate=pl.CostEstimate(
            flops=85 * 2 * 2 * BLK * BLK * 256, bytes_accessed=5 * 2**20, transcendentals=0
        ),
        name="attention_forward",
    )(order, qkv)


def attention_backward(order, qkv, grad_out, out, logsum):
    blocks = qkv.shape[0]
    wide = HEAD + EXTRA

    def kernel(order, qkv, grad_out, out, logsum, grads, query_x, grad_x, key_x, value_x, grad_q):
        row = lax.broadcasted_iota(jnp.int32, (EXTRA, BLK), 0)
        lane = lax.broadcasted_iota(jnp.int32, (BLK, EXTRA), 1)
        ones = jnp.where(lane < 3, 1.0, 0.0).astype(bf16)

        def three_rows(value):
            high = value.astype(bf16).astype(f32)
            rest = value - high
            middle = rest.astype(bf16).astype(f32)
            low = rest - middle
            return jnp.where(
                row == 0, high, jnp.where(row == 1, middle, jnp.where(row == 2, low, 0.0))
            ).astype(bf16)

        def prepare(place, carry):
            key_x[place, :, 0:HEAD] = turn(qkv[place, HEAD : 2 * HEAD, :])
            value_x[place, :, 0:HEAD] = turn(qkv[place, 2 * HEAD : 3 * HEAD, :])
            key_x[place, :, HEAD:wide] = ones
            value_x[place, :, HEAD:wide] = ones
            query_x[place, 0:HEAD, :] = qkv[place, 0:HEAD, :] * jnp.asarray(HEAD**-0.5, bf16)
            query_x[place, HEAD:wide, :] = three_rows(-logsum[place])
            grad = grad_out[place]
            delta = jnp.sum(grad.astype(f32) * out[place].astype(f32), axis=0, keepdims=True)
            grad_x[place, 0:HEAD, :] = grad
            grad_x[place, HEAD:wide, :] = three_rows(-delta)
            grad_q[place] = jnp.zeros((HEAD, BLK), f32)
            return carry

        lax.fori_loop(0, blocks, prepare, 0)
        keep = causal_keep()

        def key_block(j, carry):
            place = order[j]
            key, value = key_x[place], value_x[place]
            key_rows = qkv[place, HEAD : 2 * HEAD, :]

            def step(i, state, masked):
                grad_k, grad_v = state
                other = order[i]
                prob = jnp.exp(dot(key, query_x[other], 1, 0))
                if masked:
                    prob = jnp.where(keep, prob, 0.0)
                grad_raw = (prob * dot(value, grad_x[other], 1, 0)).astype(bf16)
                grad_v = grad_v + dot(grad_x[other, 0:HEAD, :], prob.astype(bf16), 1, 1)
                grad_k = grad_k + dot(query_x[other, 0:HEAD, :], grad_raw, 1, 1)
                grad_q[other] += dot(key_rows, grad_raw, 1, 0)
                return grad_k, grad_v

            zero = jnp.zeros((HEAD, BLK), f32)
            state = step(j, (zero, zero), True)
            grad_k, grad_v = lax.fori_loop(
                j + 1, order[2 * blocks + j] + 1, lambda i, s: step(i, s, False), state
            )
            grads[place, HEAD : 2 * HEAD, :] = grad_k.astype(bf16)
            grads[place, 2 * HEAD : 3 * HEAD, :] = grad_v.astype(bf16)
            return carry

        lax.fori_loop(0, blocks, key_block, 0)

        def finish(place, carry):
            grads[place, 0:HEAD, :] = (grad_q[place] * HEAD**-0.5).astype(bf16)
            return carry

        lax.fori_loop(0, blocks, finish, 0)

    vmem = pl.BlockSpec(memory_space=pltpu.VMEM)
    return pl.pallas_call(
        kernel,
        out_shape=jax.ShapeDtypeStruct((blocks, 3 * HEAD, BLK), bf16),
        in_specs=[pl.BlockSpec(memory_space=pltpu.SMEM), vmem, vmem, vmem, vmem],
        out_specs=vmem,
        scratch_shapes=[
            pltpu.VMEM((blocks, wide, BLK), bf16),
            pltpu.VMEM((blocks, wide, BLK), bf16),
            pltpu.VMEM((blocks, BLK, wide), bf16),
            pltpu.VMEM((blocks, BLK, wide), bf16),
            pltpu.VMEM((blocks, HEAD, BLK), f32),
        ],
        compiler_params=pltpu.CompilerParams(vmem_limit_bytes=56 * 2**20),
        cost_estimate=pl.CostEstimate(
            flops=85 * 5 * 2 * BLK * BLK * 256, bytes_accessed=10 * 2**20, transcendentals=0
        ),
        name="attention_backward",
    )(order, qkv, grad_out, out, logsum)


def row_places(first_row, length, table_flat, seq_ids):
    row_ids = first_row + jnp.arange(length, dtype=jnp.int32)
    block_ids = jnp.arange(table_flat.shape[0], dtype=jnp.int32)
    natural = jnp.sum(
        jnp.where((row_ids // BLK)[:, None] == block_ids[None, :], table_flat[None, :], 0), axis=1
    )
    sequence = jnp.sum(
        jnp.where(natural[:, None] == block_ids[None, :], seq_ids[None, :], 0), axis=1
    )
    return (natural * BLK + row_ids % BLK, sequence)


def gathered_setup(rows, table_flat, seq_ids, key_flat, value_flat):
    places, seq = row_places(lax.axis_index("ctx") * rows, rows, table_flat, seq_ids)
    pieces = (
        lax.all_gather(key_flat, "ctx", axis=0, tiled=True),
        lax.all_gather(value_flat, "ctx", axis=0, tiled=True),
    )
    stride = math.gcd(pieces[0].shape[0], 1024)
    offsets = jnp.arange(pieces[0].shape[0] // stride, dtype=jnp.int32) * stride

    def visit(offset):
        other_places, other_seq = row_places(offset, stride, table_flat, seq_ids)
        allowed = (seq[:, None] == other_seq[None, :]) & (other_places[None, :] <= places[:, None])
        blocks = [
            lax.dynamic_slice_in_dim(piece, offset, stride, 0).reshape(stride, -1, HEAD)
            for piece in pieces
        ]
        return allowed[:, None, :], blocks[0], blocks[1]

    return visit, offsets


def gathered_forward(queries, visit, offsets):
    rows, heads, _ = queries.shape

    def step(status, offset):
        allowed, keys, values = visit(offset)
        scores = jnp.einsum("qhe,khe->qhk", queries, keys, preferred_element_type=f32)
        scores = scores * HEAD**-0.5
        maxima, totals, summed = status
        new_maxima = jnp.maximum(maxima, jnp.max(jnp.where(allowed, scores, neg_large), axis=2))
        weights = jnp.where(allowed, jnp.exp(scores - new_maxima[..., None]), 0.0)
        factor = jnp.exp(maxima - new_maxima)
        totals = totals * factor + jnp.sum(weights, axis=2)
        summed = summed * factor[..., None] + jnp.einsum(
            "qhk,khe->qhe", weights.astype(bf16), values, preferred_element_type=f32
        )
        return ((new_maxima, totals, summed), None)

    initial = (
        jnp.full((rows, heads), neg_large, f32),
        jnp.zeros((rows, heads), f32),
        jnp.zeros((rows, heads, HEAD), f32),
    )
    (maxima, totals, summed), _ = lax.scan(step, initial, offsets)
    return summed / totals[..., None], maxima + jnp.log(totals)


def gathered_backward(queries, visit, offsets, grad_att, attended, logsum):
    rows, heads, _ = queries.shape
    delta = jnp.sum(grad_att.astype(f32) * attended, axis=2)

    def step(status, offset):
        allowed, keys, values = visit(offset)
        scores = jnp.einsum("qhe,khe->qhk", queries, keys, preferred_element_type=f32)
        prob = jnp.where(allowed, jnp.exp(scores * HEAD**-0.5 - logsum[..., None]), 0.0)
        grad_prob = jnp.einsum("qhe,khe->qhk", grad_att, values, preferred_element_type=f32)
        grad_raw = (prob * (grad_prob - delta[..., None]) * HEAD**-0.5).astype(bf16)
        grad_q = jnp.einsum("qhk,khe->qhe", grad_raw, keys, preferred_element_type=f32)
        grad_k = jnp.einsum("qhk,qhe->khe", grad_raw, queries, preferred_element_type=f32)
        grad_v = jnp.einsum("qhk,qhe->khe", prob.astype(bf16), grad_att, preferred_element_type=f32)
        return (
            (
                status[0] + grad_q,
                lax.dynamic_update_slice_in_dim(status[1], grad_k, offset, 0),
                lax.dynamic_update_slice_in_dim(status[2], grad_v, offset, 0),
            ),
            None,
        )

    total = rows * lax.axis_size("ctx")
    zero = jnp.zeros((total, heads, HEAD), f32)
    (grad_q, grad_k, grad_v), _ = lax.scan(
        step, (jnp.zeros((rows, heads, HEAD), f32), zero, zero), offsets
    )
    grad_k = lax.psum_scatter(grad_k, "ctx", scatter_dimension=0, tiled=True)
    grad_v = lax.psum_scatter(grad_v, "ctx", scatter_dimension=0, tiled=True)
    return grad_q, grad_k, grad_v


def norm_stats(rows):
    mean = jnp.mean(rows, axis=1, keepdims=True)
    center = rows - mean
    inverse = lax.rsqrt(jnp.mean(center * center, axis=1, keepdims=True) + epsilon)
    return mean, inverse


def norm_backward(grad_out, normed, inverse, gain):
    scaled = grad_out * gain
    grad_rows = inverse * (
        scaled
        - jnp.mean(scaled, axis=1, keepdims=True)
        - normed * jnp.mean(scaled * normed, axis=1, keepdims=True)
    )
    return (grad_rows, jnp.sum(grad_out * normed, axis=0), jnp.sum(grad_out, axis=0))


def rotate(tensor, places, direction):
    half = ROT // 2
    frequency = 10000.0 ** (-2.0 * jnp.arange(half, dtype=f32) / ROT)
    angles = frequency[:, None] * places.astype(f32)[None, :]
    cosine, sines = jnp.cos(angles), direction * jnp.sin(angles)
    first, second = tensor[..., :half, :], tensor[..., half:ROT, :]
    return jnp.concatenate(
        [
            first * cosine - second * sines,
            second * cosine + first * sines,
            tensor[..., ROT:, :],
        ],
        axis=-2,
    )


def gather(rows, axis):
    return lax.all_gather(rows, axis, axis=0, tiled=True)


def scatter(partial, axis, dim=0):
    return lax.psum_scatter(partial, axis, scatter_dimension=dim, tiled=True)


def sum_over_ctx(partial):
    lead = partial.shape
    part = scatter(partial.astype(bf16).reshape(lead[0], -1), "ctx")
    return gather(part, "ctx").reshape(lead).astype(f32)


def shards(
    layer_in,
    norm_gain,
    norm_bias,
    w_qkv,
    b_qkv,
    w_out,
    w_gate_up,
    w_down,
    cotangent,
    block_table,
    seq_ids,
):
    n_ctx, n_tp = lax.axis_size("ctx"), lax.axis_size("tp")
    ctx, tp = lax.axis_index("ctx"), lax.axis_index("tp")
    own, width = layer_in.shape
    rows = own * n_tp
    cols = w_qkv.shape[2]
    heads = cols // HEAD
    table = block_table.reshape(-1)
    blocks = table.shape[0]
    per_ctx = rows // BLK
    by_head = heads == n_ctx
    part = cols // n_ctx

    ids = jnp.arange(blocks, dtype=jnp.int32)
    located = jnp.sum(jnp.where(table[None, :] == ids[:, None], ids[None, :], 0), axis=1)
    same = seq_ids[:, None] == seq_ids[None, :]
    first = jnp.min(jnp.where(same, ids[None, :], blocks), axis=1)
    last = jnp.max(jnp.where(same, ids[None, :], -1), axis=1)
    order = jnp.concatenate([located, first, last]).astype(jnp.int32)
    places, _ = row_places(ctx * rows, rows, table, seq_ids)

    inputs = gather(layer_in, "tp")
    cot = gather(cotangent, "tp")
    w_part = lax.dynamic_slice_in_dim(w_out, ctx * part, part, 0)
    w_out_all = gather(w_part, ("tp", "ctx"))

    x = inputs.astype(f32)
    mean_one, inverse_one = norm_stats(x)
    first_low = ((x - mean_one) * inverse_one * norm_gain[0] + norm_bias[0]).astype(bf16)
    projected = (
        jnp.einsum("dcf,rd->cfr", w_qkv, first_low, preferred_element_type=f32)
        + b_qkv[:, :, None]
    ).reshape(3, heads, HEAD, rows)
    qkv = jnp.concatenate(
        [rotate(projected[0:2], places, 1.0).astype(bf16), projected[2:3].astype(bf16)], axis=0
    )

    if by_head:
        packed = (
            qkv.reshape(3, heads, HEAD, per_ctx, BLK)
            .transpose(1, 3, 0, 2, 4)
            .reshape(n_ctx, per_ctx, 3 * HEAD, BLK)
        )
        packed = lax.all_to_all(packed, "ctx", split_axis=0, concat_axis=0, tiled=True)
        packed = packed.reshape(blocks, 3 * HEAD, BLK)
        out, logsum = attention_forward(order, packed)
        attended = lax.all_to_all(
            out.reshape(n_ctx, per_ctx, HEAD, BLK), "ctx", split_axis=0, concat_axis=0, tiled=True
        )
        attended = attended.transpose(0, 2, 1, 3).reshape(cols, rows)
    else:
        queries, keys, values = [t.transpose(2, 0, 1) for t in qkv]
        visit, offsets = gathered_setup(
            rows, table, seq_ids, keys.reshape(rows, cols), values.reshape(rows, cols)
        )
        out, logsum = gathered_forward(queries, visit, offsets)
        attended = out.astype(bf16).reshape(rows, cols).T

    attended_all = gather(attended, "tp")
    middle = x + jnp.einsum("fr,fd->rd", attended_all, w_out_all, preferred_element_type=f32)
    mean_two, inverse_two = norm_stats(middle)
    normed_two = (middle - mean_two) * inverse_two
    second_low = (normed_two * norm_gain[1] + norm_bias[1]).astype(bf16)

    gate_up = jnp.einsum("rd,dcf->rcf", second_low, w_gate_up, preferred_element_type=f32)
    gate, up = gate_up[:, 0], gate_up[:, 1]
    sigmoid = jax.nn.sigmoid(gate)
    activated = gate * sigmoid
    hidden = (activated * up).astype(bf16)
    down = scatter(jnp.dot(hidden, w_down, preferred_element_type=f32).astype(bf16), "tp")
    own_middle = lax.dynamic_slice_in_dim(middle, tp * own, own, 0)
    layer_out = (own_middle + down.astype(f32)).astype(bf16)

    grad_down = lax.dot_general(hidden, cot, (((0,), (0,)), ((), ())), preferred_element_type=f32)
    grad_hidden = lax.dot_general(cot, w_down, (((1,), (1,)), ((), ())), preferred_element_type=f32)
    grad_gate = grad_hidden * up * sigmoid * (1.0 + gate * (1.0 - sigmoid))
    grad_gu = jnp.stack([grad_gate, grad_hidden * activated], axis=1).astype(bf16)
    grad_gate_up = jnp.einsum("rd,rcf->dcf", second_low, grad_gu, preferred_element_type=f32)
    grad_second = jnp.einsum("rcf,dcf->rd", grad_gu, w_gate_up, preferred_element_type=f32)

    middle_norm, gain_two, bias_two = norm_backward(
        grad_second, normed_two, inverse_two, norm_gain[1]
    )
    is_own = (jnp.arange(rows, dtype=jnp.int32) // own == tp)[:, None]
    middle_term = (middle_norm + jnp.where(is_own, cot.astype(f32), 0.0)).astype(bf16)
    grad_att = scatter(
        jnp.einsum("fd,rd->fr", w_out_all, middle_term, preferred_element_type=f32).astype(bf16),
        "tp",
    )
    out_proj = jnp.einsum("fr,rd->fd", attended_all, middle_term, preferred_element_type=f32)

    if by_head:
        grad_packed = grad_att.reshape(heads, HEAD, per_ctx, BLK).transpose(0, 2, 1, 3)
        grad_packed = lax.all_to_all(
            grad_packed, "ctx", split_axis=0, concat_axis=0, tiled=True
        ).reshape(blocks, HEAD, BLK)
        grads = attention_backward(order, packed, grad_packed, out, logsum)
        grads = lax.all_to_all(
            grads.reshape(n_ctx, per_ctx, 3 * HEAD, BLK),
            "ctx",
            split_axis=0,
            concat_axis=0,
            tiled=True,
        )
        grads = (
            grads.reshape(heads, per_ctx, 3, HEAD, BLK)
            .transpose(2, 0, 3, 1, 4)
            .reshape(3, heads, HEAD, rows)
            .astype(f32)
        )
    else:
        grads = gathered_backward(
            queries, visit, offsets, grad_att.T.reshape(rows, heads, HEAD), out, logsum
        )
        grads = jnp.stack([t.transpose(1, 2, 0) for t in grads])
    grad_projected = jnp.concatenate([rotate(grads[0:2], places, -1.0), grads[2:3]], axis=0)
    grad_projected = grad_projected.reshape(3, cols, rows).astype(bf16)

    grad_first = jnp.einsum("cfr,dcf->rd", grad_projected, w_qkv, preferred_element_type=f32)
    input_norm, gain_one, bias_one = norm_backward(
        grad_first, (x - mean_one) * inverse_one, inverse_one, norm_gain[0]
    )
    grad_input = scatter((middle_norm + input_norm).astype(bf16), "tp")
    grad_input = (cotangent.astype(f32) + grad_input.astype(f32)).astype(bf16)
    grad_qkv = jnp.einsum("rd,cfr->dcf", first_low, grad_projected, preferred_element_type=f32)
    bias_qkv = lax.psum(jnp.sum(grad_projected.astype(f32), axis=2), "ctx")

    out_proj = out_proj.astype(bf16).reshape(n_tp, n_ctx, part, width)
    out_proj = scatter(scatter(out_proj, "ctx", 1).reshape(n_tp, part, width), "tp")
    out_proj = gather(out_proj.reshape(part, width), "ctx").astype(f32)

    gains, biases = lax.psum(
        (jnp.stack([gain_one, gain_two]), jnp.stack([bias_one, bias_two])), ("ctx", "tp")
    )
    return (
        layer_out,
        grad_input,
        gains,
        biases,
        sum_over_ctx(grad_qkv),
        bias_qkv,
        out_proj,
        sum_over_ctx(grad_gate_up),
        sum_over_ctx(grad_down),
    )


def solution(mesh):
    placed = (
        P(("ctx", "tp"), None),
        P(),
        P(),
        P(None, None, "tp"),
        P(None, "tp"),
        P("tp", None),
        P(None, None, "tp"),
        P("tp", None),
        P(("ctx", "tp"), None),
        P(),
        P(),
    )
    return jax.shard_map(
        shards,
        mesh=mesh,
        in_specs=placed,
        out_specs=(
            P(("ctx", "tp"), None),
            P(("ctx", "tp"), None),
            P(),
            P(),
            P(None, None, "tp"),
            P(None, "tp"),
            P("tp", None),
            P(None, None, "tp"),
            P("tp", None),
        ),
        check_vma=False,
    )
```

```python
import math

import jax
import jax.numpy as jnp
from jax import lax
from jax.experimental import pallas as pl
from jax.experimental.pallas import tpu as pltpu
from jax.sharding import PartitionSpec as P

HEAD = 64
ROT = 16
BLK = 512
EXTRA = 16

epsilon = 1e-05
neg_large = -1e30
bf16 = jnp.bfloat16
f32 = jnp.float32


def dot(left, right, left_dim, right_dim):
    return lax.dot_general(
        left, right, (((left_dim,), (right_dim,)), ((), ())), preferred_element_type=f32
    )


def causal_keep():
    return lax.broadcasted_iota(jnp.int32, (BLK, BLK), 0) <= lax.broadcasted_iota(
        jnp.int32, (BLK, BLK), 1
    )


def turn(tile):
    return tile.astype(f32).T.astype(bf16)


def scan_chunks(devices, chunks, width, visit):
    per_block = BLK // width

    def source(device, carry):
        for chunk in range(chunks):
            place = device * (chunks // per_block) + chunk // per_block
            visit(chunk, device, place, slice((chunk % per_block) * width, (chunk % per_block + 1) * width))
        return carry

    lax.fori_loop(0, devices, source, 0)


def turn_dims(tile, cosine, sine):
    half = ROT // 2
    first, second = tile[0:half], tile[half:ROT]
    return jnp.concatenate(
        [first * cosine - second * sine, second * cosine + first * sine, tile[ROT:]], axis=0
    )


def attention_forward(order, angles, packed):
    count, devices, _, _, width = packed.shape
    blocks = devices * count * width // BLK

    def kernel(order, angles, packed, out, logsum, queries, keys, values):
        per_device = count * width // BLK
        row = lax.broadcasted_iota(jnp.int32, (EXTRA, BLK), 0)
        ones = jnp.where(row == 0, 1.0, 0.0).astype(bf16)

        def visit(chunk, device, place, lanes):
            part = packed.at[chunk]
            cosine, sine = angles[place, 0, :, lanes], angles[place, 1, :, lanes]
            query = turn_dims(part[device, 0].astype(f32), cosine, sine).astype(bf16)
            queries[place, :, lanes] = query * jnp.asarray(HEAD**-0.5, bf16)
            key = turn_dims(part[device, 1].astype(f32), cosine, sine).astype(bf16)
            keys[place, lanes, :] = turn(key)
            values[place, 0:HEAD, lanes] = part[device, 2]

        scan_chunks(devices, count, width, visit)

        def prepare(place, carry):
            values[place, HEAD : HEAD + EXTRA, :] = ones
            return carry

        lax.fori_loop(0, blocks, prepare, 0)
        keep = causal_keep()

        def query_block(i, carry):
            place = order[i]
            query = queries[place]

            def step(j, state, masked):
                maxima, summed = state
                other = order[j]
                scores = dot(keys[other], query, 1, 0)
                if masked:
                    scores = jnp.where(keep, scores, neg_large)
                new_maxima = jnp.maximum(maxima, jnp.max(scores, axis=0, keepdims=True))
                weights = jnp.exp(scores - new_maxima).astype(bf16)
                summed = summed * jnp.exp(maxima - new_maxima) + dot(values[other], weights, 1, 0)
                return new_maxima, summed

            state = (jnp.full((1, BLK), neg_large, f32), jnp.zeros((HEAD + EXTRA, BLK), f32))
            state = lax.fori_loop(order[blocks + i], i, lambda j, s: step(j, s, False), state)
            maxima, summed = step(i, state, True)
            totals = summed[HEAD : HEAD + 1]
            result = (summed[0:HEAD] / totals).astype(bf16)
            logsum[place] = maxima + jnp.log(totals)
            lane = pl.multiple_of(lax.rem(place, per_device) * BLK, BLK)
            out[place // per_device, :, pl.ds(lane, BLK)] = result
            return carry

        lax.fori_loop(0, blocks, query_block, 0)

    vmem = pl.BlockSpec(memory_space=pltpu.VMEM)
    return pl.pallas_call(
        kernel,
        out_shape=(
            jax.ShapeDtypeStruct((devices, HEAD, count * width), bf16),
            jax.ShapeDtypeStruct((blocks, 1, BLK), f32),
        ),
        in_specs=[pl.BlockSpec(memory_space=pltpu.SMEM), vmem, vmem],
        out_specs=(vmem, vmem),
        scratch_shapes=[
            pltpu.VMEM((blocks, HEAD, BLK), bf16),
            pltpu.VMEM((blocks, BLK, HEAD), bf16),
            pltpu.VMEM((blocks, HEAD + EXTRA, BLK), bf16),
        ],
        compiler_params=pltpu.CompilerParams(vmem_limit_bytes=48 * 2**20),
        cost_estimate=pl.CostEstimate(
            flops=85 * 2 * 2 * BLK * BLK * 256, bytes_accessed=5 * 2**20, transcendentals=0
        ),
        name="attention_forward",
    )(order, angles, packed)


def attention_backward(order, angles, packed, grad_out, out, logsum):
    count, devices, _, _, width = packed.shape
    blocks = devices * count * width // BLK
    wide = HEAD + EXTRA

    def kernel(
        order, angles, packed, grad_out, out, logsum,
        grads, query_x, grad_x, key_x, key_rows, value_x, grad_q,
    ):
        row = lax.broadcasted_iota(jnp.int32, (EXTRA, width), 0)
        lane_ids = lax.broadcasted_iota(jnp.int32, (BLK, EXTRA), 1)
        ones = jnp.where(lane_ids < 3, 1.0, 0.0).astype(bf16)

        def three_rows(value):
            high = value.astype(bf16).astype(f32)
            rest = value - high
            middle = rest.astype(bf16).astype(f32)
            low = rest - middle
            return jnp.where(
                row == 0, high, jnp.where(row == 1, middle, jnp.where(row == 2, low, 0.0))
            ).astype(bf16)

        def visit(chunk, device, place, lanes):
            part = packed.at[chunk]
            cosine, sine = angles[place, 0, :, lanes], angles[place, 1, :, lanes]
            query = turn_dims(part[device, 0].astype(f32), cosine, sine).astype(bf16)
            query_x[place, 0:HEAD, lanes] = query * jnp.asarray(HEAD**-0.5, bf16)
            query_x[place, HEAD:wide, lanes] = three_rows(-logsum[place, :, lanes])
            key = turn_dims(part[device, 1].astype(f32), cosine, sine).astype(bf16)
            key_rows[place, :, lanes] = key
            key_x[place, lanes, 0:HEAD] = turn(key)
            value_x[place, lanes, 0:HEAD] = turn(part[device, 2])
            own = slice(chunk * width, (chunk + 1) * width)
            grad = grad_out[device, :, own]
            delta = jnp.sum(
                grad.astype(f32) * out[device, :, own].astype(f32), axis=0, keepdims=True
            )
            grad_x[place, 0:HEAD, lanes] = grad
            grad_x[place, HEAD:wide, lanes] = three_rows(-delta)

        scan_chunks(devices, count, width, visit)

        def prepare(place, carry):
            key_x[place, :, HEAD:wide] = ones
            value_x[place, :, HEAD:wide] = ones
            grad_q[place] = jnp.zeros((HEAD, BLK), f32)
            return carry

        lax.fori_loop(0, blocks, prepare, 0)
        keep = causal_keep()
        per_device = count * width // BLK

        def store(part, place, tile):
            lane = pl.multiple_of(lax.rem(place, per_device) * BLK, BLK)
            grads[place // per_device, part, :, pl.ds(lane, BLK)] = tile

        def key_block(j, carry):
            place = order[j]
            key, value = key_x[place], value_x[place]
            key_tile = key_rows[place]

            def step(i, state, masked):
                grad_k, grad_v = state
                other = order[i]
                prob = jnp.exp(dot(key, query_x[other], 1, 0))
                if masked:
                    prob = jnp.where(keep, prob, 0.0)
                grad_raw = (prob * dot(value, grad_x[other], 1, 0)).astype(bf16)
                grad_v = grad_v + dot(grad_x[other, 0:HEAD, :], prob.astype(bf16), 1, 1)
                grad_k = grad_k + dot(query_x[other, 0:HEAD, :], grad_raw, 1, 1)
                grad_q[other] += dot(key_tile, grad_raw, 1, 0)
                return grad_k, grad_v

            zero = jnp.zeros((HEAD, BLK), f32)
            state = step(j, (zero, zero), True)
            grad_k, grad_v = lax.fori_loop(
                j + 1, order[2 * blocks + j] + 1, lambda i, s: step(i, s, False), state
            )
            cosine, sine = angles[place, 0], angles[place, 1]
            store(1, place, turn_dims(grad_k, cosine, -sine).astype(bf16))
            store(2, place, grad_v.astype(bf16))
            return carry

        lax.fori_loop(0, blocks, key_block, 0)

        def finish(place, carry):
            tile = turn_dims(grad_q[place] * HEAD**-0.5, angles[place, 0], -angles[place, 1])
            store(0, place, tile.astype(bf16))
            return carry

        lax.fori_loop(0, blocks, finish, 0)

    vmem = pl.BlockSpec(memory_space=pltpu.VMEM)
    return pl.pallas_call(
        kernel,
        out_shape=jax.ShapeDtypeStruct((devices, 3, HEAD, count * width), bf16),
        in_specs=[pl.BlockSpec(memory_space=pltpu.SMEM)] + [vmem] * 5,
        out_specs=vmem,
        scratch_shapes=[
            pltpu.VMEM((blocks, wide, BLK), bf16),
            pltpu.VMEM((blocks, wide, BLK), bf16),
            pltpu.VMEM((blocks, BLK, wide), bf16),
            pltpu.VMEM((blocks, HEAD, BLK), bf16),
            pltpu.VMEM((blocks, BLK, wide), bf16),
            pltpu.VMEM((blocks, HEAD, BLK), f32),
        ],
        compiler_params=pltpu.CompilerParams(vmem_limit_bytes=56 * 2**20),
        cost_estimate=pl.CostEstimate(
            flops=85 * 5 * 2 * BLK * BLK * 256, bytes_accessed=10 * 2**20, transcendentals=0
        ),
        name="attention_backward",
    )(order, angles, packed, grad_out, out, logsum)


def row_places(first_row, length, table_flat, seq_ids):
    row_ids = first_row + jnp.arange(length, dtype=jnp.int32)
    block_ids = jnp.arange(table_flat.shape[0], dtype=jnp.int32)
    natural = jnp.sum(
        jnp.where((row_ids // BLK)[:, None] == block_ids[None, :], table_flat[None, :], 0), axis=1
    )
    sequence = jnp.sum(
        jnp.where(natural[:, None] == block_ids[None, :], seq_ids[None, :], 0), axis=1
    )
    return (natural * BLK + row_ids % BLK, sequence)


def gathered_setup(rows, table_flat, seq_ids, key_flat, value_flat):
    places, seq = row_places(lax.axis_index("ctx") * rows, rows, table_flat, seq_ids)
    pieces = (
        lax.all_gather(key_flat, "ctx", axis=0, tiled=True),
        lax.all_gather(value_flat, "ctx", axis=0, tiled=True),
    )
    stride = math.gcd(pieces[0].shape[0], 1024)
    offsets = jnp.arange(pieces[0].shape[0] // stride, dtype=jnp.int32) * stride

    def visit(offset):
        other_places, other_seq = row_places(offset, stride, table_flat, seq_ids)
        allowed = (seq[:, None] == other_seq[None, :]) & (other_places[None, :] <= places[:, None])
        blocks = [
            lax.dynamic_slice_in_dim(piece, offset, stride, 0).reshape(stride, -1, HEAD)
            for piece in pieces
        ]
        return allowed[:, None, :], blocks[0], blocks[1]

    return visit, offsets


def gathered_forward(queries, visit, offsets):
    rows, heads, _ = queries.shape

    def step(status, offset):
        allowed, keys, values = visit(offset)
        scores = jnp.einsum("qhe,khe->qhk", queries, keys, preferred_element_type=f32)
        scores = scores * HEAD**-0.5
        maxima, totals, summed = status
        new_maxima = jnp.maximum(maxima, jnp.max(jnp.where(allowed, scores, neg_large), axis=2))
        weights = jnp.where(allowed, jnp.exp(scores - new_maxima[..., None]), 0.0)
        factor = jnp.exp(maxima - new_maxima)
        totals = totals * factor + jnp.sum(weights, axis=2)
        summed = summed * factor[..., None] + jnp.einsum(
            "qhk,khe->qhe", weights.astype(bf16), values, preferred_element_type=f32
        )
        return ((new_maxima, totals, summed), None)

    initial = (
        jnp.full((rows, heads), neg_large, f32),
        jnp.zeros((rows, heads), f32),
        jnp.zeros((rows, heads, HEAD), f32),
    )
    (maxima, totals, summed), _ = lax.scan(step, initial, offsets)
    return summed / totals[..., None], maxima + jnp.log(totals)


def gathered_backward(queries, visit, offsets, grad_att, attended, logsum):
    rows, heads, _ = queries.shape
    delta = jnp.sum(grad_att.astype(f32) * attended, axis=2)

    def step(status, offset):
        allowed, keys, values = visit(offset)
        scores = jnp.einsum("qhe,khe->qhk", queries, keys, preferred_element_type=f32)
        prob = jnp.where(allowed, jnp.exp(scores * HEAD**-0.5 - logsum[..., None]), 0.0)
        grad_prob = jnp.einsum("qhe,khe->qhk", grad_att, values, preferred_element_type=f32)
        grad_raw = (prob * (grad_prob - delta[..., None]) * HEAD**-0.5).astype(bf16)
        grad_q = jnp.einsum("qhk,khe->qhe", grad_raw, keys, preferred_element_type=f32)
        grad_k = jnp.einsum("qhk,qhe->khe", grad_raw, queries, preferred_element_type=f32)
        grad_v = jnp.einsum("qhk,qhe->khe", prob.astype(bf16), grad_att, preferred_element_type=f32)
        return (
            (
                status[0] + grad_q,
                lax.dynamic_update_slice_in_dim(status[1], grad_k, offset, 0),
                lax.dynamic_update_slice_in_dim(status[2], grad_v, offset, 0),
            ),
            None,
        )

    total = rows * lax.axis_size("ctx")
    zero = jnp.zeros((total, heads, HEAD), f32)
    (grad_q, grad_k, grad_v), _ = lax.scan(
        step, (jnp.zeros((rows, heads, HEAD), f32), zero, zero), offsets
    )
    grad_k = lax.psum_scatter(grad_k, "ctx", scatter_dimension=0, tiled=True)
    grad_v = lax.psum_scatter(grad_v, "ctx", scatter_dimension=0, tiled=True)
    return grad_q, grad_k, grad_v


MESH = pl.DeviceIdType.MESH


def greet(n_ctx, n_tp):
    ctx, tp = lax.axis_index("ctx"), lax.axis_index("tp")
    barrier = pltpu.get_barrier_semaphore()

    def greet_ctx(step, carry):
        peer = lax.rem(ctx + step, n_ctx)
        pl.semaphore_signal(barrier, inc=1, device_id=(peer, tp), device_id_type=MESH)
        return carry

    lax.fori_loop(1, n_ctx, greet_ctx, 0)
    for peer in (lax.rem(tp + 1, n_tp), lax.rem(tp + n_tp - 1, n_tp)):
        pl.semaphore_signal(barrier, inc=1, device_id=(ctx, peer), device_id_type=MESH)
    pl.semaphore_wait(barrier, n_ctx + 1)


def rows_norm(source, stored, gain, shift, mean_out, inverse_out, tile):
    def step(i, carry):
        rows = pl.ds(pl.multiple_of(i * tile, tile), tile)
        x = source(rows)
        mean = jnp.mean(x, axis=1, keepdims=True)
        center = x - mean
        inverse = lax.rsqrt(jnp.mean(center * center, axis=1, keepdims=True) + epsilon)
        stored(rows, (center * inverse * gain + shift).astype(bf16))
        mean_out[rows, :] = jnp.broadcast_to(mean, (tile, 128))
        inverse_out[rows, :] = jnp.broadcast_to(inverse, (tile, 128))
        return carry

    return step


def project_exchange(layer_in, w_part, gain, shift, w_qkv, b_qkv):
    n_ctx, n_tp = lax.axis_size("ctx"), lax.axis_size("tp")
    own, width = layer_in.shape
    part = w_part.shape[0]
    cols = w_qkv.shape[2]

    def kernel(
        x_in, w_in, gain, shift, w_qkv, b_qkv,
        xs, lows, means, inverses, ws, packed,
        outgoing, ring_send, ring_recv, w_send, w_recv, send, recv,
    ):
        ctx, tp = lax.axis_index("ctx"), lax.axis_index("tp")
        right = lax.rem(tp + 1, n_tp)
        half = own // 2

        def block(slot):
            return lax.rem(tp - slot + n_tp, n_tp)

        def ring(step, piece):
            rows = pl.ds(piece * half, half)
            return pltpu.make_async_remote_copy(
                src_ref=x_in.at[rows] if step == 0 else xs.at[block(step), rows],
                dst_ref=xs.at[block(step), rows],
                send_sem=ring_send.at[step, piece],
                recv_sem=ring_recv.at[step, piece],
                device_id=(ctx, right),
                device_id_type=MESH,
            )

        def w_ring(step):
            return pltpu.make_async_remote_copy(
                src_ref=w_in if step == 0 else ws.at[block(step)],
                dst_ref=ws.at[block(step)],
                send_sem=w_send.at[step],
                recv_sem=w_recv.at[step],
                device_id=(ctx, right),
                device_id_type=MESH,
            )

        def exchange(slot, step):
            peer = lax.rem(ctx + step, n_ctx)
            return pltpu.make_async_remote_copy(
                src_ref=outgoing.at[slot, peer],
                dst_ref=packed.at[block(slot), ctx],
                send_sem=send.at[slot, step],
                recv_sem=recv.at[slot, step],
                device_id=(peer, tp),
                device_id_type=MESH,
            )

        greet(n_ctx, n_tp)
        for piece in range(2):
            ring(0, piece).start()
        xs[tp] = x_in[...]
        ws[tp] = w_in[...]
        for slot in range(n_tp):
            if slot > 0:
                for piece in range(2):
                    ring(slot - 1, piece).wait_recv()
                    if slot < n_tp - 1:
                        ring(slot, piece).start()
            if slot == n_tp - 2:
                w_ring(0).start()
            if slot == n_tp - 1:
                w_ring(0).wait_recv()
                w_ring(1).start()

            here = block(slot)

            def stored(rows, value, here=here):
                lows[here, rows, :] = value

            step = rows_norm(
                lambda rows, here=here: xs[here, rows, :].astype(f32),
                stored, gain[...], shift[...], means.at[here], inverses.at[here], 32,
            )
            lax.fori_loop(0, own // 32, step, 0)

            def project(c, carry, slot=slot, here=here):
                value = jnp.dot(lows[here], w_qkv[c], preferred_element_type=f32) + b_qkv[c]
                outgoing[slot, :, c] = value.T.astype(bf16).reshape(n_ctx, HEAD, own)
                return carry

            lax.fori_loop(0, 3, project, 0)
            lax.fori_loop(
                1, n_ctx, lambda step, c, slot=slot: (exchange(slot, step).start(), c)[1], 0
            )
            packed[here, ctx] = outgoing[slot, ctx]
        for step in range(1, n_tp - 1):
            w_ring(step).wait_recv()
            if step < n_tp - 2:
                w_ring(step + 1).start()
        for slot in range(n_tp):
            lax.fori_loop(
                1, n_ctx, lambda step, c, slot=slot: (exchange(slot, step).wait(), c)[1], 0
            )
        for step in range(n_tp - 1):
            w_ring(step).wait_send()
            for piece in range(2):
                ring(step, piece).wait_send()

    vmem = pl.BlockSpec(memory_space=pltpu.VMEM)
    return pl.pallas_call(
        kernel,
        out_shape=(
            jax.ShapeDtypeStruct((n_tp, own, width), bf16),
            jax.ShapeDtypeStruct((n_tp, own, width), bf16),
            jax.ShapeDtypeStruct((n_tp, own, 128), f32),
            jax.ShapeDtypeStruct((n_tp, own, 128), f32),
            jax.ShapeDtypeStruct((n_tp, part, width), bf16),
            jax.ShapeDtypeStruct((n_tp, n_ctx, 3, HEAD, own), bf16),
        ),
        in_specs=[vmem] * 6,
        out_specs=(vmem,) * 6,
        scratch_shapes=[
            pltpu.VMEM((n_tp, n_ctx, 3, HEAD, own), bf16),
            pltpu.SemaphoreType.DMA((n_tp - 1, 2)),
            pltpu.SemaphoreType.DMA((n_tp - 1, 2)),
            pltpu.SemaphoreType.DMA((n_tp - 1,)),
            pltpu.SemaphoreType.DMA((n_tp - 1,)),
            pltpu.SemaphoreType.DMA((n_tp, n_ctx)),
            pltpu.SemaphoreType.DMA((n_tp, n_ctx)),
        ],
        compiler_params=pltpu.CompilerParams(
            collective_id=1, has_side_effects=True, vmem_limit_bytes=48 * 2**20
        ),
        cost_estimate=pl.CostEstimate(
            flops=2 * n_tp * own * width * 3 * cols, bytes_accessed=20 * 2**20, transcendentals=0
        ),
        name="project_exchange",
    )(layer_in, w_part, gain, shift, w_qkv.transpose(1, 0, 2), b_qkv[:, None, :])


def output_project(out, xs, w_all, gain, shift):
    n_ctx, n_tp = lax.axis_size("ctx"), lax.axis_size("tp")
    own, width = xs.shape[1:]
    cols = w_all.shape[1]
    rows_all = n_tp * own

    def kernel(
        out, xs, w_all, gain, shift,
        middle, lows, means, inverses, raw,
        ring_send, ring_recv, send, recv, own_sem,
    ):
        ctx, tp = lax.axis_index("ctx"), lax.axis_index("tp")
        right = lax.rem(tp + 1, n_tp)
        half = cols // 2

        def block(slot):
            return lax.rem(tp - slot + n_tp, n_tp)

        def ring(step, piece):
            rows = pl.ds(piece * half, half)
            return pltpu.make_async_remote_copy(
                src_ref=raw.at[block(step), rows],
                dst_ref=raw.at[block(step), rows],
                send_sem=ring_send.at[step, piece],
                recv_sem=ring_recv.at[step, piece],
                device_id=(ctx, right),
                device_id_type=MESH,
            )

        def exchange(step):
            peer = lax.rem(ctx + step, n_ctx)
            return pltpu.make_async_remote_copy(
                src_ref=out.at[peer],
                dst_ref=raw.at[tp, pl.ds(pl.multiple_of(ctx * HEAD, HEAD), HEAD)],
                send_sem=send.at[step],
                recv_sem=recv.at[step],
                device_id=(peer, tp),
                device_id_type=MESH,
            )

        greet(n_ctx, n_tp)
        lax.fori_loop(1, n_ctx, lambda step, c: (exchange(step).start(), c)[1], 0)
        keep = pltpu.make_async_copy(
            out.at[ctx], raw.at[tp, pl.ds(pl.multiple_of(ctx * HEAD, HEAD), HEAD)], own_sem
        )
        keep.start()
        keep.wait()
        lax.fori_loop(1, n_ctx, lambda step, c: (exchange(step).wait_recv(), c)[1], 0)
        for piece in range(2):
            ring(0, piece).start()
        for slot in range(n_tp):
            if slot > 0:
                for piece in range(2):
                    ring(slot - 1, piece).wait_recv()
                    if slot < n_tp - 1:
                        ring(slot, piece).start()
            here = block(slot)

            def project(place, carry, slot=slot, here=here):
                lanes = pl.ds(pl.multiple_of(place * own, own), own)
                tile = raw[here, :, lanes].astype(f32).T.astype(bf16)
                value = jnp.dot(tile, w_all[here], preferred_element_type=f32)
                if slot == 0:
                    middle[place] = xs[place].astype(f32) + value
                else:
                    middle[place] += value
                return carry

            lax.fori_loop(0, n_tp, project, 0)
        for place in range(n_tp):

            def stored(rows, value, place=place):
                lows[place, rows, :] = value

            step = rows_norm(
                lambda rows, place=place: middle[place, rows, :],
                stored, gain[...], shift[...], means.at[place], inverses.at[place], 32,
            )
            lax.fori_loop(0, own // 32, step, 0)
        lax.fori_loop(1, n_ctx, lambda step, c: (exchange(step).wait_send(), c)[1], 0)
        for step in range(n_tp - 1):
            for piece in range(2):
                ring(step, piece).wait_send()

    vmem = pl.BlockSpec(memory_space=pltpu.VMEM)
    return pl.pallas_call(
        kernel,
        out_shape=(
            jax.ShapeDtypeStruct((n_tp, own, width), f32),
            jax.ShapeDtypeStruct((n_tp, own, width), bf16),
            jax.ShapeDtypeStruct((n_tp, own, 128), f32),
            jax.ShapeDtypeStruct((n_tp, own, 128), f32),
            jax.ShapeDtypeStruct((n_tp, cols, rows_all), bf16),
        ),
        in_specs=[vmem] * 5,
        out_specs=(vmem,) * 5,
        scratch_shapes=[
            pltpu.SemaphoreType.DMA((n_tp - 1, 2)),
            pltpu.SemaphoreType.DMA((n_tp - 1, 2)),
            pltpu.SemaphoreType.DMA((n_ctx,)),
            pltpu.SemaphoreType.DMA((n_ctx,)),
            pltpu.SemaphoreType.DMA,
        ],
        compiler_params=pltpu.CompilerParams(
            collective_id=2, has_side_effects=True, vmem_limit_bytes=56 * 2**20
        ),
        cost_estimate=pl.CostEstimate(
            flops=2 * rows_all * n_tp * cols * width, bytes_accessed=30 * 2**20, transcendentals=0
        ),
        name="output_project",
    )(out, xs, w_all, gain, shift)


def norm_stats(rows):
    mean = jnp.mean(rows, axis=1, keepdims=True)
    center = rows - mean
    inverse = lax.rsqrt(jnp.mean(center * center, axis=1, keepdims=True) + epsilon)
    return mean, inverse


def norm_backward(grad_out, normed, inverse, gain):
    scaled = grad_out * gain
    grad_rows = inverse * (
        scaled
        - jnp.mean(scaled, axis=1, keepdims=True)
        - normed * jnp.mean(scaled * normed, axis=1, keepdims=True)
    )
    return (grad_rows, jnp.sum(grad_out * normed, axis=0), jnp.sum(grad_out, axis=0))


def rotate(tensor, places, direction):
    half = ROT // 2
    frequency = 10000.0 ** (-2.0 * jnp.arange(half, dtype=f32) / ROT)
    angles = frequency[:, None] * places.astype(f32)[None, :]
    cosine, sines = jnp.cos(angles), direction * jnp.sin(angles)
    first, second = tensor[..., :half, :], tensor[..., half:ROT, :]
    return jnp.concatenate(
        [
            first * cosine - second * sines,
            second * cosine + first * sines,
            tensor[..., ROT:, :],
        ],
        axis=-2,
    )


def after(value, *others):
    return lax.optimization_barrier((value, *others))[0]


def direct_gather(value):
    n_tp = lax.axis_size("tp")
    return [value] + [
        lax.ppermute(value, "tp", [(i, (i + s) % n_tp) for i in range(n_tp)])
        for s in range(1, n_tp)
    ]


def in_tp_order(arrays):
    count = len(arrays)
    shape = arrays[0].shape

    def kernel(tp, *refs):
        sources, out = refs[:count], refs[count]
        for s in range(count):
            out[lax.rem(tp[0] - s + count, count)] = sources[s][...]

    vmem = pl.BlockSpec(memory_space=pltpu.VMEM)
    return pl.pallas_call(
        kernel,
        out_shape=jax.ShapeDtypeStruct((count,) + shape, arrays[0].dtype),
        in_specs=[pl.BlockSpec(memory_space=pltpu.SMEM)] + [vmem] * count,
        out_specs=vmem,
        compiler_params=pltpu.CompilerParams(vmem_limit_bytes=32 * 2**20),
        cost_estimate=pl.CostEstimate(
            flops=0, bytes_accessed=4 * count * math.prod(shape), transcendentals=0
        ),
        name="in_tp_order",
    )(lax.axis_index("tp")[None], *arrays)


def exchange_sum(terms, axis):
    parts = lax.all_to_all(terms, axis, split_axis=0, concat_axis=0, tiled=True)
    return sum(part.astype(f32) for part in parts)


def scatter(partial, axis):
    return lax.psum_scatter(partial, axis, scatter_dimension=0, tiled=True)


def swap(value, axis, bit):
    size = lax.axis_size(axis)
    return lax.ppermute(value, axis, [(i, i ^ (1 << bit)) for i in range(size)])


def pair_sum(partial):
    size, rest = partial.shape[0], partial.shape[1:]
    side = lax.axis_index("ctx") % 2
    pairs = partial.reshape((size // 2, 2) + rest)
    kept = lax.dynamic_index_in_dim(pairs, side, 1, keepdims=False)
    sent = lax.dynamic_index_in_dim(pairs, 1 - side, 1, keepdims=False)
    return (kept.astype(f32) + swap(sent, "ctx", 0).astype(f32)).astype(bf16)


def spread_start(both, *early):
    pairs = both.shape[0]
    mine = lax.axis_index("ctx") // 2
    parts = [lax.dynamic_index_in_dim(both, mine, 0, keepdims=False)]
    for distance in range(1, pairs):
        sent = lax.dynamic_index_in_dim(both, mine ^ distance, 0, keepdims=False)
        perm = [(i, i ^ (2 * distance)) for i in range(2 * pairs)]
        parts.append(lax.ppermute(after(sent, *early) if early else sent, "ctx", perm))
    return parts


def spread_end(parts, *late):
    if late:
        parts = lax.optimization_barrier((*parts, *late))[: len(parts)]
    return sum(part.astype(f32) for part in parts).astype(bf16)


def by_ctx(partial):
    rows, cols = partial.shape
    n_ctx = lax.axis_size("ctx")
    return partial.reshape(n_ctx, rows // n_ctx, cols)


def gather(rows, axis):
    return lax.all_gather(rows, axis, axis=0, tiled=True)


def interleave(gate, up):
    rows, cols = gate.shape
    tile = 128

    def kernel(gate, up, out):
        out[:, 0, :] = gate[...].astype(f32)
        out[:, 1, :] = up[...].astype(f32)

    return pl.pallas_call(
        kernel,
        grid=(rows // tile,),
        out_shape=jax.ShapeDtypeStruct((rows, 2, cols), f32),
        in_specs=[pl.BlockSpec((tile, cols), lambda i: (i, 0))] * 2,
        out_specs=pl.BlockSpec((tile, 2, cols), lambda i: (i, 0, 0)),
        compiler_params=pltpu.CompilerParams(vmem_limit_bytes=32 * 2**20),
        cost_estimate=pl.CostEstimate(
            flops=0, bytes_accessed=12 * rows * cols, transcendentals=0
        ),
        name="interleave",
    )(gate, up)


def shards(
    layer_in,
    norm_gain,
    norm_bias,
    w_qkv,
    b_qkv,
    w_out,
    w_gate_up,
    w_down,
    cotangent,
    block_table,
    seq_ids,
):
    n_ctx, n_tp = lax.axis_size("ctx"), lax.axis_size("tp")
    ctx, tp = lax.axis_index("ctx"), lax.axis_index("tp")
    own, width = layer_in.shape
    rows = own * n_tp
    cols = w_qkv.shape[2]
    heads = cols // HEAD
    table = block_table.reshape(-1)
    blocks = table.shape[0]
    by_head = heads == n_ctx and BLK % own == 0
    part = cols // n_ctx

    ids = jnp.arange(blocks, dtype=jnp.int32)
    located = jnp.sum(jnp.where(table[None, :] == ids[:, None], ids[None, :], 0), axis=1)
    same = seq_ids[:, None] == seq_ids[None, :]
    first = jnp.min(jnp.where(same, ids[None, :], blocks), axis=1)
    last = jnp.max(jnp.where(same, ids[None, :], -1), axis=1)
    order = jnp.concatenate([located, first, last, tp[None]]).astype(jnp.int32)
    frequency = 10000.0 ** (-2.0 * jnp.arange(ROT // 2, dtype=f32) / ROT)
    positions = table[:, None] * BLK + jnp.arange(BLK, dtype=jnp.int32)[None, :]
    angles = frequency[None, :, None] * positions.astype(f32)[:, None, :]
    angles = jnp.stack([jnp.cos(angles), jnp.sin(angles)], axis=1)

    hidden_units = w_gate_up.shape[2]
    w_part = lax.dynamic_slice_in_dim(w_out, ctx * part, part, 0)
    if by_head:
        layer_in = after(layer_in, angles, order)
        xs, lows, mean_one, inverse_one, w_part, packed = project_exchange(
            layer_in, w_part, norm_gain[0:1], norm_bias[0:1], w_qkv, b_qkv
        )
        mean_one, inverse_one = [t.reshape(rows, 128)[:, :1] for t in (mean_one, inverse_one)]
        x = xs.reshape(rows, width).astype(f32)
        first_low = lows.reshape(rows, width)
        w_out_all = lax.all_gather(w_part, "ctx", axis=1, tiled=True)
        cot = direct_gather(after(cotangent, packed))
        out, logsum = attention_forward(order, angles, packed)
        middle, lows, mean_two, inverse_two, attended_all = output_project(
            out, xs, w_out_all, norm_gain[1:2], norm_bias[1:2]
        )
        cot = in_tp_order(lax.optimization_barrier((*cot, middle))[:n_tp]).reshape(rows, width)
        middle = middle.reshape(rows, width)
        mean_two, inverse_two = [t.reshape(rows, 128)[:, :1] for t in (mean_two, inverse_two)]
        normed_two = (middle - mean_two) * inverse_two
        second_low = lows.reshape(rows, width)
        attended_all = attended_all.reshape(n_tp * cols, rows)
    else:
        x = gather(layer_in, "tp").astype(f32)
        mean_one, inverse_one = norm_stats(x)
        first_low = ((x - mean_one) * inverse_one * norm_gain[0] + norm_bias[0]).astype(bf16)
        projected = (
            jnp.einsum("dcf,rd->cfr", w_qkv, first_low, preferred_element_type=f32)
            + b_qkv[:, :, None]
        ).reshape(3, heads, HEAD, rows)
        w_part = gather(w_part, "tp").reshape(n_tp, part, width)
        w_out_all = lax.all_gather(w_part, "ctx", axis=1, tiled=True)
        cot = gather(cotangent, "tp")
        places, _ = row_places(ctx * rows, rows, table, seq_ids)
        qkv = jnp.concatenate([rotate(projected[0:2], places, 1.0), projected[2:3]], axis=0)
        queries, keys, values = [t.astype(bf16).transpose(2, 0, 1) for t in qkv]
        visit, offsets = gathered_setup(
            rows, table, seq_ids, keys.reshape(rows, cols), values.reshape(rows, cols)
        )
        out, logsum = gathered_forward(queries, visit, offsets)
        attended_all = gather(out.astype(bf16).reshape(rows, cols).T, "tp")
        middle = x + jnp.einsum(
            "fr,fd->rd",
            attended_all,
            w_out_all.reshape(n_tp * cols, width),
            preferred_element_type=f32,
        )
        mean_two, inverse_two = norm_stats(middle)
        normed_two = (middle - mean_two) * inverse_two
        second_low = (normed_two * norm_gain[1] + norm_bias[1]).astype(bf16)

    grad_hidden = lax.dot_general(cot, w_down, (((1,), (1,)), ((), ())), preferred_element_type=f32)
    gate_up = jnp.einsum("rd,dcf->rcf", second_low, w_gate_up, preferred_element_type=f32)
    gate, up = gate_up[:, 0], gate_up[:, 1]
    sigmoid = jax.nn.sigmoid(gate)
    activated = gate * sigmoid
    hidden = (activated * up).astype(bf16)
    grad_gate = grad_hidden * up * sigmoid * (1.0 + gate * (1.0 - sigmoid))
    grad_gu = jnp.stack([grad_gate, grad_hidden * activated], axis=1).astype(bf16)
    grad_second = jnp.einsum("rcf,dcf->rd", grad_gu, w_gate_up, preferred_element_type=f32)

    middle_norm, gain_two, bias_two = norm_backward(
        grad_second, normed_two, inverse_two, norm_gain[1]
    )
    is_own = (jnp.arange(rows, dtype=jnp.int32) // own == tp)[:, None]
    middle_term = (middle_norm + jnp.where(is_own, cot.astype(f32), 0.0)).astype(bf16)
    grad_att = lax.dot_general(
        w_out_all.reshape(n_tp * cols, width),
        middle_term,
        (((1,), (1,)), ((), ())),
        preferred_element_type=f32,
    ).astype(bf16)

    def weight_grad(left, right, token):
        return lax.dot_general(
            after(left, token), right, (((0,), (0,)), ((), ())), preferred_element_type=f32
        ).astype(bf16)

    gate_grad = weight_grad(second_low, grad_gu[:, 0], grad_att)
    up_grad = weight_grad(second_low, grad_gu[:, 1], gate_grad)
    down_grad = weight_grad(hidden, cot, up_grad)
    out_grad = jnp.dot(
        after(attended_all, down_grad), middle_term, preferred_element_type=f32
    ).astype(bf16)
    down = jnp.dot(after(hidden, out_grad), w_down, preferred_element_type=f32).astype(bf16)
    gu_grad = jnp.concatenate([pair_sum(by_ctx(gate_grad)), pair_sum(by_ctx(up_grad))], axis=1)
    gu_parts = spread_start(gu_grad)
    other_grad = jnp.concatenate(
        [
            pair_sum(by_ctx(down_grad)),
            pair_sum(
                out_grad.reshape(n_tp, n_ctx, part, width).transpose(1, 0, 2, 3)
            ).reshape(n_ctx // 2, n_tp * part, width),
        ],
        axis=1,
    )
    grad_att = scatter(grad_att, "tp")
    grad_att, down, other_grad = lax.optimization_barrier((grad_att, down, other_grad))
    down = scatter(down, "tp")

    if by_head:
        grad_att = grad_att.reshape(heads, HEAD, rows)
        grad_att = lax.all_to_all(grad_att, "ctx", split_axis=0, concat_axis=0, tiled=True)
        gu_grad = spread_end(gu_parts, grad_att)
        other_parts = spread_start(other_grad, gu_grad)
        grads = attention_backward(order, angles, packed, after(grad_att, gu_grad), out, logsum)
        done = (grads,)
        grads = lax.all_to_all(grads, "ctx", split_axis=0, concat_axis=0, tiled=True)
        grad_projected = grads.transpose(1, 0, 2, 3).reshape(3 * cols, rows)
    else:
        grads = gathered_backward(
            queries, visit, offsets, grad_att.T.reshape(rows, heads, HEAD), out, logsum
        )
        grads = jnp.stack([t.transpose(1, 2, 0) for t in grads])
        done = (grads,)
        gu_grad = spread_end(gu_parts)
        other_parts = spread_start(other_grad, gu_grad)
        grads = jnp.concatenate([rotate(grads[0:2], places, -1.0), grads[2:3]], axis=0)
        grad_projected = grads.reshape(3 * cols, rows).astype(bf16)

    down = after(down, *done)
    own_middle = lax.dynamic_slice_in_dim(middle, tp * own, own, 0)
    layer_out = (own_middle + down.astype(f32)).astype(bf16)
    other_grad = spread_end(other_parts, *done)
    grad_projected, gu_grad, other_grad = lax.optimization_barrier(
        (grad_projected, gu_grad, other_grad)
    )
    gate_grad, up_grad = [gather(t, "ctx") for t in jnp.split(gu_grad, 2, axis=0)]
    down_grad, out_grad = jnp.split(other_grad, [down_grad.shape[0] // n_ctx], axis=0)
    down_grad = gather(down_grad, "ctx")
    out_grad = exchange_sum(out_grad.reshape(n_tp, part, width), "tp").astype(bf16)

    grad_first = jnp.einsum(
        "cfr,dcf->rd",
        grad_projected.reshape(3, cols, rows),
        w_qkv,
        preferred_element_type=f32,
    )
    input_norm, gain_one, bias_one = norm_backward(
        grad_first, (x - mean_one) * inverse_one, inverse_one, norm_gain[0]
    )
    input_term = (middle_norm + input_norm).astype(bf16)
    grad_qkv = lax.dot_general(
        first_low,
        after(grad_projected, input_term),
        (((0,), (1,)), ((), ())),
        preferred_element_type=f32,
    ).astype(bf16)
    out_grad = gather(out_grad, "ctx")
    grad_qkv = gather(spread_end(spread_start(pair_sum(by_ctx(grad_qkv)))), "ctx")
    grad_input = exchange_sum(input_term.reshape(n_tp, own, width), "tp")
    grad_input = (cotangent.astype(f32) + grad_input).astype(bf16)

    small = jnp.concatenate(
        [
            jnp.sum(grad_projected.astype(f32), axis=1),
            gain_one, gain_two, bias_one, bias_two,
        ]
    )
    small = lax.all_gather(small.reshape(-1, 128), ("ctx", "tp"), axis=0, tiled=False)
    small = small.reshape(n_ctx, n_tp, -1)
    bias_qkv = lax.dynamic_index_in_dim(small[..., : 3 * cols], tp, 1, keepdims=False)
    bias_qkv = jnp.sum(bias_qkv, axis=0).reshape(3, cols)
    norms = jnp.sum(small[..., 3 * cols :], axis=(0, 1)).reshape(2, 2, width)
    return (
        layer_out,
        grad_input,
        norms[0],
        norms[1],
        grad_qkv.reshape(width, 3, cols).astype(f32),
        bias_qkv,
        out_grad.astype(f32),
        interleave(gate_grad, up_grad),
        down_grad.astype(f32),
    )


def solution(mesh):
    placed = (
        P(("ctx", "tp"), None),
        P(),
        P(),
        P(None, None, "tp"),
        P(None, "tp"),
        P("tp", None),
        P(None, None, "tp"),
        P("tp", None),
        P(("ctx", "tp"), None),
        P(),
        P(),
    )
    return jax.shard_map(
        shards,
        mesh=mesh,
        in_specs=placed,
        out_specs=(
            P(("ctx", "tp"), None),
            P(("ctx", "tp"), None),
            P(),
            P(),
            P(None, None, "tp"),
            P(None, "tp"),
            P("tp", None),
            P(None, None, "tp"),
            P("tp", None),
        ),
        check_vma=False,
    )
```

```python
import math

import jax
import jax.numpy as jnp
from jax import lax
from jax.experimental import pallas as pl
from jax.experimental.pallas import tpu as pltpu
from jax.sharding import PartitionSpec as P

HEAD = 64
ROT = 16
BLK = 512
EXTRA = 16

epsilon = 1e-05
neg_large = -1e30
bf16 = jnp.bfloat16
f32 = jnp.float32


def dot(left, right, left_dim, right_dim):
    return lax.dot_general(
        left, right, (((left_dim,), (right_dim,)), ((), ())), preferred_element_type=f32
    )


def causal_keep():
    return lax.broadcasted_iota(jnp.int32, (BLK, BLK), 0) <= lax.broadcasted_iota(
        jnp.int32, (BLK, BLK), 1
    )


def turn(tile):
    return tile.astype(f32).T.astype(bf16)


def scan_chunks(devices, chunks, width, visit):
    per_block = BLK // width

    def source(device, carry):
        for chunk in range(chunks):
            place = device * (chunks // per_block) + chunk // per_block
            visit(chunk, device, place, slice((chunk % per_block) * width, (chunk % per_block + 1) * width))
        return carry

    lax.fori_loop(0, devices, source, 0)


def turn_dims(tile, cosine, sine):
    half = ROT // 2
    first, second = tile[0:half], tile[half:ROT]
    return jnp.concatenate(
        [first * cosine - second * sine, second * cosine + first * sine, tile[ROT:]], axis=0
    )


def attention_forward(order, angles, packed):
    count, devices, _, _, width = packed.shape
    blocks = devices * count * width // BLK

    def kernel(order, angles, packed, out, logsum, queries, keys, values):
        per_device = count * width // BLK
        row = lax.broadcasted_iota(jnp.int32, (EXTRA, BLK), 0)
        ones = jnp.where(row == 0, 1.0, 0.0).astype(bf16)

        def visit(chunk, device, place, lanes):
            part = packed.at[chunk]
            cosine, sine = angles[place, 0, :, lanes], angles[place, 1, :, lanes]
            query = turn_dims(part[device, 0].astype(f32), cosine, sine).astype(bf16)
            queries[place, :, lanes] = query * jnp.asarray(HEAD**-0.5, bf16)
            key = turn_dims(part[device, 1].astype(f32), cosine, sine).astype(bf16)
            keys[place, lanes, :] = turn(key)
            values[place, 0:HEAD, lanes] = part[device, 2]

        scan_chunks(devices, count, width, visit)

        def prepare(place, carry):
            values[place, HEAD : HEAD + EXTRA, :] = ones
            return carry

        lax.fori_loop(0, blocks, prepare, 0)
        keep = causal_keep()

        def query_block(i, carry):
            place = order[i]
            query = queries[place]

            def step(j, state, masked):
                maxima, summed = state
                other = order[j]
                scores = dot(keys[other], query, 1, 0)
                if masked:
                    scores = jnp.where(keep, scores, neg_large)
                new_maxima = jnp.maximum(maxima, jnp.max(scores, axis=0, keepdims=True))
                weights = jnp.exp(scores - new_maxima).astype(bf16)
                summed = summed * jnp.exp(maxima - new_maxima) + dot(values[other], weights, 1, 0)
                return new_maxima, summed

            state = (jnp.full((1, BLK), neg_large, f32), jnp.zeros((HEAD + EXTRA, BLK), f32))
            state = lax.fori_loop(order[blocks + i], i, lambda j, s: step(j, s, False), state)
            maxima, summed = step(i, state, True)
            totals = summed[HEAD : HEAD + 1]
            result = (summed[0:HEAD] / totals).astype(bf16)
            logsum[place] = maxima + jnp.log(totals)
            lane = pl.multiple_of(lax.rem(place, per_device) * BLK, BLK)
            out[place // per_device, :, pl.ds(lane, BLK)] = result
            return carry

        lax.fori_loop(0, blocks, query_block, 0)

    vmem = pl.BlockSpec(memory_space=pltpu.VMEM)
    return pl.pallas_call(
        kernel,
        out_shape=(
            jax.ShapeDtypeStruct((devices, HEAD, count * width), bf16),
            jax.ShapeDtypeStruct((blocks, 1, BLK), f32),
        ),
        in_specs=[pl.BlockSpec(memory_space=pltpu.SMEM), vmem, vmem],
        out_specs=(vmem, vmem),
        scratch_shapes=[
            pltpu.VMEM((blocks, HEAD, BLK), bf16),
            pltpu.VMEM((blocks, BLK, HEAD), bf16),
            pltpu.VMEM((blocks, HEAD + EXTRA, BLK), bf16),
        ],
        compiler_params=pltpu.CompilerParams(vmem_limit_bytes=60 * 2**20),
        cost_estimate=pl.CostEstimate(
            flops=85 * 2 * 2 * BLK * BLK * 256, bytes_accessed=5 * 2**20, transcendentals=0
        ),
        name="attention_forward",
    )(order, angles, packed)


def attention_backward(order, angles, packed, grad_out, out, logsum):
    count, devices, _, _, width = packed.shape
    blocks = devices * count * width // BLK
    wide = HEAD + EXTRA

    def kernel(
        order, angles, packed, grad_out, out, logsum,
        grads, query_x, grad_x, key_x, key_rows, value_x, grad_q,
    ):
        row = lax.broadcasted_iota(jnp.int32, (EXTRA, width), 0)
        lane_ids = lax.broadcasted_iota(jnp.int32, (BLK, EXTRA), 1)
        ones = jnp.where(lane_ids < 3, 1.0, 0.0).astype(bf16)

        def three_rows(value):
            high = value.astype(bf16).astype(f32)
            rest = value - high
            middle = rest.astype(bf16).astype(f32)
            low = rest - middle
            return jnp.where(
                row == 0, high, jnp.where(row == 1, middle, jnp.where(row == 2, low, 0.0))
            ).astype(bf16)

        def visit(chunk, device, place, lanes):
            part = packed.at[chunk]
            cosine, sine = angles[place, 0, :, lanes], angles[place, 1, :, lanes]
            query = turn_dims(part[device, 0].astype(f32), cosine, sine).astype(bf16)
            query_x[place, 0:HEAD, lanes] = query * jnp.asarray(HEAD**-0.5, bf16)
            query_x[place, HEAD:wide, lanes] = three_rows(-logsum[place, :, lanes])
            key = turn_dims(part[device, 1].astype(f32), cosine, sine).astype(bf16)
            key_rows[place, :, lanes] = key
            key_x[place, lanes, 0:HEAD] = turn(key)
            value_x[place, lanes, 0:HEAD] = turn(part[device, 2])
            own = slice(chunk * width, (chunk + 1) * width)
            grad = grad_out[device, :, own]
            delta = jnp.sum(
                grad.astype(f32) * out[device, :, own].astype(f32), axis=0, keepdims=True
            )
            grad_x[place, 0:HEAD, lanes] = grad
            grad_x[place, HEAD:wide, lanes] = three_rows(-delta)

        scan_chunks(devices, count, width, visit)

        def prepare(place, carry):
            key_x[place, :, HEAD:wide] = ones
            value_x[place, :, HEAD:wide] = ones
            grad_q[place] = jnp.zeros((HEAD, BLK), f32)
            return carry

        lax.fori_loop(0, blocks, prepare, 0)
        keep = causal_keep()
        per_device = count * width // BLK

        def store(part, place, tile):
            lane = pl.multiple_of(lax.rem(place, per_device) * BLK, BLK)
            grads[place // per_device, part, :, pl.ds(lane, BLK)] = tile

        def key_block(j, carry):
            place = order[j]
            key, value = key_x[place], value_x[place]
            key_tile = key_rows[place]

            def step(i, state, masked):
                grad_k, grad_v = state
                other = order[i]
                prob = jnp.exp(dot(key, query_x[other], 1, 0))
                if masked:
                    prob = jnp.where(keep, prob, 0.0)
                grad_raw = (prob * dot(value, grad_x[other], 1, 0)).astype(bf16)
                grad_v = grad_v + dot(grad_x[other, 0:HEAD, :], prob.astype(bf16), 1, 1)
                grad_k = grad_k + dot(query_x[other, 0:HEAD, :], grad_raw, 1, 1)
                grad_q[other] += dot(key_tile, grad_raw, 1, 0)
                return grad_k, grad_v

            zero = jnp.zeros((HEAD, BLK), f32)
            state = step(j, (zero, zero), True)
            grad_k, grad_v = lax.fori_loop(
                j + 1, order[2 * blocks + j] + 1, lambda i, s: step(i, s, False), state
            )
            cosine, sine = angles[place, 0], angles[place, 1]
            store(1, place, turn_dims(grad_k, cosine, -sine).astype(bf16))
            store(2, place, grad_v.astype(bf16))
            return carry

        lax.fori_loop(0, blocks, key_block, 0)

        def finish(place, carry):
            tile = turn_dims(grad_q[place] * HEAD**-0.5, angles[place, 0], -angles[place, 1])
            store(0, place, tile.astype(bf16))
            return carry

        lax.fori_loop(0, blocks, finish, 0)

    vmem = pl.BlockSpec(memory_space=pltpu.VMEM)
    return pl.pallas_call(
        kernel,
        out_shape=jax.ShapeDtypeStruct((devices, 3, HEAD, count * width), bf16),
        in_specs=[pl.BlockSpec(memory_space=pltpu.SMEM)] + [vmem] * 5,
        out_specs=vmem,
        scratch_shapes=[
            pltpu.VMEM((blocks, wide, BLK), bf16),
            pltpu.VMEM((blocks, wide, BLK), bf16),
            pltpu.VMEM((blocks, BLK, wide), bf16),
            pltpu.VMEM((blocks, HEAD, BLK), bf16),
            pltpu.VMEM((blocks, BLK, wide), bf16),
            pltpu.VMEM((blocks, HEAD, BLK), f32),
        ],
        compiler_params=pltpu.CompilerParams(vmem_limit_bytes=60 * 2**20),
        cost_estimate=pl.CostEstimate(flops=1, bytes_accessed=1, transcendentals=0),
        name="attention_backward",
    )(order, angles, packed, grad_out, out, logsum)


def row_places(first_row, length, table_flat, seq_ids):
    row_ids = first_row + jnp.arange(length, dtype=jnp.int32)
    block_ids = jnp.arange(table_flat.shape[0], dtype=jnp.int32)
    natural = jnp.sum(
        jnp.where((row_ids // BLK)[:, None] == block_ids[None, :], table_flat[None, :], 0), axis=1
    )
    sequence = jnp.sum(
        jnp.where(natural[:, None] == block_ids[None, :], seq_ids[None, :], 0), axis=1
    )
    return (natural * BLK + row_ids % BLK, sequence)


def gathered_setup(rows, table_flat, seq_ids, key_flat, value_flat):
    places, seq = row_places(lax.axis_index("ctx") * rows, rows, table_flat, seq_ids)
    pieces = (
        lax.all_gather(key_flat, "ctx", axis=0, tiled=True),
        lax.all_gather(value_flat, "ctx", axis=0, tiled=True),
    )
    stride = math.gcd(pieces[0].shape[0], 1024)
    offsets = jnp.arange(pieces[0].shape[0] // stride, dtype=jnp.int32) * stride

    def visit(offset):
        other_places, other_seq = row_places(offset, stride, table_flat, seq_ids)
        allowed = (seq[:, None] == other_seq[None, :]) & (other_places[None, :] <= places[:, None])
        blocks = [
            lax.dynamic_slice_in_dim(piece, offset, stride, 0).reshape(stride, -1, HEAD)
            for piece in pieces
        ]
        return allowed[:, None, :], blocks[0], blocks[1]

    return visit, offsets


def gathered_forward(queries, visit, offsets):
    rows, heads, _ = queries.shape

    def step(status, offset):
        allowed, keys, values = visit(offset)
        scores = jnp.einsum("qhe,khe->qhk", queries, keys, preferred_element_type=f32)
        scores = scores * HEAD**-0.5
        maxima, totals, summed = status
        new_maxima = jnp.maximum(maxima, jnp.max(jnp.where(allowed, scores, neg_large), axis=2))
        weights = jnp.where(allowed, jnp.exp(scores - new_maxima[..., None]), 0.0)
        factor = jnp.exp(maxima - new_maxima)
        totals = totals * factor + jnp.sum(weights, axis=2)
        summed = summed * factor[..., None] + jnp.einsum(
            "qhk,khe->qhe", weights.astype(bf16), values, preferred_element_type=f32
        )
        return ((new_maxima, totals, summed), None)

    initial = (
        jnp.full((rows, heads), neg_large, f32),
        jnp.zeros((rows, heads), f32),
        jnp.zeros((rows, heads, HEAD), f32),
    )
    (maxima, totals, summed), _ = lax.scan(step, initial, offsets)
    return summed / totals[..., None], maxima + jnp.log(totals)


def gathered_backward(queries, visit, offsets, grad_att, attended, logsum):
    rows, heads, _ = queries.shape
    delta = jnp.sum(grad_att.astype(f32) * attended, axis=2)

    def step(status, offset):
        allowed, keys, values = visit(offset)
        scores = jnp.einsum("qhe,khe->qhk", queries, keys, preferred_element_type=f32)
        prob = jnp.where(allowed, jnp.exp(scores * HEAD**-0.5 - logsum[..., None]), 0.0)
        grad_prob = jnp.einsum("qhe,khe->qhk", grad_att, values, preferred_element_type=f32)
        grad_raw = (prob * (grad_prob - delta[..., None]) * HEAD**-0.5).astype(bf16)
        grad_q = jnp.einsum("qhk,khe->qhe", grad_raw, keys, preferred_element_type=f32)
        grad_k = jnp.einsum("qhk,qhe->khe", grad_raw, queries, preferred_element_type=f32)
        grad_v = jnp.einsum("qhk,qhe->khe", prob.astype(bf16), grad_att, preferred_element_type=f32)
        return (
            (
                status[0] + grad_q,
                lax.dynamic_update_slice_in_dim(status[1], grad_k, offset, 0),
                lax.dynamic_update_slice_in_dim(status[2], grad_v, offset, 0),
            ),
            None,
        )

    total = rows * lax.axis_size("ctx")
    zero = jnp.zeros((total, heads, HEAD), f32)
    (grad_q, grad_k, grad_v), _ = lax.scan(
        step, (jnp.zeros((rows, heads, HEAD), f32), zero, zero), offsets
    )
    grad_k = lax.psum_scatter(grad_k, "ctx", scatter_dimension=0, tiled=True)
    grad_v = lax.psum_scatter(grad_v, "ctx", scatter_dimension=0, tiled=True)
    return grad_q, grad_k, grad_v


MESH = pl.DeviceIdType.MESH


def greet(n_ctx, n_tp):
    ctx, tp = lax.axis_index("ctx"), lax.axis_index("tp")
    barrier = pltpu.get_barrier_semaphore()

    def greet_ctx(step, carry):
        peer = lax.rem(ctx + step, n_ctx)
        pl.semaphore_signal(barrier, inc=1, device_id=(peer, tp), device_id_type=MESH)
        return carry

    lax.fori_loop(1, n_ctx, greet_ctx, 0)
    for peer in (lax.rem(tp + 1, n_tp), lax.rem(tp + n_tp - 1, n_tp)):
        pl.semaphore_signal(barrier, inc=1, device_id=(ctx, peer), device_id_type=MESH)
    pl.semaphore_wait(barrier, n_ctx + 1)


def rows_norm(source, stored, gain, shift, mean_out, inverse_out, tile):
    def step(i, carry):
        rows = pl.ds(pl.multiple_of(i * tile, tile), tile)
        x = source(rows)
        mean = jnp.mean(x, axis=1, keepdims=True)
        center = x - mean
        inverse = lax.rsqrt(jnp.mean(center * center, axis=1, keepdims=True) + epsilon)
        stored(rows, (center * inverse * gain + shift).astype(bf16))
        mean_out[rows, :] = jnp.broadcast_to(mean, (tile, 128))
        inverse_out[rows, :] = jnp.broadcast_to(inverse, (tile, 128))
        return carry

    return step


def project_exchange(layer_in, w_part, gain, shift, w_qkv, b_qkv):
    n_ctx, n_tp = lax.axis_size("ctx"), lax.axis_size("tp")
    own, width = layer_in.shape
    part = w_part.shape[0]
    cols = w_qkv.shape[2]

    def kernel(
        x_in, w_in, gain, shift, w_qkv, b_qkv,
        xs, lows, means, inverses, ws, packed,
        outgoing, ring_send, ring_recv, w_send, w_recv, send, recv,
    ):
        ctx, tp = lax.axis_index("ctx"), lax.axis_index("tp")
        right = lax.rem(tp + 1, n_tp)
        half = own // 2

        def block(slot):
            return lax.rem(tp - slot + n_tp, n_tp)

        def ring(step, piece):
            rows = pl.ds(piece * half, half)
            return pltpu.make_async_remote_copy(
                src_ref=x_in.at[rows] if step == 0 else xs.at[block(step), rows],
                dst_ref=xs.at[block(step), rows],
                send_sem=ring_send.at[step, piece],
                recv_sem=ring_recv.at[step, piece],
                device_id=(ctx, right),
                device_id_type=MESH,
            )

        def w_ring(step):
            return pltpu.make_async_remote_copy(
                src_ref=w_in if step == 0 else ws.at[block(step)],
                dst_ref=ws.at[block(step)],
                send_sem=w_send.at[step],
                recv_sem=w_recv.at[step],
                device_id=(ctx, right),
                device_id_type=MESH,
            )

        def exchange(slot, step):
            peer = lax.rem(ctx + step, n_ctx)
            return pltpu.make_async_remote_copy(
                src_ref=outgoing.at[slot, peer],
                dst_ref=packed.at[block(slot), ctx],
                send_sem=send.at[slot, step],
                recv_sem=recv.at[slot, step],
                device_id=(peer, tp),
                device_id_type=MESH,
            )

        greet(n_ctx, n_tp)
        for piece in range(2):
            ring(0, piece).start()
        xs[tp] = x_in[...]
        ws[tp] = w_in[...]
        for slot in range(n_tp):
            if slot > 0:
                for piece in range(2):
                    ring(slot - 1, piece).wait_recv()
                    if slot < n_tp - 1:
                        ring(slot, piece).start()
            if slot == n_tp - 2:
                w_ring(0).start()
            if slot == n_tp - 1:
                w_ring(0).wait_recv()
                w_ring(1).start()

            here = block(slot)

            def stored(rows, value, here=here):
                lows[here, rows, :] = value

            step = rows_norm(
                lambda rows, here=here: xs[here, rows, :].astype(f32),
                stored, gain[...], shift[...], means.at[here], inverses.at[here], 32,
            )
            lax.fori_loop(0, own // 32, step, 0)

            def project(c, carry, slot=slot, here=here):
                value = jnp.dot(lows[here], w_qkv[c], preferred_element_type=f32) + b_qkv[c]
                outgoing[slot, :, c] = value.T.astype(bf16).reshape(n_ctx, HEAD, own)
                return carry

            lax.fori_loop(0, 3, project, 0)
            lax.fori_loop(
                1, n_ctx, lambda step, c, slot=slot: (exchange(slot, step).start(), c)[1], 0
            )
            packed[here, ctx] = outgoing[slot, ctx]
        for step in range(1, n_tp - 1):
            w_ring(step).wait_recv()
            if step < n_tp - 2:
                w_ring(step + 1).start()
        for slot in range(n_tp):
            lax.fori_loop(
                1, n_ctx, lambda step, c, slot=slot: (exchange(slot, step).wait(), c)[1], 0
            )
        for step in range(n_tp - 1):
            w_ring(step).wait_send()
            for piece in range(2):
                ring(step, piece).wait_send()

    vmem = pl.BlockSpec(memory_space=pltpu.VMEM)
    return pl.pallas_call(
        kernel,
        out_shape=(
            jax.ShapeDtypeStruct((n_tp, own, width), bf16),
            jax.ShapeDtypeStruct((n_tp, own, width), bf16),
            jax.ShapeDtypeStruct((n_tp, own, 128), f32),
            jax.ShapeDtypeStruct((n_tp, own, 128), f32),
            jax.ShapeDtypeStruct((n_tp, part, width), bf16),
            jax.ShapeDtypeStruct((n_tp, n_ctx, 3, HEAD, own), bf16),
        ),
        in_specs=[vmem] * 6,
        out_specs=(vmem,) * 6,
        scratch_shapes=[
            pltpu.VMEM((n_tp, n_ctx, 3, HEAD, own), bf16),
            pltpu.SemaphoreType.DMA((n_tp - 1, 2)),
            pltpu.SemaphoreType.DMA((n_tp - 1, 2)),
            pltpu.SemaphoreType.DMA((n_tp - 1,)),
            pltpu.SemaphoreType.DMA((n_tp - 1,)),
            pltpu.SemaphoreType.DMA((n_tp, n_ctx)),
            pltpu.SemaphoreType.DMA((n_tp, n_ctx)),
        ],
        compiler_params=pltpu.CompilerParams(
            collective_id=1, has_side_effects=True, vmem_limit_bytes=60 * 2**20
        ),
        cost_estimate=pl.CostEstimate(
            flops=2 * n_tp * own * width * 3 * cols, bytes_accessed=20 * 2**20, transcendentals=0
        ),
        name="project_exchange",
    )(layer_in, w_part, gain, shift, w_qkv.transpose(1, 0, 2), b_qkv[:, None, :])


def output_project(out, xs, w_all, gain, shift):
    n_ctx, n_tp = lax.axis_size("ctx"), lax.axis_size("tp")
    own, width = xs.shape[1:]
    cols = w_all.shape[1]
    rows_all = n_tp * own

    def kernel(
        out, xs, w_all, gain, shift,
        middle, lows, means, inverses, raw,
        ring_send, ring_recv, send, recv, own_sem,
    ):
        ctx, tp = lax.axis_index("ctx"), lax.axis_index("tp")
        right = lax.rem(tp + 1, n_tp)
        half = cols // 2

        def block(slot):
            return lax.rem(tp - slot + n_tp, n_tp)

        def ring(step, piece):
            rows = pl.ds(piece * half, half)
            return pltpu.make_async_remote_copy(
                src_ref=raw.at[block(step), rows],
                dst_ref=raw.at[block(step), rows],
                send_sem=ring_send.at[step, piece],
                recv_sem=ring_recv.at[step, piece],
                device_id=(ctx, right),
                device_id_type=MESH,
            )

        def exchange(step):
            peer = lax.rem(ctx + step, n_ctx)
            return pltpu.make_async_remote_copy(
                src_ref=out.at[peer],
                dst_ref=raw.at[tp, pl.ds(pl.multiple_of(ctx * HEAD, HEAD), HEAD)],
                send_sem=send.at[step],
                recv_sem=recv.at[step],
                device_id=(peer, tp),
                device_id_type=MESH,
            )

        greet(n_ctx, n_tp)
        lax.fori_loop(1, n_ctx, lambda step, c: (exchange(step).start(), c)[1], 0)
        keep = pltpu.make_async_copy(
            out.at[ctx], raw.at[tp, pl.ds(pl.multiple_of(ctx * HEAD, HEAD), HEAD)], own_sem
        )
        keep.start()
        keep.wait()
        lax.fori_loop(1, n_ctx, lambda step, c: (exchange(step).wait_recv(), c)[1], 0)
        for piece in range(2):
            ring(0, piece).start()
        for slot in range(n_tp):
            if slot > 0:
                for piece in range(2):
                    ring(slot - 1, piece).wait_recv()
                    if slot < n_tp - 1:
                        ring(slot, piece).start()
            here = block(slot)

            def project(place, carry, slot=slot, here=here):
                lanes = pl.ds(pl.multiple_of(place * own, own), own)
                tile = raw[here, :, lanes].astype(f32).T.astype(bf16)
                value = jnp.dot(tile, w_all[here], preferred_element_type=f32)
                if slot == 0:
                    middle[place] = xs[place].astype(f32) + value
                else:
                    middle[place] += value
                return carry

            lax.fori_loop(0, n_tp, project, 0)
        for place in range(n_tp):

            def stored(rows, value, place=place):
                lows[place, rows, :] = value

            step = rows_norm(
                lambda rows, place=place: middle[place, rows, :],
                stored, gain[...], shift[...], means.at[place], inverses.at[place], 32,
            )
            lax.fori_loop(0, own // 32, step, 0)
        lax.fori_loop(1, n_ctx, lambda step, c: (exchange(step).wait_send(), c)[1], 0)
        for step in range(n_tp - 1):
            for piece in range(2):
                ring(step, piece).wait_send()

    vmem = pl.BlockSpec(memory_space=pltpu.VMEM)
    return pl.pallas_call(
        kernel,
        out_shape=(
            jax.ShapeDtypeStruct((n_tp, own, width), f32),
            jax.ShapeDtypeStruct((n_tp, own, width), bf16),
            jax.ShapeDtypeStruct((n_tp, own, 128), f32),
            jax.ShapeDtypeStruct((n_tp, own, 128), f32),
            jax.ShapeDtypeStruct((n_tp, cols, rows_all), bf16),
        ),
        in_specs=[vmem] * 5,
        out_specs=(vmem,) * 5,
        scratch_shapes=[
            pltpu.SemaphoreType.DMA((n_tp - 1, 2)),
            pltpu.SemaphoreType.DMA((n_tp - 1, 2)),
            pltpu.SemaphoreType.DMA((n_ctx,)),
            pltpu.SemaphoreType.DMA((n_ctx,)),
            pltpu.SemaphoreType.DMA,
        ],
        compiler_params=pltpu.CompilerParams(
            collective_id=2, has_side_effects=True, vmem_limit_bytes=60 * 2**20
        ),
        cost_estimate=pl.CostEstimate(
            flops=2 * rows_all * n_tp * cols * width, bytes_accessed=30 * 2**20, transcendentals=0
        ),
        name="output_project",
    )(out, xs, w_all, gain, shift)


def middle_sums(term, w_all, low, gate, up, hidden, cot, attended):
    rows, width = term.shape
    n_tp, cols, _ = w_all.shape
    n_ctx = lax.axis_size("ctx")
    units = gate.shape[1]
    share, piece = width // n_ctx, cols // n_ctx
    out_rows, down_rows = n_tp * piece, units // n_ctx
    other_rows = out_rows + down_rows
    half, heads = cols // 2, cols // 2 // HEAD
    window = min(units, (down_rows + 127 + 127) // 128 * 128)
    pair = n_ctx // 2

    def kernel(
        term_in, w_all, low, gate, up, hidden, cot, attended,
        grad_out, gate_sum, up_sum, out_sum, down_sum,
        term, w_buf, wide_buf, gate_buf, up_buf, hidden_t, att_buf, ring_buf, heads_out,
        send_one, send_two, got_one, got_two, one_a, one_b, two_a, two_b,
        load_s, w_s, att_s, ring_s, ring_r, head_s, head_r, core_s, core_r, one_s, one_r, two_s, two_r,
    ):
        ctx, tp = lax.axis_index("ctx"), lax.axis_index("tp")
        y, x, core = ctx // 4, (ctx // 2) % 2, ctx % 2
        on_core, on_x, on_y = ctx + 1 - 2 * core, ctx + 2 - 4 * x, ctx + 4 - 8 * y
        here = y * 2 + x

        def remote(source, target, send, recv, peer, near=True):
            return pltpu.make_async_remote_copy(
                src_ref=source,
                dst_ref=target,
                send_sem=send,
                recv_sem=recv,
                device_id=(peer, tp) if near else (ctx, peer),
                device_id_type=MESH,
            )

        def w_load(block, side):
            rows_in = pl.ds(side * half, half)
            return pltpu.make_async_copy(w_all.at[block, rows_in], w_buf, w_s)

        def dest(step):
            return lax.rem(tp - 1 - step + 2 * n_tp, n_tp)

        loads = [
            pltpu.make_async_copy(source, target, load_s.at[i])
            for i, (source, target) in enumerate(
                ((low, wide_buf), (gate, gate_buf), (up, up_buf), (cot, wide_buf), (hidden, gate_buf), (term_in, term))
            )
        ]
        loads[5].start()
        w_load(dest(0), 0).start()
        for i in range(3):
            loads[i].start()
        greet(n_ctx, n_tp)

        def own_term(step, side):
            w_load(dest(step), side).wait()
            return lax.dot_general(
                w_buf[...], term[...], (((1,), (1,)), ((), ())), preferred_element_type=f32
            ).reshape(heads, HEAD, rows)

        def load_after(step, side):
            @pl.when(jnp.logical_or(side == 0, step < n_tp - 1))
            def _():
                w_load(lax.rem(tp - 1 - step - side + 2 * n_tp, n_tp), 1 - side).start()

        def ring(step, side):
            return remote(
                heads_out.at[pl.ds(side * heads, heads)]
                if step == 0
                else ring_buf.at[step - 1, side],
                ring_buf.at[step, side],
                ring_s.at[step, side],
                ring_r.at[step, side],
                lax.rem(tp + 1, n_tp),
                False,
            )

        def head_copy(step):
            peer = lax.rem(ctx + step, n_ctx)
            return remote(
                heads_out.at[peer], grad_out.at[ctx], head_s.at[step], head_r.at[step], peer
            )

        def ring_next(step):
            def one_side(side, carry):
                value = own_term(step + 1, side)
                ring(step, side).wait_recv()
                value = (value + ring_buf[step, side].astype(f32)).astype(bf16)
                if step < n_tp - 2:
                    ring_buf[step, side] = value
                    ring(step + 1, side).start()
                else:
                    ring(0, side).wait_send()
                    heads_out[pl.ds(side * heads, heads)] = value
                load_after(step + 1, side)
                return carry

            lax.fori_loop(0, 2, one_side, 0)

        def ring_first(side, carry):
            heads_out[pl.ds(side * heads, heads)] = own_term(0, side).astype(bf16)
            ring(0, side).start()
            load_after(0, side)
            return carry

        loads[5].wait()
        lax.fori_loop(0, 2, ring_first, 0)

        def spot(k):
            to_y, to_x = lax.rem(k, 2), k // 2
            return 1 - y + to_y * (2 * y - 1), 1 - x + to_x * (2 * x - 1)

        def spread(got, bounds, firsts, group):
            def copy(side, i):
                if side == 0:
                    source, peer = got.at[2 * i + 1 - x, bounds[0]], on_x
                else:
                    source, peer = got.at[2 * (1 - y) + i, bounds[1]], on_y
                return remote(
                    source, firsts[side].at[i], one_s.at[group, side, i], one_r.at[group, side, i], peer
                )

            return copy

        bounds_one = (slice(0, share), slice(share, 2 * share))
        bounds_two = (slice(0, out_rows), slice(out_rows, other_rows))
        spread_one = spread(got_one, bounds_one, (one_a, one_b), 0)
        spread_two = spread(got_two, bounds_two, (two_a, two_b), 1)

        def grads_one(chunk, store):
            lanes = pl.ds(pl.multiple_of(chunk * share, share), share)
            left = wide_buf[:, lanes].T
            store(bounds_one[0], jnp.dot(left, gate_buf[...], preferred_element_type=f32))
            store(bounds_one[1], jnp.dot(left, up_buf[...], preferred_element_type=f32))

        def grads_two(chunk, store):
            load = pltpu.make_async_copy(
                attended.at[:, pl.ds(pl.multiple_of(chunk * piece, piece), piece)], att_buf, att_s
            )
            load.start()
            first = chunk * down_rows
            start = jnp.minimum(first // 128 * 128, units - window)
            lanes = pl.ds(pl.multiple_of(start, 128), window)
            hidden_t[...] = gate_buf[:, lanes].T
            down_part = hidden_t[pl.ds(pl.multiple_of(first - start, 16), down_rows), :]
            store(
                slice(out_rows, other_rows),
                jnp.dot(down_part, wide_buf[...], preferred_element_type=f32),
            )
            load.wait()
            store(
                slice(0, out_rows),
                jnp.dot(
                    att_buf[...].reshape(out_rows, rows), term[...], preferred_element_type=f32
                ),
            )

        def core_copy(group, k):
            at_y, at_x = spot(k)
            sent, got = ((send_one, got_one), (send_two, got_two))[group]
            return remote(
                sent, got.at[2 * at_y + at_x], core_s.at[group, k], core_r.at[group, k], on_core
            )

        def both_sides(group, grads, sent, got, copy, leading):
            def step(k, carry):
                sending, keeping = k < pair, k >= pair
                place_k = lax.rem(k, pair)
                at_y, at_x = spot(place_k)
                index = 2 * at_y + at_x

                @pl.when(keeping)
                def _():
                    core_copy(group, place_k).wait_recv()

                def store(place, value):
                    if place == leading:

                        @pl.when(jnp.logical_and(k >= 1, k <= pair))
                        def _():
                            core_copy(group, k - 1).wait_send()

                    @pl.when(sending)
                    def _():
                        sent[place] = value.astype(bf16)

                    @pl.when(keeping)
                    def _():
                        got[index, place] = (got[index, place].astype(f32) + value).astype(bf16)

                grads(2 * index + jnp.where(sending, 1 - core, core), store)

                @pl.when(sending)
                def _():
                    core_copy(group, place_k).start()

                @pl.when(jnp.logical_and(keeping, place_k < 2))
                def _():
                    copy(0, at_y).start()

                @pl.when(jnp.logical_and(keeping, lax.rem(place_k, 2) == 0))
                def _():
                    copy(1, at_x).start()

                return carry

            lax.fori_loop(0, 2 * pair, step, 0)

        def fold(got, bounds, firsts, copy):
            for i in range(2):
                copy(0, i).wait_recv()
                index = 2 * i + x
                got[index, bounds[0]] = (
                    got[index, bounds[0]].astype(f32) + firsts[0][i].astype(f32)
                ).astype(bf16)
                copy(1, i).wait_recv()
                index = 2 * y + i
                got[index, bounds[1]] = (
                    got[index, bounds[1]].astype(f32) + firsts[1][i].astype(f32)
                ).astype(bf16)

        def last_copy(group, side):
            got, bounds, last = (
                (got_one, bounds_one, (gate_sum, up_sum)), (got_two, bounds_two, (out_sum, down_sum))
            )[group]
            if side == 0:
                source, peer = got.at[2 * (1 - y) + x, bounds[0]], on_y
            else:
                source, peer = got.at[2 * y + 1 - x, bounds[1]], on_x
            return remote(
                source, last[side], two_s.at[group, side], two_r.at[group, side], peer
            )

        def finish(group, side, got, bounds, last):
            last_copy(group, side).wait_recv()
            return (got[here, bounds[side]].astype(f32) + last[...].astype(f32)).astype(bf16)

        for i in range(3):
            loads[i].wait()
        both_sides(0, grads_one, send_one, got_one, spread_one, bounds_one[0])
        loads[3].start()
        loads[4].start()
        ring_next(0)
        loads[4].wait()
        loads[3].wait()
        both_sides(1, grads_two, send_two, got_two, spread_two, bounds_two[1])
        ring_next(1)
        fold(got_one, bounds_one, (one_a, one_b), spread_one)
        for side in range(2):
            last_copy(0, side).start()
        for step in range(2, n_tp - 1):
            ring_next(step)
        lax.fori_loop(1, n_ctx, lambda step, c: (head_copy(step).start(), c)[1], 0)
        grad_out[ctx] = heads_out[ctx]
        fold(got_two, bounds_two, (two_a, two_b), spread_two)
        for side in range(2):
            last_copy(1, side).start()
        gate_sum[...] = finish(0, 0, got_one, bounds_one, gate_sum)
        up_sum[...] = finish(0, 1, got_one, bounds_one, up_sum)
        lax.fori_loop(1, n_ctx, lambda step, c: (head_copy(step).wait(), c)[1], 0)
        out_sum[...] = finish(1, 0, got_two, bounds_two, out_sum)
        down_sum[...] = finish(1, 1, got_two, bounds_two, down_sum)
        for step in range(1, n_tp - 1):
            for side in range(2):
                ring(step, side).wait_send()
        for group, copy in enumerate((spread_one, spread_two)):
            for side in range(2):
                last_copy(group, side).wait_send()
                for i in range(2):
                    copy(side, i).wait_send()

    vmem, anywhere = pl.BlockSpec(memory_space=pltpu.VMEM), pl.BlockSpec(memory_space=pl.ANY)
    dma = pltpu.SemaphoreType.DMA
    return pl.pallas_call(
        kernel,
        out_shape=(
            jax.ShapeDtypeStruct((n_ctx, HEAD, rows), bf16),
            jax.ShapeDtypeStruct((share, units), bf16),
            jax.ShapeDtypeStruct((share, units), bf16),
            jax.ShapeDtypeStruct((out_rows, width), bf16),
            jax.ShapeDtypeStruct((down_rows, width), bf16),
        ),
        in_specs=[anywhere] * 8,
        out_specs=(vmem,) * 5,
        scratch_shapes=[
            pltpu.VMEM((rows, width), bf16),
            pltpu.VMEM((half, width), bf16),
            pltpu.VMEM((rows, width), bf16),
            pltpu.VMEM((rows, units), bf16),
            pltpu.VMEM((rows, units), bf16),
            pltpu.VMEM((window, rows), bf16),
            pltpu.VMEM((n_tp, piece, rows), bf16),
            pltpu.VMEM((n_tp - 1, 2, heads, HEAD, rows), bf16),
            pltpu.VMEM((n_ctx, HEAD, rows), bf16),
            pltpu.VMEM((2 * share, units), bf16),
            pltpu.VMEM((other_rows, width), bf16),
            pltpu.VMEM((pair, 2 * share, units), bf16),
            pltpu.VMEM((pair, other_rows, width), bf16),
            pltpu.VMEM((2, share, units), bf16),
            pltpu.VMEM((2, share, units), bf16),
            pltpu.VMEM((2, out_rows, width), bf16),
            pltpu.VMEM((2, down_rows, width), bf16),
            dma((6,)), dma, dma,
            dma((n_tp - 1, 2)), dma((n_tp - 1, 2)),
            dma((n_ctx,)), dma((n_ctx,)),
            dma((2, pair)), dma((2, pair)),
            dma((2, 2, 2)), dma((2, 2, 2)),
            dma((2, 2)), dma((2, 2)),
        ],
        compiler_params=pltpu.CompilerParams(
            collective_id=4, has_side_effects=True, vmem_limit_bytes=60 * 2**20
        ),
        cost_estimate=pl.CostEstimate(
            flops=2 * rows * width * (2 * units + units + 2 * n_tp * cols),
            bytes_accessed=40 * 2**20,
            transcendentals=0,
        ),
        name="middle_sums",
    )(term, w_all, low, gate, up, hidden, cot, attended)


def final_sums(term, cot, low, grads, out, small):
    n_tp, own, width = term.shape
    rows = low.shape[0]
    cols = grads.shape[0]
    n_ctx = lax.axis_size("ctx")
    share = width // n_ctx
    half_rows, half_width = share // 2, width // 2
    part = out.shape[0]
    columns = cols // 3
    first_rows = small.shape[0] - 4 * width // 128

    def kernel(
        term, cot, low, grads, out, small,
        grad_in, out_all, qkv_all, small_sum,
        small_ctx, small_tp, ring_buf, q_send, q_recv, both, first_a, first_b, second,
        small_s, small_r, norm_s, norm_r, ring_s, ring_r, core_s, core_r, one_s, one_r, two_s, two_r, piece_s, piece_r,
    ):
        ctx, tp = lax.axis_index("ctx"), lax.axis_index("tp")
        y, x, core = ctx // 4, (ctx // 2) % 2, ctx % 2
        on_core, on_x, on_y = ctx + 1 - 2 * core, ctx + 2 - 4 * x, ctx + 4 - 8 * y
        across = on_x + 4 - 8 * y
        here = y * 2 + x
        barrier = pltpu.get_barrier_semaphore()
        for step in range(1, n_ctx):
            peer = lax.rem(ctx + step, n_ctx)
            pl.semaphore_signal(barrier, inc=1, device_id=(peer, tp), device_id_type=MESH)
        for step in range(1, n_tp):
            peer = lax.rem(tp + step, n_tp)
            pl.semaphore_signal(barrier, inc=1, device_id=(ctx, peer), device_id_type=MESH)
        pl.semaphore_wait(barrier, n_ctx + n_tp - 2)

        def remote(source, target, send, recv, peer, near=True):
            return pltpu.make_async_remote_copy(
                src_ref=source,
                dst_ref=target,
                send_sem=send,
                recv_sem=recv,
                device_id=(peer, tp) if near else (ctx, peer),
                device_id_type=MESH,
            )

        def ring(step, piece):
            lanes = slice(piece * half_width, (piece + 1) * half_width)
            first = term.at[lax.rem(tp - 1 + n_tp, n_tp), :, lanes]
            return remote(
                first if step == 0 else ring_buf.at[step - 1, piece],
                ring_buf.at[step, piece],
                ring_s.at[step, piece],
                ring_r.at[step, piece],
                lax.rem(tp + 1, n_tp),
                False,
            )

        def ring_next(step):
            for piece in range(2):
                lanes = slice(piece * half_width, (piece + 1) * half_width)
                ring(step, piece).wait_recv()
                block = lax.rem(tp - 2 - step + 2 * n_tp, n_tp)
                total = ring_buf[step, piece].astype(f32) + term[block, :, lanes].astype(f32)
                if step < n_tp - 2:
                    ring_buf[step, piece] = total.astype(bf16)
                    ring(step + 1, piece).start()
                else:
                    grad_in[:, lanes] = (cot[:, lanes].astype(f32) + total).astype(bf16)

        def rows_of(where, start, stop):
            return lambda chunk: where.at[chunk, start:stop]

        def qkv_rows(start, stop):
            return lambda chunk: qkv_all.at[chunk, :, start:stop]

        pieces = (
            (rows_of(out_all, 0, part), False),
            (qkv_rows(0, half_rows), True),
            (qkv_rows(half_rows, share), False),
        )

        def hop(p, index):
            where, y_first = pieces[p]
            one, two = (on_y, on_x) if y_first else (on_x, on_y)
            chunk, peer = (
                (ctx, one), (ctx, two), (ctx, on_core), (one, two),
                (one, on_core), (two, on_core), (across, on_core),
            )[index]
            place = where(chunk)
            return remote(place, place, piece_s.at[p, index], piece_r.at[p, index], peer)

        def arrived(p, index):
            where, y_first = pieces[p]
            one, two = (on_y, on_x) if y_first else (on_x, on_y)
            chunk = (
                one, two, on_core, across,
                one + on_core - ctx, two + on_core - ctx, across + on_core - ctx,
            )[index]
            place = where(chunk)
            remote(place, place, piece_s.at[p, index], piece_r.at[p, index], on_core).wait_recv()

        def gather_start(p):
            for index in (0, 1, 2):
                hop(p, index).start()

        def gather_one(p):
            arrived(p, 0)
            hop(p, 3).start()
            hop(p, 4).start()

        def gather_two(p):
            arrived(p, 1)
            hop(p, 5).start()
            arrived(p, 3)
            hop(p, 6).start()

        def gather_end(p):
            for index in (2, 4, 5, 6):
                arrived(p, index)
            for index in range(7):
                hop(p, index).wait_send()

        for piece in range(2):
            ring(0, piece).start()
        out_all[ctx] = out[...]
        gather_start(0)

        def small_copy(step):
            peer = lax.rem(ctx + step, n_ctx)
            return remote(small, small_ctx.at[ctx], small_s.at[step], small_r.at[step], peer)

        def norm_copy(step):
            peer = lax.rem(tp + step, n_tp)
            source = small_tp.at[tp]
            return remote(source, source, norm_s.at[step], norm_r.at[step], peer, False)

        for step in range(1, n_ctx):
            small_copy(step).start()
        small_ctx[ctx] = small[...]

        def weight_chunk(chunk, where):
            lanes = pl.ds(pl.multiple_of(chunk * share, share), share)
            left = low[:, lanes].astype(f32).T.astype(bf16)
            for c in range(3):
                where[c] = lax.dot_general(
                    left,
                    grads[c * columns : (c + 1) * columns],
                    (((1,), (1,)), ((), ())),
                    preferred_element_type=f32,
                ).astype(bf16)

        def core_copy(i):
            return remote(q_send.at[i], q_recv.at[i], core_s.at[i], core_r.at[i], on_core)

        def send_chunk(i, carry):
            weight_chunk(2 * i + 1 - core, q_send.at[i])
            core_copy(i).start()
            return carry

        def keep_chunk(i, carry):
            weight_chunk(2 * i + core, both.at[i])
            return carry

        lax.fori_loop(0, n_ctx // 2, send_chunk, 0)
        lax.fori_loop(0, n_ctx // 2, keep_chunk, 0)

        def add_chunk(i, carry):
            core_copy(i).wait_recv()
            both[i] = (both[i].astype(f32) + q_recv[i].astype(f32)).astype(bf16)
            return carry

        lax.fori_loop(0, n_ctx // 2, add_chunk, 0)
        top, bottom = slice(0, half_rows), slice(half_rows, share)

        def one_copy(side, i):
            if side == 0:
                source, target, peer = both.at[2 * i + 1 - x, :, top], first_a.at[i], on_x
            else:
                source, target, peer = both.at[2 * (1 - y) + i, :, bottom], first_b.at[i], on_y
            return remote(source, target, one_s.at[side, i], one_r.at[side, i], peer)

        for side in range(2):
            for i in range(2):
                one_copy(side, i).start()
        ring_next(0)
        for i in range(2):
            one_copy(0, i).wait_recv()
            spot = 2 * i + x
            both[spot, :, top] = (
                both[spot, :, top].astype(f32) + first_a[i].astype(f32)
            ).astype(bf16)
            one_copy(1, i).wait_recv()
            spot = 2 * y + i
            both[spot, :, bottom] = (
                both[spot, :, bottom].astype(f32) + first_b[i].astype(f32)
            ).astype(bf16)

        def two_copy(side):
            if side == 0:
                source, peer = both.at[2 * (1 - y) + x, :, top], on_y
            else:
                source, peer = both.at[2 * y + 1 - x, :, bottom], on_x
            return remote(source, second.at[side], two_s.at[side], two_r.at[side], peer)

        for side in range(2):
            two_copy(side).start()
        ring_next(1)
        for side, span in enumerate((top, bottom)):
            two_copy(side).wait_recv()
            qkv_all[ctx, :, span] = (
                both[here, :, span].astype(f32) + second[side].astype(f32)
            ).astype(bf16)
            gather_start(1 + side)
        for step in range(1, n_ctx):
            small_copy(step).wait_recv()
        value = sum(small_ctx[i] for i in range(n_ctx))
        small_sum[:first_rows] = value[:first_rows]
        small_tp[tp] = value[first_rows:]
        for step in range(1, n_tp):
            norm_copy(step).start()
        for p in range(3):
            gather_one(p)
        for step in range(2, n_tp - 1):
            ring_next(step)
        for p in range(3):
            gather_two(p)
        for step in range(1, n_tp):
            norm_copy(step).wait_recv()
        small_sum[first_rows:] = sum(small_tp[i] for i in range(n_tp))
        for p in range(3):
            gather_end(p)
        for step in range(1, n_ctx):
            small_copy(step).wait_send()
        for step in range(1, n_tp):
            norm_copy(step).wait_send()
        for step in range(n_tp - 1):
            for piece in range(2):
                ring(step, piece).wait_send()
        for i in range(n_ctx // 2):
            core_copy(i).wait_send()
        for side in range(2):
            two_copy(side).wait_send()
            for i in range(2):
                one_copy(side, i).wait_send()

    vmem = pl.BlockSpec(memory_space=pltpu.VMEM)
    dma = pltpu.SemaphoreType.DMA
    pair = n_ctx // 2
    return pl.pallas_call(
        kernel,
        out_shape=(
            jax.ShapeDtypeStruct((own, width), bf16),
            jax.ShapeDtypeStruct((n_ctx, part, width), bf16),
            jax.ShapeDtypeStruct((n_ctx, 3, share, columns), bf16),
            jax.ShapeDtypeStruct(small.shape, f32),
        ),
        in_specs=[vmem] * 6,
        out_specs=(vmem,) * 4,
        scratch_shapes=[
            pltpu.VMEM((n_ctx,) + small.shape, f32),
            pltpu.VMEM((n_tp, small.shape[0] - first_rows, 128), f32),
            pltpu.VMEM((n_tp - 1, 2, own, half_width), bf16),
            pltpu.VMEM((pair, 3, share, columns), bf16),
            pltpu.VMEM((pair, 3, share, columns), bf16),
            pltpu.VMEM((pair, 3, share, columns), bf16),
            pltpu.VMEM((2, 3, half_rows, columns), bf16),
            pltpu.VMEM((2, 3, half_rows, columns), bf16),
            pltpu.VMEM((2, 3, half_rows, columns), bf16),
            dma((n_ctx,)), dma((n_ctx,)),
            dma((n_tp,)), dma((n_tp,)),
            dma((n_tp - 1, 2)), dma((n_tp - 1, 2)),
            dma((pair,)), dma((pair,)),
            dma((2, 2)), dma((2, 2)),
            dma((2,)), dma((2,)),
            dma((3, 7)), dma((3, 7)),
        ],
        compiler_params=pltpu.CompilerParams(
            collective_id=3, has_side_effects=True, vmem_limit_bytes=60 * 2**20
        ),
        cost_estimate=pl.CostEstimate(
            flops=2 * rows * width * cols, bytes_accessed=50 * 2**20, transcendentals=0
        ),
        name="final_sums",
    )(term, cot, low, grads, out, small)


def norm_stats(rows):
    mean = jnp.mean(rows, axis=1, keepdims=True)
    center = rows - mean
    inverse = lax.rsqrt(jnp.mean(center * center, axis=1, keepdims=True) + epsilon)
    return mean, inverse


def norm_backward(grad_out, normed, inverse, gain):
    scaled = grad_out * gain
    grad_rows = inverse * (
        scaled
        - jnp.mean(scaled, axis=1, keepdims=True)
        - normed * jnp.mean(scaled * normed, axis=1, keepdims=True)
    )
    return (grad_rows, jnp.sum(grad_out * normed, axis=0), jnp.sum(grad_out, axis=0))


def rotate(tensor, places, direction):
    half = ROT // 2
    frequency = 10000.0 ** (-2.0 * jnp.arange(half, dtype=f32) / ROT)
    angles = frequency[:, None] * places.astype(f32)[None, :]
    cosine, sines = jnp.cos(angles), direction * jnp.sin(angles)
    first, second = tensor[..., :half, :], tensor[..., half:ROT, :]
    return jnp.concatenate(
        [
            first * cosine - second * sines,
            second * cosine + first * sines,
            tensor[..., ROT:, :],
        ],
        axis=-2,
    )


def after(value, *others):
    return lax.optimization_barrier((value, *others))[0]


def direct_gather(value):
    n_tp = lax.axis_size("tp")
    return [value] + [
        lax.ppermute(value, "tp", [(i, (i + s) % n_tp) for i in range(n_tp)])
        for s in range(1, n_tp)
    ]


def in_tp_order(arrays):
    count = len(arrays)
    shape = arrays[0].shape

    def kernel(tp, *refs):
        sources, out = refs[:count], refs[count]
        for s in range(count):
            out[lax.rem(tp[0] - s + count, count)] = sources[s][...]

    vmem = pl.BlockSpec(memory_space=pltpu.VMEM)
    return pl.pallas_call(
        kernel,
        out_shape=jax.ShapeDtypeStruct((count,) + shape, arrays[0].dtype),
        in_specs=[pl.BlockSpec(memory_space=pltpu.SMEM)] + [vmem] * count,
        out_specs=vmem,
        compiler_params=pltpu.CompilerParams(vmem_limit_bytes=60 * 2**20),
        cost_estimate=pl.CostEstimate(
            flops=0, bytes_accessed=4 * count * math.prod(shape), transcendentals=0
        ),
        name="in_tp_order",
    )(lax.axis_index("tp")[None], *arrays)


def exchange_sum(terms, axis):
    parts = lax.all_to_all(terms, axis, split_axis=0, concat_axis=0, tiled=True)
    return sum(part.astype(f32) for part in parts)


def scatter(partial, axis):
    return lax.psum_scatter(partial, axis, scatter_dimension=0, tiled=True)


def swap(value, axis, bit):
    size = lax.axis_size(axis)
    return lax.ppermute(value, axis, [(i, i ^ (1 << bit)) for i in range(size)])


def pair_sum(partial):
    size, rest = partial.shape[0], partial.shape[1:]
    side = lax.axis_index("ctx") % 2
    pairs = partial.reshape((size // 2, 2) + rest)
    kept = lax.dynamic_index_in_dim(pairs, side, 1, keepdims=False)
    sent = lax.dynamic_index_in_dim(pairs, 1 - side, 1, keepdims=False)
    return (kept.astype(f32) + swap(sent, "ctx", 0).astype(f32)).astype(bf16)


def spread_start(both, *early):
    pairs = both.shape[0]
    mine = lax.axis_index("ctx") // 2
    parts = [lax.dynamic_index_in_dim(both, mine, 0, keepdims=False)]
    for distance in range(1, pairs):
        sent = lax.dynamic_index_in_dim(both, mine ^ distance, 0, keepdims=False)
        perm = [(i, i ^ (2 * distance)) for i in range(2 * pairs)]
        parts.append(lax.ppermute(after(sent, *early) if early else sent, "ctx", perm))
    return parts


def spread_end(parts, *late):
    if late:
        parts = lax.optimization_barrier((*parts, *late))[: len(parts)]
    return sum(part.astype(f32) for part in parts).astype(bf16)


def by_ctx(partial):
    rows, cols = partial.shape
    n_ctx = lax.axis_size("ctx")
    return partial.reshape(n_ctx, rows // n_ctx, cols)


def gather(rows, axis):
    return lax.all_gather(rows, axis, axis=0, tiled=True)


def by_part(chunks):
    devices, parts, rows, cols = chunks.shape

    def kernel(source, target):
        target[...] = source[0].astype(f32)

    return pl.pallas_call(
        kernel,
        grid=(devices,),
        out_shape=jax.ShapeDtypeStruct((parts, devices * rows, cols), f32),
        in_specs=[pl.BlockSpec((1, parts, rows, cols), lambda i: (i, 0, 0, 0))],
        out_specs=pl.BlockSpec((parts, rows, cols), lambda i: (0, i, 0)),
        cost_estimate=pl.CostEstimate(
            flops=0, bytes_accessed=6 * math.prod(chunks.shape), transcendentals=0
        ),
        compiler_params=pltpu.CompilerParams(vmem_limit_bytes=60 * 2**20),
        name="by_part",
    )(chunks)


def interleave(gate, up):
    rows, cols = gate.shape
    tile = 128

    def kernel(gate, up, out):
        out[:, 0, :] = gate[...].astype(f32)
        out[:, 1, :] = up[...].astype(f32)

    return pl.pallas_call(
        kernel,
        grid=(rows // tile,),
        out_shape=jax.ShapeDtypeStruct((rows, 2, cols), f32),
        in_specs=[pl.BlockSpec((tile, cols), lambda i: (i, 0))] * 2,
        out_specs=pl.BlockSpec((tile, 2, cols), lambda i: (i, 0, 0)),
        compiler_params=pltpu.CompilerParams(vmem_limit_bytes=60 * 2**20),
        cost_estimate=pl.CostEstimate(flops=1, bytes_accessed=1, transcendentals=0),
        name="interleave",
    )(gate, up)


def shards(
    layer_in,
    norm_gain,
    norm_bias,
    w_qkv,
    b_qkv,
    w_out,
    w_gate_up,
    w_down,
    cotangent,
    block_table,
    seq_ids,
):
    n_ctx, n_tp = lax.axis_size("ctx"), lax.axis_size("tp")
    ctx, tp = lax.axis_index("ctx"), lax.axis_index("tp")
    own, width = layer_in.shape
    rows = own * n_tp
    cols = w_qkv.shape[2]
    heads = cols // HEAD
    table = block_table.reshape(-1)
    blocks = table.shape[0]
    by_head = heads == n_ctx == 8 and BLK % own == 0
    part = cols // n_ctx

    ids = jnp.arange(blocks, dtype=jnp.int32)
    located = jnp.sum(jnp.where(table[None, :] == ids[:, None], ids[None, :], 0), axis=1)
    same = seq_ids[:, None] == seq_ids[None, :]
    first = jnp.min(jnp.where(same, ids[None, :], blocks), axis=1)
    last = jnp.max(jnp.where(same, ids[None, :], -1), axis=1)
    order = jnp.concatenate([located, first, last, tp[None]]).astype(jnp.int32)
    frequency = 10000.0 ** (-2.0 * jnp.arange(ROT // 2, dtype=f32) / ROT)
    positions = table[:, None] * BLK + jnp.arange(BLK, dtype=jnp.int32)[None, :]
    angles = frequency[None, :, None] * positions.astype(f32)[:, None, :]
    angles = jnp.stack([jnp.cos(angles), jnp.sin(angles)], axis=1)

    hidden_units = w_gate_up.shape[2]
    w_part = lax.dynamic_slice_in_dim(w_out, ctx * part, part, 0)
    if by_head:
        layer_in = after(layer_in, angles, order)
        xs, lows, mean_one, inverse_one, w_part, packed = project_exchange(
            layer_in, w_part, norm_gain[0:1], norm_bias[0:1], w_qkv, b_qkv
        )
        mean_one, inverse_one = [t.reshape(rows, 128)[:, :1] for t in (mean_one, inverse_one)]
        x = xs.reshape(rows, width).astype(f32)
        first_low = lows.reshape(rows, width)
        w_out_all = lax.all_gather(w_part, "ctx", axis=1, tiled=True)
        cot = direct_gather(after(cotangent, packed))
        out, logsum = attention_forward(order, angles, packed)
        middle, lows, mean_two, inverse_two, attended_all = output_project(
            out, xs, w_out_all, norm_gain[1:2], norm_bias[1:2]
        )
        cot = in_tp_order(lax.optimization_barrier((*cot, middle))[:n_tp]).reshape(rows, width)
        middle = middle.reshape(rows, width)
        mean_two, inverse_two = [t.reshape(rows, 128)[:, :1] for t in (mean_two, inverse_two)]
        normed_two = (middle - mean_two) * inverse_two
        second_low = lows.reshape(rows, width)
        attended_all = attended_all.reshape(n_tp * cols, rows)
    else:
        x = gather(layer_in, "tp").astype(f32)
        mean_one, inverse_one = norm_stats(x)
        first_low = ((x - mean_one) * inverse_one * norm_gain[0] + norm_bias[0]).astype(bf16)
        projected = (
            jnp.einsum("dcf,rd->cfr", w_qkv, first_low, preferred_element_type=f32)
            + b_qkv[:, :, None]
        ).reshape(3, heads, HEAD, rows)
        w_part = gather(w_part, "tp").reshape(n_tp, part, width)
        w_out_all = lax.all_gather(w_part, "ctx", axis=1, tiled=True)
        cot = gather(cotangent, "tp")
        places, _ = row_places(ctx * rows, rows, table, seq_ids)
        qkv = jnp.concatenate([rotate(projected[0:2], places, 1.0), projected[2:3]], axis=0)
        queries, keys, values = [t.astype(bf16).transpose(2, 0, 1) for t in qkv]
        visit, offsets = gathered_setup(
            rows, table, seq_ids, keys.reshape(rows, cols), values.reshape(rows, cols)
        )
        out, logsum = gathered_forward(queries, visit, offsets)
        attended_all = gather(out.astype(bf16).reshape(rows, cols).T, "tp")
        middle = x + jnp.einsum(
            "fr,fd->rd",
            attended_all,
            w_out_all.reshape(n_tp * cols, width),
            preferred_element_type=f32,
        )
        mean_two, inverse_two = norm_stats(middle)
        normed_two = (middle - mean_two) * inverse_two
        second_low = (normed_two * norm_gain[1] + norm_bias[1]).astype(bf16)

    grad_hidden = lax.dot_general(cot, w_down, (((1,), (1,)), ((), ())), preferred_element_type=f32)
    gate_up = jnp.einsum("rd,dcf->rcf", second_low, w_gate_up, preferred_element_type=f32)
    gate, up = gate_up[:, 0], gate_up[:, 1]
    sigmoid = jax.nn.sigmoid(gate)
    activated = gate * sigmoid
    hidden = (activated * up).astype(bf16)
    grad_gate = grad_hidden * up * sigmoid * (1.0 + gate * (1.0 - sigmoid))
    grad_up = grad_hidden * activated
    grad_gu = jnp.stack([grad_gate, grad_up], axis=1).astype(bf16)
    grad_second = jnp.einsum("rcf,dcf->rd", grad_gu, w_gate_up, preferred_element_type=f32)

    middle_norm, gain_two, bias_two = norm_backward(
        grad_second, normed_two, inverse_two, norm_gain[1]
    )
    is_own = (jnp.arange(rows, dtype=jnp.int32) // own == tp)[:, None]
    middle_term = (middle_norm + jnp.where(is_own, cot.astype(f32), 0.0)).astype(bf16)
    if by_head:
        grad_att, gate_grad, up_grad, out_grad, down_grad = middle_sums(
            middle_term,
            w_out_all,
            second_low,
            grad_gate.astype(bf16),
            grad_up.astype(bf16),
            hidden,
            cot,
            attended_all.reshape(n_tp, cols, rows),
        )
        down = jnp.dot(after(hidden, grad_att), w_down, preferred_element_type=f32).astype(bf16)
        down = down.reshape(n_tp, own, width)
        down = [lax.dynamic_index_in_dim(down, (tp - s) % n_tp, 0, False) for s in range(n_tp)]
        down = [down[0]] + [
            lax.ppermute(down[s], "tp", [(i, (i - s) % n_tp) for i in range(n_tp)])
            for s in range(1, n_tp)
        ]
        grad_att = after(grad_att, down[0])
    else:
        grad_att = lax.dot_general(
            w_out_all.reshape(n_tp * cols, width),
            middle_term,
            (((1,), (1,)), ((), ())),
            preferred_element_type=f32,
        ).astype(bf16)
        grad_att = scatter(grad_att, "tp")
        down = jnp.dot(hidden, w_down, preferred_element_type=f32).astype(bf16)
        down = [scatter(down, "tp")]

        def weight_grad(left, right):
            return lax.dot_general(
                left, right, (((0,), (0,)), ((), ())), preferred_element_type=f32
            ).astype(bf16)

        gu_grad = jnp.concatenate(
            [pair_sum(by_ctx(weight_grad(second_low, t.astype(bf16)))) for t in (grad_gate, grad_up)],
            axis=1,
        )
        gu_grad = spread_end(spread_start(gu_grad))
        out_grad = jnp.dot(attended_all, middle_term, preferred_element_type=f32).astype(bf16)
        out_grad = out_grad.reshape(n_tp, n_ctx, part, width).transpose(1, 0, 2, 3)
        other_grad = jnp.concatenate(
            [
                pair_sum(out_grad.reshape(n_ctx, n_tp * part, width)),
                pair_sum(by_ctx(weight_grad(hidden, cot))),
            ],
            axis=1,
        )
        other_grad = spread_end(spread_start(other_grad))
        gate_grad, up_grad = jnp.split(gu_grad, 2, axis=0)
        out_grad, down_grad = jnp.split(other_grad, [n_tp * part], axis=0)
    gate_grad, up_grad = gather(gate_grad, "ctx"), gather(up_grad, "ctx")
    out_grad = scatter(out_grad, "tp")
    down_grad = gather(down_grad, "ctx")
    grad_gate_up = interleave(gate_grad, up_grad)

    if by_head:
        grads = attention_backward(order, angles, packed, grad_att, out, logsum)
        grads, *down[:-1] = lax.optimization_barrier((grads, *down[:-1]))
        grads = lax.all_to_all(grads, "ctx", split_axis=0, concat_axis=0, tiled=True)
        grads, grad_gate_up, down[-1] = lax.optimization_barrier((grads, grad_gate_up, down[-1]))
        grad_projected = grads.transpose(1, 0, 2, 3).reshape(3 * cols, rows)
    else:
        grads = gathered_backward(
            queries, visit, offsets, grad_att.T.reshape(rows, heads, HEAD), out, logsum
        )
        grads = jnp.stack([t.transpose(1, 2, 0) for t in grads])
        grads = jnp.concatenate([rotate(grads[0:2], places, -1.0), grads[2:3]], axis=0)
        grad_projected = grads.reshape(3 * cols, rows).astype(bf16)

    down = sum(t.astype(f32) for t in down)
    own_middle = lax.dynamic_slice_in_dim(middle, tp * own, own, 0)
    layer_out = (own_middle + down).astype(bf16)
    grad_first = jnp.einsum(
        "cfr,dcf->rd",
        grad_projected.reshape(3, cols, rows),
        w_qkv,
        preferred_element_type=f32,
    )
    input_norm, gain_one, bias_one = norm_backward(
        grad_first, (x - mean_one) * inverse_one, inverse_one, norm_gain[0]
    )
    input_term = (middle_norm + input_norm).astype(bf16)
    small = jnp.concatenate(
        [
            jnp.sum(grad_projected.astype(f32), axis=1),
            gain_one, gain_two, bias_one, bias_two,
        ]
    ).reshape(-1, 128)
    if by_head:
        grad_input, out_grad, grad_qkv, small = final_sums(
            input_term.reshape(n_tp, own, width),
            cotangent,
            first_low,
            grad_projected,
            out_grad,
            small,
        )
        grad_qkv = by_part(grad_qkv).transpose(1, 0, 2)
        out_grad = out_grad.reshape(cols, width)
        bias_qkv, norms = small[: 3 * cols // 128], small[3 * cols // 128 :]
    else:
        grad_qkv = lax.dot_general(
            first_low, grad_projected, (((0,), (1,)), ((), ())), preferred_element_type=f32
        ).astype(bf16)
        grad_qkv = spread_end(spread_start(pair_sum(by_ctx(grad_qkv))))
        out_grad, grad_qkv = [gather(t, "ctx") for t in (out_grad, grad_qkv)]
        grad_qkv = grad_qkv.reshape(width, 3, cols).astype(f32)
        grad_input = exchange_sum(input_term.reshape(n_tp, own, width), "tp")
        grad_input = (cotangent.astype(f32) + grad_input).astype(bf16)
        bias_qkv = lax.psum(small[: 3 * cols // 128], "ctx")
        norms = lax.psum(small[3 * cols // 128 :], ("ctx", "tp"))
    norms = norms.reshape(2, 2, width)
    return (
        layer_out,
        grad_input,
        norms[0],
        norms[1],
        grad_qkv,
        bias_qkv.reshape(3, cols),
        out_grad.astype(f32),
        grad_gate_up,
        down_grad.astype(f32),
    )


def solution(mesh):
    placed = (
        P(("ctx", "tp"), None),
        P(),
        P(),
        P(None, None, "tp"),
        P(None, "tp"),
        P("tp", None),
        P(None, None, "tp"),
        P("tp", None),
        P(("ctx", "tp"), None),
        P(),
        P(),
    )
    return jax.shard_map(
        shards,
        mesh=mesh,
        in_specs=placed,
        out_specs=(
            P(("ctx", "tp"), None),
            P(("ctx", "tp"), None),
            P(),
            P(),
            P(None, None, "tp"),
            P(None, "tp"),
            P("tp", None),
            P(None, None, "tp"),
            P("tp", None),
        ),
        check_vma=False,
    )
```

```python
import math

import jax
import jax.numpy as jnp
from jax import lax
from jax.experimental import pallas as pl
from jax.experimental.pallas import tpu as pltpu
from jax.sharding import PartitionSpec as P

HEAD = 64
ROT = 16
BLK = 512
EXTRA = 16

epsilon = 1e-05
neg_large = -1e30
bf16 = jnp.bfloat16
f32 = jnp.float32


def dot(left, right, left_dim, right_dim):
    return lax.dot_general(
        left, right, (((left_dim,), (right_dim,)), ((), ())), preferred_element_type=f32
    )


def causal_keep():
    return lax.broadcasted_iota(jnp.int32, (BLK, BLK), 0) <= lax.broadcasted_iota(
        jnp.int32, (BLK, BLK), 1
    )


def turn(tile):
    return tile.astype(f32).T.astype(bf16)


def scan_chunks(devices, chunks, width, visit):
    per_block = BLK // width

    def source(device, carry):
        for chunk in range(chunks):
            place = device * (chunks // per_block) + chunk // per_block
            visit(chunk, device, place, slice((chunk % per_block) * width, (chunk % per_block + 1) * width))
        return carry

    lax.fori_loop(0, devices, source, 0)


def turn_dims(tile, cosine, sine):
    half = ROT // 2
    first, second = tile[0:half], tile[half:ROT]
    return jnp.concatenate(
        [first * cosine - second * sine, second * cosine + first * sine, tile[ROT:]], axis=0
    )


def attention_forward(order, angles, packed):
    count, devices, _, _, width = packed.shape
    blocks = devices * count * width // BLK

    def kernel(order, angles, packed, out, logsum, queries, keys, values):
        per_device = count * width // BLK
        row = lax.broadcasted_iota(jnp.int32, (EXTRA, BLK), 0)
        ones = jnp.where(row == 0, 1.0, 0.0).astype(bf16)

        def visit(chunk, device, place, lanes):
            part = packed.at[chunk]
            cosine, sine = angles[place, 0, :, lanes], angles[place, 1, :, lanes]
            query = turn_dims(part[device, 0].astype(f32), cosine, sine).astype(bf16)
            queries[place, :, lanes] = query * jnp.asarray(HEAD**-0.5, bf16)
            key = turn_dims(part[device, 1].astype(f32), cosine, sine).astype(bf16)
            keys[place, lanes, :] = turn(key)
            values[place, 0:HEAD, lanes] = part[device, 2]

        scan_chunks(devices, count, width, visit)

        def prepare(place, carry):
            values[place, HEAD : HEAD + EXTRA, :] = ones
            return carry

        lax.fori_loop(0, blocks, prepare, 0)
        keep = causal_keep()

        def query_block(i, carry):
            place = order[i]
            query = queries[place]

            def step(keys_at, state, masked):
                maxima, summed = state
                places = [order[j] for j in keys_at]
                scores = [dot(keys[other], query, 1, 0) for other in places]
                if masked:
                    scores = [jnp.where(keep, tile, neg_large) for tile in scores]
                new_maxima = maxima
                for tile in scores:
                    new_maxima = jnp.maximum(new_maxima, jnp.max(tile, axis=0, keepdims=True))
                summed = summed * jnp.exp(maxima - new_maxima)
                for other, tile in zip(places, scores):
                    weights = jnp.exp(tile - new_maxima).astype(bf16)
                    summed = summed + dot(values[other], weights, 1, 0)
                return new_maxima, summed

            state = (jnp.full((1, BLK), neg_large, f32), jnp.zeros((HEAD + EXTRA, BLK), f32))
            first = order[blocks + i]
            triples = (i - first) // 3
            state = lax.fori_loop(
                0, triples, lambda t, s: step([first + 3 * t + u for u in range(3)], s, False), state
            )
            state = lax.fori_loop(
                first + 3 * triples, i, lambda j, s: step([j], s, False), state
            )
            maxima, summed = step([i], state, True)
            totals = summed[HEAD : HEAD + 1]
            result = (summed[0:HEAD] / totals).astype(bf16)
            logsum[place] = maxima + jnp.log(totals)
            lane = pl.multiple_of(lax.rem(place, per_device) * BLK, BLK)
            out[place // per_device, :, pl.ds(lane, BLK)] = result
            return carry

        lax.fori_loop(0, blocks, query_block, 0)

    vmem = pl.BlockSpec(memory_space=pltpu.VMEM)
    return pl.pallas_call(
        kernel,
        out_shape=(
            jax.ShapeDtypeStruct((devices, HEAD, count * width), bf16),
            jax.ShapeDtypeStruct((blocks, 1, BLK), f32),
        ),
        in_specs=[pl.BlockSpec(memory_space=pltpu.SMEM), vmem, vmem],
        out_specs=(vmem, vmem),
        scratch_shapes=[
            pltpu.VMEM((blocks, HEAD, BLK), bf16),
            pltpu.VMEM((blocks, BLK, HEAD), bf16),
            pltpu.VMEM((blocks, HEAD + EXTRA, BLK), bf16),
        ],
        compiler_params=pltpu.CompilerParams(vmem_limit_bytes=60 * 2**20),
        cost_estimate=pl.CostEstimate(
            flops=85 * 2 * 2 * BLK * BLK * 256, bytes_accessed=5 * 2**20, transcendentals=0
        ),
        name="attention_forward",
    )(order, angles, packed)


def attention_backward(order, angles, packed, grad_out, out, logsum):
    count, devices, _, _, width = packed.shape
    blocks = devices * count * width // BLK
    wide = HEAD + EXTRA

    def kernel(
        order, angles, packed, grad_out, out, logsum,
        grads, query_x, grad_x, key_x, key_rows, value_x, grad_q,
    ):
        row = lax.broadcasted_iota(jnp.int32, (EXTRA, width), 0)
        lane_ids = lax.broadcasted_iota(jnp.int32, (BLK, EXTRA), 1)
        ones = jnp.where(lane_ids < 3, 1.0, 0.0).astype(bf16)

        def three_rows(value):
            high = value.astype(bf16).astype(f32)
            rest = value - high
            middle = rest.astype(bf16).astype(f32)
            low = rest - middle
            return jnp.where(
                row == 0, high, jnp.where(row == 1, middle, jnp.where(row == 2, low, 0.0))
            ).astype(bf16)

        def visit(chunk, device, place, lanes):
            part = packed.at[chunk]
            cosine, sine = angles[place, 0, :, lanes], angles[place, 1, :, lanes]
            query = turn_dims(part[device, 0].astype(f32), cosine, sine).astype(bf16)
            query_x[place, 0:HEAD, lanes] = query * jnp.asarray(HEAD**-0.5, bf16)
            query_x[place, HEAD:wide, lanes] = three_rows(-logsum[place, :, lanes])
            key = turn_dims(part[device, 1].astype(f32), cosine, sine).astype(bf16)
            key_rows[place, :, lanes] = key
            key_x[place, lanes, 0:HEAD] = turn(key)
            value_x[place, lanes, 0:HEAD] = turn(part[device, 2])
            own = slice(chunk * width, (chunk + 1) * width)
            grad = grad_out[device, :, own]
            delta = jnp.sum(
                grad.astype(f32) * out[device, :, own].astype(f32), axis=0, keepdims=True
            )
            grad_x[place, 0:HEAD, lanes] = grad
            grad_x[place, HEAD:wide, lanes] = three_rows(-delta)

        scan_chunks(devices, count, width, visit)

        def prepare(place, carry):
            key_x[place, :, HEAD:wide] = ones
            value_x[place, :, HEAD:wide] = ones
            grad_q[place] = jnp.zeros((HEAD, BLK), f32)
            return carry

        lax.fori_loop(0, blocks, prepare, 0)
        keep = causal_keep()
        per_device = count * width // BLK

        def store(part, place, tile):
            lane = pl.multiple_of(lax.rem(place, per_device) * BLK, BLK)
            grads[place // per_device, part, :, pl.ds(lane, BLK)] = tile

        def key_block(j, carry):
            place = order[j]
            key, value = key_x[place], value_x[place]
            key_tile = key_rows[place]

            def step(queries_at, state, masked):
                grad_k, grad_v = state
                places = [order[i] for i in queries_at]
                scores = [dot(key, query_x[other], 1, 0) for other in places]
                grad_probs = [dot(value, grad_x[other], 1, 0) for other in places]
                probs = [jnp.exp(tile) for tile in scores]
                if masked:
                    probs = [jnp.where(keep, tile, 0.0) for tile in probs]
                grad_raws = [(p * g).astype(bf16) for p, g in zip(probs, grad_probs)]
                for other, prob, grad_raw in zip(places, probs, grad_raws):
                    grad_v = grad_v + dot(grad_x[other, 0:HEAD, :], prob.astype(bf16), 1, 1)
                    grad_k = grad_k + dot(query_x[other, 0:HEAD, :], grad_raw, 1, 1)
                    grad_q[other] += dot(key_tile, grad_raw, 1, 0)
                return grad_k, grad_v

            zero = jnp.zeros((HEAD, BLK), f32)
            state = step([j], (zero, zero), True)
            end = order[2 * blocks + j]
            pairs = (end - j) // 2
            state = lax.fori_loop(
                0, pairs, lambda t, s: step([j + 1 + 2 * t, j + 2 + 2 * t], s, False), state
            )
            grad_k, grad_v = lax.fori_loop(
                j + 1 + 2 * pairs, end + 1, lambda i, s: step([i], s, False), state
            )
            cosine, sine = angles[place, 0], angles[place, 1]
            store(1, place, turn_dims(grad_k, cosine, -sine).astype(bf16))
            store(2, place, grad_v.astype(bf16))
            return carry

        lax.fori_loop(0, blocks, key_block, 0)

        def finish(place, carry):
            tile = turn_dims(grad_q[place] * HEAD**-0.5, angles[place, 0], -angles[place, 1])
            store(0, place, tile.astype(bf16))
            return carry

        lax.fori_loop(0, blocks, finish, 0)

    vmem = pl.BlockSpec(memory_space=pltpu.VMEM)
    return pl.pallas_call(
        kernel,
        out_shape=jax.ShapeDtypeStruct((devices, 3, HEAD, count * width), bf16),
        in_specs=[pl.BlockSpec(memory_space=pltpu.SMEM)] + [vmem] * 5,
        out_specs=vmem,
        scratch_shapes=[
            pltpu.VMEM((blocks, wide, BLK), bf16),
            pltpu.VMEM((blocks, wide, BLK), bf16),
            pltpu.VMEM((blocks, BLK, wide), bf16),
            pltpu.VMEM((blocks, HEAD, BLK), bf16),
            pltpu.VMEM((blocks, BLK, wide), bf16),
            pltpu.VMEM((blocks, HEAD, BLK), f32),
        ],
        compiler_params=pltpu.CompilerParams(vmem_limit_bytes=60 * 2**20),
        cost_estimate=pl.CostEstimate(flops=1, bytes_accessed=1, transcendentals=0),
        name="attention_backward",
    )(order, angles, packed, grad_out, out, logsum)


def row_places(first_row, length, table_flat, seq_ids):
    row_ids = first_row + jnp.arange(length, dtype=jnp.int32)
    block_ids = jnp.arange(table_flat.shape[0], dtype=jnp.int32)
    natural = jnp.sum(
        jnp.where((row_ids // BLK)[:, None] == block_ids[None, :], table_flat[None, :], 0), axis=1
    )
    sequence = jnp.sum(
        jnp.where(natural[:, None] == block_ids[None, :], seq_ids[None, :], 0), axis=1
    )
    return (natural * BLK + row_ids % BLK, sequence)


def gathered_setup(rows, table_flat, seq_ids, key_flat, value_flat):
    places, seq = row_places(lax.axis_index("ctx") * rows, rows, table_flat, seq_ids)
    pieces = (
        lax.all_gather(key_flat, "ctx", axis=0, tiled=True),
        lax.all_gather(value_flat, "ctx", axis=0, tiled=True),
    )
    stride = math.gcd(pieces[0].shape[0], 1024)
    offsets = jnp.arange(pieces[0].shape[0] // stride, dtype=jnp.int32) * stride

    def visit(offset):
        other_places, other_seq = row_places(offset, stride, table_flat, seq_ids)
        allowed = (seq[:, None] == other_seq[None, :]) & (other_places[None, :] <= places[:, None])
        blocks = [
            lax.dynamic_slice_in_dim(piece, offset, stride, 0).reshape(stride, -1, HEAD)
            for piece in pieces
        ]
        return allowed[:, None, :], blocks[0], blocks[1]

    return visit, offsets


def gathered_forward(queries, visit, offsets):
    rows, heads, _ = queries.shape

    def step(status, offset):
        allowed, keys, values = visit(offset)
        scores = jnp.einsum("qhe,khe->qhk", queries, keys, preferred_element_type=f32)
        scores = scores * HEAD**-0.5
        maxima, totals, summed = status
        new_maxima = jnp.maximum(maxima, jnp.max(jnp.where(allowed, scores, neg_large), axis=2))
        weights = jnp.where(allowed, jnp.exp(scores - new_maxima[..., None]), 0.0)
        factor = jnp.exp(maxima - new_maxima)
        totals = totals * factor + jnp.sum(weights, axis=2)
        summed = summed * factor[..., None] + jnp.einsum(
            "qhk,khe->qhe", weights.astype(bf16), values, preferred_element_type=f32
        )
        return ((new_maxima, totals, summed), None)

    initial = (
        jnp.full((rows, heads), neg_large, f32),
        jnp.zeros((rows, heads), f32),
        jnp.zeros((rows, heads, HEAD), f32),
    )
    (maxima, totals, summed), _ = lax.scan(step, initial, offsets)
    return summed / totals[..., None], maxima + jnp.log(totals)


def gathered_backward(queries, visit, offsets, grad_att, attended, logsum):
    rows, heads, _ = queries.shape
    delta = jnp.sum(grad_att.astype(f32) * attended, axis=2)

    def step(status, offset):
        allowed, keys, values = visit(offset)
        scores = jnp.einsum("qhe,khe->qhk", queries, keys, preferred_element_type=f32)
        prob = jnp.where(allowed, jnp.exp(scores * HEAD**-0.5 - logsum[..., None]), 0.0)
        grad_prob = jnp.einsum("qhe,khe->qhk", grad_att, values, preferred_element_type=f32)
        grad_raw = (prob * (grad_prob - delta[..., None]) * HEAD**-0.5).astype(bf16)
        grad_q = jnp.einsum("qhk,khe->qhe", grad_raw, keys, preferred_element_type=f32)
        grad_k = jnp.einsum("qhk,qhe->khe", grad_raw, queries, preferred_element_type=f32)
        grad_v = jnp.einsum("qhk,qhe->khe", prob.astype(bf16), grad_att, preferred_element_type=f32)
        return (
            (
                status[0] + grad_q,
                lax.dynamic_update_slice_in_dim(status[1], grad_k, offset, 0),
                lax.dynamic_update_slice_in_dim(status[2], grad_v, offset, 0),
            ),
            None,
        )

    total = rows * lax.axis_size("ctx")
    zero = jnp.zeros((total, heads, HEAD), f32)
    (grad_q, grad_k, grad_v), _ = lax.scan(
        step, (jnp.zeros((rows, heads, HEAD), f32), zero, zero), offsets
    )
    grad_k = lax.psum_scatter(grad_k, "ctx", scatter_dimension=0, tiled=True)
    grad_v = lax.psum_scatter(grad_v, "ctx", scatter_dimension=0, tiled=True)
    return grad_q, grad_k, grad_v


MESH = pl.DeviceIdType.MESH


def greet(n_ctx, n_tp):
    ctx, tp = lax.axis_index("ctx"), lax.axis_index("tp")
    barrier = pltpu.get_barrier_semaphore()

    def greet_ctx(step, carry):
        peer = lax.rem(ctx + step, n_ctx)
        pl.semaphore_signal(barrier, inc=1, device_id=(peer, tp), device_id_type=MESH)
        return carry

    lax.fori_loop(1, n_ctx, greet_ctx, 0)
    for peer in (lax.rem(tp + 1, n_tp), lax.rem(tp + n_tp - 1, n_tp)):
        pl.semaphore_signal(barrier, inc=1, device_id=(ctx, peer), device_id_type=MESH)
    pl.semaphore_wait(barrier, n_ctx + 1)


def rows_norm(source, stored, gain, shift, mean_out, inverse_out, tile):
    def step(i, carry):
        rows = pl.ds(pl.multiple_of(i * tile, tile), tile)
        x = source(rows)
        mean = jnp.mean(x, axis=1, keepdims=True)
        center = x - mean
        inverse = lax.rsqrt(jnp.mean(center * center, axis=1, keepdims=True) + epsilon)
        stored(rows, (center * inverse * gain + shift).astype(bf16))
        mean_out[rows, :] = jnp.broadcast_to(mean, (tile, 128))
        inverse_out[rows, :] = jnp.broadcast_to(inverse, (tile, 128))
        return carry

    return step


def project_exchange(layer_in, w_part, gain, shift, w_qkv, b_qkv):
    n_ctx, n_tp = lax.axis_size("ctx"), lax.axis_size("tp")
    own, width = layer_in.shape
    part = w_part.shape[0]
    cols = w_qkv.shape[2]

    def kernel(
        x_in, w_in, gain, shift, w_qkv_in, b_qkv,
        xs_out, lows_out, means, inverses, ws, packed,
        xs, lows, w_qkv, load_s, store_s, outgoing, ring_send, ring_recv, w_send, w_recv, send, recv,
    ):
        ctx, tp = lax.axis_index("ctx"), lax.axis_index("tp")
        right = lax.rem(tp + 1, n_tp)
        half = own // 2

        def block(slot):
            return lax.rem(tp - slot + n_tp, n_tp)

        def ring(step, piece):
            rows = pl.ds(piece * half, half)
            return pltpu.make_async_remote_copy(
                src_ref=x_in.at[rows] if step == 0 else xs.at[block(step), rows],
                dst_ref=xs.at[block(step), rows],
                send_sem=ring_send.at[step, piece],
                recv_sem=ring_recv.at[step, piece],
                device_id=(ctx, right),
                device_id_type=MESH,
            )

        def w_ring(step):
            return pltpu.make_async_remote_copy(
                src_ref=w_in if step == 0 else ws.at[block(step)],
                dst_ref=ws.at[block(step)],
                send_sem=w_send.at[step],
                recv_sem=w_recv.at[step],
                device_id=(ctx, right),
                device_id_type=MESH,
            )

        def exchange(slot, step):
            peer = lax.rem(ctx + step, n_ctx)
            return pltpu.make_async_remote_copy(
                src_ref=outgoing.at[slot, peer],
                dst_ref=packed.at[block(slot), ctx],
                send_sem=send.at[slot, step],
                recv_sem=recv.at[slot, step],
                device_id=(peer, tp),
                device_id_type=MESH,
            )

        load = pltpu.make_async_copy(w_qkv_in, w_qkv, load_s)
        load.start()

        def store(slot, which):
            here = block(slot)
            source, target = ((xs, xs_out), (lows, lows_out))[which]
            return pltpu.make_async_copy(source.at[here], target.at[here], store_s.at[slot, which])

        greet(n_ctx, n_tp)
        for piece in range(2):
            ring(0, piece).start()
        xs[tp] = x_in[...]
        ws[tp] = w_in[...]
        for slot in range(n_tp):
            if slot > 0:
                for piece in range(2):
                    ring(slot - 1, piece).wait_recv()
                    if slot < n_tp - 1:
                        ring(slot, piece).start()
            if slot == n_tp - 2:
                w_ring(0).start()
            if slot == n_tp - 1:
                w_ring(0).wait_recv()
                w_ring(1).start()

            here = block(slot)

            def stored(rows, value, here=here):
                lows[here, rows, :] = value

            step = rows_norm(
                lambda rows, here=here: xs[here, rows, :].astype(f32),
                stored, gain[...], shift[...], means.at[here], inverses.at[here], 32,
            )
            lax.fori_loop(0, own // 32, step, 0)
            store(slot, 0).start()
            store(slot, 1).start()
            if slot == 0:
                load.wait()

            def project(c, carry, slot=slot, here=here):
                value = jnp.dot(lows[here], w_qkv[c], preferred_element_type=f32) + b_qkv[c]
                outgoing[slot, :, c] = value.T.astype(bf16).reshape(n_ctx, HEAD, own)
                return carry

            lax.fori_loop(0, 3, project, 0)
            lax.fori_loop(
                1, n_ctx, lambda step, c, slot=slot: (exchange(slot, step).start(), c)[1], 0
            )
            packed[here, ctx] = outgoing[slot, ctx]
        for step in range(1, n_tp - 1):
            w_ring(step).wait_recv()
            if step < n_tp - 2:
                w_ring(step + 1).start()
        for slot in range(n_tp):
            lax.fori_loop(
                1, n_ctx, lambda step, c, slot=slot: (exchange(slot, step).wait(), c)[1], 0
            )
        for slot in range(n_tp):
            store(slot, 0).wait()
            store(slot, 1).wait()
        for step in range(n_tp - 1):
            w_ring(step).wait_send()
            for piece in range(2):
                ring(step, piece).wait_send()

    vmem, anywhere = pl.BlockSpec(memory_space=pltpu.VMEM), pl.BlockSpec(memory_space=pl.ANY)
    return pl.pallas_call(
        kernel,
        out_shape=(
            jax.ShapeDtypeStruct((n_tp, own, width), bf16),
            jax.ShapeDtypeStruct((n_tp, own, width), bf16),
            jax.ShapeDtypeStruct((n_tp, own, 128), f32),
            jax.ShapeDtypeStruct((n_tp, own, 128), f32),
            jax.ShapeDtypeStruct((n_tp, part, width), bf16),
            jax.ShapeDtypeStruct((n_tp, n_ctx, 3, HEAD, own), bf16),
        ),
        in_specs=[vmem] * 4 + [anywhere, vmem],
        out_specs=(anywhere,) * 2 + (vmem,) * 4,
        scratch_shapes=[
            pltpu.VMEM((n_tp, own, width), bf16),
            pltpu.VMEM((n_tp, own, width), bf16),
            pltpu.VMEM((3, width, cols), bf16),
            pltpu.SemaphoreType.DMA,
            pltpu.SemaphoreType.DMA((n_tp, 2)),
            pltpu.VMEM((n_tp, n_ctx, 3, HEAD, own), bf16),
            pltpu.SemaphoreType.DMA((n_tp - 1, 2)),
            pltpu.SemaphoreType.DMA((n_tp - 1, 2)),
            pltpu.SemaphoreType.DMA((n_tp - 1,)),
            pltpu.SemaphoreType.DMA((n_tp - 1,)),
            pltpu.SemaphoreType.DMA((n_tp, n_ctx)),
            pltpu.SemaphoreType.DMA((n_tp, n_ctx)),
        ],
        compiler_params=pltpu.CompilerParams(
            collective_id=1, has_side_effects=True, vmem_limit_bytes=60 * 2**20
        ),
        cost_estimate=pl.CostEstimate(
            flops=2 * n_tp * own * width * 3 * cols, bytes_accessed=20 * 2**20, transcendentals=0
        ),
        name="project_exchange",
    )(layer_in, w_part, gain, shift, w_qkv.transpose(1, 0, 2), b_qkv[:, None, :])


def output_project(out, xs, w_all, gain, shift):
    n_ctx, n_tp = lax.axis_size("ctx"), lax.axis_size("tp")
    own, width = xs.shape[1:]
    cols = w_all.shape[1]
    rows_all = n_tp * own

    def kernel(
        out, xs_in, w_in, gain, shift,
        middle_out, lows_out, means, inverses, raw,
        xs, w_all, middle, lows, load_s, store_s, ring_send, ring_recv, send, recv, own_sem,
    ):
        ctx, tp = lax.axis_index("ctx"), lax.axis_index("tp")
        right = lax.rem(tp + 1, n_tp)
        half = cols // 2

        def block(slot):
            return lax.rem(tp - slot + n_tp, n_tp)

        def ring(step, piece):
            rows = pl.ds(piece * half, half)
            return pltpu.make_async_remote_copy(
                src_ref=raw.at[block(step), rows],
                dst_ref=raw.at[block(step), rows],
                send_sem=ring_send.at[step, piece],
                recv_sem=ring_recv.at[step, piece],
                device_id=(ctx, right),
                device_id_type=MESH,
            )

        def exchange(step):
            peer = lax.rem(ctx + step, n_ctx)
            return pltpu.make_async_remote_copy(
                src_ref=out.at[peer],
                dst_ref=raw.at[tp, pl.ds(pl.multiple_of(ctx * HEAD, HEAD), HEAD)],
                send_sem=send.at[step],
                recv_sem=recv.at[step],
                device_id=(peer, tp),
                device_id_type=MESH,
            )

        loads = (
            pltpu.make_async_copy(xs_in, xs, load_s.at[0]),
            pltpu.make_async_copy(w_in, w_all, load_s.at[1]),
        )
        for load in loads:
            load.start()

        def store(place, which):
            source, target = ((middle, middle_out), (lows, lows_out))[which]
            return pltpu.make_async_copy(
                source.at[place], target.at[place], store_s.at[place, which]
            )

        greet(n_ctx, n_tp)
        lax.fori_loop(1, n_ctx, lambda step, c: (exchange(step).start(), c)[1], 0)
        keep = pltpu.make_async_copy(
            out.at[ctx], raw.at[tp, pl.ds(pl.multiple_of(ctx * HEAD, HEAD), HEAD)], own_sem
        )
        keep.start()
        keep.wait()
        lax.fori_loop(1, n_ctx, lambda step, c: (exchange(step).wait_recv(), c)[1], 0)
        for piece in range(2):
            ring(0, piece).start()
        for load in loads:
            load.wait()
        for slot in range(n_tp):
            if slot > 0:
                for piece in range(2):
                    ring(slot - 1, piece).wait_recv()
                    if slot < n_tp - 1:
                        ring(slot, piece).start()
            here = block(slot)

            def project(place, carry, slot=slot, here=here):
                lanes = pl.ds(pl.multiple_of(place * own, own), own)
                tile = raw[here, :, lanes].astype(f32).T.astype(bf16)
                value = jnp.dot(tile, w_all[here], preferred_element_type=f32)
                if slot == 0:
                    middle[place] = xs[place].astype(f32) + value
                else:
                    middle[place] += value
                return carry

            lax.fori_loop(0, n_tp, project, 0)
        for place in range(n_tp):
            store(place, 0).start()

            def stored(rows, value, place=place):
                lows[place, rows, :] = value

            step = rows_norm(
                lambda rows, place=place: middle[place, rows, :],
                stored, gain[...], shift[...], means.at[place], inverses.at[place], 32,
            )
            lax.fori_loop(0, own // 32, step, 0)
            store(place, 1).start()
        lax.fori_loop(1, n_ctx, lambda step, c: (exchange(step).wait_send(), c)[1], 0)
        for place in range(n_tp):
            store(place, 0).wait()
            store(place, 1).wait()
        for step in range(n_tp - 1):
            for piece in range(2):
                ring(step, piece).wait_send()

    vmem, anywhere = pl.BlockSpec(memory_space=pltpu.VMEM), pl.BlockSpec(memory_space=pl.ANY)
    return pl.pallas_call(
        kernel,
        out_shape=(
            jax.ShapeDtypeStruct((n_tp, own, width), f32),
            jax.ShapeDtypeStruct((n_tp, own, width), bf16),
            jax.ShapeDtypeStruct((n_tp, own, 128), f32),
            jax.ShapeDtypeStruct((n_tp, own, 128), f32),
            jax.ShapeDtypeStruct((n_tp, cols, rows_all), bf16),
        ),
        in_specs=[vmem, anywhere, anywhere, vmem, vmem],
        out_specs=(anywhere,) * 2 + (vmem,) * 3,
        scratch_shapes=[
            pltpu.VMEM((n_tp, own, width), bf16),
            pltpu.VMEM((n_tp, cols, width), bf16),
            pltpu.VMEM((n_tp, own, width), f32),
            pltpu.VMEM((n_tp, own, width), bf16),
            pltpu.SemaphoreType.DMA((2,)),
            pltpu.SemaphoreType.DMA((n_tp, 2)),
            pltpu.SemaphoreType.DMA((n_tp - 1, 2)),
            pltpu.SemaphoreType.DMA((n_tp - 1, 2)),
            pltpu.SemaphoreType.DMA((n_ctx,)),
            pltpu.SemaphoreType.DMA((n_ctx,)),
            pltpu.SemaphoreType.DMA,
        ],
        compiler_params=pltpu.CompilerParams(
            collective_id=2, has_side_effects=True, vmem_limit_bytes=60 * 2**20
        ),
        cost_estimate=pl.CostEstimate(
            flops=2 * rows_all * n_tp * cols * width, bytes_accessed=30 * 2**20, transcendentals=0
        ),
        name="output_project",
    )(out, xs, w_all, gain, shift)


def middle_sums(term, w_all, low, gate, up, hidden, cot, attended, w_down):
    rows, width = term.shape
    n_tp, cols, _ = w_all.shape
    n_ctx = lax.axis_size("ctx")
    units = gate.shape[1]
    share, piece = width // n_ctx, cols // n_ctx
    out_rows, down_rows = n_tp * piece, units // n_ctx
    other_rows = out_rows + down_rows
    half, heads = cols // 2, cols // 2 // HEAD
    window = min(units, (down_rows + 127 + 127) // 128 * 128)
    pair = n_ctx // 2
    tile = 256

    def kernel(
        term_in, w_all, low, gate, up, hidden, cot, attended, w_down,
        grad_out, gate_sum, up_sum, out_sum, down_sum, *rest,
    ):
        down_terms, (
            term, w_buf, wide_buf, gate_buf, up_buf, hidden_t, att_buf, tile_in, tile_out, ring_buf, heads_out, send_one, send_two, got_one, got_two, one_a, one_b,
            two_a, two_b,
            tile_s, load_s, w_s, att_s, ring_s, ring_r, head_s, head_r, core_s, core_r, one_s, one_r, two_s, two_r,
        ) = rest[:n_tp], rest[n_tp:]
        ctx, tp = lax.axis_index("ctx"), lax.axis_index("tp")
        y, x, core = ctx // 4, (ctx // 2) % 2, ctx % 2
        on_core, on_x, on_y = ctx + 1 - 2 * core, ctx + 2 - 4 * x, ctx + 4 - 8 * y
        here = y * 2 + x

        def remote(source, target, send, recv, peer, near=True):
            return pltpu.make_async_remote_copy(
                src_ref=source,
                dst_ref=target,
                send_sem=send,
                recv_sem=recv,
                device_id=(peer, tp) if near else (ctx, peer),
                device_id_type=MESH,
            )

        def w_load(block, side):
            rows_in = pl.ds(side * half, half)
            return pltpu.make_async_copy(w_all.at[block, rows_in], w_buf, w_s)

        def dest(step):
            return lax.rem(tp - 1 - step + 2 * n_tp, n_tp)

        loads = [
            pltpu.make_async_copy(source, target, load_s.at[i])
            for i, (source, target) in enumerate(
                ((low, wide_buf), (gate, gate_buf), (up, up_buf), (cot, wide_buf), (hidden, gate_buf), (term_in, term))
            )
        ]
        loads[5].start()
        w_load(dest(0), 0).start()
        for i in range(3):
            loads[i].start()
        greet(n_ctx, n_tp)

        def own_term(step, side):
            w_load(dest(step), side).wait()
            return lax.dot_general(
                w_buf[...], term[...], (((1,), (1,)), ((), ())), preferred_element_type=f32
            ).reshape(heads, HEAD, rows)

        def load_after(step, side):
            @pl.when(jnp.logical_or(side == 0, step < n_tp - 1))
            def _():
                w_load(lax.rem(tp - 1 - step - side + 2 * n_tp, n_tp), 1 - side).start()

        def ring(step, side):
            return remote(
                heads_out.at[pl.ds(side * heads, heads)]
                if step == 0
                else ring_buf.at[step - 1, side],
                ring_buf.at[step, side],
                ring_s.at[step, side],
                ring_r.at[step, side],
                lax.rem(tp + 1, n_tp),
                False,
            )

        def head_copy(step):
            peer = lax.rem(ctx + step, n_ctx)
            return remote(
                heads_out.at[peer], grad_out.at[ctx], head_s.at[step], head_r.at[step], peer
            )

        def ring_next(step):
            def one_side(side, carry):
                value = own_term(step + 1, side)
                ring(step, side).wait_recv()
                value = (value + ring_buf[step, side].astype(f32)).astype(bf16)
                if step < n_tp - 2:
                    ring_buf[step, side] = value
                    ring(step + 1, side).start()
                else:
                    ring(0, side).wait_send()
                    heads_out[pl.ds(side * heads, heads)] = value
                load_after(step + 1, side)
                return carry

            lax.fori_loop(0, 2, one_side, 0)

        def ring_first(side, carry):
            heads_out[pl.ds(side * heads, heads)] = own_term(0, side).astype(bf16)
            ring(0, side).start()
            load_after(0, side)
            return carry

        loads[5].wait()
        lax.fori_loop(0, 2, ring_first, 0)

        def spot(k):
            to_y, to_x = lax.rem(k, 2), k // 2
            return 1 - y + to_y * (2 * y - 1), 1 - x + to_x * (2 * x - 1)

        def spread(got, bounds, firsts, group):
            def copy(side, i):
                if side == 0:
                    source, peer = got.at[2 * i + 1 - x, bounds[0]], on_x
                else:
                    source, peer = got.at[2 * (1 - y) + i, bounds[1]], on_y
                return remote(
                    source, firsts[side].at[i], one_s.at[group, side, i], one_r.at[group, side, i], peer
                )

            return copy

        bounds_one = (slice(0, share), slice(share, 2 * share))
        bounds_two = (slice(0, out_rows), slice(out_rows, other_rows))
        spread_one = spread(got_one, bounds_one, (one_a, one_b), 0)
        spread_two = spread(got_two, bounds_two, (two_a, two_b), 1)

        def grads_one(chunk, store):
            lanes = pl.ds(pl.multiple_of(chunk * share, share), share)
            left = wide_buf[:, lanes].T
            store(bounds_one[0], jnp.dot(left, gate_buf[...], preferred_element_type=f32))
            store(bounds_one[1], jnp.dot(left, up_buf[...], preferred_element_type=f32))

        def grads_two(chunk, store):
            load = pltpu.make_async_copy(
                attended.at[:, pl.ds(pl.multiple_of(chunk * piece, piece), piece)], att_buf, att_s
            )
            load.start()
            first = chunk * down_rows
            start = jnp.minimum(first // 128 * 128, units - window)
            lanes = pl.ds(pl.multiple_of(start, 128), window)
            hidden_t[...] = gate_buf[:, lanes].T
            down_part = hidden_t[pl.ds(pl.multiple_of(first - start, 16), down_rows), :]
            store(
                slice(out_rows, other_rows),
                jnp.dot(down_part, wide_buf[...], preferred_element_type=f32),
            )
            load.wait()
            store(
                slice(0, out_rows),
                jnp.dot(
                    att_buf[...].reshape(out_rows, rows), term[...], preferred_element_type=f32
                ),
            )

        def core_copy(group, k):
            at_y, at_x = spot(k)
            sent, got = ((send_one, got_one), (send_two, got_two))[group]
            return remote(
                sent, got.at[2 * at_y + at_x], core_s.at[group, k], core_r.at[group, k], on_core
            )

        def both_sides(group, grads, sent, got, copy, leading):
            def step(k, carry):
                sending, keeping = k < pair, k >= pair
                place_k = lax.rem(k, pair)
                at_y, at_x = spot(place_k)
                index = 2 * at_y + at_x

                @pl.when(keeping)
                def _():
                    core_copy(group, place_k).wait_recv()

                def store(place, value):
                    if place == leading:

                        @pl.when(jnp.logical_and(k >= 1, k <= pair))
                        def _():
                            core_copy(group, k - 1).wait_send()

                    @pl.when(sending)
                    def _():
                        sent[place] = value.astype(bf16)

                    @pl.when(keeping)
                    def _():
                        got[index, place] = (got[index, place].astype(f32) + value).astype(bf16)

                grads(2 * index + jnp.where(sending, 1 - core, core), store)

                @pl.when(sending)
                def _():
                    core_copy(group, place_k).start()

                @pl.when(jnp.logical_and(keeping, place_k < 2))
                def _():
                    copy(0, at_y).start()

                @pl.when(jnp.logical_and(keeping, lax.rem(place_k, 2) == 0))
                def _():
                    copy(1, at_x).start()

                return carry

            lax.fori_loop(0, 2 * pair, step, 0)

        def fold(got, bounds, firsts, copy):
            for i in range(2):
                copy(0, i).wait_recv()
                index = 2 * i + x
                got[index, bounds[0]] = (
                    got[index, bounds[0]].astype(f32) + firsts[0][i].astype(f32)
                ).astype(bf16)
                copy(1, i).wait_recv()
                index = 2 * y + i
                got[index, bounds[1]] = (
                    got[index, bounds[1]].astype(f32) + firsts[1][i].astype(f32)
                ).astype(bf16)

        def last_copy(group, side):
            got, bounds, last = (
                (got_one, bounds_one, (gate_sum, up_sum)), (got_two, bounds_two, (out_sum, down_sum))
            )[group]
            if side == 0:
                source, peer = got.at[2 * (1 - y) + x, bounds[0]], on_y
            else:
                source, peer = got.at[2 * y + 1 - x, bounds[1]], on_x
            return remote(
                source, last[side], two_s.at[group, side], two_r.at[group, side], peer
            )

        def finish(group, side, got, bounds, last):
            last_copy(group, side).wait_recv()
            return (got[here, bounds[side]].astype(f32) + last[...].astype(f32)).astype(bf16)

        for i in range(3):
            loads[i].wait()
        both_sides(0, grads_one, send_one, got_one, spread_one, bounds_one[0])
        loads[3].start()
        loads[4].start()
        ring_next(0)
        loads[4].wait()
        loads[3].wait()
        both_sides(1, grads_two, send_two, got_two, spread_two, bounds_two[1])
        ring_next(1)
        fold(got_one, bounds_one, (one_a, one_b), spread_one)
        for side in range(2):
            last_copy(0, side).start()
        for step in range(2, n_tp - 1):
            ring_next(step)
        lax.fori_loop(1, n_ctx, lambda step, c: (head_copy(step).start(), c)[1], 0)
        grad_out[ctx] = heads_out[ctx]

        def down_tile(t, carry):
            lanes = pl.ds(pl.multiple_of(t * tile, tile), tile)
            load = pltpu.make_async_copy(w_down.at[:, lanes], tile_in, tile_s.at[0])
            load.start()
            load.wait()
            for s in range(n_tp):
                own_rows = rows // n_tp
                block = lax.rem(tp - s + n_tp, n_tp)
                left = gate_buf[pl.ds(pl.multiple_of(block * own_rows, own_rows), own_rows), :]
                value = jnp.dot(left, tile_in[...], preferred_element_type=f32)
                tile_out[s] = value.astype(bf16)
                pltpu.make_async_copy(
                    tile_out.at[s], down_terms[s].at[:, lanes], tile_s.at[s + 1]
                ).start()
            for s in range(n_tp):
                pltpu.make_async_copy(
                    tile_out.at[s], down_terms[s].at[:, lanes], tile_s.at[s + 1]
                ).wait()
            return carry

        lax.fori_loop(0, width // tile, down_tile, 0)
        fold(got_two, bounds_two, (two_a, two_b), spread_two)
        for side in range(2):
            last_copy(1, side).start()
        gate_sum[...] = finish(0, 0, got_one, bounds_one, gate_sum)
        up_sum[...] = finish(0, 1, got_one, bounds_one, up_sum)
        lax.fori_loop(1, n_ctx, lambda step, c: (head_copy(step).wait(), c)[1], 0)
        out_sum[...] = finish(1, 0, got_two, bounds_two, out_sum)
        down_sum[...] = finish(1, 1, got_two, bounds_two, down_sum)
        for step in range(1, n_tp - 1):
            for side in range(2):
                ring(step, side).wait_send()
        for group, copy in enumerate((spread_one, spread_two)):
            for side in range(2):
                last_copy(group, side).wait_send()
                for i in range(2):
                    copy(side, i).wait_send()

    vmem, anywhere = pl.BlockSpec(memory_space=pltpu.VMEM), pl.BlockSpec(memory_space=pl.ANY)
    dma = pltpu.SemaphoreType.DMA
    return pl.pallas_call(
        kernel,
        out_shape=(
            jax.ShapeDtypeStruct((n_ctx, HEAD, rows), bf16),
            jax.ShapeDtypeStruct((share, units), bf16),
            jax.ShapeDtypeStruct((share, units), bf16),
            jax.ShapeDtypeStruct((out_rows, width), bf16),
            jax.ShapeDtypeStruct((down_rows, width), bf16),
        )
        + (jax.ShapeDtypeStruct((rows // n_tp, width), bf16),) * n_tp,
        in_specs=[anywhere] * 9,
        out_specs=(vmem,) * 5 + (anywhere,) * n_tp,
        scratch_shapes=[
            pltpu.VMEM((rows, width), bf16),
            pltpu.VMEM((half, width), bf16),
            pltpu.VMEM((rows, width), bf16),
            pltpu.VMEM((rows, units), bf16),
            pltpu.VMEM((rows, units), bf16),
            pltpu.VMEM((window, rows), bf16),
            pltpu.VMEM((n_tp, piece, rows), bf16),
            pltpu.VMEM((units, tile), bf16),
            pltpu.VMEM((n_tp, rows // n_tp, tile), bf16),
            pltpu.VMEM((n_tp - 1, 2, heads, HEAD, rows), bf16),
            pltpu.VMEM((n_ctx, HEAD, rows), bf16),
            pltpu.VMEM((2 * share, units), bf16),
            pltpu.VMEM((other_rows, width), bf16),
            pltpu.VMEM((pair, 2 * share, units), bf16),
            pltpu.VMEM((pair, other_rows, width), bf16),
            pltpu.VMEM((2, share, units), bf16),
            pltpu.VMEM((2, share, units), bf16),
            pltpu.VMEM((2, out_rows, width), bf16),
            pltpu.VMEM((2, down_rows, width), bf16),
            dma((n_tp + 1,)), dma((6,)), dma, dma,
            dma((n_tp - 1, 2)), dma((n_tp - 1, 2)),
            dma((n_ctx,)), dma((n_ctx,)),
            dma((2, pair)), dma((2, pair)),
            dma((2, 2, 2)), dma((2, 2, 2)),
            dma((2, 2)), dma((2, 2)),
        ],
        compiler_params=pltpu.CompilerParams(
            collective_id=4, has_side_effects=True, vmem_limit_bytes=62 * 2**20
        ),
        cost_estimate=pl.CostEstimate(
            flops=2 * rows * width * (2 * units + units + 2 * n_tp * cols),
            bytes_accessed=40 * 2**20,
            transcendentals=0,
        ),
        name="middle_sums",
    )(term, w_all, low, gate, up, hidden, cot, attended, w_down)


def final_sums(term, xs, means, inverses, gain, low, grads, w_qkv, out, small_two):
    n_tp, own, width = term.shape
    rows = low.shape[0]
    n_ctx = lax.axis_size("ctx")
    cols = 3 * n_ctx * HEAD
    tile = 32
    share = width // n_ctx
    half_rows, half_width = share // 2, width // 2
    part = out.shape[0] // n_tp
    columns = cols // 3
    first_rows, norm_rows = cols // 128, width // 128
    small_shape = (first_rows + 4 * norm_rows, 128)

    def kernel(
        term_in, xs, means, inverses, gain, low_in, mine, w_in, out, small_two,
        grad_in, out_all, qkv_all, small_sum,
        term, low, w_qkv, x_buf, grads, back, sums, small, load_s, x_s, swap_s, swap_r, out_recv, out_s, out_r,
        small_ctx, small_tp, ring_buf, q_send, q_recv, both, first_a, first_b, second,
        small_s, small_r, norm_s, norm_r, ring_s, ring_r, core_s, core_r, one_s, one_r, two_s, two_r, piece_s, piece_r,
    ):
        ctx, tp = lax.axis_index("ctx"), lax.axis_index("tp")
        y, x, core = ctx // 4, (ctx // 2) % 2, ctx % 2
        on_core, on_x, on_y = ctx + 1 - 2 * core, ctx + 2 - 4 * x, ctx + 4 - 8 * y
        across = on_x + 4 - 8 * y
        here = y * 2 + x
        loads = [
            pltpu.make_async_copy(source, target, load_s.at[i])
            for i, (source, target) in enumerate(((w_in, w_qkv), (term_in, term), (low_in, low)))
        ]
        for load in loads:
            load.start()
        barrier = pltpu.get_barrier_semaphore()
        for step in range(1, n_ctx):
            peer = lax.rem(ctx + step, n_ctx)
            pl.semaphore_signal(barrier, inc=1, device_id=(peer, tp), device_id_type=MESH)
        for step in range(1, n_tp):
            peer = lax.rem(tp + step, n_tp)
            pl.semaphore_signal(barrier, inc=1, device_id=(ctx, peer), device_id_type=MESH)
        pl.semaphore_wait(barrier, n_ctx + n_tp - 2)

        def remote(source, target, send, recv, peer, near=True):
            return pltpu.make_async_remote_copy(
                src_ref=source,
                dst_ref=target,
                send_sem=send,
                recv_sem=recv,
                device_id=(peer, tp) if near else (ctx, peer),
                device_id_type=MESH,
            )

        def ring(step, piece):
            lanes = slice(piece * half_width, (piece + 1) * half_width)
            first = term.at[lax.rem(tp - 1 + n_tp, n_tp), :, lanes]
            return remote(
                first if step == 0 else ring_buf.at[step - 1, piece],
                ring_buf.at[step, piece],
                ring_s.at[step, piece],
                ring_r.at[step, piece],
                lax.rem(tp + 1, n_tp),
                False,
            )

        def ring_next(step):
            for piece in range(2):
                lanes = slice(piece * half_width, (piece + 1) * half_width)
                ring(step, piece).wait_recv()
                block = lax.rem(tp - 2 - step + 2 * n_tp, n_tp)
                total = ring_buf[step, piece].astype(f32) + term[block, :, lanes].astype(f32)
                if step < n_tp - 2:
                    ring_buf[step, piece] = total.astype(bf16)
                    ring(step + 1, piece).start()
                else:
                    grad_in[:, lanes] = total.astype(bf16)

        def rows_of(where, start, stop):
            return lambda chunk: where.at[chunk, start:stop]

        def qkv_rows(start, stop):
            return lambda chunk: qkv_all.at[chunk, :, start:stop]

        pieces = (
            (rows_of(out_all, 0, part), False),
            (qkv_rows(0, half_rows), True),
            (qkv_rows(half_rows, share), False),
        )

        def hop(p, index):
            where, y_first = pieces[p]
            one, two = (on_y, on_x) if y_first else (on_x, on_y)
            chunk, peer = (
                (ctx, one), (ctx, two), (ctx, on_core), (one, two),
                (one, on_core), (two, on_core), (across, on_core),
            )[index]
            place = where(chunk)
            return remote(place, place, piece_s.at[p, index], piece_r.at[p, index], peer)

        def arrived(p, index):
            where, y_first = pieces[p]
            one, two = (on_y, on_x) if y_first else (on_x, on_y)
            chunk = (
                one, two, on_core, across,
                one + on_core - ctx, two + on_core - ctx, across + on_core - ctx,
            )[index]
            place = where(chunk)
            remote(place, place, piece_s.at[p, index], piece_r.at[p, index], on_core).wait_recv()

        def gather_start(p):
            for index in (0, 1, 2):
                hop(p, index).start()

        def gather_one(p):
            arrived(p, 0)
            hop(p, 3).start()
            hop(p, 4).start()

        def gather_two(p):
            arrived(p, 1)
            hop(p, 5).start()
            arrived(p, 3)
            hop(p, 6).start()

        def gather_end(p):
            for index in (2, 4, 5, 6):
                arrived(p, index)
            for index in range(7):
                hop(p, index).wait_send()

        def dest(step):
            return lax.rem(tp - 1 - step + 2 * n_tp, n_tp)

        def exchange(step, at):
            lanes = pl.ds(pl.multiple_of(dest(step) * own, own), own)
            peer = lax.rem(ctx + at, n_ctx)
            return remote(
                mine.at[peer, :, :, lanes],
                grads.at[:, ctx, :, lanes],
                swap_s.at[step, at],
                swap_r.at[step, at],
                peer,
            )

        def out_exchange(step):
            peer = lax.rem(tp + step, n_tp)
            return remote(
                out.at[pl.ds(pl.multiple_of(peer * part, part), part)],
                out_recv.at[step - 1],
                out_s.at[step - 1],
                out_r.at[step - 1],
                peer,
                False,
            )

        def x_load(step):
            return pltpu.make_async_copy(xs.at[dest(step)], x_buf, x_s)

        for step in range(n_tp):
            lax.fori_loop(
                1, n_ctx, lambda at, c, step=step: (exchange(step, at).start(), c)[1], 0
            )
        x_load(0).start()
        grads[:, ctx] = mine[ctx]
        for step in range(1, n_tp):
            out_exchange(step).start()
        sums[...] = jnp.zeros_like(sums)

        def wait_rows(step):
            lax.fori_loop(1, n_ctx, lambda at, c: (exchange(step, at).wait_recv(), c)[1], 0)

        def back_rows(step):
            block = dest(step)
            lanes = pl.ds(pl.multiple_of(block * own, own), own)
            for c in range(3):
                left = grads[c, :, :, lanes].reshape(columns, own).T
                value = lax.dot_general(
                    left, w_qkv[c], (((1,), (1,)), ((), ())), preferred_element_type=f32
                )
                if c == 0:
                    back[...] = value
                else:
                    back[...] += value
            x_load(step).wait()

            def norm_rows_back(i, carry):
                span = pl.ds(pl.multiple_of(i * tile, tile), tile)
                inverse = inverses[block, span, :][:, :1]
                normed = (x_buf[span, :].astype(f32) - means[block, span, :][:, :1]) * inverse
                value = back[span, :]
                scaled = value * gain[...]
                grad = inverse * (
                    scaled
                    - jnp.mean(scaled, axis=1, keepdims=True)
                    - normed * jnp.mean(scaled * normed, axis=1, keepdims=True)
                )
                sums[0:1] += jnp.sum(value * normed, axis=0, keepdims=True)
                sums[1:2] += jnp.sum(value, axis=0, keepdims=True)
                term[block, span, :] = (term[block, span, :].astype(f32) + grad).astype(bf16)
                return carry

            lax.fori_loop(0, own // tile, norm_rows_back, 0)
            if step < n_tp - 1:
                x_load(step + 1).start()

        def small_copy(step):
            peer = lax.rem(ctx + step, n_ctx)
            return remote(small, small_ctx.at[ctx], small_s.at[step], small_r.at[step], peer)

        def norm_copy(step):
            peer = lax.rem(tp + step, n_tp)
            source = small_tp.at[tp]
            return remote(source, source, norm_s.at[step], norm_r.at[step], peer, False)

        for load in loads:
            load.wait()
        wait_rows(0)
        back_rows(0)
        for piece in range(2):
            ring(0, piece).start()
        for step in range(1, n_tp - 1):
            wait_rows(step)
            back_rows(step)
        total = out[pl.ds(pl.multiple_of(tp * part, part), part)].astype(f32)
        for step in range(1, n_tp):
            out_exchange(step).wait_recv()
            total = total + out_recv[step - 1].astype(f32)
        out_all[ctx] = total.astype(bf16)
        gather_start(0)
        wait_rows(n_tp - 1)

        def weight_chunk(chunk, where):
            lanes = pl.ds(pl.multiple_of(chunk * share, share), share)
            left = low[:, lanes].T
            for c in range(3):
                where[c] = lax.dot_general(
                    left,
                    grads[c].reshape(columns, rows),
                    (((1,), (1,)), ((), ())),
                    preferred_element_type=f32,
                ).astype(bf16)

        def core_copy(i):
            return remote(q_send.at[i], q_recv.at[i], core_s.at[i], core_r.at[i], on_core)

        def send_chunk(i, carry):
            weight_chunk(2 * i + 1 - core, q_send.at[i])
            core_copy(i).start()
            return carry

        def keep_chunk(i, carry):
            weight_chunk(2 * i + core, both.at[i])
            return carry

        lax.fori_loop(0, n_ctx // 2, send_chunk, 0)
        back_rows(n_tp - 1)
        ring_next(0)
        lax.fori_loop(0, n_ctx // 2, keep_chunk, 0)

        def add_chunk(i, carry):
            core_copy(i).wait_recv()
            both[i] = (both[i].astype(f32) + q_recv[i].astype(f32)).astype(bf16)
            return carry

        lax.fori_loop(0, n_ctx // 2, add_chunk, 0)
        ones = jnp.ones((8, rows), bf16)
        for c in range(3):
            value = lax.dot_general(
                ones, grads[c].reshape(columns, rows), (((1,), (1,)), ((), ())),
                preferred_element_type=f32,
            )
            for t in range(columns // 128):
                row = c * columns // 128 + t
                small[row : row + 1] = value[0:1, t * 128 : (t + 1) * 128]
        for t in range(norm_rows):
            for which in range(2):
                row = first_rows + 2 * which * norm_rows + t
                small[row : row + 1] = sums[which : which + 1, t * 128 : (t + 1) * 128]
        for which in range(2):
            row = first_rows + (2 * which + 1) * norm_rows
            small[row : row + norm_rows] = small_two[which]
        small_ctx[ctx] = small[...]
        top, bottom = slice(0, half_rows), slice(half_rows, share)

        def one_copy(side, i):
            if side == 0:
                source, target, peer = both.at[2 * i + 1 - x, :, top], first_a.at[i], on_x
            else:
                source, target, peer = both.at[2 * (1 - y) + i, :, bottom], first_b.at[i], on_y
            return remote(source, target, one_s.at[side, i], one_r.at[side, i], peer)

        for side in range(2):
            for i in range(2):
                one_copy(side, i).start()
        for step in range(1, n_ctx):
            small_copy(step).start()
        for i in range(2):
            one_copy(0, i).wait_recv()
            spot = 2 * i + x
            both[spot, :, top] = (
                both[spot, :, top].astype(f32) + first_a[i].astype(f32)
            ).astype(bf16)
            one_copy(1, i).wait_recv()
            spot = 2 * y + i
            both[spot, :, bottom] = (
                both[spot, :, bottom].astype(f32) + first_b[i].astype(f32)
            ).astype(bf16)

        def two_copy(side):
            if side == 0:
                source, peer = both.at[2 * (1 - y) + x, :, top], on_y
            else:
                source, peer = both.at[2 * y + 1 - x, :, bottom], on_x
            return remote(source, second.at[side], two_s.at[side], two_r.at[side], peer)

        for side in range(2):
            two_copy(side).start()
        ring_next(1)
        for side, span in enumerate((top, bottom)):
            two_copy(side).wait_recv()
            qkv_all[ctx, :, span] = (
                both[here, :, span].astype(f32) + second[side].astype(f32)
            ).astype(bf16)
            gather_start(1 + side)
        for step in range(1, n_ctx):
            small_copy(step).wait_recv()
        value = sum(small_ctx[i] for i in range(n_ctx))
        small_sum[:first_rows] = value[:first_rows]
        small_tp[tp] = value[first_rows:]
        for step in range(1, n_tp):
            norm_copy(step).start()
        for p in range(3):
            gather_one(p)
        for step in range(2, n_tp - 1):
            ring_next(step)
        for p in range(3):
            gather_two(p)
        for step in range(1, n_tp):
            norm_copy(step).wait_recv()
        small_sum[first_rows:] = sum(small_tp[i] for i in range(n_tp))
        for p in range(3):
            gather_end(p)
        for step in range(1, n_tp):
            out_exchange(step).wait_send()
        for step in range(n_tp):
            lax.fori_loop(
                1, n_ctx, lambda at, c, step=step: (exchange(step, at).wait_send(), c)[1], 0
            )
        for step in range(1, n_ctx):
            small_copy(step).wait_send()
        for step in range(1, n_tp):
            norm_copy(step).wait_send()
        for step in range(n_tp - 1):
            for piece in range(2):
                ring(step, piece).wait_send()
        for i in range(n_ctx // 2):
            core_copy(i).wait_send()
        for side in range(2):
            two_copy(side).wait_send()
            for i in range(2):
                one_copy(side, i).wait_send()

    vmem, anywhere = pl.BlockSpec(memory_space=pltpu.VMEM), pl.BlockSpec(memory_space=pl.ANY)
    dma = pltpu.SemaphoreType.DMA
    pair = n_ctx // 2
    return pl.pallas_call(
        kernel,
        out_shape=(
            jax.ShapeDtypeStruct((own, width), bf16),
            jax.ShapeDtypeStruct((n_ctx, part, width), bf16),
            jax.ShapeDtypeStruct((n_ctx, 3, share, columns), bf16),
            jax.ShapeDtypeStruct(small_shape, f32),
        ),
        in_specs=[anywhere, anywhere, vmem, vmem, vmem, anywhere, vmem, anywhere, vmem, vmem],
        out_specs=(vmem,) * 4,
        scratch_shapes=[
            pltpu.VMEM(term.shape, bf16),
            pltpu.VMEM(low.shape, bf16),
            pltpu.VMEM((3, width, columns), bf16),
            pltpu.VMEM((own, width), bf16),
            pltpu.VMEM((3, n_ctx, HEAD, rows), bf16),
            pltpu.VMEM((own, width), f32),
            pltpu.VMEM((8, width), f32),
            pltpu.VMEM(small_shape, f32),
            dma((3,)), dma,
            dma((n_tp, n_ctx)), dma((n_tp, n_ctx)),
            pltpu.VMEM((n_tp - 1, part, width), bf16),
            dma((n_tp - 1,)), dma((n_tp - 1,)),
            pltpu.VMEM((n_ctx,) + small_shape, f32),
            pltpu.VMEM((n_tp, 4 * norm_rows, 128), f32),
            pltpu.VMEM((n_tp - 1, 2, own, half_width), bf16),
            pltpu.VMEM((pair, 3, share, columns), bf16),
            pltpu.VMEM((pair, 3, share, columns), bf16),
            pltpu.VMEM((pair, 3, share, columns), bf16),
            pltpu.VMEM((2, 3, half_rows, columns), bf16),
            pltpu.VMEM((2, 3, half_rows, columns), bf16),
            pltpu.VMEM((2, 3, half_rows, columns), bf16),
            dma((n_ctx,)), dma((n_ctx,)),
            dma((n_tp,)), dma((n_tp,)),
            dma((n_tp - 1, 2)), dma((n_tp - 1, 2)),
            dma((pair,)), dma((pair,)),
            dma((2, 2)), dma((2, 2)),
            dma((2,)), dma((2,)),
            dma((3, 7)), dma((3, 7)),
        ],
        compiler_params=pltpu.CompilerParams(
            collective_id=3, has_side_effects=True, vmem_limit_bytes=60 * 2**20
        ),
        cost_estimate=pl.CostEstimate(
            flops=2 * rows * width * cols, bytes_accessed=50 * 2**20, transcendentals=0
        ),
        name="final_sums",
    )(
        term, xs, means, inverses, gain, low, grads, w_qkv.transpose(1, 0, 2), out, small_two
    )


def norm_stats(rows):
    mean = jnp.mean(rows, axis=1, keepdims=True)
    center = rows - mean
    inverse = lax.rsqrt(jnp.mean(center * center, axis=1, keepdims=True) + epsilon)
    return mean, inverse


def norm_backward(grad_out, normed, inverse, gain):
    scaled = grad_out * gain
    grad_rows = inverse * (
        scaled
        - jnp.mean(scaled, axis=1, keepdims=True)
        - normed * jnp.mean(scaled * normed, axis=1, keepdims=True)
    )
    return (grad_rows, jnp.sum(grad_out * normed, axis=0), jnp.sum(grad_out, axis=0))


def rotate(tensor, places, direction):
    half = ROT // 2
    frequency = 10000.0 ** (-2.0 * jnp.arange(half, dtype=f32) / ROT)
    angles = frequency[:, None] * places.astype(f32)[None, :]
    cosine, sines = jnp.cos(angles), direction * jnp.sin(angles)
    first, second = tensor[..., :half, :], tensor[..., half:ROT, :]
    return jnp.concatenate(
        [
            first * cosine - second * sines,
            second * cosine + first * sines,
            tensor[..., ROT:, :],
        ],
        axis=-2,
    )


def after(value, *others):
    return lax.optimization_barrier((value, *others))[0]


def direct_gather(value, count):
    n_tp = lax.axis_size("tp")
    return [value] + [
        lax.ppermute(value, "tp", [(i, (i + s) % n_tp) for i in range(n_tp)])
        for s in range(1, count)
    ]


def in_tp_order(arrays):
    count = len(arrays)
    shape = arrays[0].shape

    def kernel(tp, *refs):
        sources, out = refs[:count], refs[count]
        for s in range(count):
            out[lax.rem(tp[0] - s + count, count)] = sources[s][...]

    vmem = pl.BlockSpec(memory_space=pltpu.VMEM)
    return pl.pallas_call(
        kernel,
        out_shape=jax.ShapeDtypeStruct((count,) + shape, arrays[0].dtype),
        in_specs=[pl.BlockSpec(memory_space=pltpu.SMEM)] + [vmem] * count,
        out_specs=vmem,
        compiler_params=pltpu.CompilerParams(vmem_limit_bytes=60 * 2**20),
        cost_estimate=pl.CostEstimate(
            flops=0, bytes_accessed=4 * count * math.prod(shape), transcendentals=0
        ),
        name="in_tp_order",
    )(lax.axis_index("tp")[None], *arrays)


def exchange_sum(terms, axis):
    parts = lax.all_to_all(terms, axis, split_axis=0, concat_axis=0, tiled=True)
    return sum(part.astype(f32) for part in parts)


def scatter(partial, axis):
    return lax.psum_scatter(partial, axis, scatter_dimension=0, tiled=True)


def swap(value, axis, bit):
    size = lax.axis_size(axis)
    return lax.ppermute(value, axis, [(i, i ^ (1 << bit)) for i in range(size)])


def pair_sum(partial):
    size, rest = partial.shape[0], partial.shape[1:]
    side = lax.axis_index("ctx") % 2
    pairs = partial.reshape((size // 2, 2) + rest)
    kept = lax.dynamic_index_in_dim(pairs, side, 1, keepdims=False)
    sent = lax.dynamic_index_in_dim(pairs, 1 - side, 1, keepdims=False)
    return (kept.astype(f32) + swap(sent, "ctx", 0).astype(f32)).astype(bf16)


def spread_start(both, *early):
    pairs = both.shape[0]
    mine = lax.axis_index("ctx") // 2
    parts = [lax.dynamic_index_in_dim(both, mine, 0, keepdims=False)]
    for distance in range(1, pairs):
        sent = lax.dynamic_index_in_dim(both, mine ^ distance, 0, keepdims=False)
        perm = [(i, i ^ (2 * distance)) for i in range(2 * pairs)]
        parts.append(lax.ppermute(after(sent, *early) if early else sent, "ctx", perm))
    return parts


def spread_end(parts, *late):
    if late:
        parts = lax.optimization_barrier((*parts, *late))[: len(parts)]
    return sum(part.astype(f32) for part in parts).astype(bf16)


def by_ctx(partial):
    rows, cols = partial.shape
    n_ctx = lax.axis_size("ctx")
    return partial.reshape(n_ctx, rows // n_ctx, cols)


def gather(rows, axis):
    return lax.all_gather(rows, axis, axis=0, tiled=True)


def widen(chunks, down, out):
    devices, parts, rows, cols = chunks.shape

    def kernel(chunks, down, out, chunks_wide, down_wide, out_wide):
        chunks_wide[...] = chunks[0].astype(f32)
        down_wide[...] = down[0].astype(f32)
        out_wide[...] = out[0].astype(f32)

    others = (down.shape[1:], out.shape[1:])
    return pl.pallas_call(
        kernel,
        grid=(devices,),
        out_shape=[jax.ShapeDtypeStruct((parts, devices * rows, cols), f32)]
        + [jax.ShapeDtypeStruct((devices * shape[0], shape[1]), f32) for shape in others],
        in_specs=[pl.BlockSpec((1, parts, rows, cols), lambda i: (i, 0, 0, 0))]
        + [pl.BlockSpec((1,) + shape, lambda i: (i, 0, 0)) for shape in others],
        out_specs=[pl.BlockSpec((parts, rows, cols), lambda i: (0, i, 0))]
        + [pl.BlockSpec(shape, lambda i: (i, 0)) for shape in others],
        cost_estimate=pl.CostEstimate(
            flops=0, bytes_accessed=6 * math.prod(chunks.shape), transcendentals=0
        ),
        compiler_params=pltpu.CompilerParams(vmem_limit_bytes=60 * 2**20),
        name="widen",
    )(chunks, down, out)


def interleave(gate, up):
    rows, cols = gate.shape
    tile = 128

    def kernel(gate, up, out):
        out[:, 0, :] = gate[...].astype(f32)
        out[:, 1, :] = up[...].astype(f32)

    return pl.pallas_call(
        kernel,
        grid=(rows // tile,),
        out_shape=jax.ShapeDtypeStruct((rows, 2, cols), f32),
        in_specs=[pl.BlockSpec((tile, cols), lambda i: (i, 0))] * 2,
        out_specs=pl.BlockSpec((tile, 2, cols), lambda i: (i, 0, 0)),
        compiler_params=pltpu.CompilerParams(vmem_limit_bytes=60 * 2**20),
        cost_estimate=pl.CostEstimate(flops=1, bytes_accessed=1, transcendentals=0),
        name="interleave",
    )(gate, up)


def shards(
    layer_in,
    norm_gain,
    norm_bias,
    w_qkv,
    b_qkv,
    w_out,
    w_gate_up,
    w_down,
    cotangent,
    block_table,
    seq_ids,
):
    n_ctx, n_tp = lax.axis_size("ctx"), lax.axis_size("tp")
    ctx, tp = lax.axis_index("ctx"), lax.axis_index("tp")
    own, width = layer_in.shape
    rows = own * n_tp
    cols = w_qkv.shape[2]
    heads = cols // HEAD
    table = block_table.reshape(-1)
    blocks = table.shape[0]
    by_head = heads == n_ctx == 8 and BLK % own == 0
    part = cols // n_ctx

    ids = jnp.arange(blocks, dtype=jnp.int32)
    located = jnp.sum(jnp.where(table[None, :] == ids[:, None], ids[None, :], 0), axis=1)
    same = seq_ids[:, None] == seq_ids[None, :]
    first = jnp.min(jnp.where(same, ids[None, :], blocks), axis=1)
    last = jnp.max(jnp.where(same, ids[None, :], -1), axis=1)
    order = jnp.concatenate([located, first, last, tp[None]]).astype(jnp.int32)
    frequency = 10000.0 ** (-2.0 * jnp.arange(ROT // 2, dtype=f32) / ROT)
    positions = table[:, None] * BLK + jnp.arange(BLK, dtype=jnp.int32)[None, :]
    angles = frequency[None, :, None] * positions.astype(f32)[:, None, :]
    angles = jnp.stack([jnp.cos(angles), jnp.sin(angles)], axis=1)

    hidden_units = w_gate_up.shape[2]
    w_part = lax.dynamic_slice_in_dim(w_out, ctx * part, part, 0)
    if by_head:
        layer_in = after(layer_in, angles, order)
        xs, lows, mean_one, inverse_one, w_part, packed = project_exchange(
            layer_in, w_part, norm_gain[0:1], norm_bias[0:1], w_qkv, b_qkv
        )
        first_low = lows.reshape(rows, width)
        w_out_all = lax.all_gather(w_part, "ctx", axis=1, tiled=True)
        cot = direct_gather(after(cotangent, packed), n_tp - 1)
        out, logsum = attention_forward(order, angles, packed)
        middle, lows, mean_two, inverse_two, attended_all = output_project(
            out, xs, w_out_all, norm_gain[1:2], norm_bias[1:2]
        )
        cot = list(lax.optimization_barrier((*cot, middle))[: n_tp - 1])
        late = after(cotangent, middle)
        cot.append(lax.ppermute(late, "tp", [(i, (i + n_tp - 1) % n_tp) for i in range(n_tp)]))
        cot = in_tp_order(cot).reshape(rows, width)
        middle = middle.reshape(rows, width)
        mean_two, inverse_two = [t.reshape(rows, 128)[:, :1] for t in (mean_two, inverse_two)]
        normed_two = (middle - mean_two) * inverse_two
        second_low = lows.reshape(rows, width)
        attended_all = attended_all.reshape(n_tp * cols, rows)
    else:
        x = gather(layer_in, "tp").astype(f32)
        mean_one, inverse_one = norm_stats(x)
        first_low = ((x - mean_one) * inverse_one * norm_gain[0] + norm_bias[0]).astype(bf16)
        projected = (
            jnp.einsum("dcf,rd->cfr", w_qkv, first_low, preferred_element_type=f32)
            + b_qkv[:, :, None]
        ).reshape(3, heads, HEAD, rows)
        w_part = gather(w_part, "tp").reshape(n_tp, part, width)
        w_out_all = lax.all_gather(w_part, "ctx", axis=1, tiled=True)
        cot = gather(cotangent, "tp")
        places, _ = row_places(ctx * rows, rows, table, seq_ids)
        qkv = jnp.concatenate([rotate(projected[0:2], places, 1.0), projected[2:3]], axis=0)
        queries, keys, values = [t.astype(bf16).transpose(2, 0, 1) for t in qkv]
        visit, offsets = gathered_setup(
            rows, table, seq_ids, keys.reshape(rows, cols), values.reshape(rows, cols)
        )
        out, logsum = gathered_forward(queries, visit, offsets)
        attended_all = gather(out.astype(bf16).reshape(rows, cols).T, "tp")
        middle = x + jnp.einsum(
            "fr,fd->rd",
            attended_all,
            w_out_all.reshape(n_tp * cols, width),
            preferred_element_type=f32,
        )
        mean_two, inverse_two = norm_stats(middle)
        normed_two = (middle - mean_two) * inverse_two
        second_low = (normed_two * norm_gain[1] + norm_bias[1]).astype(bf16)

    grad_hidden = lax.dot_general(cot, w_down, (((1,), (1,)), ((), ())), preferred_element_type=f32)
    gate_up = jnp.einsum("rd,dcf->rcf", second_low, w_gate_up, preferred_element_type=f32)
    gate, up = gate_up[:, 0], gate_up[:, 1]
    sigmoid = jax.nn.sigmoid(gate)
    activated = gate * sigmoid
    hidden = (activated * up).astype(bf16)
    grad_gate = grad_hidden * up * sigmoid * (1.0 + gate * (1.0 - sigmoid))
    grad_up = grad_hidden * activated
    grad_gu = jnp.stack([grad_gate, grad_up], axis=1).astype(bf16)
    grad_second = jnp.einsum("rcf,dcf->rd", grad_gu, w_gate_up, preferred_element_type=f32)

    middle_norm, gain_two, bias_two = norm_backward(
        grad_second, normed_two, inverse_two, norm_gain[1]
    )
    is_own = (jnp.arange(rows, dtype=jnp.int32) // own == tp)[:, None]
    middle_term = (middle_norm + jnp.where(is_own, cot.astype(f32), 0.0)).astype(bf16)
    if by_head:
        grad_att, gate_grad, up_grad, out_grad, down_grad, *down = middle_sums(
            middle_term,
            w_out_all,
            second_low,
            grad_gate.astype(bf16),
            grad_up.astype(bf16),
            hidden,
            cot,
            attended_all.reshape(n_tp, cols, rows),
            w_down,
        )
        down = [down[0]] + [
            lax.ppermute(down[s], "tp", [(i, (i - s) % n_tp) for i in range(n_tp)])
            for s in range(1, n_tp)
        ]
    else:
        grad_att = lax.dot_general(
            w_out_all.reshape(n_tp * cols, width),
            middle_term,
            (((1,), (1,)), ((), ())),
            preferred_element_type=f32,
        ).astype(bf16)
        grad_att = scatter(grad_att, "tp")
        down = jnp.dot(hidden, w_down, preferred_element_type=f32).astype(bf16)
        down = [scatter(down, "tp")]

        def weight_grad(left, right):
            return lax.dot_general(
                left, right, (((0,), (0,)), ((), ())), preferred_element_type=f32
            ).astype(bf16)

        gu_grad = jnp.concatenate(
            [pair_sum(by_ctx(weight_grad(second_low, t.astype(bf16)))) for t in (grad_gate, grad_up)],
            axis=1,
        )
        gu_grad = spread_end(spread_start(gu_grad))
        out_grad = jnp.dot(attended_all, middle_term, preferred_element_type=f32).astype(bf16)
        out_grad = out_grad.reshape(n_tp, n_ctx, part, width).transpose(1, 0, 2, 3)
        other_grad = jnp.concatenate(
            [
                pair_sum(out_grad.reshape(n_ctx, n_tp * part, width)),
                pair_sum(by_ctx(weight_grad(hidden, cot))),
            ],
            axis=1,
        )
        other_grad = spread_end(spread_start(other_grad))
        gate_grad, up_grad = jnp.split(gu_grad, 2, axis=0)
        out_grad, down_grad = jnp.split(other_grad, [n_tp * part], axis=0)
    gate_grad, up_grad = gather(gate_grad, "ctx"), gather(up_grad, "ctx")
    down_grad = gather(down_grad, "ctx")
    grad_gate_up = interleave(gate_grad, up_grad)

    if by_head:
        grads = attention_backward(order, angles, packed, grad_att, out, logsum)
        grads, *down[:-1] = lax.optimization_barrier((grads, *down[:-1]))
        grad_input, out_grad, grad_qkv, small = final_sums(
            middle_term.reshape(n_tp, own, width),
            xs,
            mean_one,
            inverse_one,
            norm_gain[0:1],
            first_low,
            grads,
            w_qkv,
            out_grad,
            jnp.stack([gain_two, bias_two]).reshape(2, -1, 128),
        )
        grad_input, down[-1] = lax.optimization_barrier((grad_input, down[-1]))
        grad_qkv, down_grad, out_grad = widen(
            grad_qkv, down_grad.reshape(n_ctx, -1, width), out_grad
        )
        grad_qkv = grad_qkv.transpose(1, 0, 2)
        bias_qkv, norms = small[: 3 * cols // 128], small[3 * cols // 128 :]
    else:
        grads = gathered_backward(
            queries, visit, offsets, grad_att.T.reshape(rows, heads, HEAD), out, logsum
        )
        grads = jnp.stack([t.transpose(1, 2, 0) for t in grads])
        grads = jnp.concatenate([rotate(grads[0:2], places, -1.0), grads[2:3]], axis=0)
        grad_projected = grads.reshape(3 * cols, rows).astype(bf16)
        grad_first = jnp.einsum(
            "cfr,dcf->rd",
            grad_projected.reshape(3, cols, rows),
            w_qkv,
            preferred_element_type=f32,
        )
        input_norm, gain_one, bias_one = norm_backward(
            grad_first, (x - mean_one) * inverse_one, inverse_one, norm_gain[0]
        )
        grad_input = middle_term.astype(f32) + input_norm
        grad_input = exchange_sum(grad_input.astype(bf16).reshape(n_tp, own, width), "tp")
        grad_input = grad_input.astype(bf16)
        grad_qkv = lax.dot_general(
            first_low, grad_projected, (((0,), (1,)), ((), ())), preferred_element_type=f32
        ).astype(bf16)
        grad_qkv = spread_end(spread_start(pair_sum(by_ctx(grad_qkv))))
        out_grad = exchange_sum(out_grad.reshape(n_tp, part, width), "tp").astype(bf16)
        out_grad, grad_qkv = [gather(t, "ctx").astype(f32) for t in (out_grad, grad_qkv)]
        grad_qkv = grad_qkv.reshape(width, 3, cols)
        down_grad = down_grad.astype(f32)
        bias_qkv = lax.psum(jnp.sum(grad_projected.astype(f32), axis=1), "ctx")
        norms = jnp.stack([gain_one, gain_two, bias_one, bias_two])
        norms = lax.psum(norms, ("ctx", "tp"))
    own_middle = lax.dynamic_slice_in_dim(middle, tp * own, own, 0)
    layer_out = (own_middle + sum(t.astype(f32) for t in down)).astype(bf16)
    norms = norms.reshape(2, 2, width)
    return (
        layer_out,
        grad_input,
        norms[0],
        norms[1],
        grad_qkv,
        bias_qkv.reshape(3, cols),
        out_grad,
        grad_gate_up,
        down_grad,
    )


def solution(mesh):
    placed = (
        P(("ctx", "tp"), None),
        P(),
        P(),
        P(None, None, "tp"),
        P(None, "tp"),
        P("tp", None),
        P(None, None, "tp"),
        P("tp", None),
        P(("ctx", "tp"), None),
        P(),
        P(),
    )
    return jax.shard_map(
        shards,
        mesh=mesh,
        in_specs=placed,
        out_specs=(
            P(("ctx", "tp"), None),
            P(("ctx", "tp"), None),
            P(),
            P(),
            P(None, None, "tp"),
            P(None, "tp"),
            P("tp", None),
            P(None, None, "tp"),
            P("tp", None),
        ),
        check_vma=False,
    )
```

```python
import math

import jax
import jax.numpy as jnp
from jax import lax
from jax.experimental import pallas as pl
from jax.experimental.pallas import tpu as pltpu
from jax.sharding import PartitionSpec as P

HEAD = 64
ROT = 16
BLK = 512
EXTRA = 16

epsilon = 1e-05
neg_large = -1e30
bf16 = jnp.bfloat16
f32 = jnp.float32


def dot(left, right, left_dim, right_dim):
    return lax.dot_general(
        left, right, (((left_dim,), (right_dim,)), ((), ())), preferred_element_type=f32
    )


def causal_keep():
    return lax.broadcasted_iota(jnp.int32, (BLK, BLK), 0) <= lax.broadcasted_iota(
        jnp.int32, (BLK, BLK), 1
    )


def turn(tile):
    return tile.astype(f32).T.astype(bf16)


def scan_chunks(devices, chunks, width, visit):
    per_block = BLK // width

    def source(device, carry):
        for chunk in range(chunks):
            place = device * (chunks // per_block) + chunk // per_block
            visit(chunk, device, place, slice((chunk % per_block) * width, (chunk % per_block + 1) * width))
        return carry

    lax.fori_loop(0, devices, source, 0)


def turn_dims(tile, cosine, sine):
    half = ROT // 2
    first, second = tile[0:half], tile[half:ROT]
    return jnp.concatenate(
        [first * cosine - second * sine, second * cosine + first * sine, tile[ROT:]], axis=0
    )


def attention_forward(order, angles, packed):
    count, devices, _, _, width = packed.shape
    blocks = devices * count * width // BLK

    def kernel(order, angles, packed, out, logsum, queries, keys, values):
        per_device = count * width // BLK
        row = lax.broadcasted_iota(jnp.int32, (EXTRA, BLK), 0)
        ones = jnp.where(row == 0, 1.0, 0.0).astype(bf16)

        def visit(chunk, device, place, lanes):
            part = packed.at[chunk]
            cosine, sine = angles[place, 0, :, lanes], angles[place, 1, :, lanes]
            query = turn_dims(part[device, 0].astype(f32), cosine, sine).astype(bf16)
            queries[place, :, lanes] = query * jnp.asarray(HEAD**-0.5, bf16)
            key = turn_dims(part[device, 1].astype(f32), cosine, sine).astype(bf16)
            keys[place, lanes, :] = turn(key)
            values[place, 0:HEAD, lanes] = part[device, 2]

        scan_chunks(devices, count, width, visit)

        def prepare(place, carry):
            values[place, HEAD : HEAD + EXTRA, :] = ones
            return carry

        lax.fori_loop(0, blocks, prepare, 0)
        keep = causal_keep()

        def query_block(i, carry):
            place = order[i]
            query = queries[place]

            def step(keys_at, state, masked):
                maxima, summed = state
                places = [order[j] for j in keys_at]
                scores = [dot(keys[other], query, 1, 0) for other in places]
                if masked:
                    scores = [jnp.where(keep, tile, neg_large) for tile in scores]
                new_maxima = maxima
                for tile in scores:
                    new_maxima = jnp.maximum(new_maxima, jnp.max(tile, axis=0, keepdims=True))
                summed = summed * jnp.exp(maxima - new_maxima)
                for other, tile in zip(places, scores):
                    weights = jnp.exp(tile - new_maxima).astype(bf16)
                    summed = summed + dot(values[other], weights, 1, 0)
                return new_maxima, summed

            state = (jnp.full((1, BLK), neg_large, f32), jnp.zeros((HEAD + EXTRA, BLK), f32))
            first = order[blocks + i]
            triples = (i - first) // 3
            state = lax.fori_loop(
                0, triples, lambda t, s: step([first + 3 * t + u for u in range(3)], s, False), state
            )
            state = lax.fori_loop(
                first + 3 * triples, i, lambda j, s: step([j], s, False), state
            )
            maxima, summed = step([i], state, True)
            totals = summed[HEAD : HEAD + 1]
            result = (summed[0:HEAD] / totals).astype(bf16)
            logsum[place] = maxima + jnp.log(totals)
            lane = pl.multiple_of(lax.rem(place, per_device) * BLK, BLK)
            out[place // per_device, :, pl.ds(lane, BLK)] = result
            return carry

        lax.fori_loop(0, blocks, query_block, 0)

    vmem = pl.BlockSpec(memory_space=pltpu.VMEM)
    return pl.pallas_call(
        kernel,
        out_shape=(
            jax.ShapeDtypeStruct((devices, HEAD, count * width), bf16),
            jax.ShapeDtypeStruct((blocks, 1, BLK), f32),
        ),
        in_specs=[pl.BlockSpec(memory_space=pltpu.SMEM), vmem, vmem],
        out_specs=(vmem, vmem),
        scratch_shapes=[
            pltpu.VMEM((blocks, HEAD, BLK), bf16),
            pltpu.VMEM((blocks, BLK, HEAD), bf16),
            pltpu.VMEM((blocks, HEAD + EXTRA, BLK), bf16),
        ],
        compiler_params=pltpu.CompilerParams(vmem_limit_bytes=60 * 2**20),
        cost_estimate=pl.CostEstimate(
            flops=85 * 2 * 2 * BLK * BLK * 256, bytes_accessed=5 * 2**20, transcendentals=0
        ),
        name="attention_forward",
    )(order, angles, packed)


def attention_backward(order, angles, packed, grad_out, out, logsum):
    count, devices, _, _, width = packed.shape
    blocks = devices * count * width // BLK
    wide = HEAD + EXTRA

    def kernel(
        order, angles, packed, grad_out, out, logsum,
        grads, query_x, grad_x, key_x, key_rows, value_x, grad_q,
    ):
        row = lax.broadcasted_iota(jnp.int32, (EXTRA, width), 0)
        lane_ids = lax.broadcasted_iota(jnp.int32, (BLK, EXTRA), 1)
        ones = jnp.where(lane_ids < 3, 1.0, 0.0).astype(bf16)

        def three_rows(value):
            high = value.astype(bf16).astype(f32)
            rest = value - high
            middle = rest.astype(bf16).astype(f32)
            low = rest - middle
            return jnp.where(
                row == 0, high, jnp.where(row == 1, middle, jnp.where(row == 2, low, 0.0))
            ).astype(bf16)

        def visit(chunk, device, place, lanes):
            part = packed.at[chunk]
            cosine, sine = angles[place, 0, :, lanes], angles[place, 1, :, lanes]
            query = turn_dims(part[device, 0].astype(f32), cosine, sine).astype(bf16)
            query_x[place, 0:HEAD, lanes] = query * jnp.asarray(HEAD**-0.5, bf16)
            query_x[place, HEAD:wide, lanes] = three_rows(-logsum[place, :, lanes])
            key = turn_dims(part[device, 1].astype(f32), cosine, sine).astype(bf16)
            key_rows[place, :, lanes] = key
            key_x[place, lanes, 0:HEAD] = turn(key)
            value_x[place, lanes, 0:HEAD] = turn(part[device, 2])
            own = slice(chunk * width, (chunk + 1) * width)
            grad = grad_out[device, :, own]
            delta = jnp.sum(
                grad.astype(f32) * out[device, :, own].astype(f32), axis=0, keepdims=True
            )
            grad_x[place, 0:HEAD, lanes] = grad
            grad_x[place, HEAD:wide, lanes] = three_rows(-delta)

        scan_chunks(devices, count, width, visit)

        def prepare(place, carry):
            key_x[place, :, HEAD:wide] = ones
            value_x[place, :, HEAD:wide] = ones
            grad_q[place] = jnp.zeros((HEAD, BLK), f32)
            return carry

        lax.fori_loop(0, blocks, prepare, 0)
        keep = causal_keep()
        per_device = count * width // BLK

        def store(part, place, tile):
            lane = pl.multiple_of(lax.rem(place, per_device) * BLK, BLK)
            grads[place // per_device, part, :, pl.ds(lane, BLK)] = tile

        def key_block(j, carry):
            place = order[j]
            key, value = key_x[place], value_x[place]
            key_tile = key_rows[place]

            def step(queries_at, state, masked):
                grad_k, grad_v = state
                places = [order[i] for i in queries_at]
                scores = [dot(key, query_x[other], 1, 0) for other in places]
                grad_probs = [dot(value, grad_x[other], 1, 0) for other in places]
                probs = [jnp.exp(tile) for tile in scores]
                if masked:
                    probs = [jnp.where(keep, tile, 0.0) for tile in probs]
                grad_raws = [(p * g).astype(bf16) for p, g in zip(probs, grad_probs)]
                for other, prob, grad_raw in zip(places, probs, grad_raws):
                    grad_v = grad_v + dot(grad_x[other, 0:HEAD, :], prob.astype(bf16), 1, 1)
                    grad_k = grad_k + dot(query_x[other, 0:HEAD, :], grad_raw, 1, 1)
                    grad_q[other] += dot(key_tile, grad_raw, 1, 0)
                return grad_k, grad_v

            zero = jnp.zeros((HEAD, BLK), f32)
            state = step([j], (zero, zero), True)
            end = order[2 * blocks + j]
            pairs = (end - j) // 2
            state = lax.fori_loop(
                0, pairs, lambda t, s: step([j + 1 + 2 * t, j + 2 + 2 * t], s, False), state
            )
            grad_k, grad_v = lax.fori_loop(
                j + 1 + 2 * pairs, end + 1, lambda i, s: step([i], s, False), state
            )
            cosine, sine = angles[place, 0], angles[place, 1]
            store(1, place, turn_dims(grad_k, cosine, -sine).astype(bf16))
            store(2, place, grad_v.astype(bf16))
            return carry

        lax.fori_loop(0, blocks, key_block, 0)

        def finish(place, carry):
            tile = turn_dims(grad_q[place] * HEAD**-0.5, angles[place, 0], -angles[place, 1])
            store(0, place, tile.astype(bf16))
            return carry

        lax.fori_loop(0, blocks, finish, 0)

    vmem = pl.BlockSpec(memory_space=pltpu.VMEM)
    return pl.pallas_call(
        kernel,
        out_shape=jax.ShapeDtypeStruct((devices, 3, HEAD, count * width), bf16),
        in_specs=[pl.BlockSpec(memory_space=pltpu.SMEM)] + [vmem] * 5,
        out_specs=vmem,
        scratch_shapes=[
            pltpu.VMEM((blocks, wide, BLK), bf16),
            pltpu.VMEM((blocks, wide, BLK), bf16),
            pltpu.VMEM((blocks, BLK, wide), bf16),
            pltpu.VMEM((blocks, HEAD, BLK), bf16),
            pltpu.VMEM((blocks, BLK, wide), bf16),
            pltpu.VMEM((blocks, HEAD, BLK), f32),
        ],
        compiler_params=pltpu.CompilerParams(vmem_limit_bytes=60 * 2**20),
        cost_estimate=pl.CostEstimate(flops=1, bytes_accessed=1, transcendentals=0),
        name="attention_backward",
    )(order, angles, packed, grad_out, out, logsum)


def row_places(first_row, length, table_flat, seq_ids):
    row_ids = first_row + jnp.arange(length, dtype=jnp.int32)
    block_ids = jnp.arange(table_flat.shape[0], dtype=jnp.int32)
    natural = jnp.sum(
        jnp.where((row_ids // BLK)[:, None] == block_ids[None, :], table_flat[None, :], 0), axis=1
    )
    sequence = jnp.sum(
        jnp.where(natural[:, None] == block_ids[None, :], seq_ids[None, :], 0), axis=1
    )
    return (natural * BLK + row_ids % BLK, sequence)


def gathered_setup(rows, table_flat, seq_ids, key_flat, value_flat):
    places, seq = row_places(lax.axis_index("ctx") * rows, rows, table_flat, seq_ids)
    pieces = (
        lax.all_gather(key_flat, "ctx", axis=0, tiled=True),
        lax.all_gather(value_flat, "ctx", axis=0, tiled=True),
    )
    stride = math.gcd(pieces[0].shape[0], 1024)
    offsets = jnp.arange(pieces[0].shape[0] // stride, dtype=jnp.int32) * stride

    def visit(offset):
        other_places, other_seq = row_places(offset, stride, table_flat, seq_ids)
        allowed = (seq[:, None] == other_seq[None, :]) & (other_places[None, :] <= places[:, None])
        blocks = [
            lax.dynamic_slice_in_dim(piece, offset, stride, 0).reshape(stride, -1, HEAD)
            for piece in pieces
        ]
        return allowed[:, None, :], blocks[0], blocks[1]

    return visit, offsets


def gathered_forward(queries, visit, offsets):
    rows, heads, _ = queries.shape

    def step(status, offset):
        allowed, keys, values = visit(offset)
        scores = jnp.einsum("qhe,khe->qhk", queries, keys, preferred_element_type=f32)
        scores = scores * HEAD**-0.5
        maxima, totals, summed = status
        new_maxima = jnp.maximum(maxima, jnp.max(jnp.where(allowed, scores, neg_large), axis=2))
        weights = jnp.where(allowed, jnp.exp(scores - new_maxima[..., None]), 0.0)
        factor = jnp.exp(maxima - new_maxima)
        totals = totals * factor + jnp.sum(weights, axis=2)
        summed = summed * factor[..., None] + jnp.einsum(
            "qhk,khe->qhe", weights.astype(bf16), values, preferred_element_type=f32
        )
        return ((new_maxima, totals, summed), None)

    initial = (
        jnp.full((rows, heads), neg_large, f32),
        jnp.zeros((rows, heads), f32),
        jnp.zeros((rows, heads, HEAD), f32),
    )
    (maxima, totals, summed), _ = lax.scan(step, initial, offsets)
    return summed / totals[..., None], maxima + jnp.log(totals)


def gathered_backward(queries, visit, offsets, grad_att, attended, logsum):
    rows, heads, _ = queries.shape
    delta = jnp.sum(grad_att.astype(f32) * attended, axis=2)

    def step(status, offset):
        allowed, keys, values = visit(offset)
        scores = jnp.einsum("qhe,khe->qhk", queries, keys, preferred_element_type=f32)
        prob = jnp.where(allowed, jnp.exp(scores * HEAD**-0.5 - logsum[..., None]), 0.0)
        grad_prob = jnp.einsum("qhe,khe->qhk", grad_att, values, preferred_element_type=f32)
        grad_raw = (prob * (grad_prob - delta[..., None]) * HEAD**-0.5).astype(bf16)
        grad_q = jnp.einsum("qhk,khe->qhe", grad_raw, keys, preferred_element_type=f32)
        grad_k = jnp.einsum("qhk,qhe->khe", grad_raw, queries, preferred_element_type=f32)
        grad_v = jnp.einsum("qhk,qhe->khe", prob.astype(bf16), grad_att, preferred_element_type=f32)
        return (
            (
                status[0] + grad_q,
                lax.dynamic_update_slice_in_dim(status[1], grad_k, offset, 0),
                lax.dynamic_update_slice_in_dim(status[2], grad_v, offset, 0),
            ),
            None,
        )

    total = rows * lax.axis_size("ctx")
    zero = jnp.zeros((total, heads, HEAD), f32)
    (grad_q, grad_k, grad_v), _ = lax.scan(
        step, (jnp.zeros((rows, heads, HEAD), f32), zero, zero), offsets
    )
    grad_k = lax.psum_scatter(grad_k, "ctx", scatter_dimension=0, tiled=True)
    grad_v = lax.psum_scatter(grad_v, "ctx", scatter_dimension=0, tiled=True)
    return grad_q, grad_k, grad_v


MESH = pl.DeviceIdType.MESH


def greet(n_ctx, n_tp):
    ctx, tp = lax.axis_index("ctx"), lax.axis_index("tp")
    barrier = pltpu.get_barrier_semaphore()

    def greet_ctx(step, carry):
        peer = lax.rem(ctx + step, n_ctx)
        pl.semaphore_signal(barrier, inc=1, device_id=(peer, tp), device_id_type=MESH)
        return carry

    lax.fori_loop(1, n_ctx, greet_ctx, 0)
    for peer in (lax.rem(tp + 1, n_tp), lax.rem(tp + n_tp - 1, n_tp)):
        pl.semaphore_signal(barrier, inc=1, device_id=(ctx, peer), device_id_type=MESH)
    pl.semaphore_wait(barrier, n_ctx + 1)


def rows_norm(source, stored, gain, shift, mean_out, inverse_out, tile):
    def step(i, carry):
        rows = pl.ds(pl.multiple_of(i * tile, tile), tile)
        x = source(rows)
        mean = jnp.mean(x, axis=1, keepdims=True)
        center = x - mean
        inverse = lax.rsqrt(jnp.mean(center * center, axis=1, keepdims=True) + epsilon)
        stored(rows, (center * inverse * gain + shift).astype(bf16))
        mean_out[rows, :] = jnp.broadcast_to(mean, (tile, 128))
        inverse_out[rows, :] = jnp.broadcast_to(inverse, (tile, 128))
        return carry

    return step


def project_exchange(layer_in, w_part, gain, shift, w_qkv, b_qkv):
    n_ctx, n_tp = lax.axis_size("ctx"), lax.axis_size("tp")
    own, width = layer_in.shape
    part = w_part.shape[0]
    cols = w_qkv.shape[2]

    def kernel(
        x_in, w_in, gain, shift, w_qkv_in, b_qkv,
        xs_out, lows_out, means, inverses, ws, packed,
        xs, lows, w_qkv, load_s, store_s, outgoing, ring_send, ring_recv, w_send, w_recv, send, recv,
    ):
        ctx, tp = lax.axis_index("ctx"), lax.axis_index("tp")
        right = lax.rem(tp + 1, n_tp)
        half = own // 2

        def block(slot):
            return lax.rem(tp - slot + n_tp, n_tp)

        def ring(step, piece):
            rows = pl.ds(piece * half, half)
            return pltpu.make_async_remote_copy(
                src_ref=x_in.at[rows] if step == 0 else xs.at[block(step), rows],
                dst_ref=xs.at[block(step), rows],
                send_sem=ring_send.at[step, piece],
                recv_sem=ring_recv.at[step, piece],
                device_id=(ctx, right),
                device_id_type=MESH,
            )

        def w_ring(step):
            return pltpu.make_async_remote_copy(
                src_ref=w_in if step == 0 else ws.at[block(step)],
                dst_ref=ws.at[block(step)],
                send_sem=w_send.at[step],
                recv_sem=w_recv.at[step],
                device_id=(ctx, right),
                device_id_type=MESH,
            )

        def exchange(slot, step):
            peer = lax.rem(ctx + step, n_ctx)
            return pltpu.make_async_remote_copy(
                src_ref=outgoing.at[slot, peer],
                dst_ref=packed.at[block(slot), ctx],
                send_sem=send.at[slot, step],
                recv_sem=recv.at[slot, step],
                device_id=(peer, tp),
                device_id_type=MESH,
            )

        load = pltpu.make_async_copy(w_qkv_in, w_qkv, load_s)
        load.start()

        def store(slot, which):
            here = block(slot)
            source, target = ((xs, xs_out), (lows, lows_out))[which]
            return pltpu.make_async_copy(source.at[here], target.at[here], store_s.at[slot, which])

        greet(n_ctx, n_tp)
        for piece in range(2):
            ring(0, piece).start()
        xs[tp] = x_in[...]
        ws[tp] = w_in[...]
        for slot in range(n_tp):
            if slot > 0:
                for piece in range(2):
                    ring(slot - 1, piece).wait_recv()
                    if slot < n_tp - 1:
                        ring(slot, piece).start()
            if slot == n_tp - 2:
                w_ring(0).start()
            if slot == n_tp - 1:
                w_ring(0).wait_recv()
                w_ring(1).start()

            here = block(slot)

            def stored(rows, value, here=here):
                lows[here, rows, :] = value

            step = rows_norm(
                lambda rows, here=here: xs[here, rows, :].astype(f32),
                stored, gain[...], shift[...], means.at[here], inverses.at[here], 32,
            )
            lax.fori_loop(0, own // 32, step, 0)
            store(slot, 0).start()
            store(slot, 1).start()
            if slot == 0:
                load.wait()

            def project(c, carry, slot=slot, here=here):
                value = jnp.dot(lows[here], w_qkv[c], preferred_element_type=f32) + b_qkv[c]
                outgoing[slot, :, c] = value.T.astype(bf16).reshape(n_ctx, HEAD, own)
                return carry

            lax.fori_loop(0, 3, project, 0)
            lax.fori_loop(
                1, n_ctx, lambda step, c, slot=slot: (exchange(slot, step).start(), c)[1], 0
            )
            packed[here, ctx] = outgoing[slot, ctx]
        for step in range(1, n_tp - 1):
            w_ring(step).wait_recv()
            if step < n_tp - 2:
                w_ring(step + 1).start()
        for slot in range(n_tp):
            lax.fori_loop(
                1, n_ctx, lambda step, c, slot=slot: (exchange(slot, step).wait(), c)[1], 0
            )
        for slot in range(n_tp):
            store(slot, 0).wait()
            store(slot, 1).wait()
        for step in range(n_tp - 1):
            w_ring(step).wait_send()
            for piece in range(2):
                ring(step, piece).wait_send()

    vmem, anywhere = pl.BlockSpec(memory_space=pltpu.VMEM), pl.BlockSpec(memory_space=pl.ANY)
    return pl.pallas_call(
        kernel,
        out_shape=(
            jax.ShapeDtypeStruct((n_tp, own, width), bf16),
            jax.ShapeDtypeStruct((n_tp, own, width), bf16),
            jax.ShapeDtypeStruct((n_tp, own, 128), f32),
            jax.ShapeDtypeStruct((n_tp, own, 128), f32),
            jax.ShapeDtypeStruct((n_tp, part, width), bf16),
            jax.ShapeDtypeStruct((n_tp, n_ctx, 3, HEAD, own), bf16),
        ),
        in_specs=[vmem] * 4 + [anywhere, vmem],
        out_specs=(anywhere,) * 2 + (vmem,) * 4,
        scratch_shapes=[
            pltpu.VMEM((n_tp, own, width), bf16),
            pltpu.VMEM((n_tp, own, width), bf16),
            pltpu.VMEM((3, width, cols), bf16),
            pltpu.SemaphoreType.DMA,
            pltpu.SemaphoreType.DMA((n_tp, 2)),
            pltpu.VMEM((n_tp, n_ctx, 3, HEAD, own), bf16),
            pltpu.SemaphoreType.DMA((n_tp - 1, 2)),
            pltpu.SemaphoreType.DMA((n_tp - 1, 2)),
            pltpu.SemaphoreType.DMA((n_tp - 1,)),
            pltpu.SemaphoreType.DMA((n_tp - 1,)),
            pltpu.SemaphoreType.DMA((n_tp, n_ctx)),
            pltpu.SemaphoreType.DMA((n_tp, n_ctx)),
        ],
        compiler_params=pltpu.CompilerParams(
            collective_id=1, has_side_effects=True, vmem_limit_bytes=60 * 2**20
        ),
        cost_estimate=pl.CostEstimate(
            flops=2 * n_tp * own * width * 3 * cols, bytes_accessed=20 * 2**20, transcendentals=0
        ),
        name="project_exchange",
    )(layer_in, w_part, gain, shift, w_qkv.transpose(1, 0, 2), b_qkv[:, None, :])


def output_project(out, xs, w_all, gain, shift):
    n_ctx, n_tp = lax.axis_size("ctx"), lax.axis_size("tp")
    own, width = xs.shape[1:]
    cols = w_all.shape[1]
    rows_all = n_tp * own

    def kernel(
        out, xs_in, w_in, gain, shift,
        middle_out, lows_out, means, inverses, raw,
        xs, w_all, middle, lows, load_s, store_s, ring_send, ring_recv, send, recv, own_sem,
    ):
        ctx, tp = lax.axis_index("ctx"), lax.axis_index("tp")
        right = lax.rem(tp + 1, n_tp)
        half = cols // 2

        def block(slot):
            return lax.rem(tp - slot + n_tp, n_tp)

        def ring(step, piece):
            rows = pl.ds(piece * half, half)
            return pltpu.make_async_remote_copy(
                src_ref=raw.at[block(step), rows],
                dst_ref=raw.at[block(step), rows],
                send_sem=ring_send.at[step, piece],
                recv_sem=ring_recv.at[step, piece],
                device_id=(ctx, right),
                device_id_type=MESH,
            )

        def exchange(step):
            peer = lax.rem(ctx + step, n_ctx)
            return pltpu.make_async_remote_copy(
                src_ref=out.at[peer],
                dst_ref=raw.at[tp, pl.ds(pl.multiple_of(ctx * HEAD, HEAD), HEAD)],
                send_sem=send.at[step],
                recv_sem=recv.at[step],
                device_id=(peer, tp),
                device_id_type=MESH,
            )

        loads = (
            pltpu.make_async_copy(xs_in, xs, load_s.at[0]),
            pltpu.make_async_copy(w_in, w_all, load_s.at[1]),
        )
        for load in loads:
            load.start()

        def store(place, which):
            source, target = ((middle, middle_out), (lows, lows_out))[which]
            return pltpu.make_async_copy(
                source.at[place], target.at[place], store_s.at[place, which]
            )

        greet(n_ctx, n_tp)
        lax.fori_loop(1, n_ctx, lambda step, c: (exchange(step).start(), c)[1], 0)
        keep = pltpu.make_async_copy(
            out.at[ctx], raw.at[tp, pl.ds(pl.multiple_of(ctx * HEAD, HEAD), HEAD)], own_sem
        )
        keep.start()
        keep.wait()
        lax.fori_loop(1, n_ctx, lambda step, c: (exchange(step).wait_recv(), c)[1], 0)
        for piece in range(2):
            ring(0, piece).start()
        for load in loads:
            load.wait()
        for slot in range(n_tp):
            if slot > 0:
                for piece in range(2):
                    ring(slot - 1, piece).wait_recv()
                    if slot < n_tp - 1:
                        ring(slot, piece).start()
            here = block(slot)

            def project(place, carry, slot=slot, here=here):
                lanes = pl.ds(pl.multiple_of(place * own, own), own)
                tile = raw[here, :, lanes].astype(f32).T.astype(bf16)
                value = jnp.dot(tile, w_all[here], preferred_element_type=f32)
                if slot == 0:
                    middle[place] = xs[place].astype(f32) + value
                else:
                    middle[place] += value
                return carry

            lax.fori_loop(0, n_tp, project, 0)
        for place in range(n_tp):
            store(place, 0).start()

            def stored(rows, value, place=place):
                lows[place, rows, :] = value

            step = rows_norm(
                lambda rows, place=place: middle[place, rows, :],
                stored, gain[...], shift[...], means.at[place], inverses.at[place], 32,
            )
            lax.fori_loop(0, own // 32, step, 0)
            store(place, 1).start()
        lax.fori_loop(1, n_ctx, lambda step, c: (exchange(step).wait_send(), c)[1], 0)
        for place in range(n_tp):
            store(place, 0).wait()
            store(place, 1).wait()
        for step in range(n_tp - 1):
            for piece in range(2):
                ring(step, piece).wait_send()

    vmem, anywhere = pl.BlockSpec(memory_space=pltpu.VMEM), pl.BlockSpec(memory_space=pl.ANY)
    return pl.pallas_call(
        kernel,
        out_shape=(
            jax.ShapeDtypeStruct((n_tp, own, width), f32),
            jax.ShapeDtypeStruct((n_tp, own, width), bf16),
            jax.ShapeDtypeStruct((n_tp, own, 128), f32),
            jax.ShapeDtypeStruct((n_tp, own, 128), f32),
            jax.ShapeDtypeStruct((n_tp, cols, rows_all), bf16),
        ),
        in_specs=[vmem, anywhere, anywhere, vmem, vmem],
        out_specs=(anywhere,) * 2 + (vmem,) * 3,
        scratch_shapes=[
            pltpu.VMEM((n_tp, own, width), bf16),
            pltpu.VMEM((n_tp, cols, width), bf16),
            pltpu.VMEM((n_tp, own, width), f32),
            pltpu.VMEM((n_tp, own, width), bf16),
            pltpu.SemaphoreType.DMA((2,)),
            pltpu.SemaphoreType.DMA((n_tp, 2)),
            pltpu.SemaphoreType.DMA((n_tp - 1, 2)),
            pltpu.SemaphoreType.DMA((n_tp - 1, 2)),
            pltpu.SemaphoreType.DMA((n_ctx,)),
            pltpu.SemaphoreType.DMA((n_ctx,)),
            pltpu.SemaphoreType.DMA,
        ],
        compiler_params=pltpu.CompilerParams(
            collective_id=2, has_side_effects=True, vmem_limit_bytes=60 * 2**20
        ),
        cost_estimate=pl.CostEstimate(
            flops=2 * rows_all * n_tp * cols * width, bytes_accessed=30 * 2**20, transcendentals=0
        ),
        name="output_project",
    )(out, xs, w_all, gain, shift)


def middle_sums(term, w_all, low, gate, up, hidden, cot, attended, w_down):
    rows, width = term.shape
    n_tp, cols, _ = w_all.shape
    n_ctx = lax.axis_size("ctx")
    units = gate.shape[1]
    share, piece = width // n_ctx, cols // n_ctx
    out_rows, down_rows = n_tp * piece, units // n_ctx
    other_rows = out_rows + down_rows
    half, heads = cols // 2, cols // 2 // HEAD
    window = min(units, (down_rows + 127 + 127) // 128 * 128)
    pair = n_ctx // 2
    tile = 256

    def kernel(
        term_in, w_all, low, gate, up, hidden, cot, attended, w_down,
        grad_out, gate_sum, up_sum, out_kept, out_sent, down_kept, down_sent, *rest,
    ):
        down_terms, down_far, (
            term, w_buf, wide_buf, gate_buf, up_buf, hidden_t, att_buf, tile_in, tile_out, far, ring_buf, heads_out, send_one, send_two, got_one, got_two, one_a, one_b,
            two_a, two_b,
            tile_s, far_s, load_s, w_s, att_s, ring_s, ring_r, head_s, head_r, core_s, core_r, one_s, one_r, two_s, two_r,
        ) = rest[: n_tp - 1], rest[n_tp - 1], rest[n_tp:]
        ctx, tp = lax.axis_index("ctx"), lax.axis_index("tp")
        y, x, core = ctx // 4, (ctx // 2) % 2, ctx % 2
        on_core, on_x, on_y = ctx + 1 - 2 * core, ctx + 2 - 4 * x, ctx + 4 - 8 * y
        here = y * 2 + x

        def remote(source, target, send, recv, peer, near=True):
            return pltpu.make_async_remote_copy(
                src_ref=source,
                dst_ref=target,
                send_sem=send,
                recv_sem=recv,
                device_id=(peer, tp) if near else (ctx, peer),
                device_id_type=MESH,
            )

        def w_load(block, side):
            rows_in = pl.ds(side * half, half)
            return pltpu.make_async_copy(w_all.at[block, rows_in], w_buf, w_s)

        def dest(step):
            return lax.rem(tp - 1 - step + 2 * n_tp, n_tp)

        loads = [
            pltpu.make_async_copy(source, target, load_s.at[i])
            for i, (source, target) in enumerate(
                ((low, wide_buf), (gate, gate_buf), (up, up_buf), (cot, wide_buf), (hidden, gate_buf), (term_in, term))
            )
        ]
        loads[5].start()
        w_load(dest(0), 0).start()
        for i in range(3):
            loads[i].start()
        greet(n_ctx, n_tp)

        def own_term(step, side):
            w_load(dest(step), side).wait()
            return lax.dot_general(
                w_buf[...], term[...], (((1,), (1,)), ((), ())), preferred_element_type=f32
            ).reshape(heads, HEAD, rows)

        def load_after(step, side):
            @pl.when(jnp.logical_or(side == 0, step < n_tp - 1))
            def _():
                w_load(lax.rem(tp - 1 - step - side + 2 * n_tp, n_tp), 1 - side).start()

        def ring(step, side):
            return remote(
                heads_out.at[pl.ds(side * heads, heads)]
                if step == 0
                else ring_buf.at[step - 1, side],
                ring_buf.at[step, side],
                ring_s.at[step, side],
                ring_r.at[step, side],
                lax.rem(tp + 1, n_tp),
                False,
            )

        def head_copy(step):
            peer = lax.rem(ctx + step, n_ctx)
            return remote(
                heads_out.at[peer], grad_out.at[ctx], head_s.at[step], head_r.at[step], peer
            )

        def ring_next(step):
            def one_side(side, carry):
                value = own_term(step + 1, side)
                ring(step, side).wait_recv()
                value = (value + ring_buf[step, side].astype(f32)).astype(bf16)
                if step < n_tp - 2:
                    ring_buf[step, side] = value
                    ring(step + 1, side).start()
                else:
                    ring(0, side).wait_send()
                    heads_out[pl.ds(side * heads, heads)] = value
                load_after(step + 1, side)
                return carry

            lax.fori_loop(0, 2, one_side, 0)

        def ring_first(side, carry):
            heads_out[pl.ds(side * heads, heads)] = own_term(0, side).astype(bf16)
            ring(0, side).start()
            load_after(0, side)
            return carry

        loads[5].wait()
        lax.fori_loop(0, 2, ring_first, 0)

        def spot(k):
            to_y, to_x = lax.rem(k, 2), k // 2
            return 1 - y + to_y * (2 * y - 1), 1 - x + to_x * (2 * x - 1)

        def spread(got, bounds, firsts, group):
            def copy(side, i):
                if side == 0:
                    source, peer = got.at[2 * i + 1 - x, bounds[0]], on_x
                else:
                    source, peer = got.at[2 * (1 - y) + i, bounds[1]], on_y
                return remote(
                    source, firsts[side].at[i], one_s.at[group, side, i], one_r.at[group, side, i], peer
                )

            return copy

        bounds_one = (slice(0, share), slice(share, 2 * share))
        bounds_two = (slice(0, out_rows), slice(out_rows, other_rows))
        spread_one = spread(got_one, bounds_one, (one_a, one_b), 0)
        spread_two = spread(got_two, bounds_two, (two_a, two_b), 1)

        def grads_one(chunk, store):
            lanes = pl.ds(pl.multiple_of(chunk * share, share), share)
            left = wide_buf[:, lanes].T
            store(bounds_one[0], jnp.dot(left, gate_buf[...], preferred_element_type=f32))
            store(bounds_one[1], jnp.dot(left, up_buf[...], preferred_element_type=f32))

        def grads_two(chunk, store):
            load = pltpu.make_async_copy(
                attended.at[:, pl.ds(pl.multiple_of(chunk * piece, piece), piece)], att_buf, att_s
            )
            load.start()
            first = chunk * down_rows
            start = jnp.minimum(first // 128 * 128, units - window)
            lanes = pl.ds(pl.multiple_of(start, 128), window)
            hidden_t[...] = gate_buf[:, lanes].T
            down_part = hidden_t[pl.ds(pl.multiple_of(first - start, 16), down_rows), :]
            store(
                slice(out_rows, other_rows),
                jnp.dot(down_part, wide_buf[...], preferred_element_type=f32),
            )
            load.wait()
            store(
                slice(0, out_rows),
                jnp.dot(
                    att_buf[...].reshape(out_rows, rows), term[...], preferred_element_type=f32
                ),
            )

        def core_copy(group, k):
            at_y, at_x = spot(k)
            sent, got = ((send_one, got_one), (send_two, got_two))[group]
            return remote(
                sent, got.at[2 * at_y + at_x], core_s.at[group, k], core_r.at[group, k], on_core
            )

        def both_sides(group, grads, sent, got, copy, leading):
            def step(k, carry):
                sending = jnp.logical_or(k == 0, jnp.logical_and(lax.rem(k, 2) == 1, k < 2 * pair - 1))
                keeping = jnp.logical_not(sending)
                behind = (k + k // (2 * pair - 1)) // 2 - 1
                place_k = jnp.where(sending, (k + 1) // 2, behind)
                at_y, at_x = spot(place_k)
                index = 2 * at_y + at_x

                @pl.when(keeping)
                def _():
                    core_copy(group, place_k).wait_recv()

                def store(place, value):
                    if place == leading:

                        @pl.when(jnp.logical_and(sending, k >= 1))
                        def _():
                            core_copy(group, place_k - 1).wait_send()

                    @pl.when(sending)
                    def _():
                        sent[place] = value.astype(bf16)

                    @pl.when(keeping)
                    def _():
                        got[index, place] = (got[index, place].astype(f32) + value).astype(bf16)

                grads(2 * index + jnp.where(sending, 1 - core, core), store)

                @pl.when(sending)
                def _():
                    core_copy(group, place_k).start()

                @pl.when(jnp.logical_and(keeping, place_k < 2))
                def _():
                    copy(0, at_y).start()

                @pl.when(jnp.logical_and(keeping, lax.rem(place_k, 2) == 0))
                def _():
                    copy(1, at_x).start()

                return carry

            lax.fori_loop(0, 2 * pair, step, 0)
            core_copy(group, pair - 1).wait_send()

        def fold(got, bounds, firsts, copy):
            for i in range(2):
                copy(0, i).wait_recv()
                index = 2 * i + x
                got[index, bounds[0]] = (
                    got[index, bounds[0]].astype(f32) + firsts[0][i].astype(f32)
                ).astype(bf16)
                copy(1, i).wait_recv()
                index = 2 * y + i
                got[index, bounds[1]] = (
                    got[index, bounds[1]].astype(f32) + firsts[1][i].astype(f32)
                ).astype(bf16)

        def last_copy(group, side):
            got, bounds, last = got_one, bounds_one, (gate_sum, up_sum)
            if side == 0:
                source, peer = got.at[2 * (1 - y) + x, bounds[0]], on_y
            else:
                source, peer = got.at[2 * y + 1 - x, bounds[1]], on_x
            return remote(
                source, last[side], two_s.at[group, side], two_r.at[group, side], peer
            )

        def finish(group, side, got, bounds, last):
            last_copy(group, side).wait_recv()
            return (got[here, bounds[side]].astype(f32) + last[...].astype(f32)).astype(bf16)

        for i in range(3):
            loads[i].wait()
        both_sides(0, grads_one, send_one, got_one, spread_one, bounds_one[0])
        loads[3].start()
        loads[4].start()
        ring_next(0)
        loads[4].wait()
        loads[3].wait()
        both_sides(1, grads_two, send_two, got_two, spread_two, bounds_two[1])
        ring_next(1)
        fold(got_one, bounds_one, (one_a, one_b), spread_one)
        for side in range(2):
            last_copy(0, side).start()
        def down_tile(t, carry):
            lanes = pl.ds(pl.multiple_of(t * tile, tile), tile)
            load = pltpu.make_async_copy(w_down.at[:, lanes], tile_in, tile_s.at[0])
            load.start()
            load.wait()
            for s in range(n_tp):
                own_rows = rows // n_tp
                block = lax.rem(tp - s + n_tp, n_tp)
                left = gate_buf[pl.ds(pl.multiple_of(block * own_rows, own_rows), own_rows), :]
                value = jnp.dot(left, tile_in[...], preferred_element_type=f32)
                if s == n_tp - 1:
                    far[:, lanes] = value.astype(bf16)
                    continue
                tile_out[s] = value.astype(bf16)
                pltpu.make_async_copy(
                    tile_out.at[s], down_terms[s].at[:, lanes], tile_s.at[s + 1]
                ).start()
            for s in range(n_tp - 1):
                pltpu.make_async_copy(
                    tile_out.at[s], down_terms[s].at[:, lanes], tile_s.at[s + 1]
                ).wait()
            return carry

        lax.fori_loop(0, width // tile, down_tile, 0)
        far_copy = remote(
            far, down_far, far_s.at[0], far_s.at[1], lax.rem(tp + 1, n_tp), False
        )
        far_copy.start()
        for step in range(2, n_tp - 1):
            ring_next(step)
        lax.fori_loop(1, n_ctx, lambda step, c: (head_copy(step).start(), c)[1], 0)
        grad_out[ctx] = heads_out[ctx]

        fold(got_two, bounds_two, (two_a, two_b), spread_two)
        out_kept[...] = got_two[here, bounds_two[0]]
        out_sent[...] = got_two[2 * (1 - y) + x, bounds_two[0]]
        down_kept[...] = got_two[here, bounds_two[1]]
        down_sent[...] = got_two[2 * y + 1 - x, bounds_two[1]]
        gate_sum[...] = finish(0, 0, got_one, bounds_one, gate_sum)
        up_sum[...] = finish(0, 1, got_one, bounds_one, up_sum)
        lax.fori_loop(1, n_ctx, lambda step, c: (head_copy(step).wait(), c)[1], 0)
        far_copy.wait()
        for step in range(1, n_tp - 1):
            for side in range(2):
                ring(step, side).wait_send()
        for group, copy in enumerate((spread_one, spread_two)):
            for side in range(2):
                if group == 0:
                    last_copy(group, side).wait_send()
                for i in range(2):
                    copy(side, i).wait_send()

    vmem, anywhere = pl.BlockSpec(memory_space=pltpu.VMEM), pl.BlockSpec(memory_space=pl.ANY)
    dma = pltpu.SemaphoreType.DMA
    return pl.pallas_call(
        kernel,
        out_shape=(
            jax.ShapeDtypeStruct((n_ctx, HEAD, rows), bf16),
            jax.ShapeDtypeStruct((share, units), bf16),
            jax.ShapeDtypeStruct((share, units), bf16),
            jax.ShapeDtypeStruct((out_rows, width), bf16),
            jax.ShapeDtypeStruct((out_rows, width), bf16),
            jax.ShapeDtypeStruct((down_rows, width), bf16),
            jax.ShapeDtypeStruct((down_rows, width), bf16),
        )
        + (jax.ShapeDtypeStruct((rows // n_tp, width), bf16),) * n_tp,
        in_specs=[anywhere] * 9,
        out_specs=(vmem,) * 7 + (anywhere,) * (n_tp - 1) + (vmem,),
        scratch_shapes=[
            pltpu.VMEM((rows, width), bf16),
            pltpu.VMEM((half, width), bf16),
            pltpu.VMEM((rows, width), bf16),
            pltpu.VMEM((rows, units), bf16),
            pltpu.VMEM((rows, units), bf16),
            pltpu.VMEM((window, rows), bf16),
            pltpu.VMEM((n_tp, piece, rows), bf16),
            pltpu.VMEM((units, tile), bf16),
            pltpu.VMEM((n_tp - 1, rows // n_tp, tile), bf16),
            pltpu.VMEM((rows // n_tp, width), bf16),
            pltpu.VMEM((n_tp - 1, 2, heads, HEAD, rows), bf16),
            pltpu.VMEM((n_ctx, HEAD, rows), bf16),
            pltpu.VMEM((2 * share, units), bf16),
            pltpu.VMEM((other_rows, width), bf16),
            pltpu.VMEM((pair, 2 * share, units), bf16),
            pltpu.VMEM((pair, other_rows, width), bf16),
            pltpu.VMEM((2, share, units), bf16),
            pltpu.VMEM((2, share, units), bf16),
            pltpu.VMEM((2, out_rows, width), bf16),
            pltpu.VMEM((2, down_rows, width), bf16),
            dma((n_tp,)), dma((2,)), dma((6,)), dma, dma,
            dma((n_tp - 1, 2)), dma((n_tp - 1, 2)),
            dma((n_ctx,)), dma((n_ctx,)),
            dma((2, pair)), dma((2, pair)),
            dma((2, 2, 2)), dma((2, 2, 2)),
            dma((2, 2)), dma((2, 2)),
        ],
        compiler_params=pltpu.CompilerParams(
            collective_id=4, has_side_effects=True, vmem_limit_bytes=62 * 2**20
        ),
        cost_estimate=pl.CostEstimate(
            flops=2 * rows * width * (2 * units + units + 2 * n_tp * cols),
            bytes_accessed=40 * 2**20,
            transcendentals=0,
        ),
        name="middle_sums",
    )(term, w_all, low, gate, up, hidden, cot, attended, w_down)


def final_sums(term, xs, means, inverses, gain, low, grads, w_qkv, out, small_two):
    n_tp, own, width = term.shape
    rows = low.shape[0]
    n_ctx = lax.axis_size("ctx")
    cols = 3 * n_ctx * HEAD
    tile = 32
    share = width // n_ctx
    half_rows, half_width = share // 2, width // 2
    part = out.shape[0] // n_tp
    columns = cols // 3
    first_rows, norm_rows = cols // 128, width // 128
    small_shape = (first_rows + 4 * norm_rows, 128)

    def kernel(
        term_in, xs, means, inverses, gain, low_in, mine, w_in, out, small_two,
        grad_in, out_all, qkv_all, small_sum,
        term, low_part, low_t, w_qkv, x_buf, grads, turned, back, sums, small, load_s, x_s, swap_s, swap_r, out_recv, out_s, out_r,
        small_ctx, small_tp, ring_buf, q_send, q_recv, both, first_a, first_b, second,
        small_s, small_r, norm_s, norm_r, ring_s, ring_r, core_s, core_r, one_s, one_r, two_s, two_r, piece_s, piece_r,
    ):
        ctx, tp = lax.axis_index("ctx"), lax.axis_index("tp")
        y, x, core = ctx // 4, (ctx // 2) % 2, ctx % 2
        on_core, on_x, on_y = ctx + 1 - 2 * core, ctx + 2 - 4 * x, ctx + 4 - 8 * y
        across = on_x + 4 - 8 * y
        here = y * 2 + x
        loads = [
            pltpu.make_async_copy(source, target, load_s.at[i])
            for i, (source, target) in enumerate(((w_in, w_qkv), (term_in, term)))
        ]
        for load in loads:
            load.start()
        barrier = pltpu.get_barrier_semaphore()
        for step in range(1, n_ctx):
            peer = lax.rem(ctx + step, n_ctx)
            pl.semaphore_signal(barrier, inc=1, device_id=(peer, tp), device_id_type=MESH)
        for step in range(1, n_tp):
            peer = lax.rem(tp + step, n_tp)
            pl.semaphore_signal(barrier, inc=1, device_id=(ctx, peer), device_id_type=MESH)
        pl.semaphore_wait(barrier, n_ctx + n_tp - 2)

        def remote(source, target, send, recv, peer, near=True):
            return pltpu.make_async_remote_copy(
                src_ref=source,
                dst_ref=target,
                send_sem=send,
                recv_sem=recv,
                device_id=(peer, tp) if near else (ctx, peer),
                device_id_type=MESH,
            )

        def ring(step, piece):
            lanes = slice(piece * half_width, (piece + 1) * half_width)
            first = term.at[lax.rem(tp - 1 + n_tp, n_tp), :, lanes]
            return remote(
                first if step == 0 else ring_buf.at[step - 1, piece],
                ring_buf.at[step, piece],
                ring_s.at[step, piece],
                ring_r.at[step, piece],
                lax.rem(tp + 1, n_tp),
                False,
            )

        def ring_next(step):
            for piece in range(2):
                lanes = slice(piece * half_width, (piece + 1) * half_width)
                ring(step, piece).wait_recv()
                block = lax.rem(tp - 2 - step + 2 * n_tp, n_tp)
                total = ring_buf[step, piece].astype(f32) + term[block, :, lanes].astype(f32)
                if step < n_tp - 2:
                    ring_buf[step, piece] = total.astype(bf16)
                    ring(step + 1, piece).start()
                else:
                    grad_in[:, lanes] = total.astype(bf16)

        def rows_of(where, start, stop):
            return lambda chunk: where.at[chunk, start:stop]

        def qkv_rows(start, stop):
            return lambda chunk: qkv_all.at[chunk, :, start:stop]

        pieces = (
            (rows_of(out_all, 0, part), False),
            (qkv_rows(0, half_rows), True),
            (qkv_rows(half_rows, share), False),
        )

        def hop(p, index):
            where, y_first = pieces[p]
            one, two = (on_y, on_x) if y_first else (on_x, on_y)
            chunk, peer = (
                (ctx, one), (ctx, two), (ctx, on_core), (one, two),
                (one, on_core), (two, on_core), (across, on_core),
            )[index]
            place = where(chunk)
            return remote(place, place, piece_s.at[p, index], piece_r.at[p, index], peer)

        def arrived(p, index):
            where, y_first = pieces[p]
            one, two = (on_y, on_x) if y_first else (on_x, on_y)
            chunk = (
                one, two, on_core, across,
                one + on_core - ctx, two + on_core - ctx, across + on_core - ctx,
            )[index]
            place = where(chunk)
            remote(place, place, piece_s.at[p, index], piece_r.at[p, index], on_core).wait_recv()

        def gather_start(p):
            for index in (0, 1, 2):
                hop(p, index).start()

        def gather_one(p):
            arrived(p, 0)
            hop(p, 3).start()
            hop(p, 4).start()

        def gather_two(p):
            arrived(p, 1)
            hop(p, 5).start()
            arrived(p, 3)
            hop(p, 6).start()

        def gather_end(p):
            for index in (2, 4, 5, 6):
                arrived(p, index)
            for index in range(7):
                hop(p, index).wait_send()

        def dest(step):
            return lax.rem(tp - 1 - step + 2 * n_tp, n_tp)

        def exchange(step, at):
            lanes = pl.ds(pl.multiple_of(dest(step) * own, own), own)
            peer = lax.rem(ctx + at, n_ctx)
            return remote(
                mine.at[peer, :, :, lanes],
                grads.at[:, ctx, :, lanes],
                swap_s.at[step, at],
                swap_r.at[step, at],
                peer,
            )

        def out_rows(step):
            return pl.ds(pl.multiple_of(dest(step) * part, part), part)

        def out_ring(step):
            return remote(
                out.at[out_rows(0)] if step == 0 else out_recv.at[step - 1],
                out_recv.at[step],
                out_s.at[step],
                out_r.at[step],
                lax.rem(tp + 1, n_tp),
                False,
            )

        def out_next(step):
            out_ring(step).wait_recv()
            total = out_recv[step].astype(f32) + out[out_rows(step + 1)].astype(f32)
            if step < n_tp - 2:
                out_recv[step] = total.astype(bf16)
                out_ring(step + 1).start()
            else:
                out_all[ctx] = total.astype(bf16)

        def x_load(step):
            return pltpu.make_async_copy(xs.at[dest(step)], x_buf, x_s)

        for step in range(n_tp):
            lax.fori_loop(
                1, n_ctx, lambda at, c, step=step: (exchange(step, at).start(), c)[1], 0
            )
        x_load(0).start()
        grads[:, ctx] = mine[ctx]
        out_ring(0).start()
        sums[...] = jnp.zeros_like(sums)

        def wait_rows(step):
            lax.fori_loop(1, n_ctx, lambda at, c: (exchange(step, at).wait_recv(), c)[1], 0)
            lanes = pl.ds(pl.multiple_of(dest(step) * own, own), own)
            for c in range(3):
                turned[c, lanes, :] = grads[c, :, :, lanes].reshape(columns, own).T

        def back_rows(step):
            block = dest(step)
            lanes = pl.ds(pl.multiple_of(block * own, own), own)
            for c in range(3):
                value = lax.dot_general(
                    turned[c, lanes, :], w_qkv[c], (((1,), (1,)), ((), ())), preferred_element_type=f32
                )
                if c == 0:
                    back[...] = value
                else:
                    back[...] += value
            x_load(step).wait()

            def norm_rows_back(i, carry):
                span = pl.ds(pl.multiple_of(i * tile, tile), tile)
                inverse = inverses[block, span, :][:, :1]
                normed = (x_buf[span, :].astype(f32) - means[block, span, :][:, :1]) * inverse
                value = back[span, :]
                scaled = value * gain[...]
                grad = inverse * (
                    scaled
                    - jnp.mean(scaled, axis=1, keepdims=True)
                    - normed * jnp.mean(scaled * normed, axis=1, keepdims=True)
                )
                sums[0:1] += jnp.sum(value * normed, axis=0, keepdims=True)
                sums[1:2] += jnp.sum(value, axis=0, keepdims=True)
                term[block, span, :] = (term[block, span, :].astype(f32) + grad).astype(bf16)
                return carry

            lax.fori_loop(0, own // tile, norm_rows_back, 0)
            if step < n_tp - 1:
                x_load(step + 1).start()

        def small_copy(step):
            peer = lax.rem(ctx + step, n_ctx)
            return remote(small, small_ctx.at[ctx], small_s.at[step], small_r.at[step], peer)

        def norm_copy(step):
            peer = lax.rem(tp + step, n_tp)
            source = small_tp.at[tp]
            return remote(source, source, norm_s.at[step], norm_r.at[step], peer, False)


        def turn_low(i, carry):
            lanes = pl.ds(pl.multiple_of(i * share, share), share)
            load = pltpu.make_async_copy(low_in.at[:, lanes], low_part, load_s.at[2])
            load.start()
            load.wait()
            low_t[i] = low_part[...].T
            return carry

        lax.fori_loop(0, n_ctx, turn_low, 0)
        for load in loads:
            load.wait()
        wait_rows(0)
        back_rows(0)
        for piece in range(2):
            ring(0, piece).start()
        for step in range(1, n_tp - 1):
            if step == 1:
                out_next(0)
            wait_rows(step)
            back_rows(step)
        wait_rows(n_tp - 1)

        def core_copy(i):
            return remote(q_send.at[i], q_recv.at[i], core_s.at[i], core_r.at[i], on_core)

        top, bottom = slice(0, half_rows), slice(half_rows, share)

        def one_copy(side, i):
            if side == 0:
                source, target, peer = both.at[2 * i + 1 - x, :, top], first_a.at[i], on_x
            else:
                source, target, peer = both.at[2 * (1 - y) + i, :, bottom], first_b.at[i], on_y
            return remote(source, target, one_s.at[side, i], one_r.at[side, i], peer)

        def chunk_step(k, carry):
            sending = jnp.logical_or(k == 0, jnp.logical_and(lax.rem(k, 2) == 1, k < n_ctx - 1))
            keeping = jnp.logical_not(sending)
            place_k = jnp.where(sending, (k + 1) // 2, (k + k // (n_ctx - 1)) // 2 - 1)
            at_y = 1 - y + lax.rem(place_k, 2) * (2 * y - 1)
            at_x = 1 - x + place_k // 2 * (2 * x - 1)
            index = 2 * at_y + at_x

            @pl.when(keeping)
            def _():
                core_copy(index).wait_recv()

            chunk = 2 * index + jnp.where(sending, 1 - core, core)
            for c in range(3):
                value = jnp.dot(low_t[chunk], turned[c], preferred_element_type=f32)

                @pl.when(sending)
                def _():
                    q_send[index, c] = value.astype(bf16)

                @pl.when(keeping)
                def _():
                    both[index, c] = (value + q_recv[index, c].astype(f32)).astype(bf16)

            @pl.when(sending)
            def _():
                core_copy(index).start()

            @pl.when(jnp.logical_and(keeping, place_k < 2))
            def _():
                one_copy(0, at_y).start()

            @pl.when(jnp.logical_and(keeping, lax.rem(place_k, 2) == 0))
            def _():
                one_copy(1, at_x).start()

            return carry

        lax.fori_loop(0, n_ctx // 2, chunk_step, 0)
        for step in range(1, n_tp - 2):
            out_next(step)
        ring_next(0)
        lax.fori_loop(n_ctx // 2, n_ctx, chunk_step, 0)
        back_rows(n_tp - 1)
        ones = jnp.ones((8, rows), bf16)
        for c in range(3):
            value = jnp.dot(ones, turned[c], preferred_element_type=f32)
            for t in range(columns // 128):
                row = c * columns // 128 + t
                small[row : row + 1] = value[0:1, t * 128 : (t + 1) * 128]
        for t in range(norm_rows):
            for which in range(2):
                row = first_rows + 2 * which * norm_rows + t
                small[row : row + 1] = sums[which : which + 1, t * 128 : (t + 1) * 128]
        for which in range(2):
            row = first_rows + (2 * which + 1) * norm_rows
            small[row : row + norm_rows] = small_two[which]
        small_ctx[ctx] = small[...]
        for step in range(1, n_ctx):
            small_copy(step).start()
        for i in range(2):
            one_copy(0, i).wait_recv()
            spot = 2 * i + x
            both[spot, :, top] = (
                both[spot, :, top].astype(f32) + first_a[i].astype(f32)
            ).astype(bf16)
            one_copy(1, i).wait_recv()
            spot = 2 * y + i
            both[spot, :, bottom] = (
                both[spot, :, bottom].astype(f32) + first_b[i].astype(f32)
            ).astype(bf16)

        def two_copy(side):
            if side == 0:
                source, peer = both.at[2 * (1 - y) + x, :, top], on_y
            else:
                source, peer = both.at[2 * y + 1 - x, :, bottom], on_x
            return remote(source, second.at[side], two_s.at[side], two_r.at[side], peer)

        for side in range(2):
            two_copy(side).start()
        out_next(n_tp - 2)
        gather_start(0)
        ring_next(1)
        for side, span in enumerate((top, bottom)):
            two_copy(side).wait_recv()
            qkv_all[ctx, :, span] = (
                both[here, :, span].astype(f32) + second[side].astype(f32)
            ).astype(bf16)
            gather_start(1 + side)
        for step in range(1, n_ctx):
            small_copy(step).wait_recv()
        value = sum(small_ctx[i] for i in range(n_ctx))
        small_sum[:first_rows] = value[:first_rows]
        small_tp[tp] = value[first_rows:]
        for step in range(1, n_tp):
            norm_copy(step).start()
        for p in range(3):
            gather_one(p)
        for step in range(2, n_tp - 1):
            ring_next(step)
        for p in range(3):
            gather_two(p)
        for step in range(1, n_tp):
            norm_copy(step).wait_recv()
        small_sum[first_rows:] = sum(small_tp[i] for i in range(n_tp))
        for p in range(3):
            gather_end(p)
        for step in range(n_tp - 1):
            out_ring(step).wait_send()
        for step in range(n_tp):
            lax.fori_loop(
                1, n_ctx, lambda at, c, step=step: (exchange(step, at).wait_send(), c)[1], 0
            )
        for step in range(1, n_ctx):
            small_copy(step).wait_send()
        for step in range(1, n_tp):
            norm_copy(step).wait_send()
        for step in range(n_tp - 1):
            for piece in range(2):
                ring(step, piece).wait_send()
        for i in range(n_ctx // 2):
            core_copy(i).wait_send()
        for side in range(2):
            two_copy(side).wait_send()
            for i in range(2):
                one_copy(side, i).wait_send()

    vmem, anywhere = pl.BlockSpec(memory_space=pltpu.VMEM), pl.BlockSpec(memory_space=pl.ANY)
    dma = pltpu.SemaphoreType.DMA
    pair = n_ctx // 2
    return pl.pallas_call(
        kernel,
        out_shape=(
            jax.ShapeDtypeStruct((own, width), bf16),
            jax.ShapeDtypeStruct((n_ctx, part, width), bf16),
            jax.ShapeDtypeStruct((n_ctx, 3, share, columns), bf16),
            jax.ShapeDtypeStruct(small_shape, f32),
        ),
        in_specs=[anywhere, anywhere, vmem, vmem, vmem, anywhere, vmem, anywhere, vmem, vmem],
        out_specs=(vmem,) * 4,
        scratch_shapes=[
            pltpu.VMEM(term.shape, bf16),
            pltpu.VMEM((rows, share), bf16),
            pltpu.VMEM((n_ctx, share, rows), bf16),
            pltpu.VMEM((3, width, columns), bf16),
            pltpu.VMEM((own, width), bf16),
            pltpu.VMEM((3, n_ctx, HEAD, rows), bf16),
            pltpu.VMEM((3, rows, columns), bf16),
            pltpu.VMEM((own, width), f32),
            pltpu.VMEM((8, width), f32),
            pltpu.VMEM(small_shape, f32),
            dma((3,)), dma,
            dma((n_tp, n_ctx)), dma((n_tp, n_ctx)),
            pltpu.VMEM((n_tp - 1, part, width), bf16),
            dma((n_tp - 1,)), dma((n_tp - 1,)),
            pltpu.VMEM((n_ctx,) + small_shape, f32),
            pltpu.VMEM((n_tp, 4 * norm_rows, 128), f32),
            pltpu.VMEM((n_tp - 1, 2, own, half_width), bf16),
            pltpu.VMEM((pair, 3, share, columns), bf16),
            pltpu.VMEM((pair, 3, share, columns), bf16),
            pltpu.VMEM((pair, 3, share, columns), bf16),
            pltpu.VMEM((2, 3, half_rows, columns), bf16),
            pltpu.VMEM((2, 3, half_rows, columns), bf16),
            pltpu.VMEM((2, 3, half_rows, columns), bf16),
            dma((n_ctx,)), dma((n_ctx,)),
            dma((n_tp,)), dma((n_tp,)),
            dma((n_tp - 1, 2)), dma((n_tp - 1, 2)),
            dma((pair,)), dma((pair,)),
            dma((2, 2)), dma((2, 2)),
            dma((2,)), dma((2,)),
            dma((3, 7)), dma((3, 7)),
        ],
        compiler_params=pltpu.CompilerParams(
            collective_id=3, has_side_effects=True, vmem_limit_bytes=62 * 2**20
        ),
        cost_estimate=pl.CostEstimate(
            flops=2 * rows * width * cols, bytes_accessed=50 * 2**20, transcendentals=0
        ),
        name="final_sums",
    )(
        term, xs, means, inverses, gain, low, grads, w_qkv.transpose(1, 0, 2), out, small_two
    )


def norm_stats(rows):
    mean = jnp.mean(rows, axis=1, keepdims=True)
    center = rows - mean
    inverse = lax.rsqrt(jnp.mean(center * center, axis=1, keepdims=True) + epsilon)
    return mean, inverse


def norm_backward(grad_out, normed, inverse, gain):
    scaled = grad_out * gain
    grad_rows = inverse * (
        scaled
        - jnp.mean(scaled, axis=1, keepdims=True)
        - normed * jnp.mean(scaled * normed, axis=1, keepdims=True)
    )
    return (grad_rows, jnp.sum(grad_out * normed, axis=0), jnp.sum(grad_out, axis=0))


def rotate(tensor, places, direction):
    half = ROT // 2
    frequency = 10000.0 ** (-2.0 * jnp.arange(half, dtype=f32) / ROT)
    angles = frequency[:, None] * places.astype(f32)[None, :]
    cosine, sines = jnp.cos(angles), direction * jnp.sin(angles)
    first, second = tensor[..., :half, :], tensor[..., half:ROT, :]
    return jnp.concatenate(
        [
            first * cosine - second * sines,
            second * cosine + first * sines,
            tensor[..., ROT:, :],
        ],
        axis=-2,
    )


def after(value, *others):
    return lax.optimization_barrier((value, *others))[0]


def direct_gather(value, count):
    n_tp = lax.axis_size("tp")
    return [value] + [
        lax.ppermute(value, "tp", [(i, (i + s) % n_tp) for i in range(n_tp)])
        for s in range(1, count)
    ]


def in_tp_order(arrays):
    count = len(arrays)
    shape = arrays[0].shape

    def kernel(tp, *refs):
        sources, out = refs[:count], refs[count]
        for s in range(count):
            out[lax.rem(tp[0] - s + count, count)] = sources[s][...]

    vmem = pl.BlockSpec(memory_space=pltpu.VMEM)
    return pl.pallas_call(
        kernel,
        out_shape=jax.ShapeDtypeStruct((count,) + shape, arrays[0].dtype),
        in_specs=[pl.BlockSpec(memory_space=pltpu.SMEM)] + [vmem] * count,
        out_specs=vmem,
        compiler_params=pltpu.CompilerParams(vmem_limit_bytes=60 * 2**20),
        cost_estimate=pl.CostEstimate(
            flops=0, bytes_accessed=4 * count * math.prod(shape), transcendentals=0
        ),
        name="in_tp_order",
    )(lax.axis_index("tp")[None], *arrays)


def exchange_sum(terms, axis):
    parts = lax.all_to_all(terms, axis, split_axis=0, concat_axis=0, tiled=True)
    return sum(part.astype(f32) for part in parts)


def scatter(partial, axis):
    return lax.psum_scatter(partial, axis, scatter_dimension=0, tiled=True)


def swap(value, axis, bit):
    size = lax.axis_size(axis)
    return lax.ppermute(value, axis, [(i, i ^ (1 << bit)) for i in range(size)])


def pair_sum(partial):
    size, rest = partial.shape[0], partial.shape[1:]
    side = lax.axis_index("ctx") % 2
    pairs = partial.reshape((size // 2, 2) + rest)
    kept = lax.dynamic_index_in_dim(pairs, side, 1, keepdims=False)
    sent = lax.dynamic_index_in_dim(pairs, 1 - side, 1, keepdims=False)
    return (kept.astype(f32) + swap(sent, "ctx", 0).astype(f32)).astype(bf16)


def spread_start(both, *early):
    pairs = both.shape[0]
    mine = lax.axis_index("ctx") // 2
    parts = [lax.dynamic_index_in_dim(both, mine, 0, keepdims=False)]
    for distance in range(1, pairs):
        sent = lax.dynamic_index_in_dim(both, mine ^ distance, 0, keepdims=False)
        perm = [(i, i ^ (2 * distance)) for i in range(2 * pairs)]
        parts.append(lax.ppermute(after(sent, *early) if early else sent, "ctx", perm))
    return parts


def spread_end(parts, *late):
    if late:
        parts = lax.optimization_barrier((*parts, *late))[: len(parts)]
    return sum(part.astype(f32) for part in parts).astype(bf16)


def by_ctx(partial):
    rows, cols = partial.shape
    n_ctx = lax.axis_size("ctx")
    return partial.reshape(n_ctx, rows // n_ctx, cols)


def gather(rows, axis):
    return lax.all_gather(rows, axis, axis=0, tiled=True)


def widen(chunks, down, out):
    devices, parts, rows, cols = chunks.shape

    def kernel(chunks, down, out, chunks_wide, down_wide, out_wide):
        chunks_wide[...] = chunks[0].astype(f32)
        down_wide[...] = down[0].astype(f32)
        out_wide[...] = out[0].astype(f32)

    others = (down.shape[1:], out.shape[1:])
    return pl.pallas_call(
        kernel,
        grid=(devices,),
        out_shape=[jax.ShapeDtypeStruct((parts, devices * rows, cols), f32)]
        + [jax.ShapeDtypeStruct((devices * shape[0], shape[1]), f32) for shape in others],
        in_specs=[pl.BlockSpec((1, parts, rows, cols), lambda i: (i, 0, 0, 0))]
        + [pl.BlockSpec((1,) + shape, lambda i: (i, 0, 0)) for shape in others],
        out_specs=[pl.BlockSpec((parts, rows, cols), lambda i: (0, i, 0))]
        + [pl.BlockSpec(shape, lambda i: (i, 0)) for shape in others],
        cost_estimate=pl.CostEstimate(
            flops=0, bytes_accessed=6 * math.prod(chunks.shape), transcendentals=0
        ),
        compiler_params=pltpu.CompilerParams(vmem_limit_bytes=60 * 2**20),
        name="widen",
    )(chunks, down, out)


def interleave(gate, up):
    rows, cols = gate.shape
    tile = 128

    def kernel(gate, up, out):
        out[:, 0, :] = gate[...].astype(f32)
        out[:, 1, :] = up[...].astype(f32)

    return pl.pallas_call(
        kernel,
        grid=(rows // tile,),
        out_shape=jax.ShapeDtypeStruct((rows, 2, cols), f32),
        in_specs=[pl.BlockSpec((tile, cols), lambda i: (i, 0))] * 2,
        out_specs=pl.BlockSpec((tile, 2, cols), lambda i: (i, 0, 0)),
        compiler_params=pltpu.CompilerParams(vmem_limit_bytes=60 * 2**20),
        cost_estimate=pl.CostEstimate(flops=1, bytes_accessed=1, transcendentals=0),
        name="interleave",
    )(gate, up)


def shards(
    layer_in,
    norm_gain,
    norm_bias,
    w_qkv,
    b_qkv,
    w_out,
    w_gate_up,
    w_down,
    cotangent,
    block_table,
    seq_ids,
):
    n_ctx, n_tp = lax.axis_size("ctx"), lax.axis_size("tp")
    ctx, tp = lax.axis_index("ctx"), lax.axis_index("tp")
    own, width = layer_in.shape
    rows = own * n_tp
    cols = w_qkv.shape[2]
    heads = cols // HEAD
    table = block_table.reshape(-1)
    blocks = table.shape[0]
    by_head = heads == n_ctx == 8 and BLK % own == 0
    part = cols // n_ctx

    ids = jnp.arange(blocks, dtype=jnp.int32)
    located = jnp.sum(jnp.where(table[None, :] == ids[:, None], ids[None, :], 0), axis=1)
    same = seq_ids[:, None] == seq_ids[None, :]
    first = jnp.min(jnp.where(same, ids[None, :], blocks), axis=1)
    last = jnp.max(jnp.where(same, ids[None, :], -1), axis=1)
    order = jnp.concatenate([located, first, last, tp[None]]).astype(jnp.int32)
    frequency = 10000.0 ** (-2.0 * jnp.arange(ROT // 2, dtype=f32) / ROT)
    positions = table[:, None] * BLK + jnp.arange(BLK, dtype=jnp.int32)[None, :]
    angles = frequency[None, :, None] * positions.astype(f32)[:, None, :]
    angles = jnp.stack([jnp.cos(angles), jnp.sin(angles)], axis=1)

    hidden_units = w_gate_up.shape[2]
    w_part = lax.dynamic_slice_in_dim(w_out, ctx * part, part, 0)
    if by_head:
        layer_in = after(layer_in, angles, order)
        xs, lows, mean_one, inverse_one, w_part, packed = project_exchange(
            layer_in, w_part, norm_gain[0:1], norm_bias[0:1], w_qkv, b_qkv
        )
        first_low = lows.reshape(rows, width)
        w_out_all = lax.all_gather(w_part, "ctx", axis=1, tiled=True)
        cot = direct_gather(after(cotangent, packed), n_tp - 1)
        out, logsum = attention_forward(order, angles, packed)
        middle, lows, mean_two, inverse_two, attended_all = output_project(
            out, xs, w_out_all, norm_gain[1:2], norm_bias[1:2]
        )
        cot = list(lax.optimization_barrier((*cot, middle))[: n_tp - 1])
        late = after(cotangent, middle)
        cot.append(lax.ppermute(late, "tp", [(i, (i + n_tp - 1) % n_tp) for i in range(n_tp)]))
        cot = in_tp_order(cot).reshape(rows, width)
        middle = middle.reshape(rows, width)
        mean_two, inverse_two = [t.reshape(rows, 128)[:, :1] for t in (mean_two, inverse_two)]
        normed_two = (middle - mean_two) * inverse_two
        second_low = lows.reshape(rows, width)
        attended_all = attended_all.reshape(n_tp * cols, rows)
    else:
        x = gather(layer_in, "tp").astype(f32)
        mean_one, inverse_one = norm_stats(x)
        first_low = ((x - mean_one) * inverse_one * norm_gain[0] + norm_bias[0]).astype(bf16)
        projected = (
            jnp.einsum("dcf,rd->cfr", w_qkv, first_low, preferred_element_type=f32)
            + b_qkv[:, :, None]
        ).reshape(3, heads, HEAD, rows)
        w_part = gather(w_part, "tp").reshape(n_tp, part, width)
        w_out_all = lax.all_gather(w_part, "ctx", axis=1, tiled=True)
        cot = gather(cotangent, "tp")
        places, _ = row_places(ctx * rows, rows, table, seq_ids)
        qkv = jnp.concatenate([rotate(projected[0:2], places, 1.0), projected[2:3]], axis=0)
        queries, keys, values = [t.astype(bf16).transpose(2, 0, 1) for t in qkv]
        visit, offsets = gathered_setup(
            rows, table, seq_ids, keys.reshape(rows, cols), values.reshape(rows, cols)
        )
        out, logsum = gathered_forward(queries, visit, offsets)
        attended_all = gather(out.astype(bf16).reshape(rows, cols).T, "tp")
        middle = x + jnp.einsum(
            "fr,fd->rd",
            attended_all,
            w_out_all.reshape(n_tp * cols, width),
            preferred_element_type=f32,
        )
        mean_two, inverse_two = norm_stats(middle)
        normed_two = (middle - mean_two) * inverse_two
        second_low = (normed_two * norm_gain[1] + norm_bias[1]).astype(bf16)

    grad_hidden = lax.dot_general(cot, w_down, (((1,), (1,)), ((), ())), preferred_element_type=f32)
    gate_up = jnp.einsum("rd,dcf->rcf", second_low, w_gate_up, preferred_element_type=f32)
    gate, up = gate_up[:, 0], gate_up[:, 1]
    sigmoid = jax.nn.sigmoid(gate)
    activated = gate * sigmoid
    hidden = (activated * up).astype(bf16)
    grad_gate = grad_hidden * up * sigmoid * (1.0 + gate * (1.0 - sigmoid))
    grad_up = grad_hidden * activated
    grad_gu = jnp.stack([grad_gate, grad_up], axis=1).astype(bf16)
    grad_second = jnp.einsum("rcf,dcf->rd", grad_gu, w_gate_up, preferred_element_type=f32)

    middle_norm, gain_two, bias_two = norm_backward(
        grad_second, normed_two, inverse_two, norm_gain[1]
    )
    is_own = (jnp.arange(rows, dtype=jnp.int32) // own == tp)[:, None]
    middle_term = (middle_norm + jnp.where(is_own, cot.astype(f32), 0.0)).astype(bf16)
    if by_head:
        grad_att, gate_grad, up_grad, out_grad, out_sent, down_grad, down_sent, *down = middle_sums(
            middle_term,
            w_out_all,
            second_low,
            grad_gate.astype(bf16),
            grad_up.astype(bf16),
            hidden,
            cot,
            attended_all.reshape(n_tp, cols, rows),
            w_down,
        )
        down = [down[0], down[-1]] + [
            lax.ppermute(down[s], "tp", [(i, (i - s) % n_tp) for i in range(n_tp)])
            for s in range(1, n_tp - 1)
        ]
    else:
        grad_att = lax.dot_general(
            w_out_all.reshape(n_tp * cols, width),
            middle_term,
            (((1,), (1,)), ((), ())),
            preferred_element_type=f32,
        ).astype(bf16)
        grad_att = scatter(grad_att, "tp")
        down = jnp.dot(hidden, w_down, preferred_element_type=f32).astype(bf16)
        down = [scatter(down, "tp")]

        def weight_grad(left, right):
            return lax.dot_general(
                left, right, (((0,), (0,)), ((), ())), preferred_element_type=f32
            ).astype(bf16)

        gu_grad = jnp.concatenate(
            [pair_sum(by_ctx(weight_grad(second_low, t.astype(bf16)))) for t in (grad_gate, grad_up)],
            axis=1,
        )
        gu_grad = spread_end(spread_start(gu_grad))
        out_grad = jnp.dot(attended_all, middle_term, preferred_element_type=f32).astype(bf16)
        out_grad = out_grad.reshape(n_tp, n_ctx, part, width).transpose(1, 0, 2, 3)
        other_grad = jnp.concatenate(
            [
                pair_sum(out_grad.reshape(n_ctx, n_tp * part, width)),
                pair_sum(by_ctx(weight_grad(hidden, cot))),
            ],
            axis=1,
        )
        other_grad = spread_end(spread_start(other_grad))
        gate_grad, up_grad = jnp.split(gu_grad, 2, axis=0)
        out_grad, down_grad = jnp.split(other_grad, [n_tp * part], axis=0)
    gate_grad, up_grad = gather(gate_grad, "ctx"), gather(up_grad, "ctx")
    grad_gate_up = interleave(gate_grad, up_grad)

    if by_head:
        grads = attention_backward(order, angles, packed, grad_att, out, logsum)
        out_sent = lax.ppermute(out_sent, "ctx", [(i, i ^ 4) for i in range(n_ctx)])
        down_sent = lax.ppermute(down_sent, "ctx", [(i, i ^ 2) for i in range(n_ctx)])
        grads, out_sent, down_sent, *down = lax.optimization_barrier(
            (grads, out_sent, down_sent, *down)
        )
        out_grad = (out_grad.astype(f32) + out_sent.astype(f32)).astype(bf16)
        down_grad = (down_grad.astype(f32) + down_sent.astype(f32)).astype(bf16)
        down_grad = gather(down_grad, "ctx")
        grad_input, out_grad, grad_qkv, small = final_sums(
            middle_term.reshape(n_tp, own, width),
            xs,
            mean_one,
            inverse_one,
            norm_gain[0:1],
            first_low,
            grads,
            w_qkv,
            out_grad,
            jnp.stack([gain_two, bias_two]).reshape(2, -1, 128),
        )
        grad_input, *down = lax.optimization_barrier((grad_input, *down))
        grad_qkv, down_grad, out_grad = widen(
            grad_qkv, down_grad.reshape(n_ctx, -1, width), out_grad
        )
        grad_qkv = grad_qkv.transpose(1, 0, 2)
        bias_qkv, norms = small[: 3 * cols // 128], small[3 * cols // 128 :]
    else:
        grads = gathered_backward(
            queries, visit, offsets, grad_att.T.reshape(rows, heads, HEAD), out, logsum
        )
        grads = jnp.stack([t.transpose(1, 2, 0) for t in grads])
        grads = jnp.concatenate([rotate(grads[0:2], places, -1.0), grads[2:3]], axis=0)
        grad_projected = grads.reshape(3 * cols, rows).astype(bf16)
        grad_first = jnp.einsum(
            "cfr,dcf->rd",
            grad_projected.reshape(3, cols, rows),
            w_qkv,
            preferred_element_type=f32,
        )
        input_norm, gain_one, bias_one = norm_backward(
            grad_first, (x - mean_one) * inverse_one, inverse_one, norm_gain[0]
        )
        grad_input = middle_term.astype(f32) + input_norm
        grad_input = exchange_sum(grad_input.astype(bf16).reshape(n_tp, own, width), "tp")
        grad_input = grad_input.astype(bf16)
        grad_qkv = lax.dot_general(
            first_low, grad_projected, (((0,), (1,)), ((), ())), preferred_element_type=f32
        ).astype(bf16)
        grad_qkv = spread_end(spread_start(pair_sum(by_ctx(grad_qkv))))
        out_grad = exchange_sum(out_grad.reshape(n_tp, part, width), "tp").astype(bf16)
        out_grad, grad_qkv = [gather(t, "ctx").astype(f32) for t in (out_grad, grad_qkv)]
        grad_qkv = grad_qkv.reshape(width, 3, cols)
        down_grad = gather(down_grad, "ctx").astype(f32)
        bias_qkv = lax.psum(jnp.sum(grad_projected.astype(f32), axis=1), "ctx")
        norms = jnp.stack([gain_one, gain_two, bias_one, bias_two])
        norms = lax.psum(norms, ("ctx", "tp"))
    own_middle = lax.dynamic_slice_in_dim(middle, tp * own, own, 0)
    layer_out = (own_middle + sum(t.astype(f32) for t in down)).astype(bf16)
    norms = norms.reshape(2, 2, width)
    return (
        layer_out,
        grad_input,
        norms[0],
        norms[1],
        grad_qkv,
        bias_qkv.reshape(3, cols),
        out_grad,
        grad_gate_up,
        down_grad,
    )


def solution(mesh):
    placed = (
        P(("ctx", "tp"), None),
        P(),
        P(),
        P(None, None, "tp"),
        P(None, "tp"),
        P("tp", None),
        P(None, None, "tp"),
        P("tp", None),
        P(("ctx", "tp"), None),
        P(),
        P(),
    )
    return jax.shard_map(
        shards,
        mesh=mesh,
        in_specs=placed,
        out_specs=(
            P(("ctx", "tp"), None),
            P(("ctx", "tp"), None),
            P(),
            P(),
            P(None, None, "tp"),
            P(None, "tp"),
            P("tp", None),
            P(None, None, "tp"),
            P("tp", None),
        ),
        check_vma=False,
    )
```

```python
import math

import jax
import jax.numpy as jnp
from jax import lax
from jax.experimental import pallas as pl
from jax.experimental.pallas import tpu as pltpu
from jax.sharding import PartitionSpec as P

HEAD = 64
ROT = 16
BLK = 512
EXTRA = 16

epsilon = 1e-05
neg_large = -1e30
bf16 = jnp.bfloat16
f32 = jnp.float32


def dot(left, right, left_dim, right_dim):
    return lax.dot_general(
        left, right, (((left_dim,), (right_dim,)), ((), ())), preferred_element_type=f32
    )


def causal_keep():
    return lax.broadcasted_iota(jnp.int32, (BLK, BLK), 0) <= lax.broadcasted_iota(
        jnp.int32, (BLK, BLK), 1
    )


def turn(tile):
    return tile.astype(f32).T.astype(bf16)


def scan_chunks(devices, chunks, width, visit):
    per_block = BLK // width

    def source(device, carry):
        for chunk in range(chunks):
            place = device * (chunks // per_block) + chunk // per_block
            visit(chunk, device, place, slice((chunk % per_block) * width, (chunk % per_block + 1) * width))
        return carry

    lax.fori_loop(0, devices, source, 0)


def turn_dims(tile, cosine, sine):
    half = ROT // 2
    first, second = tile[0:half], tile[half:ROT]
    return jnp.concatenate(
        [first * cosine - second * sine, second * cosine + first * sine, tile[ROT:]], axis=0
    )


def attention_forward(order, angles, packed):
    count, devices, _, _, width = packed.shape
    blocks = devices * count * width // BLK

    def kernel(order, angles, packed, out, logsum, queries, keys, values):
        per_device = count * width // BLK
        row = lax.broadcasted_iota(jnp.int32, (EXTRA, BLK), 0)
        ones = jnp.where(row == 0, 1.0, 0.0).astype(bf16)

        def visit(chunk, device, place, lanes):
            part = packed.at[chunk]
            cosine, sine = angles[place, 0, :, lanes], angles[place, 1, :, lanes]
            query = turn_dims(part[device, 0].astype(f32), cosine, sine).astype(bf16)
            queries[place, :, lanes] = query * jnp.asarray(HEAD**-0.5, bf16)
            key = turn_dims(part[device, 1].astype(f32), cosine, sine).astype(bf16)
            keys[place, lanes, :] = turn(key)
            values[place, 0:HEAD, lanes] = part[device, 2]

        scan_chunks(devices, count, width, visit)

        def prepare(place, carry):
            values[place, HEAD : HEAD + EXTRA, :] = ones
            return carry

        lax.fori_loop(0, blocks, prepare, 0)
        keep = causal_keep()

        def query_block(i, carry):
            place = order[i]
            query = queries[place]

            def step(keys_at, state, masked):
                maxima, summed = state
                places = [order[j] for j in keys_at]
                scores = [dot(keys[other], query, 1, 0) for other in places]
                if masked:
                    scores = [jnp.where(keep, tile, neg_large) for tile in scores]
                new_maxima = maxima
                for tile in scores:
                    new_maxima = jnp.maximum(new_maxima, jnp.max(tile, axis=0, keepdims=True))
                summed = summed * jnp.exp(maxima - new_maxima)
                for other, tile in zip(places, scores):
                    weights = jnp.exp(tile - new_maxima).astype(bf16)
                    summed = summed + dot(values[other], weights, 1, 0)
                return new_maxima, summed

            state = (jnp.full((1, BLK), neg_large, f32), jnp.zeros((HEAD + EXTRA, BLK), f32))
            first = order[blocks + i]
            triples = (i - first) // 3
            state = lax.fori_loop(
                0, triples, lambda t, s: step([first + 3 * t + u for u in range(3)], s, False), state
            )
            state = lax.fori_loop(
                first + 3 * triples, i, lambda j, s: step([j], s, False), state
            )
            maxima, summed = step([i], state, True)
            totals = summed[HEAD : HEAD + 1]
            result = (summed[0:HEAD] / totals).astype(bf16)
            logsum[place] = maxima + jnp.log(totals)
            lane = pl.multiple_of(lax.rem(place, per_device) * BLK, BLK)
            out[place // per_device, :, pl.ds(lane, BLK)] = result
            return carry

        lax.fori_loop(0, blocks, query_block, 0)

    vmem = pl.BlockSpec(memory_space=pltpu.VMEM)
    return pl.pallas_call(
        kernel,
        out_shape=(
            jax.ShapeDtypeStruct((devices, HEAD, count * width), bf16),
            jax.ShapeDtypeStruct((blocks, 1, BLK), f32),
        ),
        in_specs=[pl.BlockSpec(memory_space=pltpu.SMEM), vmem, vmem],
        out_specs=(vmem, vmem),
        scratch_shapes=[
            pltpu.VMEM((blocks, HEAD, BLK), bf16),
            pltpu.VMEM((blocks, BLK, HEAD), bf16),
            pltpu.VMEM((blocks, HEAD + EXTRA, BLK), bf16),
        ],
        compiler_params=pltpu.CompilerParams(vmem_limit_bytes=60 * 2**20),
        cost_estimate=pl.CostEstimate(
            flops=85 * 2 * 2 * BLK * BLK * 256, bytes_accessed=5 * 2**20, transcendentals=0
        ),
        name="attention_forward",
    )(order, angles, packed)


def attention_backward(order, angles, packed, grad_out, out, logsum):
    count, devices, _, _, width = packed.shape
    blocks = devices * count * width // BLK
    wide = HEAD + EXTRA

    def kernel(
        order, angles, packed, grad_out, out, logsum,
        grads, query_x, grad_x, key_x, key_rows, value_x, grad_q,
    ):
        row = lax.broadcasted_iota(jnp.int32, (EXTRA, width), 0)
        lane_ids = lax.broadcasted_iota(jnp.int32, (BLK, EXTRA), 1)
        ones = jnp.where(lane_ids < 3, 1.0, 0.0).astype(bf16)

        def three_rows(value):
            high = value.astype(bf16).astype(f32)
            rest = value - high
            middle = rest.astype(bf16).astype(f32)
            low = rest - middle
            return jnp.where(
                row == 0, high, jnp.where(row == 1, middle, jnp.where(row == 2, low, 0.0))
            ).astype(bf16)

        def visit(chunk, device, place, lanes):
            part = packed.at[chunk]
            cosine, sine = angles[place, 0, :, lanes], angles[place, 1, :, lanes]
            query = turn_dims(part[device, 0].astype(f32), cosine, sine).astype(bf16)
            query_x[place, 0:HEAD, lanes] = query * jnp.asarray(HEAD**-0.5, bf16)
            query_x[place, HEAD:wide, lanes] = three_rows(-logsum[place, :, lanes])
            key = turn_dims(part[device, 1].astype(f32), cosine, sine).astype(bf16)
            key_rows[place, :, lanes] = key
            key_x[place, lanes, 0:HEAD] = turn(key)
            value_x[place, lanes, 0:HEAD] = turn(part[device, 2])
            own = slice(chunk * width, (chunk + 1) * width)
            grad = grad_out[device, :, own]
            delta = jnp.sum(
                grad.astype(f32) * out[device, :, own].astype(f32), axis=0, keepdims=True
            )
            grad_x[place, 0:HEAD, lanes] = grad
            grad_x[place, HEAD:wide, lanes] = three_rows(-delta)

        scan_chunks(devices, count, width, visit)

        def prepare(place, carry):
            key_x[place, :, HEAD:wide] = ones
            value_x[place, :, HEAD:wide] = ones
            grad_q[place] = jnp.zeros((HEAD, BLK), f32)
            return carry

        lax.fori_loop(0, blocks, prepare, 0)
        keep = causal_keep()
        per_device = count * width // BLK

        def store(part, place, tile):
            lane = pl.multiple_of(lax.rem(place, per_device) * BLK, BLK)
            grads[place // per_device, part, :, pl.ds(lane, BLK)] = tile

        def key_block(j, carry):
            place = order[j]
            key, value = key_x[place], value_x[place]
            key_tile = key_rows[place]

            def step(queries_at, state, masked):
                grad_k, grad_v = state
                places = [order[i] for i in queries_at]
                scores = [dot(key, query_x[other], 1, 0) for other in places]
                grad_probs = [dot(value, grad_x[other], 1, 0) for other in places]
                probs = [jnp.exp(tile) for tile in scores]
                if masked:
                    probs = [jnp.where(keep, tile, 0.0) for tile in probs]
                grad_raws = [(p * g).astype(bf16) for p, g in zip(probs, grad_probs)]
                for other, prob, grad_raw in zip(places, probs, grad_raws):
                    grad_v = grad_v + dot(grad_x[other, 0:HEAD, :], prob.astype(bf16), 1, 1)
                    grad_k = grad_k + dot(query_x[other, 0:HEAD, :], grad_raw, 1, 1)
                    grad_q[other] += dot(key_tile, grad_raw, 1, 0)
                return grad_k, grad_v

            zero = jnp.zeros((HEAD, BLK), f32)
            state = step([j], (zero, zero), True)
            end = order[2 * blocks + j]
            pairs = (end - j) // 2
            state = lax.fori_loop(
                0, pairs, lambda t, s: step([j + 1 + 2 * t, j + 2 + 2 * t], s, False), state
            )
            grad_k, grad_v = lax.fori_loop(
                j + 1 + 2 * pairs, end + 1, lambda i, s: step([i], s, False), state
            )
            cosine, sine = angles[place, 0], angles[place, 1]
            store(1, place, turn_dims(grad_k, cosine, -sine).astype(bf16))
            store(2, place, grad_v.astype(bf16))
            return carry

        lax.fori_loop(0, blocks, key_block, 0)

        def finish(place, carry):
            tile = turn_dims(grad_q[place] * HEAD**-0.5, angles[place, 0], -angles[place, 1])
            store(0, place, tile.astype(bf16))
            return carry

        lax.fori_loop(0, blocks, finish, 0)

    vmem = pl.BlockSpec(memory_space=pltpu.VMEM)
    return pl.pallas_call(
        kernel,
        out_shape=jax.ShapeDtypeStruct((devices, 3, HEAD, count * width), bf16),
        in_specs=[pl.BlockSpec(memory_space=pltpu.SMEM)] + [vmem] * 5,
        out_specs=vmem,
        scratch_shapes=[
            pltpu.VMEM((blocks, wide, BLK), bf16),
            pltpu.VMEM((blocks, wide, BLK), bf16),
            pltpu.VMEM((blocks, BLK, wide), bf16),
            pltpu.VMEM((blocks, HEAD, BLK), bf16),
            pltpu.VMEM((blocks, BLK, wide), bf16),
            pltpu.VMEM((blocks, HEAD, BLK), f32),
        ],
        compiler_params=pltpu.CompilerParams(vmem_limit_bytes=60 * 2**20),
        cost_estimate=pl.CostEstimate(flops=1, bytes_accessed=1, transcendentals=0),
        name="attention_backward",
    )(order, angles, packed, grad_out, out, logsum)


def row_places(first_row, length, table_flat, seq_ids):
    row_ids = first_row + jnp.arange(length, dtype=jnp.int32)
    block_ids = jnp.arange(table_flat.shape[0], dtype=jnp.int32)
    natural = jnp.sum(
        jnp.where((row_ids // BLK)[:, None] == block_ids[None, :], table_flat[None, :], 0), axis=1
    )
    sequence = jnp.sum(
        jnp.where(natural[:, None] == block_ids[None, :], seq_ids[None, :], 0), axis=1
    )
    return (natural * BLK + row_ids % BLK, sequence)


def gathered_setup(rows, table_flat, seq_ids, key_flat, value_flat):
    places, seq = row_places(lax.axis_index("ctx") * rows, rows, table_flat, seq_ids)
    pieces = (
        lax.all_gather(key_flat, "ctx", axis=0, tiled=True),
        lax.all_gather(value_flat, "ctx", axis=0, tiled=True),
    )
    stride = math.gcd(pieces[0].shape[0], 1024)
    offsets = jnp.arange(pieces[0].shape[0] // stride, dtype=jnp.int32) * stride

    def visit(offset):
        other_places, other_seq = row_places(offset, stride, table_flat, seq_ids)
        allowed = (seq[:, None] == other_seq[None, :]) & (other_places[None, :] <= places[:, None])
        blocks = [
            lax.dynamic_slice_in_dim(piece, offset, stride, 0).reshape(stride, -1, HEAD)
            for piece in pieces
        ]
        return allowed[:, None, :], blocks[0], blocks[1]

    return visit, offsets


def gathered_forward(queries, visit, offsets):
    rows, heads, _ = queries.shape

    def step(status, offset):
        allowed, keys, values = visit(offset)
        scores = jnp.einsum("qhe,khe->qhk", queries, keys, preferred_element_type=f32)
        scores = scores * HEAD**-0.5
        maxima, totals, summed = status
        new_maxima = jnp.maximum(maxima, jnp.max(jnp.where(allowed, scores, neg_large), axis=2))
        weights = jnp.where(allowed, jnp.exp(scores - new_maxima[..., None]), 0.0)
        factor = jnp.exp(maxima - new_maxima)
        totals = totals * factor + jnp.sum(weights, axis=2)
        summed = summed * factor[..., None] + jnp.einsum(
            "qhk,khe->qhe", weights.astype(bf16), values, preferred_element_type=f32
        )
        return ((new_maxima, totals, summed), None)

    initial = (
        jnp.full((rows, heads), neg_large, f32),
        jnp.zeros((rows, heads), f32),
        jnp.zeros((rows, heads, HEAD), f32),
    )
    (maxima, totals, summed), _ = lax.scan(step, initial, offsets)
    return summed / totals[..., None], maxima + jnp.log(totals)


def gathered_backward(queries, visit, offsets, grad_att, attended, logsum):
    rows, heads, _ = queries.shape
    delta = jnp.sum(grad_att.astype(f32) * attended, axis=2)

    def step(status, offset):
        allowed, keys, values = visit(offset)
        scores = jnp.einsum("qhe,khe->qhk", queries, keys, preferred_element_type=f32)
        prob = jnp.where(allowed, jnp.exp(scores * HEAD**-0.5 - logsum[..., None]), 0.0)
        grad_prob = jnp.einsum("qhe,khe->qhk", grad_att, values, preferred_element_type=f32)
        grad_raw = (prob * (grad_prob - delta[..., None]) * HEAD**-0.5).astype(bf16)
        grad_q = jnp.einsum("qhk,khe->qhe", grad_raw, keys, preferred_element_type=f32)
        grad_k = jnp.einsum("qhk,qhe->khe", grad_raw, queries, preferred_element_type=f32)
        grad_v = jnp.einsum("qhk,qhe->khe", prob.astype(bf16), grad_att, preferred_element_type=f32)
        return (
            (
                status[0] + grad_q,
                lax.dynamic_update_slice_in_dim(status[1], grad_k, offset, 0),
                lax.dynamic_update_slice_in_dim(status[2], grad_v, offset, 0),
            ),
            None,
        )

    total = rows * lax.axis_size("ctx")
    zero = jnp.zeros((total, heads, HEAD), f32)
    (grad_q, grad_k, grad_v), _ = lax.scan(
        step, (jnp.zeros((rows, heads, HEAD), f32), zero, zero), offsets
    )
    grad_k = lax.psum_scatter(grad_k, "ctx", scatter_dimension=0, tiled=True)
    grad_v = lax.psum_scatter(grad_v, "ctx", scatter_dimension=0, tiled=True)
    return grad_q, grad_k, grad_v


MESH = pl.DeviceIdType.MESH


def greet(n_ctx, n_tp):
    ctx, tp = lax.axis_index("ctx"), lax.axis_index("tp")
    barrier = pltpu.get_barrier_semaphore()

    def greet_ctx(step, carry):
        peer = lax.rem(ctx + step, n_ctx)
        pl.semaphore_signal(barrier, inc=1, device_id=(peer, tp), device_id_type=MESH)
        return carry

    lax.fori_loop(1, n_ctx, greet_ctx, 0)
    for peer in (lax.rem(tp + 1, n_tp), lax.rem(tp + n_tp - 1, n_tp)):
        pl.semaphore_signal(barrier, inc=1, device_id=(ctx, peer), device_id_type=MESH)
    pl.semaphore_wait(barrier, n_ctx + 1)


def rows_norm(source, stored, gain, shift, mean_out, inverse_out, tile):
    def step(i, carry):
        rows = pl.ds(pl.multiple_of(i * tile, tile), tile)
        x = source(rows)
        mean = jnp.mean(x, axis=1, keepdims=True)
        center = x - mean
        inverse = lax.rsqrt(jnp.mean(center * center, axis=1, keepdims=True) + epsilon)
        stored(rows, (center * inverse * gain + shift).astype(bf16))
        mean_out[rows, :] = jnp.broadcast_to(mean, (tile, 128))
        inverse_out[rows, :] = jnp.broadcast_to(inverse, (tile, 128))
        return carry

    return step


def project_exchange(layer_in, w_part, gain, shift, w_qkv, b_qkv):
    n_ctx, n_tp = lax.axis_size("ctx"), lax.axis_size("tp")
    own, width = layer_in.shape
    part = w_part.shape[0]
    cols = w_qkv.shape[2]

    def kernel(
        x_in, w_in, gain, shift, w_qkv_in, b_qkv,
        xs_out, lows_out, means, inverses, ws, packed,
        xs, lows, w_qkv, load_s, store_s, outgoing, ring_send, ring_recv, w_send, w_recv, send, recv,
    ):
        ctx, tp = lax.axis_index("ctx"), lax.axis_index("tp")
        right = lax.rem(tp + 1, n_tp)
        half = own // 2

        def block(slot):
            return lax.rem(tp - slot + n_tp, n_tp)

        def ring(step, piece):
            rows = pl.ds(piece * half, half)
            return pltpu.make_async_remote_copy(
                src_ref=x_in.at[rows] if step == 0 else xs.at[block(step), rows],
                dst_ref=xs.at[block(step), rows],
                send_sem=ring_send.at[step, piece],
                recv_sem=ring_recv.at[step, piece],
                device_id=(ctx, right),
                device_id_type=MESH,
            )

        def w_ring(step):
            return pltpu.make_async_remote_copy(
                src_ref=w_in if step == 0 else ws.at[block(step)],
                dst_ref=ws.at[block(step)],
                send_sem=w_send.at[step],
                recv_sem=w_recv.at[step],
                device_id=(ctx, right),
                device_id_type=MESH,
            )

        def exchange(slot, step):
            peer = lax.rem(ctx + step, n_ctx)
            return pltpu.make_async_remote_copy(
                src_ref=outgoing.at[slot, peer],
                dst_ref=packed.at[block(slot), ctx],
                send_sem=send.at[slot, step],
                recv_sem=recv.at[slot, step],
                device_id=(peer, tp),
                device_id_type=MESH,
            )

        load = pltpu.make_async_copy(w_qkv_in, w_qkv, load_s)
        load.start()

        def store(slot, which):
            here = block(slot)
            source, target = ((xs, xs_out), (lows, lows_out))[which]
            return pltpu.make_async_copy(source.at[here], target.at[here], store_s.at[slot, which])

        greet(n_ctx, n_tp)
        for piece in range(2):
            ring(0, piece).start()
        xs[tp] = x_in[...]
        ws[tp] = w_in[...]
        for slot in range(n_tp):
            if slot > 0:
                for piece in range(2):
                    ring(slot - 1, piece).wait_recv()
                    if slot < n_tp - 1:
                        ring(slot, piece).start()
            if slot == n_tp - 2:
                w_ring(0).start()
            if slot == n_tp - 1:
                w_ring(0).wait_recv()
                w_ring(1).start()

            here = block(slot)

            def stored(rows, value, here=here):
                lows[here, rows, :] = value

            step = rows_norm(
                lambda rows, here=here: xs[here, rows, :].astype(f32),
                stored, gain[...], shift[...], means.at[here], inverses.at[here], 32,
            )
            lax.fori_loop(0, own // 32, step, 0)
            store(slot, 0).start()
            store(slot, 1).start()
            if slot == 0:
                load.wait()

            def project(c, carry, slot=slot, here=here):
                value = jnp.dot(lows[here], w_qkv[c], preferred_element_type=f32) + b_qkv[c]
                outgoing[slot, :, c] = value.T.astype(bf16).reshape(n_ctx, HEAD, own)
                return carry

            lax.fori_loop(0, 3, project, 0)
            lax.fori_loop(
                1, n_ctx, lambda step, c, slot=slot: (exchange(slot, step).start(), c)[1], 0
            )
            packed[here, ctx] = outgoing[slot, ctx]
        for step in range(1, n_tp - 1):
            w_ring(step).wait_recv()
            if step < n_tp - 2:
                w_ring(step + 1).start()
        for slot in range(n_tp):
            lax.fori_loop(
                1, n_ctx, lambda step, c, slot=slot: (exchange(slot, step).wait(), c)[1], 0
            )
        for slot in range(n_tp):
            store(slot, 0).wait()
            store(slot, 1).wait()
        for step in range(n_tp - 1):
            w_ring(step).wait_send()
            for piece in range(2):
                ring(step, piece).wait_send()

    vmem, anywhere = pl.BlockSpec(memory_space=pltpu.VMEM), pl.BlockSpec(memory_space=pl.ANY)
    return pl.pallas_call(
        kernel,
        out_shape=(
            jax.ShapeDtypeStruct((n_tp, own, width), bf16),
            jax.ShapeDtypeStruct((n_tp, own, width), bf16),
            jax.ShapeDtypeStruct((n_tp, own, 128), f32),
            jax.ShapeDtypeStruct((n_tp, own, 128), f32),
            jax.ShapeDtypeStruct((n_tp, part, width), bf16),
            jax.ShapeDtypeStruct((n_tp, n_ctx, 3, HEAD, own), bf16),
        ),
        in_specs=[vmem] * 4 + [anywhere, vmem],
        out_specs=(anywhere,) * 2 + (vmem,) * 4,
        scratch_shapes=[
            pltpu.VMEM((n_tp, own, width), bf16),
            pltpu.VMEM((n_tp, own, width), bf16),
            pltpu.VMEM((3, width, cols), bf16),
            pltpu.SemaphoreType.DMA,
            pltpu.SemaphoreType.DMA((n_tp, 2)),
            pltpu.VMEM((n_tp, n_ctx, 3, HEAD, own), bf16),
            pltpu.SemaphoreType.DMA((n_tp - 1, 2)),
            pltpu.SemaphoreType.DMA((n_tp - 1, 2)),
            pltpu.SemaphoreType.DMA((n_tp - 1,)),
            pltpu.SemaphoreType.DMA((n_tp - 1,)),
            pltpu.SemaphoreType.DMA((n_tp, n_ctx)),
            pltpu.SemaphoreType.DMA((n_tp, n_ctx)),
        ],
        compiler_params=pltpu.CompilerParams(
            collective_id=1, has_side_effects=True, vmem_limit_bytes=60 * 2**20
        ),
        cost_estimate=pl.CostEstimate(
            flops=2 * n_tp * own * width * 3 * cols, bytes_accessed=20 * 2**20, transcendentals=0
        ),
        name="project_exchange",
    )(layer_in, w_part, gain, shift, w_qkv.transpose(1, 0, 2), b_qkv[:, None, :])


def output_project(out, xs, w_all, gain, shift):
    n_ctx, n_tp = lax.axis_size("ctx"), lax.axis_size("tp")
    own, width = xs.shape[1:]
    cols = w_all.shape[1]
    rows_all = n_tp * own

    def kernel(
        out, xs_in, w_in, gain, shift,
        middle_out, lows_out, means, inverses, raw,
        xs, w_all, middle, lows, load_s, store_s, ring_send, ring_recv, send, recv, own_sem,
    ):
        ctx, tp = lax.axis_index("ctx"), lax.axis_index("tp")
        right = lax.rem(tp + 1, n_tp)
        half = cols // 2

        def block(slot):
            return lax.rem(tp - slot + n_tp, n_tp)

        def ring(step, piece):
            rows = pl.ds(piece * half, half)
            return pltpu.make_async_remote_copy(
                src_ref=raw.at[block(step), rows],
                dst_ref=raw.at[block(step), rows],
                send_sem=ring_send.at[step, piece],
                recv_sem=ring_recv.at[step, piece],
                device_id=(ctx, right),
                device_id_type=MESH,
            )

        def exchange(step):
            peer = lax.rem(ctx + step, n_ctx)
            return pltpu.make_async_remote_copy(
                src_ref=out.at[peer],
                dst_ref=raw.at[tp, pl.ds(pl.multiple_of(ctx * HEAD, HEAD), HEAD)],
                send_sem=send.at[step],
                recv_sem=recv.at[step],
                device_id=(peer, tp),
                device_id_type=MESH,
            )

        loads = (
            pltpu.make_async_copy(xs_in, xs, load_s.at[0]),
            pltpu.make_async_copy(w_in, w_all, load_s.at[1]),
        )
        for load in loads:
            load.start()

        def store(place, which):
            source, target = ((middle, middle_out), (lows, lows_out))[which]
            return pltpu.make_async_copy(
                source.at[place], target.at[place], store_s.at[place, which]
            )

        greet(n_ctx, n_tp)
        lax.fori_loop(1, n_ctx, lambda step, c: (exchange(step).start(), c)[1], 0)
        keep = pltpu.make_async_copy(
            out.at[ctx], raw.at[tp, pl.ds(pl.multiple_of(ctx * HEAD, HEAD), HEAD)], own_sem
        )
        keep.start()
        keep.wait()
        lax.fori_loop(1, n_ctx, lambda step, c: (exchange(step).wait_recv(), c)[1], 0)
        for piece in range(2):
            ring(0, piece).start()
        for load in loads:
            load.wait()
        for slot in range(n_tp):
            if slot > 0:
                for piece in range(2):
                    ring(slot - 1, piece).wait_recv()
                    if slot < n_tp - 1:
                        ring(slot, piece).start()
            here = block(slot)

            def project(place, carry, slot=slot, here=here):
                lanes = pl.ds(pl.multiple_of(place * own, own), own)
                tile = raw[here, :, lanes].astype(f32).T.astype(bf16)
                value = jnp.dot(tile, w_all[here], preferred_element_type=f32)
                if slot == 0:
                    middle[place] = xs[place].astype(f32) + value
                else:
                    middle[place] += value
                return carry

            lax.fori_loop(0, n_tp, project, 0)
        for place in range(n_tp):
            store(place, 0).start()

            def stored(rows, value, place=place):
                lows[place, rows, :] = value

            step = rows_norm(
                lambda rows, place=place: middle[place, rows, :],
                stored, gain[...], shift[...], means.at[place], inverses.at[place], 32,
            )
            lax.fori_loop(0, own // 32, step, 0)
            store(place, 1).start()
        lax.fori_loop(1, n_ctx, lambda step, c: (exchange(step).wait_send(), c)[1], 0)
        for place in range(n_tp):
            store(place, 0).wait()
            store(place, 1).wait()
        for step in range(n_tp - 1):
            for piece in range(2):
                ring(step, piece).wait_send()

    vmem, anywhere = pl.BlockSpec(memory_space=pltpu.VMEM), pl.BlockSpec(memory_space=pl.ANY)
    return pl.pallas_call(
        kernel,
        out_shape=(
            jax.ShapeDtypeStruct((n_tp, own, width), f32),
            jax.ShapeDtypeStruct((n_tp, own, width), bf16),
            jax.ShapeDtypeStruct((n_tp, own, 128), f32),
            jax.ShapeDtypeStruct((n_tp, own, 128), f32),
            jax.ShapeDtypeStruct((n_tp, cols, rows_all), bf16),
        ),
        in_specs=[vmem, anywhere, anywhere, vmem, vmem],
        out_specs=(anywhere,) * 2 + (vmem,) * 3,
        scratch_shapes=[
            pltpu.VMEM((n_tp, own, width), bf16),
            pltpu.VMEM((n_tp, cols, width), bf16),
            pltpu.VMEM((n_tp, own, width), f32),
            pltpu.VMEM((n_tp, own, width), bf16),
            pltpu.SemaphoreType.DMA((2,)),
            pltpu.SemaphoreType.DMA((n_tp, 2)),
            pltpu.SemaphoreType.DMA((n_tp - 1, 2)),
            pltpu.SemaphoreType.DMA((n_tp - 1, 2)),
            pltpu.SemaphoreType.DMA((n_ctx,)),
            pltpu.SemaphoreType.DMA((n_ctx,)),
            pltpu.SemaphoreType.DMA,
        ],
        compiler_params=pltpu.CompilerParams(
            collective_id=2, has_side_effects=True, vmem_limit_bytes=60 * 2**20
        ),
        cost_estimate=pl.CostEstimate(
            flops=2 * rows_all * n_tp * cols * width, bytes_accessed=30 * 2**20, transcendentals=0
        ),
        name="output_project",
    )(out, xs, w_all, gain, shift)


def middle_sums(term, w_all, low, gate, up, hidden, cot, attended, w_down):
    rows, width = term.shape
    n_tp, cols, _ = w_all.shape
    n_ctx = lax.axis_size("ctx")
    units = gate.shape[1]
    share, piece = width // n_ctx, cols // n_ctx
    out_rows, down_rows = n_tp * piece, units // n_ctx
    other_rows = out_rows + down_rows
    half, heads = cols // 2, cols // 2 // HEAD
    window = min(units, (down_rows + 127 + 127) // 128 * 128)
    pair = n_ctx // 2
    tile = 256

    def kernel(
        term_in, w_all, low, gate, up, hidden, cot, attended, w_down,
        grad_out, gate_sum, up_sum, out_kept, out_sent, down_kept, down_sent, *rest,
    ):
        down_terms, down_far, (
            term, w_buf, wide_buf, gate_buf, up_buf, hidden_t, att_buf, tile_in, tile_out, far, ring_buf, heads_out, send_one, send_two, got_one, got_two, one_a, one_b,
            two_a, two_b,
            tile_s, far_s, load_s, w_s, att_s, ring_s, ring_r, head_s, head_r, core_s, core_r, one_s, one_r, two_s, two_r,
        ) = rest[: n_tp - 1], rest[n_tp - 1], rest[n_tp:]
        ctx, tp = lax.axis_index("ctx"), lax.axis_index("tp")
        y, x, core = ctx // 4, (ctx // 2) % 2, ctx % 2
        on_core, on_x, on_y = ctx + 1 - 2 * core, ctx + 2 - 4 * x, ctx + 4 - 8 * y
        here = y * 2 + x

        def remote(source, target, send, recv, peer, near=True):
            return pltpu.make_async_remote_copy(
                src_ref=source,
                dst_ref=target,
                send_sem=send,
                recv_sem=recv,
                device_id=(peer, tp) if near else (ctx, peer),
                device_id_type=MESH,
            )

        def w_load(block, side):
            rows_in = pl.ds(side * half, half)
            return pltpu.make_async_copy(w_all.at[block, rows_in], w_buf, w_s)

        def dest(step):
            return lax.rem(tp - 1 - step + 2 * n_tp, n_tp)

        loads = [
            pltpu.make_async_copy(source, target, load_s.at[i])
            for i, (source, target) in enumerate(
                ((low, wide_buf), (gate, gate_buf), (up, up_buf), (cot, wide_buf), (hidden, gate_buf), (term_in, term))
            )
        ]
        loads[5].start()
        w_load(dest(0), 0).start()
        for i in range(3):
            loads[i].start()
        greet(n_ctx, n_tp)

        def own_term(step, side):
            w_load(dest(step), side).wait()
            return lax.dot_general(
                w_buf[...], term[...], (((1,), (1,)), ((), ())), preferred_element_type=f32
            ).reshape(heads, HEAD, rows)

        def load_after(step, side):
            @pl.when(jnp.logical_or(side == 0, step < n_tp - 1))
            def _():
                w_load(lax.rem(tp - 1 - step - side + 2 * n_tp, n_tp), 1 - side).start()

        def ring(step, side):
            return remote(
                heads_out.at[pl.ds(side * heads, heads)]
                if step == 0
                else ring_buf.at[step - 1, side],
                ring_buf.at[step, side],
                ring_s.at[step, side],
                ring_r.at[step, side],
                lax.rem(tp + 1, n_tp),
                False,
            )

        def head_copy(step):
            peer = lax.rem(ctx + step, n_ctx)
            return remote(
                heads_out.at[peer], grad_out.at[ctx], head_s.at[step], head_r.at[step], peer
            )

        def ring_next(step):
            def one_side(side, carry):
                value = own_term(step + 1, side)
                ring(step, side).wait_recv()
                value = (value + ring_buf[step, side].astype(f32)).astype(bf16)
                if step < n_tp - 2:
                    ring_buf[step, side] = value
                    ring(step + 1, side).start()
                else:
                    ring(0, side).wait_send()
                    heads_out[pl.ds(side * heads, heads)] = value
                load_after(step + 1, side)
                return carry

            lax.fori_loop(0, 2, one_side, 0)

        def ring_first(side, carry):
            heads_out[pl.ds(side * heads, heads)] = own_term(0, side).astype(bf16)
            ring(0, side).start()
            load_after(0, side)
            return carry

        loads[5].wait()
        lax.fori_loop(0, 2, ring_first, 0)

        def spot(k):
            to_y, to_x = lax.rem(k, 2), k // 2
            return 1 - y + to_y * (2 * y - 1), 1 - x + to_x * (2 * x - 1)

        def spread(got, bounds, firsts, group):
            def copy(side, i):
                if side == 0:
                    source, peer = got.at[2 * i + 1 - x, bounds[0]], on_x
                else:
                    source, peer = got.at[2 * (1 - y) + i, bounds[1]], on_y
                return remote(
                    source, firsts[side].at[i], one_s.at[group, side, i], one_r.at[group, side, i], peer
                )

            return copy

        bounds_one = (slice(0, share), slice(share, 2 * share))
        bounds_two = (slice(0, out_rows), slice(out_rows, other_rows))
        spread_one = spread(got_one, bounds_one, (one_a, one_b), 0)
        spread_two = spread(got_two, bounds_two, (two_a, two_b), 1)

        def grads_one(chunk, store):
            lanes = pl.ds(pl.multiple_of(chunk * share, share), share)
            left = wide_buf[:, lanes].T
            store(bounds_one[0], jnp.dot(left, gate_buf[...], preferred_element_type=f32))
            store(bounds_one[1], jnp.dot(left, up_buf[...], preferred_element_type=f32))

        def grads_two(chunk, store):
            load = pltpu.make_async_copy(
                attended.at[:, pl.ds(pl.multiple_of(chunk * piece, piece), piece)], att_buf, att_s
            )
            load.start()
            first = chunk * down_rows
            start = jnp.minimum(first // 128 * 128, units - window)
            lanes = pl.ds(pl.multiple_of(start, 128), window)
            hidden_t[...] = gate_buf[:, lanes].T
            down_part = hidden_t[pl.ds(pl.multiple_of(first - start, 16), down_rows), :]
            store(
                slice(out_rows, other_rows),
                jnp.dot(down_part, wide_buf[...], preferred_element_type=f32),
            )
            load.wait()
            store(
                slice(0, out_rows),
                jnp.dot(
                    att_buf[...].reshape(out_rows, rows), term[...], preferred_element_type=f32
                ),
            )

        def core_copy(group, k):
            at_y, at_x = spot(k)
            sent, got = ((send_one, got_one), (send_two, got_two))[group]
            return remote(
                sent, got.at[2 * at_y + at_x], core_s.at[group, k], core_r.at[group, k], on_core
            )

        def both_sides(group, grads, sent, got, copy, leading):
            def step(k, carry):
                sending = jnp.logical_or(k == 0, jnp.logical_and(lax.rem(k, 2) == 1, k < 2 * pair - 1))
                keeping = jnp.logical_not(sending)
                behind = (k + k // (2 * pair - 1)) // 2 - 1
                place_k = jnp.where(sending, (k + 1) // 2, behind)
                at_y, at_x = spot(place_k)
                index = 2 * at_y + at_x

                @pl.when(keeping)
                def _():
                    core_copy(group, place_k).wait_recv()

                def store(place, value):
                    if place == leading:

                        @pl.when(jnp.logical_and(sending, k >= 1))
                        def _():
                            core_copy(group, place_k - 1).wait_send()

                    @pl.when(sending)
                    def _():
                        sent[place] = value.astype(bf16)

                    @pl.when(keeping)
                    def _():
                        got[index, place] = (got[index, place].astype(f32) + value).astype(bf16)

                grads(2 * index + jnp.where(sending, 1 - core, core), store)

                @pl.when(sending)
                def _():
                    core_copy(group, place_k).start()

                @pl.when(jnp.logical_and(keeping, place_k < 2))
                def _():
                    copy(0, at_y).start()

                @pl.when(jnp.logical_and(keeping, lax.rem(place_k, 2) == 0))
                def _():
                    copy(1, at_x).start()

                return carry

            lax.fori_loop(0, 2 * pair, step, 0)
            core_copy(group, pair - 1).wait_send()

        def fold(got, bounds, firsts, copy):
            for i in range(2):
                copy(0, i).wait_recv()
                index = 2 * i + x
                got[index, bounds[0]] = (
                    got[index, bounds[0]].astype(f32) + firsts[0][i].astype(f32)
                ).astype(bf16)
                copy(1, i).wait_recv()
                index = 2 * y + i
                got[index, bounds[1]] = (
                    got[index, bounds[1]].astype(f32) + firsts[1][i].astype(f32)
                ).astype(bf16)

        def last_copy(group, side):
            got, bounds, last = got_one, bounds_one, (gate_sum, up_sum)
            if side == 0:
                source, peer = got.at[2 * (1 - y) + x, bounds[0]], on_y
            else:
                source, peer = got.at[2 * y + 1 - x, bounds[1]], on_x
            return remote(
                source, last[side], two_s.at[group, side], two_r.at[group, side], peer
            )

        def finish(group, side, got, bounds, last):
            last_copy(group, side).wait_recv()
            return (got[here, bounds[side]].astype(f32) + last[...].astype(f32)).astype(bf16)

        for i in range(3):
            loads[i].wait()
        both_sides(0, grads_one, send_one, got_one, spread_one, bounds_one[0])
        loads[3].start()
        loads[4].start()
        ring_next(0)
        loads[4].wait()
        loads[3].wait()
        both_sides(1, grads_two, send_two, got_two, spread_two, bounds_two[1])
        ring_next(1)
        fold(got_one, bounds_one, (one_a, one_b), spread_one)
        for side in range(2):
            last_copy(0, side).start()
        def down_tile(t, carry):
            lanes = pl.ds(pl.multiple_of(t * tile, tile), tile)
            load = pltpu.make_async_copy(w_down.at[:, lanes], tile_in, tile_s.at[0])
            load.start()
            load.wait()
            for s in range(n_tp):
                own_rows = rows // n_tp
                block = lax.rem(tp - s + n_tp, n_tp)
                left = gate_buf[pl.ds(pl.multiple_of(block * own_rows, own_rows), own_rows), :]
                value = jnp.dot(left, tile_in[...], preferred_element_type=f32)
                if s == n_tp - 1:
                    far[:, lanes] = value.astype(bf16)
                    continue
                tile_out[s] = value.astype(bf16)
                pltpu.make_async_copy(
                    tile_out.at[s], down_terms[s].at[:, lanes], tile_s.at[s + 1]
                ).start()
            for s in range(n_tp - 1):
                pltpu.make_async_copy(
                    tile_out.at[s], down_terms[s].at[:, lanes], tile_s.at[s + 1]
                ).wait()
            return carry

        lax.fori_loop(0, width // tile, down_tile, 0)
        far_copy = remote(
            far, down_far, far_s.at[0], far_s.at[1], lax.rem(tp + 1, n_tp), False
        )
        far_copy.start()
        for step in range(2, n_tp - 1):
            ring_next(step)
        lax.fori_loop(1, n_ctx, lambda step, c: (head_copy(step).start(), c)[1], 0)
        grad_out[ctx] = heads_out[ctx]

        fold(got_two, bounds_two, (two_a, two_b), spread_two)
        out_kept[...] = got_two[here, bounds_two[0]]
        out_sent[...] = got_two[2 * (1 - y) + x, bounds_two[0]]
        down_kept[...] = got_two[here, bounds_two[1]]
        down_sent[...] = got_two[2 * y + 1 - x, bounds_two[1]]
        gate_sum[...] = finish(0, 0, got_one, bounds_one, gate_sum)
        up_sum[...] = finish(0, 1, got_one, bounds_one, up_sum)
        lax.fori_loop(1, n_ctx, lambda step, c: (head_copy(step).wait(), c)[1], 0)
        far_copy.wait()
        for step in range(1, n_tp - 1):
            for side in range(2):
                ring(step, side).wait_send()
        for group, copy in enumerate((spread_one, spread_two)):
            for side in range(2):
                if group == 0:
                    last_copy(group, side).wait_send()
                for i in range(2):
                    copy(side, i).wait_send()

    vmem, anywhere = pl.BlockSpec(memory_space=pltpu.VMEM), pl.BlockSpec(memory_space=pl.ANY)
    dma = pltpu.SemaphoreType.DMA
    return pl.pallas_call(
        kernel,
        out_shape=(
            jax.ShapeDtypeStruct((n_ctx, HEAD, rows), bf16),
            jax.ShapeDtypeStruct((share, units), bf16),
            jax.ShapeDtypeStruct((share, units), bf16),
            jax.ShapeDtypeStruct((out_rows, width), bf16),
            jax.ShapeDtypeStruct((out_rows, width), bf16),
            jax.ShapeDtypeStruct((down_rows, width), bf16),
            jax.ShapeDtypeStruct((down_rows, width), bf16),
        )
        + (jax.ShapeDtypeStruct((rows // n_tp, width), bf16),) * n_tp,
        in_specs=[anywhere] * 9,
        out_specs=(vmem,) * 7 + (anywhere,) * (n_tp - 1) + (vmem,),
        scratch_shapes=[
            pltpu.VMEM((rows, width), bf16),
            pltpu.VMEM((half, width), bf16),
            pltpu.VMEM((rows, width), bf16),
            pltpu.VMEM((rows, units), bf16),
            pltpu.VMEM((rows, units), bf16),
            pltpu.VMEM((window, rows), bf16),
            pltpu.VMEM((n_tp, piece, rows), bf16),
            pltpu.VMEM((units, tile), bf16),
            pltpu.VMEM((n_tp - 1, rows // n_tp, tile), bf16),
            pltpu.VMEM((rows // n_tp, width), bf16),
            pltpu.VMEM((n_tp - 1, 2, heads, HEAD, rows), bf16),
            pltpu.VMEM((n_ctx, HEAD, rows), bf16),
            pltpu.VMEM((2 * share, units), bf16),
            pltpu.VMEM((other_rows, width), bf16),
            pltpu.VMEM((pair, 2 * share, units), bf16),
            pltpu.VMEM((pair, other_rows, width), bf16),
            pltpu.VMEM((2, share, units), bf16),
            pltpu.VMEM((2, share, units), bf16),
            pltpu.VMEM((2, out_rows, width), bf16),
            pltpu.VMEM((2, down_rows, width), bf16),
            dma((n_tp,)), dma((2,)), dma((6,)), dma, dma,
            dma((n_tp - 1, 2)), dma((n_tp - 1, 2)),
            dma((n_ctx,)), dma((n_ctx,)),
            dma((2, pair)), dma((2, pair)),
            dma((2, 2, 2)), dma((2, 2, 2)),
            dma((2, 2)), dma((2, 2)),
        ],
        compiler_params=pltpu.CompilerParams(
            collective_id=4, has_side_effects=True, vmem_limit_bytes=62 * 2**20
        ),
        cost_estimate=pl.CostEstimate(
            flops=2 * rows * width * (2 * units + units + 2 * n_tp * cols),
            bytes_accessed=40 * 2**20,
            transcendentals=0,
        ),
        name="middle_sums",
    )(term, w_all, low, gate, up, hidden, cot, attended, w_down)


def final_sums(term, xs, means, inverses, gain, low, grads, w_qkv, out, small_two):
    n_tp, own, width = term.shape
    rows = low.shape[0]
    n_ctx = lax.axis_size("ctx")
    cols = 3 * n_ctx * HEAD
    tile = 32
    share = width // n_ctx
    half_rows, half_width = share // 2, width // 2
    part = out.shape[0] // n_tp
    columns = cols // 3
    first_rows, norm_rows = cols // 128, width // 128
    small_shape = (first_rows + 4 * norm_rows, 128)

    def kernel(
        term_in, xs, means, inverses, gain, low_in, mine, w_in, out, small_two,
        grad_in, out_all, qkv_all, small_sum,
        term, low_part, low_t, w_qkv, x_buf, grads, turned, back, sums, small, load_s, x_s, swap_s, swap_r, out_recv, out_s, out_r,
        small_ctx, small_tp, ring_buf, q_send, q_recv, both, first_a, first_b, second,
        small_s, small_r, norm_s, norm_r, ring_s, ring_r, core_s, core_r, one_s, one_r, two_s, two_r, piece_s, piece_r,
    ):
        ctx, tp = lax.axis_index("ctx"), lax.axis_index("tp")
        y, x, core = ctx // 4, (ctx // 2) % 2, ctx % 2
        on_core, on_x, on_y = ctx + 1 - 2 * core, ctx + 2 - 4 * x, ctx + 4 - 8 * y
        across = on_x + 4 - 8 * y
        here = y * 2 + x
        loads = [
            pltpu.make_async_copy(source, target, load_s.at[i])
            for i, (source, target) in enumerate(((w_in, w_qkv), (term_in, term)))
        ]
        for load in loads:
            load.start()
        barrier = pltpu.get_barrier_semaphore()
        for step in range(1, n_ctx):
            peer = lax.rem(ctx + step, n_ctx)
            pl.semaphore_signal(barrier, inc=1, device_id=(peer, tp), device_id_type=MESH)
        for step in range(1, n_tp):
            peer = lax.rem(tp + step, n_tp)
            pl.semaphore_signal(barrier, inc=1, device_id=(ctx, peer), device_id_type=MESH)
        pl.semaphore_wait(barrier, n_ctx + n_tp - 2)

        def remote(source, target, send, recv, peer, near=True):
            return pltpu.make_async_remote_copy(
                src_ref=source,
                dst_ref=target,
                send_sem=send,
                recv_sem=recv,
                device_id=(peer, tp) if near else (ctx, peer),
                device_id_type=MESH,
            )

        def ring(step, piece):
            lanes = slice(piece * half_width, (piece + 1) * half_width)
            first = term.at[lax.rem(tp - 1 + n_tp, n_tp), :, lanes]
            return remote(
                first if step == 0 else ring_buf.at[step - 1, piece],
                ring_buf.at[step, piece],
                ring_s.at[step, piece],
                ring_r.at[step, piece],
                lax.rem(tp + 1, n_tp),
                False,
            )

        def ring_next(step):
            for piece in range(2):
                lanes = slice(piece * half_width, (piece + 1) * half_width)
                ring(step, piece).wait_recv()
                block = lax.rem(tp - 2 - step + 2 * n_tp, n_tp)
                total = ring_buf[step, piece].astype(f32) + term[block, :, lanes].astype(f32)
                if step < n_tp - 2:
                    ring_buf[step, piece] = total.astype(bf16)
                    ring(step + 1, piece).start()
                else:
                    grad_in[:, lanes] = total.astype(bf16)

        def rows_of(where, start, stop):
            return lambda chunk: where.at[chunk, start:stop]

        def qkv_rows(start, stop):
            return lambda chunk: qkv_all.at[chunk, :, start:stop]

        pieces = (
            (rows_of(out_all, 0, part), False),
            (qkv_rows(0, half_rows), True),
            (qkv_rows(half_rows, share), False),
        )

        def hop(p, index):
            where, y_first = pieces[p]
            one, two = (on_y, on_x) if y_first else (on_x, on_y)
            chunk, peer = (
                (ctx, one), (ctx, two), (ctx, on_core), (one, two),
                (one, on_core), (two, on_core), (across, on_core),
            )[index]
            place = where(chunk)
            return remote(place, place, piece_s.at[p, index], piece_r.at[p, index], peer)

        def arrived(p, index):
            where, y_first = pieces[p]
            one, two = (on_y, on_x) if y_first else (on_x, on_y)
            chunk = (
                one, two, on_core, across,
                one + on_core - ctx, two + on_core - ctx, across + on_core - ctx,
            )[index]
            place = where(chunk)
            remote(place, place, piece_s.at[p, index], piece_r.at[p, index], on_core).wait_recv()

        def gather_start(p):
            for index in (0, 1, 2):
                hop(p, index).start()

        def gather_one(p):
            arrived(p, 0)
            hop(p, 3).start()
            hop(p, 4).start()

        def gather_two(p):
            arrived(p, 1)
            hop(p, 5).start()
            arrived(p, 3)
            hop(p, 6).start()

        def gather_end(p):
            for index in (2, 4, 5, 6):
                arrived(p, index)
            for index in range(7):
                hop(p, index).wait_send()

        def dest(step):
            return lax.rem(tp - 1 - step + 2 * n_tp, n_tp)

        def exchange(step, at):
            lanes = pl.ds(pl.multiple_of(dest(step) * own, own), own)
            peer = lax.rem(ctx + at, n_ctx)
            return remote(
                mine.at[peer, :, :, lanes],
                grads.at[:, ctx, :, lanes],
                swap_s.at[step, at],
                swap_r.at[step, at],
                peer,
            )

        def out_rows(step):
            return pl.ds(pl.multiple_of(dest(step) * part, part), part)

        def out_ring(step):
            return remote(
                out.at[out_rows(0)] if step == 0 else out_recv.at[step - 1],
                out_recv.at[step],
                out_s.at[step],
                out_r.at[step],
                lax.rem(tp + 1, n_tp),
                False,
            )

        def out_next(step):
            out_ring(step).wait_recv()
            total = out_recv[step].astype(f32) + out[out_rows(step + 1)].astype(f32)
            if step < n_tp - 2:
                out_recv[step] = total.astype(bf16)
                out_ring(step + 1).start()
            else:
                out_all[ctx] = total.astype(bf16)

        def x_load(step):
            return pltpu.make_async_copy(xs.at[dest(step)], x_buf, x_s)

        for step in range(n_tp):
            lax.fori_loop(
                1, n_ctx, lambda at, c, step=step: (exchange(step, at).start(), c)[1], 0
            )
        x_load(0).start()
        grads[:, ctx] = mine[ctx]
        out_ring(0).start()
        sums[...] = jnp.zeros_like(sums)

        def wait_rows(step):
            lax.fori_loop(1, n_ctx, lambda at, c: (exchange(step, at).wait_recv(), c)[1], 0)
            lanes = pl.ds(pl.multiple_of(dest(step) * own, own), own)
            for c in range(3):
                turned[c, lanes, :] = grads[c, :, :, lanes].reshape(columns, own).T

        def back_rows(step):
            block = dest(step)
            lanes = pl.ds(pl.multiple_of(block * own, own), own)
            for c in range(3):
                value = lax.dot_general(
                    turned[c, lanes, :], w_qkv[c], (((1,), (1,)), ((), ())), preferred_element_type=f32
                )
                if c == 0:
                    back[...] = value
                else:
                    back[...] += value
            x_load(step).wait()

            def norm_rows_back(i, carry):
                span = pl.ds(pl.multiple_of(i * tile, tile), tile)
                inverse = inverses[block, span, :][:, :1]
                normed = (x_buf[span, :].astype(f32) - means[block, span, :][:, :1]) * inverse
                value = back[span, :]
                scaled = value * gain[...]
                grad = inverse * (
                    scaled
                    - jnp.mean(scaled, axis=1, keepdims=True)
                    - normed * jnp.mean(scaled * normed, axis=1, keepdims=True)
                )
                sums[0:1] += jnp.sum(value * normed, axis=0, keepdims=True)
                sums[1:2] += jnp.sum(value, axis=0, keepdims=True)
                term[block, span, :] = (term[block, span, :].astype(f32) + grad).astype(bf16)
                return carry

            lax.fori_loop(0, own // tile, norm_rows_back, 0)
            if step < n_tp - 1:
                x_load(step + 1).start()

        def small_copy(step):
            peer = lax.rem(ctx + step, n_ctx)
            return remote(small, small_ctx.at[ctx], small_s.at[step], small_r.at[step], peer)

        def norm_copy(step):
            peer = lax.rem(tp + step, n_tp)
            source = small_tp.at[tp]
            return remote(source, source, norm_s.at[step], norm_r.at[step], peer, False)


        def turn_low(i, carry):
            lanes = pl.ds(pl.multiple_of(i * share, share), share)
            load = pltpu.make_async_copy(low_in.at[:, lanes], low_part, load_s.at[2])
            load.start()
            load.wait()
            low_t[i] = low_part[...].T
            return carry

        lax.fori_loop(0, n_ctx, turn_low, 0)
        for load in loads:
            load.wait()
        wait_rows(0)
        back_rows(0)
        for piece in range(2):
            ring(0, piece).start()
        for step in range(1, n_tp - 1):
            if step == 1:
                out_next(0)
            wait_rows(step)
            back_rows(step)
        wait_rows(n_tp - 1)

        def core_copy(i):
            return remote(q_send.at[i], q_recv.at[i], core_s.at[i], core_r.at[i], on_core)

        top, bottom = slice(0, half_rows), slice(half_rows, share)

        def one_copy(side, i):
            if side == 0:
                source, target, peer = both.at[2 * i + 1 - x, :, top], first_a.at[i], on_x
            else:
                source, target, peer = both.at[2 * (1 - y) + i, :, bottom], first_b.at[i], on_y
            return remote(source, target, one_s.at[side, i], one_r.at[side, i], peer)

        def chunk_step(k, carry):
            sending = jnp.logical_or(k == 0, jnp.logical_and(lax.rem(k, 2) == 1, k < n_ctx - 1))
            keeping = jnp.logical_not(sending)
            place_k = jnp.where(sending, (k + 1) // 2, (k + k // (n_ctx - 1)) // 2 - 1)
            at_y = 1 - y + lax.rem(place_k, 2) * (2 * y - 1)
            at_x = 1 - x + place_k // 2 * (2 * x - 1)
            index = 2 * at_y + at_x

            @pl.when(keeping)
            def _():
                core_copy(index).wait_recv()

            chunk = 2 * index + jnp.where(sending, 1 - core, core)
            for c in range(3):
                value = jnp.dot(low_t[chunk], turned[c], preferred_element_type=f32)

                @pl.when(sending)
                def _():
                    q_send[index, c] = value.astype(bf16)

                @pl.when(keeping)
                def _():
                    both[index, c] = (value + q_recv[index, c].astype(f32)).astype(bf16)

            @pl.when(sending)
            def _():
                core_copy(index).start()

            @pl.when(jnp.logical_and(keeping, place_k < 2))
            def _():
                one_copy(0, at_y).start()

            @pl.when(jnp.logical_and(keeping, lax.rem(place_k, 2) == 0))
            def _():
                one_copy(1, at_x).start()

            return carry

        lax.fori_loop(0, n_ctx // 2, chunk_step, 0)
        for step in range(1, n_tp - 2):
            out_next(step)
        ring_next(0)
        lax.fori_loop(n_ctx // 2, n_ctx, chunk_step, 0)
        back_rows(n_tp - 1)
        ones = jnp.ones((8, rows), bf16)
        for c in range(3):
            value = jnp.dot(ones, turned[c], preferred_element_type=f32)
            for t in range(columns // 128):
                row = c * columns // 128 + t
                small[row : row + 1] = value[0:1, t * 128 : (t + 1) * 128]
        for t in range(norm_rows):
            for which in range(2):
                row = first_rows + 2 * which * norm_rows + t
                small[row : row + 1] = sums[which : which + 1, t * 128 : (t + 1) * 128]
        for which in range(2):
            row = first_rows + (2 * which + 1) * norm_rows
            small[row : row + norm_rows] = small_two[which]
        small_ctx[ctx] = small[...]
        for step in range(1, n_ctx):
            small_copy(step).start()
        for i in range(2):
            one_copy(0, i).wait_recv()
            spot = 2 * i + x
            both[spot, :, top] = (
                both[spot, :, top].astype(f32) + first_a[i].astype(f32)
            ).astype(bf16)
            one_copy(1, i).wait_recv()
            spot = 2 * y + i
            both[spot, :, bottom] = (
                both[spot, :, bottom].astype(f32) + first_b[i].astype(f32)
            ).astype(bf16)

        def two_copy(side):
            if side == 0:
                source, peer = both.at[2 * (1 - y) + x, :, top], on_y
            else:
                source, peer = both.at[2 * y + 1 - x, :, bottom], on_x
            return remote(source, second.at[side], two_s.at[side], two_r.at[side], peer)

        for side in range(2):
            two_copy(side).start()
        out_next(n_tp - 2)
        gather_start(0)
        ring_next(1)
        for side, span in enumerate((top, bottom)):
            two_copy(side).wait_recv()
            qkv_all[ctx, :, span] = (
                both[here, :, span].astype(f32) + second[side].astype(f32)
            ).astype(bf16)
            gather_start(1 + side)
        for step in range(1, n_ctx):
            small_copy(step).wait_recv()
        value = sum(small_ctx[i] for i in range(n_ctx))
        small_sum[:first_rows] = value[:first_rows]
        small_tp[tp] = value[first_rows:]
        for step in range(1, n_tp):
            norm_copy(step).start()
        for p in range(3):
            gather_one(p)
        for step in range(2, n_tp - 1):
            ring_next(step)
        for p in range(3):
            gather_two(p)
        for step in range(1, n_tp):
            norm_copy(step).wait_recv()
        small_sum[first_rows:] = sum(small_tp[i] for i in range(n_tp))
        for p in range(3):
            gather_end(p)
        for step in range(n_tp - 1):
            out_ring(step).wait_send()
        for step in range(n_tp):
            lax.fori_loop(
                1, n_ctx, lambda at, c, step=step: (exchange(step, at).wait_send(), c)[1], 0
            )
        for step in range(1, n_ctx):
            small_copy(step).wait_send()
        for step in range(1, n_tp):
            norm_copy(step).wait_send()
        for step in range(n_tp - 1):
            for piece in range(2):
                ring(step, piece).wait_send()
        for i in range(n_ctx // 2):
            core_copy(i).wait_send()
        for side in range(2):
            two_copy(side).wait_send()
            for i in range(2):
                one_copy(side, i).wait_send()

    vmem, anywhere = pl.BlockSpec(memory_space=pltpu.VMEM), pl.BlockSpec(memory_space=pl.ANY)
    dma = pltpu.SemaphoreType.DMA
    pair = n_ctx // 2
    return pl.pallas_call(
        kernel,
        out_shape=(
            jax.ShapeDtypeStruct((own, width), bf16),
            jax.ShapeDtypeStruct((n_ctx, part, width), bf16),
            jax.ShapeDtypeStruct((n_ctx, 3, share, columns), bf16),
            jax.ShapeDtypeStruct(small_shape, f32),
        ),
        in_specs=[anywhere, anywhere, vmem, vmem, vmem, anywhere, vmem, anywhere, vmem, vmem],
        out_specs=(vmem,) * 4,
        scratch_shapes=[
            pltpu.VMEM(term.shape, bf16),
            pltpu.VMEM((rows, share), bf16),
            pltpu.VMEM((n_ctx, share, rows), bf16),
            pltpu.VMEM((3, width, columns), bf16),
            pltpu.VMEM((own, width), bf16),
            pltpu.VMEM((3, n_ctx, HEAD, rows), bf16),
            pltpu.VMEM((3, rows, columns), bf16),
            pltpu.VMEM((own, width), f32),
            pltpu.VMEM((8, width), f32),
            pltpu.VMEM(small_shape, f32),
            dma((3,)), dma,
            dma((n_tp, n_ctx)), dma((n_tp, n_ctx)),
            pltpu.VMEM((n_tp - 1, part, width), bf16),
            dma((n_tp - 1,)), dma((n_tp - 1,)),
            pltpu.VMEM((n_ctx,) + small_shape, f32),
            pltpu.VMEM((n_tp, 4 * norm_rows, 128), f32),
            pltpu.VMEM((n_tp - 1, 2, own, half_width), bf16),
            pltpu.VMEM((pair, 3, share, columns), bf16),
            pltpu.VMEM((pair, 3, share, columns), bf16),
            pltpu.VMEM((pair, 3, share, columns), bf16),
            pltpu.VMEM((2, 3, half_rows, columns), bf16),
            pltpu.VMEM((2, 3, half_rows, columns), bf16),
            pltpu.VMEM((2, 3, half_rows, columns), bf16),
            dma((n_ctx,)), dma((n_ctx,)),
            dma((n_tp,)), dma((n_tp,)),
            dma((n_tp - 1, 2)), dma((n_tp - 1, 2)),
            dma((pair,)), dma((pair,)),
            dma((2, 2)), dma((2, 2)),
            dma((2,)), dma((2,)),
            dma((3, 7)), dma((3, 7)),
        ],
        compiler_params=pltpu.CompilerParams(
            collective_id=3, has_side_effects=True, vmem_limit_bytes=62 * 2**20
        ),
        cost_estimate=pl.CostEstimate(
            flops=2 * rows * width * cols, bytes_accessed=50 * 2**20, transcendentals=0
        ),
        name="final_sums",
    )(
        term, xs, means, inverses, gain, low, grads, w_qkv.transpose(1, 0, 2), out, small_two
    )


def norm_stats(rows):
    mean = jnp.mean(rows, axis=1, keepdims=True)
    center = rows - mean
    inverse = lax.rsqrt(jnp.mean(center * center, axis=1, keepdims=True) + epsilon)
    return mean, inverse


def norm_backward(grad_out, normed, inverse, gain):
    scaled = grad_out * gain
    grad_rows = inverse * (
        scaled
        - jnp.mean(scaled, axis=1, keepdims=True)
        - normed * jnp.mean(scaled * normed, axis=1, keepdims=True)
    )
    return (grad_rows, jnp.sum(grad_out * normed, axis=0), jnp.sum(grad_out, axis=0))


def rotate(tensor, places, direction):
    half = ROT // 2
    frequency = 10000.0 ** (-2.0 * jnp.arange(half, dtype=f32) / ROT)
    angles = frequency[:, None] * places.astype(f32)[None, :]
    cosine, sines = jnp.cos(angles), direction * jnp.sin(angles)
    first, second = tensor[..., :half, :], tensor[..., half:ROT, :]
    return jnp.concatenate(
        [
            first * cosine - second * sines,
            second * cosine + first * sines,
            tensor[..., ROT:, :],
        ],
        axis=-2,
    )


def after(value, *others):
    return lax.optimization_barrier((value, *others))[0]


def direct_gather(value, count):
    n_tp = lax.axis_size("tp")
    return [value] + [
        lax.ppermute(value, "tp", [(i, (i + s) % n_tp) for i in range(n_tp)])
        for s in range(1, count)
    ]


def in_tp_order(arrays):
    count = len(arrays)
    shape = arrays[0].shape

    def kernel(tp, *refs):
        sources, out = refs[:count], refs[count]
        for s in range(count):
            out[lax.rem(tp[0] - s + count, count)] = sources[s][...]

    vmem = pl.BlockSpec(memory_space=pltpu.VMEM)
    return pl.pallas_call(
        kernel,
        out_shape=jax.ShapeDtypeStruct((count,) + shape, arrays[0].dtype),
        in_specs=[pl.BlockSpec(memory_space=pltpu.SMEM)] + [vmem] * count,
        out_specs=vmem,
        compiler_params=pltpu.CompilerParams(vmem_limit_bytes=60 * 2**20),
        cost_estimate=pl.CostEstimate(
            flops=0, bytes_accessed=4 * count * math.prod(shape), transcendentals=0
        ),
        name="in_tp_order",
    )(lax.axis_index("tp")[None], *arrays)


def exchange_sum(terms, axis):
    parts = lax.all_to_all(terms, axis, split_axis=0, concat_axis=0, tiled=True)
    return sum(part.astype(f32) for part in parts)


def scatter(partial, axis):
    return lax.psum_scatter(partial, axis, scatter_dimension=0, tiled=True)


def swap(value, axis, bit):
    size = lax.axis_size(axis)
    return lax.ppermute(value, axis, [(i, i ^ (1 << bit)) for i in range(size)])


def pair_sum(partial):
    size, rest = partial.shape[0], partial.shape[1:]
    side = lax.axis_index("ctx") % 2
    pairs = partial.reshape((size // 2, 2) + rest)
    kept = lax.dynamic_index_in_dim(pairs, side, 1, keepdims=False)
    sent = lax.dynamic_index_in_dim(pairs, 1 - side, 1, keepdims=False)
    return (kept.astype(f32) + swap(sent, "ctx", 0).astype(f32)).astype(bf16)


def spread_start(both, *early):
    pairs = both.shape[0]
    mine = lax.axis_index("ctx") // 2
    parts = [lax.dynamic_index_in_dim(both, mine, 0, keepdims=False)]
    for distance in range(1, pairs):
        sent = lax.dynamic_index_in_dim(both, mine ^ distance, 0, keepdims=False)
        perm = [(i, i ^ (2 * distance)) for i in range(2 * pairs)]
        parts.append(lax.ppermute(after(sent, *early) if early else sent, "ctx", perm))
    return parts


def spread_end(parts, *late):
    if late:
        parts = lax.optimization_barrier((*parts, *late))[: len(parts)]
    return sum(part.astype(f32) for part in parts).astype(bf16)


def by_ctx(partial):
    rows, cols = partial.shape
    n_ctx = lax.axis_size("ctx")
    return partial.reshape(n_ctx, rows // n_ctx, cols)


def gather(rows, axis):
    return lax.all_gather(rows, axis, axis=0, tiled=True)


def middle_backward(grad, middle, means, inverses, gain, cot, own):
    rows, width = grad.shape
    tile = math.gcd(own, 128)

    def kernel(tp, grad, middle, means, inverses, gain, cot, term, sums):
        i = pl.program_id(0)
        inverse = inverses[...][:, :1]
        normed = (middle[...] - means[...][:, :1]) * inverse
        value = grad[...]
        scaled = value * gain[...]
        result = inverse * (
            scaled
            - jnp.mean(scaled, axis=1, keepdims=True)
            - normed * jnp.mean(scaled * normed, axis=1, keepdims=True)
        )
        is_own = jnp.where(i * tile // own == tp[0], 1.0, 0.0)
        term[...] = (result + is_own * cot[...].astype(f32)).astype(bf16)

        @pl.when(i == 0)
        def _():
            sums[...] = jnp.zeros_like(sums)

        sums[0:1] += jnp.sum(value * normed, axis=0, keepdims=True)
        sums[1:2] += jnp.sum(value, axis=0, keepdims=True)

    def by_rows(cols):
        return pl.BlockSpec((tile, cols), lambda i: (i, 0))

    return pl.pallas_call(
        kernel,
        grid=(rows // tile,),
        out_shape=(
            jax.ShapeDtypeStruct((rows, width), bf16),
            jax.ShapeDtypeStruct((8, width), f32),
        ),
        in_specs=[
            pl.BlockSpec(memory_space=pltpu.SMEM),
            by_rows(width), by_rows(width), by_rows(128), by_rows(128),
            pl.BlockSpec((1, width), lambda i: (0, 0)),
            by_rows(width),
        ],
        out_specs=(by_rows(width), pl.BlockSpec((8, width), lambda i: (0, 0))),
        cost_estimate=pl.CostEstimate(
            flops=20 * rows * width, bytes_accessed=12 * rows * width, transcendentals=0
        ),
        compiler_params=pltpu.CompilerParams(vmem_limit_bytes=60 * 2**20),
        name="middle_backward",
    )(lax.axis_index("tp")[None], grad, middle, means, inverses, gain, cot)


def widen(chunks, down, out):
    devices, parts, rows, cols = chunks.shape
    step = math.gcd(devices, 2)

    def kernel(chunks, down, out, chunks_wide, down_wide, out_wide):
        for i in range(step):
            chunks_wide[:, i * rows : (i + 1) * rows] = chunks[i].astype(f32)
            for source, target in ((down, down_wide), (out, out_wide)):
                high = source.shape[1]
                target[i * high : (i + 1) * high] = source[i].astype(f32)

    others = (down.shape[1:], out.shape[1:])
    return pl.pallas_call(
        kernel,
        grid=(devices // step,),
        out_shape=[jax.ShapeDtypeStruct((parts, devices * rows, cols), f32)]
        + [jax.ShapeDtypeStruct((devices * shape[0], shape[1]), f32) for shape in others],
        in_specs=[pl.BlockSpec((step, parts, rows, cols), lambda i: (i, 0, 0, 0))]
        + [pl.BlockSpec((step,) + shape, lambda i: (i, 0, 0)) for shape in others],
        out_specs=[pl.BlockSpec((parts, step * rows, cols), lambda i: (0, i, 0))]
        + [pl.BlockSpec((step * shape[0], shape[1]), lambda i: (i, 0)) for shape in others],
        cost_estimate=pl.CostEstimate(
            flops=0, bytes_accessed=6 * math.prod(chunks.shape), transcendentals=0
        ),
        compiler_params=pltpu.CompilerParams(vmem_limit_bytes=60 * 2**20),
        name="widen",
    )(chunks, down, out)


def interleave(gate, up):
    rows, cols = gate.shape
    tile = math.gcd(rows, 512)

    def kernel(gate, up, out):
        out[:, 0, :] = gate[...].astype(f32)
        out[:, 1, :] = up[...].astype(f32)

    return pl.pallas_call(
        kernel,
        grid=(rows // tile,),
        out_shape=jax.ShapeDtypeStruct((rows, 2, cols), f32),
        in_specs=[pl.BlockSpec((tile, cols), lambda i: (i, 0))] * 2,
        out_specs=pl.BlockSpec((tile, 2, cols), lambda i: (i, 0, 0)),
        compiler_params=pltpu.CompilerParams(vmem_limit_bytes=60 * 2**20),
        cost_estimate=pl.CostEstimate(flops=1, bytes_accessed=1, transcendentals=0),
        name="interleave",
    )(gate, up)


def shards(
    layer_in,
    norm_gain,
    norm_bias,
    w_qkv,
    b_qkv,
    w_out,
    w_gate_up,
    w_down,
    cotangent,
    block_table,
    seq_ids,
):
    n_ctx, n_tp = lax.axis_size("ctx"), lax.axis_size("tp")
    ctx, tp = lax.axis_index("ctx"), lax.axis_index("tp")
    own, width = layer_in.shape
    rows = own * n_tp
    cols = w_qkv.shape[2]
    heads = cols // HEAD
    table = block_table.reshape(-1)
    blocks = table.shape[0]
    by_head = heads == n_ctx == 8 and BLK % own == 0
    part = cols // n_ctx

    ids = jnp.arange(blocks, dtype=jnp.int32)
    located = jnp.sum(jnp.where(table[None, :] == ids[:, None], ids[None, :], 0), axis=1)
    same = seq_ids[:, None] == seq_ids[None, :]
    first = jnp.min(jnp.where(same, ids[None, :], blocks), axis=1)
    last = jnp.max(jnp.where(same, ids[None, :], -1), axis=1)
    order = jnp.concatenate([located, first, last, tp[None]]).astype(jnp.int32)
    frequency = 10000.0 ** (-2.0 * jnp.arange(ROT // 2, dtype=f32) / ROT)
    positions = table[:, None] * BLK + jnp.arange(BLK, dtype=jnp.int32)[None, :]
    angles = frequency[None, :, None] * positions.astype(f32)[:, None, :]
    angles = jnp.stack([jnp.cos(angles), jnp.sin(angles)], axis=1)

    hidden_units = w_gate_up.shape[2]
    w_part = lax.dynamic_slice_in_dim(w_out, ctx * part, part, 0)
    if by_head:
        layer_in = after(layer_in, angles, order)
        xs, lows, mean_one, inverse_one, w_part, packed = project_exchange(
            layer_in, w_part, norm_gain[0:1], norm_bias[0:1], w_qkv, b_qkv
        )
        first_low = lows.reshape(rows, width)
        w_out_all = lax.all_gather(w_part, "ctx", axis=1, tiled=True)
        cot = direct_gather(after(cotangent, packed), n_tp - 1)
        out, logsum = attention_forward(order, angles, packed)
        middle, lows, mean_two, inverse_two, attended_all = output_project(
            out, xs, w_out_all, norm_gain[1:2], norm_bias[1:2]
        )
        cot = list(lax.optimization_barrier((*cot, middle))[: n_tp - 1])
        late = after(cotangent, middle)
        cot.append(lax.ppermute(late, "tp", [(i, (i + n_tp - 1) % n_tp) for i in range(n_tp)]))
        cot = in_tp_order(cot).reshape(rows, width)
        middle = middle.reshape(rows, width)
        mean_two, inverse_two = [t.reshape(rows, 128) for t in (mean_two, inverse_two)]
        second_low = lows.reshape(rows, width)
        attended_all = attended_all.reshape(n_tp * cols, rows)
    else:
        x = gather(layer_in, "tp").astype(f32)
        mean_one, inverse_one = norm_stats(x)
        first_low = ((x - mean_one) * inverse_one * norm_gain[0] + norm_bias[0]).astype(bf16)
        projected = (
            jnp.einsum("dcf,rd->cfr", w_qkv, first_low, preferred_element_type=f32)
            + b_qkv[:, :, None]
        ).reshape(3, heads, HEAD, rows)
        w_part = gather(w_part, "tp").reshape(n_tp, part, width)
        w_out_all = lax.all_gather(w_part, "ctx", axis=1, tiled=True)
        cot = gather(cotangent, "tp")
        places, _ = row_places(ctx * rows, rows, table, seq_ids)
        qkv = jnp.concatenate([rotate(projected[0:2], places, 1.0), projected[2:3]], axis=0)
        queries, keys, values = [t.astype(bf16).transpose(2, 0, 1) for t in qkv]
        visit, offsets = gathered_setup(
            rows, table, seq_ids, keys.reshape(rows, cols), values.reshape(rows, cols)
        )
        out, logsum = gathered_forward(queries, visit, offsets)
        attended_all = gather(out.astype(bf16).reshape(rows, cols).T, "tp")
        middle = x + jnp.einsum(
            "fr,fd->rd",
            attended_all,
            w_out_all.reshape(n_tp * cols, width),
            preferred_element_type=f32,
        )
        mean_two, inverse_two = norm_stats(middle)
        normed_two = (middle - mean_two) * inverse_two
        second_low = (normed_two * norm_gain[1] + norm_bias[1]).astype(bf16)

    grad_hidden = lax.dot_general(cot, w_down, (((1,), (1,)), ((), ())), preferred_element_type=f32)
    gate_up = jnp.einsum("rd,dcf->rcf", second_low, w_gate_up, preferred_element_type=f32)
    gate, up = gate_up[:, 0], gate_up[:, 1]
    sigmoid = jax.nn.sigmoid(gate)
    activated = gate * sigmoid
    hidden = (activated * up).astype(bf16)
    grad_gate = grad_hidden * up * sigmoid * (1.0 + gate * (1.0 - sigmoid))
    grad_up = grad_hidden * activated
    grad_gu = jnp.stack([grad_gate, grad_up], axis=1).astype(bf16)
    grad_second = jnp.einsum("rcf,dcf->rd", grad_gu, w_gate_up, preferred_element_type=f32)

    if by_head:
        middle_term, sums = middle_backward(
            grad_second, middle, mean_two, inverse_two, norm_gain[1:2], cot, own
        )
        gain_two, bias_two = sums[0], sums[1]
    else:
        middle_norm, gain_two, bias_two = norm_backward(
            grad_second, normed_two, inverse_two, norm_gain[1]
        )
        is_own = (jnp.arange(rows, dtype=jnp.int32) // own == tp)[:, None]
        middle_term = (middle_norm + jnp.where(is_own, cot.astype(f32), 0.0)).astype(bf16)

    if by_head:
        grad_att, gate_grad, up_grad, out_grad, out_sent, down_grad, down_sent, *down = middle_sums(
            middle_term,
            w_out_all,
            second_low,
            grad_gate.astype(bf16),
            grad_up.astype(bf16),
            hidden,
            cot,
            attended_all.reshape(n_tp, cols, rows),
            w_down,
        )
        down = [down[0], down[-1]] + [
            lax.ppermute(down[s], "tp", [(i, (i - s) % n_tp) for i in range(n_tp)])
            for s in range(1, n_tp - 1)
        ]
    else:
        grad_att = lax.dot_general(
            w_out_all.reshape(n_tp * cols, width),
            middle_term,
            (((1,), (1,)), ((), ())),
            preferred_element_type=f32,
        ).astype(bf16)
        grad_att = scatter(grad_att, "tp")
        down = jnp.dot(hidden, w_down, preferred_element_type=f32).astype(bf16)
        down = [scatter(down, "tp")]

        def weight_grad(left, right):
            return lax.dot_general(
                left, right, (((0,), (0,)), ((), ())), preferred_element_type=f32
            ).astype(bf16)

        gu_grad = jnp.concatenate(
            [pair_sum(by_ctx(weight_grad(second_low, t.astype(bf16)))) for t in (grad_gate, grad_up)],
            axis=1,
        )
        gu_grad = spread_end(spread_start(gu_grad))
        out_grad = jnp.dot(attended_all, middle_term, preferred_element_type=f32).astype(bf16)
        out_grad = out_grad.reshape(n_tp, n_ctx, part, width).transpose(1, 0, 2, 3)
        other_grad = jnp.concatenate(
            [
                pair_sum(out_grad.reshape(n_ctx, n_tp * part, width)),
                pair_sum(by_ctx(weight_grad(hidden, cot))),
            ],
            axis=1,
        )
        other_grad = spread_end(spread_start(other_grad))
        gate_grad, up_grad = jnp.split(gu_grad, 2, axis=0)
        out_grad, down_grad = jnp.split(other_grad, [n_tp * part], axis=0)
    gate_grad, up_grad = gather(gate_grad, "ctx"), gather(up_grad, "ctx")
    grad_gate_up = interleave(gate_grad, up_grad)

    if by_head:
        grads = attention_backward(order, angles, packed, grad_att, out, logsum)
        out_sent = lax.ppermute(out_sent, "ctx", [(i, i ^ 4) for i in range(n_ctx)])
        down_sent = lax.ppermute(down_sent, "ctx", [(i, i ^ 2) for i in range(n_ctx)])
        grads, out_sent, down_sent, *down = lax.optimization_barrier(
            (grads, out_sent, down_sent, *down)
        )
        out_grad = (out_grad.astype(f32) + out_sent.astype(f32)).astype(bf16)
        down_grad = (down_grad.astype(f32) + down_sent.astype(f32)).astype(bf16)
        down_grad = gather(down_grad, "ctx")
        grad_input, out_grad, grad_qkv, small = final_sums(
            middle_term.reshape(n_tp, own, width),
            xs,
            mean_one,
            inverse_one,
            norm_gain[0:1],
            first_low,
            grads,
            w_qkv,
            out_grad,
            jnp.stack([gain_two, bias_two]).reshape(2, -1, 128),
        )
        grad_input, *down = lax.optimization_barrier((grad_input, *down))
        grad_qkv, down_grad, out_grad = widen(
            grad_qkv, down_grad.reshape(n_ctx, -1, width), out_grad
        )
        grad_qkv = grad_qkv.transpose(1, 0, 2)
        bias_qkv, norms = small[: 3 * cols // 128], small[3 * cols // 128 :]
    else:
        grads = gathered_backward(
            queries, visit, offsets, grad_att.T.reshape(rows, heads, HEAD), out, logsum
        )
        grads = jnp.stack([t.transpose(1, 2, 0) for t in grads])
        grads = jnp.concatenate([rotate(grads[0:2], places, -1.0), grads[2:3]], axis=0)
        grad_projected = grads.reshape(3 * cols, rows).astype(bf16)
        grad_first = jnp.einsum(
            "cfr,dcf->rd",
            grad_projected.reshape(3, cols, rows),
            w_qkv,
            preferred_element_type=f32,
        )
        input_norm, gain_one, bias_one = norm_backward(
            grad_first, (x - mean_one) * inverse_one, inverse_one, norm_gain[0]
        )
        grad_input = middle_term.astype(f32) + input_norm
        grad_input = exchange_sum(grad_input.astype(bf16).reshape(n_tp, own, width), "tp")
        grad_input = grad_input.astype(bf16)
        grad_qkv = lax.dot_general(
            first_low, grad_projected, (((0,), (1,)), ((), ())), preferred_element_type=f32
        ).astype(bf16)
        grad_qkv = spread_end(spread_start(pair_sum(by_ctx(grad_qkv))))
        out_grad = exchange_sum(out_grad.reshape(n_tp, part, width), "tp").astype(bf16)
        out_grad, grad_qkv = [gather(t, "ctx").astype(f32) for t in (out_grad, grad_qkv)]
        grad_qkv = grad_qkv.reshape(width, 3, cols)
        down_grad = gather(down_grad, "ctx").astype(f32)
        bias_qkv = lax.psum(jnp.sum(grad_projected.astype(f32), axis=1), "ctx")
        norms = jnp.stack([gain_one, gain_two, bias_one, bias_two])
        norms = lax.psum(norms, ("ctx", "tp"))
    own_middle = lax.dynamic_slice_in_dim(middle, tp * own, own, 0)
    layer_out = (own_middle + sum(t.astype(f32) for t in down)).astype(bf16)
    norms = norms.reshape(2, 2, width)
    return (
        layer_out,
        grad_input,
        norms[0],
        norms[1],
        grad_qkv,
        bias_qkv.reshape(3, cols),
        out_grad,
        grad_gate_up,
        down_grad,
    )


def solution(mesh):
    placed = (
        P(("ctx", "tp"), None),
        P(),
        P(),
        P(None, None, "tp"),
        P(None, "tp"),
        P("tp", None),
        P(None, None, "tp"),
        P("tp", None),
        P(("ctx", "tp"), None),
        P(),
        P(),
    )
    return jax.shard_map(
        shards,
        mesh=mesh,
        in_specs=placed,
        out_specs=(
            P(("ctx", "tp"), None),
            P(("ctx", "tp"), None),
            P(),
            P(),
            P(None, None, "tp"),
            P(None, "tp"),
            P("tp", None),
            P(None, None, "tp"),
            P("tp", None),
        ),
        check_vma=False,
    )
```

```python
import math

import jax
import jax.numpy as jnp
from jax import lax
from jax.experimental import pallas as pl
from jax.experimental.pallas import tpu as pltpu
from jax.sharding import PartitionSpec as P

HEAD = 64
ROT = 16
BLK = 512
EXTRA = 16

epsilon = 1e-05
neg_large = -1e30
bf16 = jnp.bfloat16
f32 = jnp.float32


def dot(left, right, left_dim, right_dim):
    return lax.dot_general(
        left, right, (((left_dim,), (right_dim,)), ((), ())), preferred_element_type=f32
    )


def causal_keep():
    return lax.broadcasted_iota(jnp.int32, (BLK, BLK), 0) <= lax.broadcasted_iota(
        jnp.int32, (BLK, BLK), 1
    )


def turn(tile):
    return tile.astype(f32).T.astype(bf16)


def scan_chunks(devices, chunks, width, visit):
    per_block = BLK // width

    def source(device, carry):
        for chunk in range(chunks):
            place = device * (chunks // per_block) + chunk // per_block
            visit(chunk, device, place, slice((chunk % per_block) * width, (chunk % per_block + 1) * width))
        return carry

    lax.fori_loop(0, devices, source, 0)


def turn_dims(tile, cosine, sine):
    half = ROT // 2
    first, second = tile[0:half], tile[half:ROT]
    return jnp.concatenate(
        [first * cosine - second * sine, second * cosine + first * sine, tile[ROT:]], axis=0
    )


def attention_forward(order, angles, packed):
    count, devices, _, _, width = packed.shape
    blocks = devices * count * width // BLK

    def kernel(order, angles, packed, out, logsum, queries, keys, values):
        per_device = count * width // BLK
        row = lax.broadcasted_iota(jnp.int32, (EXTRA, BLK), 0)
        ones = jnp.where(row == 0, 1.0, 0.0).astype(bf16)

        def visit(chunk, device, place, lanes):
            part = packed.at[chunk]
            cosine, sine = angles[place, 0, :, lanes], angles[place, 1, :, lanes]
            query = turn_dims(part[device, 0].astype(f32), cosine, sine).astype(bf16)
            queries[place, :, lanes] = query * jnp.asarray(HEAD**-0.5, bf16)
            key = turn_dims(part[device, 1].astype(f32), cosine, sine).astype(bf16)
            keys[place, lanes, :] = turn(key)
            values[place, 0:HEAD, lanes] = part[device, 2]

        scan_chunks(devices, count, width, visit)

        def prepare(place, carry):
            values[place, HEAD : HEAD + EXTRA, :] = ones
            return carry

        lax.fori_loop(0, blocks, prepare, 0)
        keep = causal_keep()

        def query_block(i, carry):
            place = order[i]
            query = queries[place]

            def step(keys_at, state, masked):
                maxima, summed = state
                places = [order[j] for j in keys_at]
                scores = [dot(keys[other], query, 1, 0) for other in places]
                if masked:
                    scores = [jnp.where(keep, tile, neg_large) for tile in scores]
                new_maxima = maxima
                for tile in scores:
                    new_maxima = jnp.maximum(new_maxima, jnp.max(tile, axis=0, keepdims=True))
                summed = summed * jnp.exp(maxima - new_maxima)
                for other, tile in zip(places, scores):
                    weights = jnp.exp(tile - new_maxima).astype(bf16)
                    summed = summed + dot(values[other], weights, 1, 0)
                return new_maxima, summed

            state = (jnp.full((1, BLK), neg_large, f32), jnp.zeros((HEAD + EXTRA, BLK), f32))
            first = order[blocks + i]
            triples = (i - first) // 3
            state = lax.fori_loop(
                0, triples, lambda t, s: step([first + 3 * t + u for u in range(3)], s, False), state
            )
            state = lax.fori_loop(
                first + 3 * triples, i, lambda j, s: step([j], s, False), state
            )
            maxima, summed = step([i], state, True)
            totals = summed[HEAD : HEAD + 1]
            result = (summed[0:HEAD] / totals).astype(bf16)
            logsum[place] = maxima + jnp.log(totals)
            lane = pl.multiple_of(lax.rem(place, per_device) * BLK, BLK)
            out[place // per_device, :, pl.ds(lane, BLK)] = result
            return carry

        lax.fori_loop(0, blocks, query_block, 0)

    vmem = pl.BlockSpec(memory_space=pltpu.VMEM)
    return pl.pallas_call(
        kernel,
        out_shape=(
            jax.ShapeDtypeStruct((devices, HEAD, count * width), bf16),
            jax.ShapeDtypeStruct((blocks, 1, BLK), f32),
        ),
        in_specs=[pl.BlockSpec(memory_space=pltpu.SMEM), vmem, vmem],
        out_specs=(vmem, vmem),
        scratch_shapes=[
            pltpu.VMEM((blocks, HEAD, BLK), bf16),
            pltpu.VMEM((blocks, BLK, HEAD), bf16),
            pltpu.VMEM((blocks, HEAD + EXTRA, BLK), bf16),
        ],
        compiler_params=pltpu.CompilerParams(vmem_limit_bytes=60 * 2**20),
        cost_estimate=pl.CostEstimate(
            flops=85 * 2 * 2 * BLK * BLK * 256, bytes_accessed=5 * 2**20, transcendentals=0
        ),
        name="attention_forward",
    )(order, angles, packed)


def attention_backward(order, angles, packed, grad_out, out, logsum):
    count, devices, _, _, width = packed.shape
    blocks = devices * count * width // BLK
    wide = HEAD + EXTRA

    def kernel(
        order, angles, packed, grad_out, out, logsum,
        grads, query_x, grad_x, key_x, key_rows, value_x, grad_q,
    ):
        row = lax.broadcasted_iota(jnp.int32, (EXTRA, width), 0)
        lane_ids = lax.broadcasted_iota(jnp.int32, (BLK, EXTRA), 1)
        ones = jnp.where(lane_ids < 3, 1.0, 0.0).astype(bf16)

        def three_rows(value):
            high = value.astype(bf16).astype(f32)
            rest = value - high
            middle = rest.astype(bf16).astype(f32)
            low = rest - middle
            return jnp.where(
                row == 0, high, jnp.where(row == 1, middle, jnp.where(row == 2, low, 0.0))
            ).astype(bf16)

        def visit(chunk, device, place, lanes):
            part = packed.at[chunk]
            cosine, sine = angles[place, 0, :, lanes], angles[place, 1, :, lanes]
            query = turn_dims(part[device, 0].astype(f32), cosine, sine).astype(bf16)
            query_x[place, 0:HEAD, lanes] = query * jnp.asarray(HEAD**-0.5, bf16)
            query_x[place, HEAD:wide, lanes] = three_rows(-logsum[place, :, lanes])
            key = turn_dims(part[device, 1].astype(f32), cosine, sine).astype(bf16)
            key_rows[place, :, lanes] = key
            key_x[place, lanes, 0:HEAD] = turn(key)
            value_x[place, lanes, 0:HEAD] = turn(part[device, 2])
            own = slice(chunk * width, (chunk + 1) * width)
            grad = grad_out[device, :, own]
            delta = jnp.sum(
                grad.astype(f32) * out[device, :, own].astype(f32), axis=0, keepdims=True
            )
            grad_x[place, 0:HEAD, lanes] = grad
            grad_x[place, HEAD:wide, lanes] = three_rows(-delta)

        scan_chunks(devices, count, width, visit)

        def prepare(place, carry):
            key_x[place, :, HEAD:wide] = ones
            value_x[place, :, HEAD:wide] = ones
            grad_q[place] = jnp.zeros((HEAD, BLK), f32)
            return carry

        lax.fori_loop(0, blocks, prepare, 0)
        keep = causal_keep()
        per_device = count * width // BLK

        def store(part, place, tile):
            lane = pl.multiple_of(lax.rem(place, per_device) * BLK, BLK)
            grads[place // per_device, part, :, pl.ds(lane, BLK)] = tile

        def key_block(j, carry):
            place = order[j]
            key, value = key_x[place], value_x[place]
            key_tile = key_rows[place]

            def step(queries_at, state, masked):
                grad_k, grad_v = state
                places = [order[i] for i in queries_at]
                scores = [dot(key, query_x[other], 1, 0) for other in places]
                grad_probs = [dot(value, grad_x[other], 1, 0) for other in places]
                probs = [jnp.exp(tile) for tile in scores]
                if masked:
                    probs = [jnp.where(keep, tile, 0.0) for tile in probs]
                grad_raws = [(p * g).astype(bf16) for p, g in zip(probs, grad_probs)]
                for other, prob, grad_raw in zip(places, probs, grad_raws):
                    grad_v = grad_v + dot(grad_x[other, 0:HEAD, :], prob.astype(bf16), 1, 1)
                    grad_k = grad_k + dot(query_x[other, 0:HEAD, :], grad_raw, 1, 1)
                    grad_q[other] += dot(key_tile, grad_raw, 1, 0)
                return grad_k, grad_v

            zero = jnp.zeros((HEAD, BLK), f32)
            state = step([j], (zero, zero), True)
            end = order[2 * blocks + j]
            pairs = (end - j) // 2
            state = lax.fori_loop(
                0, pairs, lambda t, s: step([j + 1 + 2 * t, j + 2 + 2 * t], s, False), state
            )
            grad_k, grad_v = lax.fori_loop(
                j + 1 + 2 * pairs, end + 1, lambda i, s: step([i], s, False), state
            )
            cosine, sine = angles[place, 0], angles[place, 1]
            store(1, place, turn_dims(grad_k, cosine, -sine).astype(bf16))
            store(2, place, grad_v.astype(bf16))
            return carry

        lax.fori_loop(0, blocks, key_block, 0)

        def finish(place, carry):
            tile = turn_dims(grad_q[place] * HEAD**-0.5, angles[place, 0], -angles[place, 1])
            store(0, place, tile.astype(bf16))
            return carry

        lax.fori_loop(0, blocks, finish, 0)

    vmem = pl.BlockSpec(memory_space=pltpu.VMEM)
    return pl.pallas_call(
        kernel,
        out_shape=jax.ShapeDtypeStruct((devices, 3, HEAD, count * width), bf16),
        in_specs=[pl.BlockSpec(memory_space=pltpu.SMEM)] + [vmem] * 5,
        out_specs=vmem,
        scratch_shapes=[
            pltpu.VMEM((blocks, wide, BLK), bf16),
            pltpu.VMEM((blocks, wide, BLK), bf16),
            pltpu.VMEM((blocks, BLK, wide), bf16),
            pltpu.VMEM((blocks, HEAD, BLK), bf16),
            pltpu.VMEM((blocks, BLK, wide), bf16),
            pltpu.VMEM((blocks, HEAD, BLK), f32),
        ],
        compiler_params=pltpu.CompilerParams(vmem_limit_bytes=60 * 2**20),
        cost_estimate=pl.CostEstimate(flops=1, bytes_accessed=1, transcendentals=0),
        name="attention_backward",
    )(order, angles, packed, grad_out, out, logsum)


def row_places(first_row, length, table_flat, seq_ids):
    row_ids = first_row + jnp.arange(length, dtype=jnp.int32)
    block_ids = jnp.arange(table_flat.shape[0], dtype=jnp.int32)
    natural = jnp.sum(
        jnp.where((row_ids // BLK)[:, None] == block_ids[None, :], table_flat[None, :], 0), axis=1
    )
    sequence = jnp.sum(
        jnp.where(natural[:, None] == block_ids[None, :], seq_ids[None, :], 0), axis=1
    )
    return (natural * BLK + row_ids % BLK, sequence)


def gathered_setup(rows, table_flat, seq_ids, key_flat, value_flat):
    places, seq = row_places(lax.axis_index("ctx") * rows, rows, table_flat, seq_ids)
    pieces = (
        lax.all_gather(key_flat, "ctx", axis=0, tiled=True),
        lax.all_gather(value_flat, "ctx", axis=0, tiled=True),
    )
    stride = math.gcd(pieces[0].shape[0], 1024)
    offsets = jnp.arange(pieces[0].shape[0] // stride, dtype=jnp.int32) * stride

    def visit(offset):
        other_places, other_seq = row_places(offset, stride, table_flat, seq_ids)
        allowed = (seq[:, None] == other_seq[None, :]) & (other_places[None, :] <= places[:, None])
        blocks = [
            lax.dynamic_slice_in_dim(piece, offset, stride, 0).reshape(stride, -1, HEAD)
            for piece in pieces
        ]
        return allowed[:, None, :], blocks[0], blocks[1]

    return visit, offsets


def gathered_forward(queries, visit, offsets):
    rows, heads, _ = queries.shape

    def step(status, offset):
        allowed, keys, values = visit(offset)
        scores = jnp.einsum("qhe,khe->qhk", queries, keys, preferred_element_type=f32)
        scores = scores * HEAD**-0.5
        maxima, totals, summed = status
        new_maxima = jnp.maximum(maxima, jnp.max(jnp.where(allowed, scores, neg_large), axis=2))
        weights = jnp.where(allowed, jnp.exp(scores - new_maxima[..., None]), 0.0)
        factor = jnp.exp(maxima - new_maxima)
        totals = totals * factor + jnp.sum(weights, axis=2)
        summed = summed * factor[..., None] + jnp.einsum(
            "qhk,khe->qhe", weights.astype(bf16), values, preferred_element_type=f32
        )
        return ((new_maxima, totals, summed), None)

    initial = (
        jnp.full((rows, heads), neg_large, f32),
        jnp.zeros((rows, heads), f32),
        jnp.zeros((rows, heads, HEAD), f32),
    )
    (maxima, totals, summed), _ = lax.scan(step, initial, offsets)
    return summed / totals[..., None], maxima + jnp.log(totals)


def gathered_backward(queries, visit, offsets, grad_att, attended, logsum):
    rows, heads, _ = queries.shape
    delta = jnp.sum(grad_att.astype(f32) * attended, axis=2)

    def step(status, offset):
        allowed, keys, values = visit(offset)
        scores = jnp.einsum("qhe,khe->qhk", queries, keys, preferred_element_type=f32)
        prob = jnp.where(allowed, jnp.exp(scores * HEAD**-0.5 - logsum[..., None]), 0.0)
        grad_prob = jnp.einsum("qhe,khe->qhk", grad_att, values, preferred_element_type=f32)
        grad_raw = (prob * (grad_prob - delta[..., None]) * HEAD**-0.5).astype(bf16)
        grad_q = jnp.einsum("qhk,khe->qhe", grad_raw, keys, preferred_element_type=f32)
        grad_k = jnp.einsum("qhk,qhe->khe", grad_raw, queries, preferred_element_type=f32)
        grad_v = jnp.einsum("qhk,qhe->khe", prob.astype(bf16), grad_att, preferred_element_type=f32)
        return (
            (
                status[0] + grad_q,
                lax.dynamic_update_slice_in_dim(status[1], grad_k, offset, 0),
                lax.dynamic_update_slice_in_dim(status[2], grad_v, offset, 0),
            ),
            None,
        )

    total = rows * lax.axis_size("ctx")
    zero = jnp.zeros((total, heads, HEAD), f32)
    (grad_q, grad_k, grad_v), _ = lax.scan(
        step, (jnp.zeros((rows, heads, HEAD), f32), zero, zero), offsets
    )
    grad_k = lax.psum_scatter(grad_k, "ctx", scatter_dimension=0, tiled=True)
    grad_v = lax.psum_scatter(grad_v, "ctx", scatter_dimension=0, tiled=True)
    return grad_q, grad_k, grad_v


MESH = pl.DeviceIdType.MESH


def greet(n_ctx, n_tp):
    ctx, tp = lax.axis_index("ctx"), lax.axis_index("tp")
    barrier = pltpu.get_barrier_semaphore()

    def greet_ctx(step, carry):
        peer = lax.rem(ctx + step, n_ctx)
        pl.semaphore_signal(barrier, inc=1, device_id=(peer, tp), device_id_type=MESH)
        return carry

    lax.fori_loop(1, n_ctx, greet_ctx, 0)
    for peer in (lax.rem(tp + 1, n_tp), lax.rem(tp + n_tp - 1, n_tp)):
        pl.semaphore_signal(barrier, inc=1, device_id=(ctx, peer), device_id_type=MESH)
    pl.semaphore_wait(barrier, n_ctx + 1)


def rows_norm(source, stored, gain, shift, mean_out, inverse_out, tile):
    def step(i, carry):
        rows = pl.ds(pl.multiple_of(i * tile, tile), tile)
        x = source(rows)
        mean = jnp.mean(x, axis=1, keepdims=True)
        center = x - mean
        inverse = lax.rsqrt(jnp.mean(center * center, axis=1, keepdims=True) + epsilon)
        stored(rows, (center * inverse * gain + shift).astype(bf16))
        mean_out[rows, :] = jnp.broadcast_to(mean, (tile, 128))
        inverse_out[rows, :] = jnp.broadcast_to(inverse, (tile, 128))
        return carry

    return step


def project_exchange(layer_in, w_part, gain, shift, w_qkv, b_qkv):
    n_ctx, n_tp = lax.axis_size("ctx"), lax.axis_size("tp")
    own, width = layer_in.shape
    part = w_part.shape[0]
    cols = w_qkv.shape[2]

    def kernel(
        x_in, w_in, gain, shift, w_qkv_in, b_qkv,
        xs_out, lows_out, means, inverses, ws, packed,
        xs, lows, w_qkv, load_s, store_s, outgoing, ring_send, ring_recv, w_send, w_recv, send, recv,
    ):
        ctx, tp = lax.axis_index("ctx"), lax.axis_index("tp")
        right = lax.rem(tp + 1, n_tp)
        half = own // 2

        def block(slot):
            return lax.rem(tp - slot + n_tp, n_tp)

        def ring(step, piece):
            rows = pl.ds(piece * half, half)
            return pltpu.make_async_remote_copy(
                src_ref=x_in.at[rows] if step == 0 else xs.at[block(step), rows],
                dst_ref=xs.at[block(step), rows],
                send_sem=ring_send.at[step, piece],
                recv_sem=ring_recv.at[step, piece],
                device_id=(ctx, right),
                device_id_type=MESH,
            )

        def w_ring(step):
            return pltpu.make_async_remote_copy(
                src_ref=w_in if step == 0 else ws.at[block(step)],
                dst_ref=ws.at[block(step)],
                send_sem=w_send.at[step],
                recv_sem=w_recv.at[step],
                device_id=(ctx, right),
                device_id_type=MESH,
            )

        def exchange(slot, step):
            peer = lax.rem(ctx + step, n_ctx)
            return pltpu.make_async_remote_copy(
                src_ref=outgoing.at[slot, peer],
                dst_ref=packed.at[block(slot), ctx],
                send_sem=send.at[slot, step],
                recv_sem=recv.at[slot, step],
                device_id=(peer, tp),
                device_id_type=MESH,
            )

        load = pltpu.make_async_copy(w_qkv_in, w_qkv, load_s)
        load.start()

        def store(slot, which):
            here = block(slot)
            source, target = ((xs, xs_out), (lows, lows_out))[which]
            return pltpu.make_async_copy(source.at[here], target.at[here], store_s.at[slot, which])

        greet(n_ctx, n_tp)
        for piece in range(2):
            ring(0, piece).start()
        xs[tp] = x_in[...]
        ws[tp] = w_in[...]
        for slot in range(n_tp):
            if slot > 0:
                for piece in range(2):
                    ring(slot - 1, piece).wait_recv()
                    if slot < n_tp - 1:
                        ring(slot, piece).start()
            if slot == n_tp - 2:
                w_ring(0).start()
            if slot == n_tp - 1:
                w_ring(0).wait_recv()
                w_ring(1).start()

            here = block(slot)

            def stored(rows, value, here=here):
                lows[here, rows, :] = value

            step = rows_norm(
                lambda rows, here=here: xs[here, rows, :].astype(f32),
                stored, gain[...], shift[...], means.at[here], inverses.at[here], 32,
            )
            lax.fori_loop(0, own // 32, step, 0)
            store(slot, 0).start()
            store(slot, 1).start()
            if slot == 0:
                load.wait()

            def project(c, carry, slot=slot, here=here):
                value = jnp.dot(lows[here], w_qkv[c], preferred_element_type=f32) + b_qkv[c]
                outgoing[slot, :, c] = value.T.astype(bf16).reshape(n_ctx, HEAD, own)
                return carry

            lax.fori_loop(0, 3, project, 0)
            lax.fori_loop(
                1, n_ctx, lambda step, c, slot=slot: (exchange(slot, step).start(), c)[1], 0
            )
            packed[here, ctx] = outgoing[slot, ctx]
        for step in range(1, n_tp - 1):
            w_ring(step).wait_recv()
            if step < n_tp - 2:
                w_ring(step + 1).start()
        for slot in range(n_tp):
            lax.fori_loop(
                1, n_ctx, lambda step, c, slot=slot: (exchange(slot, step).wait(), c)[1], 0
            )
        for slot in range(n_tp):
            store(slot, 0).wait()
            store(slot, 1).wait()
        for step in range(n_tp - 1):
            w_ring(step).wait_send()
            for piece in range(2):
                ring(step, piece).wait_send()

    vmem, anywhere = pl.BlockSpec(memory_space=pltpu.VMEM), pl.BlockSpec(memory_space=pl.ANY)
    return pl.pallas_call(
        kernel,
        out_shape=(
            jax.ShapeDtypeStruct((n_tp, own, width), bf16),
            jax.ShapeDtypeStruct((n_tp, own, width), bf16),
            jax.ShapeDtypeStruct((n_tp, own, 128), f32),
            jax.ShapeDtypeStruct((n_tp, own, 128), f32),
            jax.ShapeDtypeStruct((n_tp, part, width), bf16),
            jax.ShapeDtypeStruct((n_tp, n_ctx, 3, HEAD, own), bf16),
        ),
        in_specs=[vmem] * 4 + [anywhere, vmem],
        out_specs=(anywhere,) * 2 + (vmem,) * 4,
        scratch_shapes=[
            pltpu.VMEM((n_tp, own, width), bf16),
            pltpu.VMEM((n_tp, own, width), bf16),
            pltpu.VMEM((3, width, cols), bf16),
            pltpu.SemaphoreType.DMA,
            pltpu.SemaphoreType.DMA((n_tp, 2)),
            pltpu.VMEM((n_tp, n_ctx, 3, HEAD, own), bf16),
            pltpu.SemaphoreType.DMA((n_tp - 1, 2)),
            pltpu.SemaphoreType.DMA((n_tp - 1, 2)),
            pltpu.SemaphoreType.DMA((n_tp - 1,)),
            pltpu.SemaphoreType.DMA((n_tp - 1,)),
            pltpu.SemaphoreType.DMA((n_tp, n_ctx)),
            pltpu.SemaphoreType.DMA((n_tp, n_ctx)),
        ],
        compiler_params=pltpu.CompilerParams(
            collective_id=1, has_side_effects=True, vmem_limit_bytes=60 * 2**20
        ),
        cost_estimate=pl.CostEstimate(
            flops=2 * n_tp * own * width * 3 * cols, bytes_accessed=20 * 2**20, transcendentals=0
        ),
        name="project_exchange",
    )(layer_in, w_part, gain, shift, w_qkv.transpose(1, 0, 2), b_qkv[:, None, :])


def output_project(out, xs, w_all, gain, shift):
    n_ctx, n_tp = lax.axis_size("ctx"), lax.axis_size("tp")
    own, width = xs.shape[1:]
    cols = w_all.shape[1]
    rows_all = n_tp * own

    def kernel(
        out, xs_in, w_in, gain, shift,
        middle_out, lows_out, means, inverses, raw,
        xs, w_all, middle, lows, load_s, store_s, ring_send, ring_recv, send, recv, own_sem,
    ):
        ctx, tp = lax.axis_index("ctx"), lax.axis_index("tp")
        right = lax.rem(tp + 1, n_tp)
        half = cols // 2

        def block(slot):
            return lax.rem(tp - slot + n_tp, n_tp)

        def ring(step, piece):
            rows = pl.ds(piece * half, half)
            return pltpu.make_async_remote_copy(
                src_ref=raw.at[block(step), rows],
                dst_ref=raw.at[block(step), rows],
                send_sem=ring_send.at[step, piece],
                recv_sem=ring_recv.at[step, piece],
                device_id=(ctx, right),
                device_id_type=MESH,
            )

        def exchange(step):
            peer = lax.rem(ctx + step, n_ctx)
            return pltpu.make_async_remote_copy(
                src_ref=out.at[peer],
                dst_ref=raw.at[tp, pl.ds(pl.multiple_of(ctx * HEAD, HEAD), HEAD)],
                send_sem=send.at[step],
                recv_sem=recv.at[step],
                device_id=(peer, tp),
                device_id_type=MESH,
            )

        loads = (
            pltpu.make_async_copy(xs_in, xs, load_s.at[0]),
            pltpu.make_async_copy(w_in, w_all, load_s.at[1]),
        )
        for load in loads:
            load.start()

        def store(place, which):
            source, target = ((middle, middle_out), (lows, lows_out))[which]
            return pltpu.make_async_copy(
                source.at[place], target.at[place], store_s.at[place, which]
            )

        greet(n_ctx, n_tp)
        lax.fori_loop(1, n_ctx, lambda step, c: (exchange(step).start(), c)[1], 0)
        keep = pltpu.make_async_copy(
            out.at[ctx], raw.at[tp, pl.ds(pl.multiple_of(ctx * HEAD, HEAD), HEAD)], own_sem
        )
        keep.start()
        keep.wait()
        lax.fori_loop(1, n_ctx, lambda step, c: (exchange(step).wait_recv(), c)[1], 0)
        for piece in range(2):
            ring(0, piece).start()
        for load in loads:
            load.wait()
        for slot in range(n_tp):
            here = block(slot)
            for piece in range(2):
                if slot > 0:
                    ring(slot - 1, piece).wait_recv()
                    if slot < n_tp - 1:
                        ring(slot, piece).start()
                span = slice(piece * half, (piece + 1) * half)

                def project(place, carry, first=slot + piece == 0, here=here, span=span):
                    lanes = pl.ds(pl.multiple_of(place * own, own), own)
                    value = jnp.dot(
                        raw[here, span, lanes].T, w_all[here, span], preferred_element_type=f32
                    )
                    if first:
                        middle[place] = xs[place].astype(f32) + value
                    else:
                        middle[place] += value
                    return carry

                lax.fori_loop(0, n_tp, project, 0)
        for place in range(n_tp):
            store(place, 0).start()

            def stored(rows, value, place=place):
                lows[place, rows, :] = value

            step = rows_norm(
                lambda rows, place=place: middle[place, rows, :],
                stored, gain[...], shift[...], means.at[place], inverses.at[place], 32,
            )
            lax.fori_loop(0, own // 32, step, 0)
            store(place, 1).start()
        lax.fori_loop(1, n_ctx, lambda step, c: (exchange(step).wait_send(), c)[1], 0)
        for place in range(n_tp):
            store(place, 0).wait()
            store(place, 1).wait()
        for step in range(n_tp - 1):
            for piece in range(2):
                ring(step, piece).wait_send()

    vmem, anywhere = pl.BlockSpec(memory_space=pltpu.VMEM), pl.BlockSpec(memory_space=pl.ANY)
    return pl.pallas_call(
        kernel,
        out_shape=(
            jax.ShapeDtypeStruct((n_tp, own, width), f32),
            jax.ShapeDtypeStruct((n_tp, own, width), bf16),
            jax.ShapeDtypeStruct((n_tp, own, 128), f32),
            jax.ShapeDtypeStruct((n_tp, own, 128), f32),
            jax.ShapeDtypeStruct((n_tp, cols, rows_all), bf16),
        ),
        in_specs=[vmem, anywhere, anywhere, vmem, vmem],
        out_specs=(anywhere,) * 2 + (vmem,) * 3,
        scratch_shapes=[
            pltpu.VMEM((n_tp, own, width), bf16),
            pltpu.VMEM((n_tp, cols, width), bf16),
            pltpu.VMEM((n_tp, own, width), f32),
            pltpu.VMEM((n_tp, own, width), bf16),
            pltpu.SemaphoreType.DMA((2,)),
            pltpu.SemaphoreType.DMA((n_tp, 2)),
            pltpu.SemaphoreType.DMA((n_tp - 1, 2)),
            pltpu.SemaphoreType.DMA((n_tp - 1, 2)),
            pltpu.SemaphoreType.DMA((n_ctx,)),
            pltpu.SemaphoreType.DMA((n_ctx,)),
            pltpu.SemaphoreType.DMA,
        ],
        compiler_params=pltpu.CompilerParams(
            collective_id=2, has_side_effects=True, vmem_limit_bytes=60 * 2**20
        ),
        cost_estimate=pl.CostEstimate(
            flops=2 * rows_all * n_tp * cols * width, bytes_accessed=30 * 2**20, transcendentals=0
        ),
        name="output_project",
    )(out, xs, w_all, gain, shift)


def middle_sums(term, w_all, low, gate, up, hidden, cot, attended, w_down):
    rows, width = term.shape
    n_tp, cols, _ = w_all.shape
    n_ctx = lax.axis_size("ctx")
    units = gate.shape[1]
    share, piece = width // n_ctx, cols // n_ctx
    out_rows, down_rows = n_tp * piece, units // n_ctx
    other_rows = out_rows + down_rows
    half, heads = cols // 2, cols // 2 // HEAD
    window = min(units, (down_rows + 127 + 127) // 128 * 128)
    pair = n_ctx // 2
    tile = 256

    def kernel(
        term_in, w_all, low, gate, up, hidden, cot, attended, w_down,
        grad_out, gate_sum, up_sum, out_kept, out_sent, down_kept, down_sent, *rest,
    ):
        down_terms, down_far, (
            term, w_buf, wide_buf, gate_buf, up_buf, hidden_t, att_buf, tile_in, tile_out, far, ring_buf, heads_out, send_one, send_two, got_one, got_two, one_a, one_b,
            two_a, two_b,
            tile_s, far_s, load_s, w_s, att_s, ring_s, ring_r, head_s, head_r, core_s, core_r, one_s, one_r, two_s, two_r,
        ) = rest[: n_tp - 1], rest[n_tp - 1], rest[n_tp:]
        ctx, tp = lax.axis_index("ctx"), lax.axis_index("tp")
        y, x, core = ctx // 4, (ctx // 2) % 2, ctx % 2
        on_core, on_x, on_y = ctx + 1 - 2 * core, ctx + 2 - 4 * x, ctx + 4 - 8 * y
        here = y * 2 + x

        def remote(source, target, send, recv, peer, near=True):
            return pltpu.make_async_remote_copy(
                src_ref=source,
                dst_ref=target,
                send_sem=send,
                recv_sem=recv,
                device_id=(peer, tp) if near else (ctx, peer),
                device_id_type=MESH,
            )

        def w_load(block, side):
            rows_in = pl.ds(side * half, half)
            return pltpu.make_async_copy(w_all.at[block, rows_in], w_buf, w_s)

        def dest(step):
            return lax.rem(tp - 1 - step + 2 * n_tp, n_tp)

        loads = [
            pltpu.make_async_copy(source, target, load_s.at[i])
            for i, (source, target) in enumerate(
                ((low, wide_buf), (gate, gate_buf), (up, up_buf), (cot, wide_buf), (hidden, gate_buf), (term_in, term))
            )
        ]
        loads[5].start()
        w_load(dest(0), 0).start()
        for i in range(3):
            loads[i].start()
        greet(n_ctx, n_tp)

        def own_term(step, side):
            w_load(dest(step), side).wait()
            return lax.dot_general(
                w_buf[...], term[...], (((1,), (1,)), ((), ())), preferred_element_type=f32
            ).reshape(heads, HEAD, rows)

        def load_after(step, side):
            @pl.when(jnp.logical_or(side == 0, step < n_tp - 1))
            def _():
                w_load(lax.rem(tp - 1 - step - side + 2 * n_tp, n_tp), 1 - side).start()

        def ring(step, side):
            return remote(
                heads_out.at[pl.ds(side * heads, heads)]
                if step == 0
                else ring_buf.at[step - 1, side],
                ring_buf.at[step, side],
                ring_s.at[step, side],
                ring_r.at[step, side],
                lax.rem(tp + 1, n_tp),
                False,
            )

        def head_copy(step):
            peer = lax.rem(ctx + step, n_ctx)
            return remote(
                heads_out.at[peer], grad_out.at[ctx], head_s.at[step], head_r.at[step], peer
            )

        def ring_next(step):
            def one_side(side, carry):
                value = own_term(step + 1, side)
                ring(step, side).wait_recv()
                value = (value + ring_buf[step, side].astype(f32)).astype(bf16)
                if step < n_tp - 2:
                    ring_buf[step, side] = value
                    ring(step + 1, side).start()
                else:
                    ring(0, side).wait_send()
                    heads_out[pl.ds(side * heads, heads)] = value
                load_after(step + 1, side)
                return carry

            lax.fori_loop(0, 2, one_side, 0)

        def ring_first(side, carry):
            heads_out[pl.ds(side * heads, heads)] = own_term(0, side).astype(bf16)
            ring(0, side).start()
            load_after(0, side)
            return carry

        loads[5].wait()
        lax.fori_loop(0, 2, ring_first, 0)

        def spot(k):
            to_y, to_x = lax.rem(k, 2), k // 2
            return 1 - y + to_y * (2 * y - 1), 1 - x + to_x * (2 * x - 1)

        def spread(got, bounds, firsts, group):
            def copy(side, i):
                if side == 0:
                    source, peer = got.at[2 * i + 1 - x, bounds[0]], on_x
                else:
                    source, peer = got.at[2 * (1 - y) + i, bounds[1]], on_y
                return remote(
                    source, firsts[side].at[i], one_s.at[group, side, i], one_r.at[group, side, i], peer
                )

            return copy

        bounds_one = (slice(0, share), slice(share, 2 * share))
        bounds_two = (slice(0, out_rows), slice(out_rows, other_rows))
        spread_one = spread(got_one, bounds_one, (one_a, one_b), 0)
        spread_two = spread(got_two, bounds_two, (two_a, two_b), 1)

        def grads_one(chunk, store):
            lanes = pl.ds(pl.multiple_of(chunk * share, share), share)
            left = wide_buf[:, lanes].T
            store(bounds_one[0], jnp.dot(left, gate_buf[...], preferred_element_type=f32))
            store(bounds_one[1], jnp.dot(left, up_buf[...], preferred_element_type=f32))

        def grads_two(chunk, store):
            load = pltpu.make_async_copy(
                attended.at[:, pl.ds(pl.multiple_of(chunk * piece, piece), piece)], att_buf, att_s
            )
            load.start()
            first = chunk * down_rows
            start = jnp.minimum(first // 128 * 128, units - window)
            lanes = pl.ds(pl.multiple_of(start, 128), window)
            hidden_t[...] = gate_buf[:, lanes].T
            down_part = hidden_t[pl.ds(pl.multiple_of(first - start, 16), down_rows), :]
            store(
                slice(out_rows, other_rows),
                jnp.dot(down_part, wide_buf[...], preferred_element_type=f32),
            )
            load.wait()
            store(
                slice(0, out_rows),
                jnp.dot(
                    att_buf[...].reshape(out_rows, rows), term[...], preferred_element_type=f32
                ),
            )

        def core_copy(group, k):
            at_y, at_x = spot(k)
            sent, got = ((send_one, got_one), (send_two, got_two))[group]
            return remote(
                sent, got.at[2 * at_y + at_x], core_s.at[group, k], core_r.at[group, k], on_core
            )

        def both_sides(group, grads, sent, got, copy, leading):
            def step(k, carry):
                sending = jnp.logical_or(k == 0, jnp.logical_and(lax.rem(k, 2) == 1, k < 2 * pair - 1))
                keeping = jnp.logical_not(sending)
                behind = (k + k // (2 * pair - 1)) // 2 - 1
                place_k = jnp.where(sending, (k + 1) // 2, behind)
                at_y, at_x = spot(place_k)
                index = 2 * at_y + at_x

                @pl.when(keeping)
                def _():
                    core_copy(group, place_k).wait_recv()

                def store(place, value):
                    if place == leading:

                        @pl.when(jnp.logical_and(sending, k >= 1))
                        def _():
                            core_copy(group, place_k - 1).wait_send()

                    @pl.when(sending)
                    def _():
                        sent[place] = value.astype(bf16)

                    @pl.when(keeping)
                    def _():
                        got[index, place] = (got[index, place].astype(f32) + value).astype(bf16)

                grads(2 * index + jnp.where(sending, 1 - core, core), store)

                @pl.when(sending)
                def _():
                    core_copy(group, place_k).start()

                @pl.when(jnp.logical_and(keeping, place_k < 2))
                def _():
                    copy(0, at_y).start()

                @pl.when(jnp.logical_and(keeping, lax.rem(place_k, 2) == 0))
                def _():
                    copy(1, at_x).start()

                return carry

            lax.fori_loop(0, 2 * pair, step, 0)
            core_copy(group, pair - 1).wait_send()

        def fold(got, bounds, firsts, copy):
            for i in range(2):
                copy(0, i).wait_recv()
                index = 2 * i + x
                got[index, bounds[0]] = (
                    got[index, bounds[0]].astype(f32) + firsts[0][i].astype(f32)
                ).astype(bf16)
                copy(1, i).wait_recv()
                index = 2 * y + i
                got[index, bounds[1]] = (
                    got[index, bounds[1]].astype(f32) + firsts[1][i].astype(f32)
                ).astype(bf16)

        def last_copy(group, side):
            got, bounds, last = got_one, bounds_one, (gate_sum, up_sum)
            if side == 0:
                source, peer = got.at[2 * (1 - y) + x, bounds[0]], on_y
            else:
                source, peer = got.at[2 * y + 1 - x, bounds[1]], on_x
            return remote(
                source, last[side], two_s.at[group, side], two_r.at[group, side], peer
            )

        def finish(group, side, got, bounds, last):
            last_copy(group, side).wait_recv()
            return (got[here, bounds[side]].astype(f32) + last[...].astype(f32)).astype(bf16)

        for i in range(3):
            loads[i].wait()
        both_sides(0, grads_one, send_one, got_one, spread_one, bounds_one[0])
        loads[3].start()
        loads[4].start()
        ring_next(0)
        loads[4].wait()
        loads[3].wait()
        both_sides(1, grads_two, send_two, got_two, spread_two, bounds_two[1])
        ring_next(1)
        fold(got_one, bounds_one, (one_a, one_b), spread_one)
        for side in range(2):
            last_copy(0, side).start()
        def down_tile(t, carry):
            lanes = pl.ds(pl.multiple_of(t * tile, tile), tile)
            load = pltpu.make_async_copy(w_down.at[:, lanes], tile_in, tile_s.at[0])
            load.start()
            load.wait()
            for s in range(n_tp):
                own_rows = rows // n_tp
                block = lax.rem(tp - s + n_tp, n_tp)
                left = gate_buf[pl.ds(pl.multiple_of(block * own_rows, own_rows), own_rows), :]
                value = jnp.dot(left, tile_in[...], preferred_element_type=f32)
                if s == n_tp - 1:
                    far[:, lanes] = value.astype(bf16)
                    continue
                tile_out[s] = value.astype(bf16)
                pltpu.make_async_copy(
                    tile_out.at[s], down_terms[s].at[:, lanes], tile_s.at[s + 1]
                ).start()
            for s in range(n_tp - 1):
                pltpu.make_async_copy(
                    tile_out.at[s], down_terms[s].at[:, lanes], tile_s.at[s + 1]
                ).wait()
            return carry

        lax.fori_loop(0, width // tile, down_tile, 0)
        far_copy = remote(
            far, down_far, far_s.at[0], far_s.at[1], lax.rem(tp + 1, n_tp), False
        )
        far_copy.start()
        for step in range(2, n_tp - 1):
            ring_next(step)
        lax.fori_loop(1, n_ctx, lambda step, c: (head_copy(step).start(), c)[1], 0)
        grad_out[ctx] = heads_out[ctx]

        fold(got_two, bounds_two, (two_a, two_b), spread_two)
        out_kept[...] = got_two[here, bounds_two[0]]
        out_sent[...] = got_two[2 * (1 - y) + x, bounds_two[0]]
        down_kept[...] = got_two[here, bounds_two[1]]
        down_sent[...] = got_two[2 * y + 1 - x, bounds_two[1]]
        gate_sum[...] = finish(0, 0, got_one, bounds_one, gate_sum)
        up_sum[...] = finish(0, 1, got_one, bounds_one, up_sum)
        lax.fori_loop(1, n_ctx, lambda step, c: (head_copy(step).wait(), c)[1], 0)
        far_copy.wait()
        for step in range(1, n_tp - 1):
            for side in range(2):
                ring(step, side).wait_send()
        for group, copy in enumerate((spread_one, spread_two)):
            for side in range(2):
                if group == 0:
                    last_copy(group, side).wait_send()
                for i in range(2):
                    copy(side, i).wait_send()

    vmem, anywhere = pl.BlockSpec(memory_space=pltpu.VMEM), pl.BlockSpec(memory_space=pl.ANY)
    dma = pltpu.SemaphoreType.DMA
    return pl.pallas_call(
        kernel,
        out_shape=(
            jax.ShapeDtypeStruct((n_ctx, HEAD, rows), bf16),
            jax.ShapeDtypeStruct((share, units), bf16),
            jax.ShapeDtypeStruct((share, units), bf16),
            jax.ShapeDtypeStruct((out_rows, width), bf16),
            jax.ShapeDtypeStruct((out_rows, width), bf16),
            jax.ShapeDtypeStruct((down_rows, width), bf16),
            jax.ShapeDtypeStruct((down_rows, width), bf16),
        )
        + (jax.ShapeDtypeStruct((rows // n_tp, width), bf16),) * n_tp,
        in_specs=[anywhere] * 9,
        out_specs=(vmem,) * 7 + (anywhere,) * (n_tp - 1) + (vmem,),
        scratch_shapes=[
            pltpu.VMEM((rows, width), bf16),
            pltpu.VMEM((half, width), bf16),
            pltpu.VMEM((rows, width), bf16),
            pltpu.VMEM((rows, units), bf16),
            pltpu.VMEM((rows, units), bf16),
            pltpu.VMEM((window, rows), bf16),
            pltpu.VMEM((n_tp, piece, rows), bf16),
            pltpu.VMEM((units, tile), bf16),
            pltpu.VMEM((n_tp - 1, rows // n_tp, tile), bf16),
            pltpu.VMEM((rows // n_tp, width), bf16),
            pltpu.VMEM((n_tp - 1, 2, heads, HEAD, rows), bf16),
            pltpu.VMEM((n_ctx, HEAD, rows), bf16),
            pltpu.VMEM((2 * share, units), bf16),
            pltpu.VMEM((other_rows, width), bf16),
            pltpu.VMEM((pair, 2 * share, units), bf16),
            pltpu.VMEM((pair, other_rows, width), bf16),
            pltpu.VMEM((2, share, units), bf16),
            pltpu.VMEM((2, share, units), bf16),
            pltpu.VMEM((2, out_rows, width), bf16),
            pltpu.VMEM((2, down_rows, width), bf16),
            dma((n_tp,)), dma((2,)), dma((6,)), dma, dma,
            dma((n_tp - 1, 2)), dma((n_tp - 1, 2)),
            dma((n_ctx,)), dma((n_ctx,)),
            dma((2, pair)), dma((2, pair)),
            dma((2, 2, 2)), dma((2, 2, 2)),
            dma((2, 2)), dma((2, 2)),
        ],
        compiler_params=pltpu.CompilerParams(
            collective_id=4, has_side_effects=True, vmem_limit_bytes=62 * 2**20
        ),
        cost_estimate=pl.CostEstimate(
            flops=2 * rows * width * (2 * units + units + 2 * n_tp * cols),
            bytes_accessed=40 * 2**20,
            transcendentals=0,
        ),
        name="middle_sums",
    )(term, w_all, low, gate, up, hidden, cot, attended, w_down)


def final_sums(term, xs, means, inverses, gain, low, grads, w_qkv, out, small_two):
    n_tp, own, width = term.shape
    rows = low.shape[0]
    n_ctx = lax.axis_size("ctx")
    cols = 3 * n_ctx * HEAD
    tile = 32
    share = width // n_ctx
    half_rows, half_width = share // 2, width // 2
    part = out.shape[0] // n_tp
    columns = cols // 3
    first_rows, norm_rows = cols // 128, width // 128
    small_shape = (first_rows + 4 * norm_rows, 128)

    def kernel(
        term_in, xs, means, inverses, gain, low_in, mine, w_in, out, small_two,
        grad_in, out_all, qkv_all, small_sum,
        term, low_part, low_t, w_qkv, x_buf, grads, turned, back, sums, small, load_s, x_s, swap_s, swap_r, out_recv, out_s, out_r,
        small_ctx, small_tp, ring_buf, q_send, q_recv, both, first_a, first_b, second,
        small_s, small_r, norm_s, norm_r, ring_s, ring_r, core_s, core_r, one_s, one_r, two_s, two_r, piece_s, piece_r,
    ):
        ctx, tp = lax.axis_index("ctx"), lax.axis_index("tp")
        y, x, core = ctx // 4, (ctx // 2) % 2, ctx % 2
        on_core, on_x, on_y = ctx + 1 - 2 * core, ctx + 2 - 4 * x, ctx + 4 - 8 * y
        across = on_x + 4 - 8 * y
        here = y * 2 + x
        loads = [
            pltpu.make_async_copy(source, target, load_s.at[i])
            for i, (source, target) in enumerate(((w_in, w_qkv), (term_in, term)))
        ]
        for load in loads:
            load.start()
        barrier = pltpu.get_barrier_semaphore()
        for step in range(1, n_ctx):
            peer = lax.rem(ctx + step, n_ctx)
            pl.semaphore_signal(barrier, inc=1, device_id=(peer, tp), device_id_type=MESH)
        for step in range(1, n_tp):
            peer = lax.rem(tp + step, n_tp)
            pl.semaphore_signal(barrier, inc=1, device_id=(ctx, peer), device_id_type=MESH)
        pl.semaphore_wait(barrier, n_ctx + n_tp - 2)

        def remote(source, target, send, recv, peer, near=True):
            return pltpu.make_async_remote_copy(
                src_ref=source,
                dst_ref=target,
                send_sem=send,
                recv_sem=recv,
                device_id=(peer, tp) if near else (ctx, peer),
                device_id_type=MESH,
            )

        def ring(step, piece):
            lanes = slice(piece * half_width, (piece + 1) * half_width)
            first = term.at[lax.rem(tp - 1 + n_tp, n_tp), :, lanes]
            return remote(
                first if step == 0 else ring_buf.at[step - 1, piece],
                ring_buf.at[step, piece],
                ring_s.at[step, piece],
                ring_r.at[step, piece],
                lax.rem(tp + 1, n_tp),
                False,
            )

        def ring_next(step):
            for piece in range(2):
                lanes = slice(piece * half_width, (piece + 1) * half_width)
                ring(step, piece).wait_recv()
                block = lax.rem(tp - 2 - step + 2 * n_tp, n_tp)
                total = ring_buf[step, piece].astype(f32) + term[block, :, lanes].astype(f32)
                if step < n_tp - 2:
                    ring_buf[step, piece] = total.astype(bf16)
                    ring(step + 1, piece).start()
                else:
                    grad_in[:, lanes] = total.astype(bf16)

        def rows_of(where, start, stop):
            return lambda chunk: where.at[chunk, start:stop]

        def qkv_rows(start, stop):
            return lambda chunk: qkv_all.at[chunk, :, start:stop]

        pieces = (
            (rows_of(out_all, 0, part), False),
            (qkv_rows(0, half_rows), True),
            (qkv_rows(half_rows, share), False),
        )

        def hop(p, index):
            where, y_first = pieces[p]
            one, two = (on_y, on_x) if y_first else (on_x, on_y)
            chunk, peer = (
                (ctx, one), (ctx, two), (ctx, on_core), (one, two),
                (one, on_core), (two, on_core), (across, on_core),
            )[index]
            place = where(chunk)
            return remote(place, place, piece_s.at[p, index], piece_r.at[p, index], peer)

        def arrived(p, index):
            where, y_first = pieces[p]
            one, two = (on_y, on_x) if y_first else (on_x, on_y)
            chunk = (
                one, two, on_core, across,
                one + on_core - ctx, two + on_core - ctx, across + on_core - ctx,
            )[index]
            place = where(chunk)
            remote(place, place, piece_s.at[p, index], piece_r.at[p, index], on_core).wait_recv()

        def gather_start(p):
            for index in (0, 1, 2):
                hop(p, index).start()

        def gather_one(p):
            arrived(p, 0)
            hop(p, 3).start()
            hop(p, 4).start()

        def gather_two(p):
            arrived(p, 1)
            hop(p, 5).start()
            arrived(p, 3)
            hop(p, 6).start()

        def gather_end(p):
            for index in (2, 4, 5, 6):
                arrived(p, index)
            for index in range(7):
                hop(p, index).wait_send()

        def dest(step):
            return lax.rem(tp - 1 - step + 2 * n_tp, n_tp)

        def exchange(step, at):
            lanes = pl.ds(pl.multiple_of(dest(step) * own, own), own)
            peer = lax.rem(ctx + at, n_ctx)
            return remote(
                mine.at[peer, :, :, lanes],
                grads.at[:, ctx, :, lanes],
                swap_s.at[step, at],
                swap_r.at[step, at],
                peer,
            )

        def out_rows(step):
            return pl.ds(pl.multiple_of(dest(step) * part, part), part)

        def out_ring(step):
            return remote(
                out.at[out_rows(0)] if step == 0 else out_recv.at[step - 1],
                out_recv.at[step],
                out_s.at[step],
                out_r.at[step],
                lax.rem(tp + 1, n_tp),
                False,
            )

        def out_next(step):
            out_ring(step).wait_recv()
            total = out_recv[step].astype(f32) + out[out_rows(step + 1)].astype(f32)
            if step < n_tp - 2:
                out_recv[step] = total.astype(bf16)
                out_ring(step + 1).start()
            else:
                out_all[ctx] = total.astype(bf16)

        def x_load(step):
            return pltpu.make_async_copy(xs.at[dest(step)], x_buf, x_s)

        for step in range(n_tp):
            lax.fori_loop(
                1, n_ctx, lambda at, c, step=step: (exchange(step, at).start(), c)[1], 0
            )
        x_load(0).start()
        grads[:, ctx] = mine[ctx]
        out_ring(0).start()
        sums[...] = jnp.zeros_like(sums)

        def wait_rows(step):
            lax.fori_loop(1, n_ctx, lambda at, c: (exchange(step, at).wait_recv(), c)[1], 0)
            lanes = pl.ds(pl.multiple_of(dest(step) * own, own), own)
            for c in range(3):
                turned[c, lanes, :] = grads[c, :, :, lanes].reshape(columns, own).T

        def back_rows(step):
            block = dest(step)
            lanes = pl.ds(pl.multiple_of(block * own, own), own)
            for c in range(3):
                value = lax.dot_general(
                    turned[c, lanes, :], w_qkv[c], (((1,), (1,)), ((), ())), preferred_element_type=f32
                )
                if c == 0:
                    back[...] = value
                else:
                    back[...] += value
            x_load(step).wait()

            def norm_rows_back(i, carry):
                span = pl.ds(pl.multiple_of(i * tile, tile), tile)
                inverse = inverses[block, span, :][:, :1]
                normed = (x_buf[span, :].astype(f32) - means[block, span, :][:, :1]) * inverse
                value = back[span, :]
                scaled = value * gain[...]
                grad = inverse * (
                    scaled
                    - jnp.mean(scaled, axis=1, keepdims=True)
                    - normed * jnp.mean(scaled * normed, axis=1, keepdims=True)
                )
                sums[0:1] += jnp.sum(value * normed, axis=0, keepdims=True)
                sums[1:2] += jnp.sum(value, axis=0, keepdims=True)
                term[block, span, :] = (term[block, span, :].astype(f32) + grad).astype(bf16)
                return carry

            lax.fori_loop(0, own // tile, norm_rows_back, 0)
            if step < n_tp - 1:
                x_load(step + 1).start()

        def small_copy(step):
            peer = lax.rem(ctx + step, n_ctx)
            return remote(small, small_ctx.at[ctx], small_s.at[step], small_r.at[step], peer)

        def norm_copy(step):
            peer = lax.rem(tp + step, n_tp)
            source = small_tp.at[tp]
            return remote(source, source, norm_s.at[step], norm_r.at[step], peer, False)


        def turn_low(i, carry):
            lanes = pl.ds(pl.multiple_of(i * share, share), share)
            load = pltpu.make_async_copy(low_in.at[:, lanes], low_part, load_s.at[2])
            load.start()
            load.wait()
            low_t[i] = low_part[...].T
            return carry

        lax.fori_loop(0, n_ctx, turn_low, 0)
        for load in loads:
            load.wait()
        wait_rows(0)
        back_rows(0)
        for piece in range(2):
            ring(0, piece).start()
        for step in range(1, n_tp - 1):
            if step == 1:
                out_next(0)
            wait_rows(step)
            back_rows(step)
        wait_rows(n_tp - 1)

        def core_copy(i):
            return remote(q_send.at[i], q_recv.at[i], core_s.at[i], core_r.at[i], on_core)

        top, bottom = slice(0, half_rows), slice(half_rows, share)

        def one_copy(side, i):
            if side == 0:
                source, target, peer = both.at[2 * i + 1 - x, :, top], first_a.at[i], on_x
            else:
                source, target, peer = both.at[2 * (1 - y) + i, :, bottom], first_b.at[i], on_y
            return remote(source, target, one_s.at[side, i], one_r.at[side, i], peer)

        def chunk_step(k, carry):
            sending = jnp.logical_or(k == 0, jnp.logical_and(lax.rem(k, 2) == 1, k < n_ctx - 1))
            keeping = jnp.logical_not(sending)
            place_k = jnp.where(sending, (k + 1) // 2, (k + k // (n_ctx - 1)) // 2 - 1)
            at_y = 1 - y + lax.rem(place_k, 2) * (2 * y - 1)
            at_x = 1 - x + place_k // 2 * (2 * x - 1)
            index = 2 * at_y + at_x

            @pl.when(keeping)
            def _():
                core_copy(index).wait_recv()

            chunk = 2 * index + jnp.where(sending, 1 - core, core)
            for c in range(3):
                value = jnp.dot(low_t[chunk], turned[c], preferred_element_type=f32)

                @pl.when(sending)
                def _():
                    q_send[index, c] = value.astype(bf16)

                @pl.when(keeping)
                def _():
                    both[index, c] = (value + q_recv[index, c].astype(f32)).astype(bf16)

            @pl.when(sending)
            def _():
                core_copy(index).start()

            @pl.when(jnp.logical_and(keeping, place_k < 2))
            def _():
                one_copy(0, at_y).start()

            @pl.when(jnp.logical_and(keeping, lax.rem(place_k, 2) == 0))
            def _():
                one_copy(1, at_x).start()

            return carry

        lax.fori_loop(0, n_ctx // 2, chunk_step, 0)
        for step in range(1, n_tp - 2):
            out_next(step)
        ring_next(0)
        lax.fori_loop(n_ctx // 2, n_ctx, chunk_step, 0)
        back_rows(n_tp - 1)
        ones = jnp.ones((8, rows), bf16)
        for c in range(3):
            value = jnp.dot(ones, turned[c], preferred_element_type=f32)
            for t in range(columns // 128):
                row = c * columns // 128 + t
                small[row : row + 1] = value[0:1, t * 128 : (t + 1) * 128]
        for t in range(norm_rows):
            for which in range(2):
                row = first_rows + 2 * which * norm_rows + t
                small[row : row + 1] = sums[which : which + 1, t * 128 : (t + 1) * 128]
        for which in range(2):
            row = first_rows + (2 * which + 1) * norm_rows
            small[row : row + norm_rows] = small_two[which]
        small_ctx[ctx] = small[...]
        for step in range(1, n_ctx):
            small_copy(step).start()
        for i in range(2):
            one_copy(0, i).wait_recv()
            spot = 2 * i + x
            both[spot, :, top] = (
                both[spot, :, top].astype(f32) + first_a[i].astype(f32)
            ).astype(bf16)
            one_copy(1, i).wait_recv()
            spot = 2 * y + i
            both[spot, :, bottom] = (
                both[spot, :, bottom].astype(f32) + first_b[i].astype(f32)
            ).astype(bf16)

        def two_copy(side):
            if side == 0:
                source, peer = both.at[2 * (1 - y) + x, :, top], on_y
            else:
                source, peer = both.at[2 * y + 1 - x, :, bottom], on_x
            return remote(source, second.at[side], two_s.at[side], two_r.at[side], peer)

        for side in range(2):
            two_copy(side).start()
        out_next(n_tp - 2)
        gather_start(0)
        ring_next(1)
        for side, span in enumerate((top, bottom)):
            two_copy(side).wait_recv()
            qkv_all[ctx, :, span] = (
                both[here, :, span].astype(f32) + second[side].astype(f32)
            ).astype(bf16)
            gather_start(1 + side)
        for step in range(1, n_ctx):
            small_copy(step).wait_recv()
        value = sum(small_ctx[i] for i in range(n_ctx))
        small_sum[:first_rows] = value[:first_rows]
        small_tp[tp] = value[first_rows:]
        for step in range(1, n_tp):
            norm_copy(step).start()
        for p in range(3):
            gather_one(p)
        for step in range(2, n_tp - 1):
            ring_next(step)
        for p in range(3):
            gather_two(p)
        for step in range(1, n_tp):
            norm_copy(step).wait_recv()
        small_sum[first_rows:] = sum(small_tp[i] for i in range(n_tp))
        for p in range(3):
            gather_end(p)
        for step in range(n_tp - 1):
            out_ring(step).wait_send()
        for step in range(n_tp):
            lax.fori_loop(
                1, n_ctx, lambda at, c, step=step: (exchange(step, at).wait_send(), c)[1], 0
            )
        for step in range(1, n_ctx):
            small_copy(step).wait_send()
        for step in range(1, n_tp):
            norm_copy(step).wait_send()
        for step in range(n_tp - 1):
            for piece in range(2):
                ring(step, piece).wait_send()
        for i in range(n_ctx // 2):
            core_copy(i).wait_send()
        for side in range(2):
            two_copy(side).wait_send()
            for i in range(2):
                one_copy(side, i).wait_send()

    vmem, anywhere = pl.BlockSpec(memory_space=pltpu.VMEM), pl.BlockSpec(memory_space=pl.ANY)
    dma = pltpu.SemaphoreType.DMA
    pair = n_ctx // 2
    return pl.pallas_call(
        kernel,
        out_shape=(
            jax.ShapeDtypeStruct((own, width), bf16),
            jax.ShapeDtypeStruct((n_ctx, part, width), bf16),
            jax.ShapeDtypeStruct((n_ctx, 3, share, columns), bf16),
            jax.ShapeDtypeStruct(small_shape, f32),
        ),
        in_specs=[anywhere, anywhere, vmem, vmem, vmem, anywhere, vmem, anywhere, vmem, vmem],
        out_specs=(vmem,) * 4,
        scratch_shapes=[
            pltpu.VMEM(term.shape, bf16),
            pltpu.VMEM((rows, share), bf16),
            pltpu.VMEM((n_ctx, share, rows), bf16),
            pltpu.VMEM((3, width, columns), bf16),
            pltpu.VMEM((own, width), bf16),
            pltpu.VMEM((3, n_ctx, HEAD, rows), bf16),
            pltpu.VMEM((3, rows, columns), bf16),
            pltpu.VMEM((own, width), f32),
            pltpu.VMEM((8, width), f32),
            pltpu.VMEM(small_shape, f32),
            dma((3,)), dma,
            dma((n_tp, n_ctx)), dma((n_tp, n_ctx)),
            pltpu.VMEM((n_tp - 1, part, width), bf16),
            dma((n_tp - 1,)), dma((n_tp - 1,)),
            pltpu.VMEM((n_ctx,) + small_shape, f32),
            pltpu.VMEM((n_tp, 4 * norm_rows, 128), f32),
            pltpu.VMEM((n_tp - 1, 2, own, half_width), bf16),
            pltpu.VMEM((pair, 3, share, columns), bf16),
            pltpu.VMEM((pair, 3, share, columns), bf16),
            pltpu.VMEM((pair, 3, share, columns), bf16),
            pltpu.VMEM((2, 3, half_rows, columns), bf16),
            pltpu.VMEM((2, 3, half_rows, columns), bf16),
            pltpu.VMEM((2, 3, half_rows, columns), bf16),
            dma((n_ctx,)), dma((n_ctx,)),
            dma((n_tp,)), dma((n_tp,)),
            dma((n_tp - 1, 2)), dma((n_tp - 1, 2)),
            dma((pair,)), dma((pair,)),
            dma((2, 2)), dma((2, 2)),
            dma((2,)), dma((2,)),
            dma((3, 7)), dma((3, 7)),
        ],
        compiler_params=pltpu.CompilerParams(
            collective_id=3, has_side_effects=True, vmem_limit_bytes=62 * 2**20
        ),
        cost_estimate=pl.CostEstimate(
            flops=2 * rows * width * cols, bytes_accessed=50 * 2**20, transcendentals=0
        ),
        name="final_sums",
    )(
        term, xs, means, inverses, gain, low, grads, w_qkv.transpose(1, 0, 2), out, small_two
    )


def norm_stats(rows):
    mean = jnp.mean(rows, axis=1, keepdims=True)
    center = rows - mean
    inverse = lax.rsqrt(jnp.mean(center * center, axis=1, keepdims=True) + epsilon)
    return mean, inverse


def norm_backward(grad_out, normed, inverse, gain):
    scaled = grad_out * gain
    grad_rows = inverse * (
        scaled
        - jnp.mean(scaled, axis=1, keepdims=True)
        - normed * jnp.mean(scaled * normed, axis=1, keepdims=True)
    )
    return (grad_rows, jnp.sum(grad_out * normed, axis=0), jnp.sum(grad_out, axis=0))


def rotate(tensor, places, direction):
    half = ROT // 2
    frequency = 10000.0 ** (-2.0 * jnp.arange(half, dtype=f32) / ROT)
    angles = frequency[:, None] * places.astype(f32)[None, :]
    cosine, sines = jnp.cos(angles), direction * jnp.sin(angles)
    first, second = tensor[..., :half, :], tensor[..., half:ROT, :]
    return jnp.concatenate(
        [
            first * cosine - second * sines,
            second * cosine + first * sines,
            tensor[..., ROT:, :],
        ],
        axis=-2,
    )


def after(value, *others):
    return lax.optimization_barrier((value, *others))[0]


def direct_gather(value, count):
    n_tp = lax.axis_size("tp")
    return [value] + [
        lax.ppermute(value, "tp", [(i, (i + s) % n_tp) for i in range(n_tp)])
        for s in range(1, count)
    ]


def in_tp_order(arrays):
    count = len(arrays)
    shape = arrays[0].shape

    def kernel(tp, *refs):
        sources, out = refs[:count], refs[count]
        for s in range(count):
            out[lax.rem(tp[0] - s + count, count)] = sources[s][...]

    vmem = pl.BlockSpec(memory_space=pltpu.VMEM)
    return pl.pallas_call(
        kernel,
        out_shape=jax.ShapeDtypeStruct((count,) + shape, arrays[0].dtype),
        in_specs=[pl.BlockSpec(memory_space=pltpu.SMEM)] + [vmem] * count,
        out_specs=vmem,
        compiler_params=pltpu.CompilerParams(vmem_limit_bytes=60 * 2**20),
        cost_estimate=pl.CostEstimate(
            flops=0, bytes_accessed=4 * count * math.prod(shape), transcendentals=0
        ),
        name="in_tp_order",
    )(lax.axis_index("tp")[None], *arrays)


def exchange_sum(terms, axis):
    parts = lax.all_to_all(terms, axis, split_axis=0, concat_axis=0, tiled=True)
    return sum(part.astype(f32) for part in parts)


def scatter(partial, axis):
    return lax.psum_scatter(partial, axis, scatter_dimension=0, tiled=True)


def swap(value, axis, bit):
    size = lax.axis_size(axis)
    return lax.ppermute(value, axis, [(i, i ^ (1 << bit)) for i in range(size)])


def pair_sum(partial):
    size, rest = partial.shape[0], partial.shape[1:]
    side = lax.axis_index("ctx") % 2
    pairs = partial.reshape((size // 2, 2) + rest)
    kept = lax.dynamic_index_in_dim(pairs, side, 1, keepdims=False)
    sent = lax.dynamic_index_in_dim(pairs, 1 - side, 1, keepdims=False)
    return (kept.astype(f32) + swap(sent, "ctx", 0).astype(f32)).astype(bf16)


def spread_start(both, *early):
    pairs = both.shape[0]
    mine = lax.axis_index("ctx") // 2
    parts = [lax.dynamic_index_in_dim(both, mine, 0, keepdims=False)]
    for distance in range(1, pairs):
        sent = lax.dynamic_index_in_dim(both, mine ^ distance, 0, keepdims=False)
        perm = [(i, i ^ (2 * distance)) for i in range(2 * pairs)]
        parts.append(lax.ppermute(after(sent, *early) if early else sent, "ctx", perm))
    return parts


def spread_end(parts, *late):
    if late:
        parts = lax.optimization_barrier((*parts, *late))[: len(parts)]
    return sum(part.astype(f32) for part in parts).astype(bf16)


def by_ctx(partial):
    rows, cols = partial.shape
    n_ctx = lax.axis_size("ctx")
    return partial.reshape(n_ctx, rows // n_ctx, cols)


def gather(rows, axis):
    return lax.all_gather(rows, axis, axis=0, tiled=True)


def middle_backward(grad, middle, means, inverses, gain, cot, own):
    rows, width = grad.shape
    tile = math.gcd(own, 128)

    def kernel(tp, grad, middle, means, inverses, gain, cot, term, sums):
        i = pl.program_id(0)
        inverse = inverses[...][:, :1]
        normed = (middle[...] - means[...][:, :1]) * inverse
        value = grad[...]
        scaled = value * gain[...]
        result = inverse * (
            scaled
            - jnp.mean(scaled, axis=1, keepdims=True)
            - normed * jnp.mean(scaled * normed, axis=1, keepdims=True)
        )
        is_own = jnp.where(i * tile // own == tp[0], 1.0, 0.0)
        term[...] = (result + is_own * cot[...].astype(f32)).astype(bf16)

        @pl.when(i == 0)
        def _():
            sums[...] = jnp.zeros_like(sums)

        sums[0:1] += jnp.sum(value * normed, axis=0, keepdims=True)
        sums[1:2] += jnp.sum(value, axis=0, keepdims=True)

    def by_rows(cols):
        return pl.BlockSpec((tile, cols), lambda i: (i, 0))

    return pl.pallas_call(
        kernel,
        grid=(rows // tile,),
        out_shape=(
            jax.ShapeDtypeStruct((rows, width), bf16),
            jax.ShapeDtypeStruct((8, width), f32),
        ),
        in_specs=[
            pl.BlockSpec(memory_space=pltpu.SMEM),
            by_rows(width), by_rows(width), by_rows(128), by_rows(128),
            pl.BlockSpec((1, width), lambda i: (0, 0)),
            by_rows(width),
        ],
        out_specs=(by_rows(width), pl.BlockSpec((8, width), lambda i: (0, 0))),
        cost_estimate=pl.CostEstimate(
            flops=20 * rows * width, bytes_accessed=12 * rows * width, transcendentals=0
        ),
        compiler_params=pltpu.CompilerParams(vmem_limit_bytes=60 * 2**20),
        name="middle_backward",
    )(lax.axis_index("tp")[None], grad, middle, means, inverses, gain, cot)


def widen(chunks, down, out):
    devices, parts, rows, cols = chunks.shape
    step = math.gcd(devices, 2)

    def kernel(chunks, down, out, chunks_wide, down_wide, out_wide):
        for i in range(step):
            chunks_wide[:, i * rows : (i + 1) * rows] = chunks[i].astype(f32)
            for source, target in ((down, down_wide), (out, out_wide)):
                high = source.shape[1]
                target[i * high : (i + 1) * high] = source[i].astype(f32)

    others = (down.shape[1:], out.shape[1:])
    return pl.pallas_call(
        kernel,
        grid=(devices // step,),
        out_shape=[jax.ShapeDtypeStruct((parts, devices * rows, cols), f32)]
        + [jax.ShapeDtypeStruct((devices * shape[0], shape[1]), f32) for shape in others],
        in_specs=[pl.BlockSpec((step, parts, rows, cols), lambda i: (i, 0, 0, 0))]
        + [pl.BlockSpec((step,) + shape, lambda i: (i, 0, 0)) for shape in others],
        out_specs=[pl.BlockSpec((parts, step * rows, cols), lambda i: (0, i, 0))]
        + [pl.BlockSpec((step * shape[0], shape[1]), lambda i: (i, 0)) for shape in others],
        cost_estimate=pl.CostEstimate(
            flops=0, bytes_accessed=6 * math.prod(chunks.shape), transcendentals=0
        ),
        compiler_params=pltpu.CompilerParams(vmem_limit_bytes=60 * 2**20),
        name="widen",
    )(chunks, down, out)


def interleave(gate, up):
    rows, cols = gate.shape
    tile = math.gcd(rows, 512)

    def kernel(gate, up, out):
        out[:, 0, :] = gate[...].astype(f32)
        out[:, 1, :] = up[...].astype(f32)

    return pl.pallas_call(
        kernel,
        grid=(rows // tile,),
        out_shape=jax.ShapeDtypeStruct((rows, 2, cols), f32),
        in_specs=[pl.BlockSpec((tile, cols), lambda i: (i, 0))] * 2,
        out_specs=pl.BlockSpec((tile, 2, cols), lambda i: (i, 0, 0)),
        compiler_params=pltpu.CompilerParams(vmem_limit_bytes=60 * 2**20),
        cost_estimate=pl.CostEstimate(flops=1, bytes_accessed=1, transcendentals=0),
        name="interleave",
    )(gate, up)


def shards(
    layer_in,
    norm_gain,
    norm_bias,
    w_qkv,
    b_qkv,
    w_out,
    w_gate_up,
    w_down,
    cotangent,
    block_table,
    seq_ids,
):
    n_ctx, n_tp = lax.axis_size("ctx"), lax.axis_size("tp")
    ctx, tp = lax.axis_index("ctx"), lax.axis_index("tp")
    own, width = layer_in.shape
    rows = own * n_tp
    cols = w_qkv.shape[2]
    heads = cols // HEAD
    table = block_table.reshape(-1)
    blocks = table.shape[0]
    by_head = heads == n_ctx == 8 and BLK % own == 0
    part = cols // n_ctx

    ids = jnp.arange(blocks, dtype=jnp.int32)
    located = jnp.sum(jnp.where(table[None, :] == ids[:, None], ids[None, :], 0), axis=1)
    same = seq_ids[:, None] == seq_ids[None, :]
    first = jnp.min(jnp.where(same, ids[None, :], blocks), axis=1)
    last = jnp.max(jnp.where(same, ids[None, :], -1), axis=1)
    order = jnp.concatenate([located, first, last, tp[None]]).astype(jnp.int32)
    frequency = 10000.0 ** (-2.0 * jnp.arange(ROT // 2, dtype=f32) / ROT)
    positions = table[:, None] * BLK + jnp.arange(BLK, dtype=jnp.int32)[None, :]
    angles = frequency[None, :, None] * positions.astype(f32)[:, None, :]
    angles = jnp.stack([jnp.cos(angles), jnp.sin(angles)], axis=1)

    hidden_units = w_gate_up.shape[2]
    w_part = lax.dynamic_slice_in_dim(w_out, ctx * part, part, 0)
    if by_head:
        layer_in = after(layer_in, angles, order)
        xs, lows, mean_one, inverse_one, w_part, packed = project_exchange(
            layer_in, w_part, norm_gain[0:1], norm_bias[0:1], w_qkv, b_qkv
        )
        first_low = lows.reshape(rows, width)
        w_out_all = lax.all_gather(w_part, "ctx", axis=1, tiled=True)
        cot = direct_gather(after(cotangent, packed), n_tp - 1)
        out, logsum = attention_forward(order, angles, packed)
        middle, lows, mean_two, inverse_two, attended_all = output_project(
            out, xs, w_out_all, norm_gain[1:2], norm_bias[1:2]
        )
        cot = list(lax.optimization_barrier((*cot, middle))[: n_tp - 1])
        late = after(cotangent, middle)
        cot.append(lax.ppermute(late, "tp", [(i, (i + n_tp - 1) % n_tp) for i in range(n_tp)]))
        cot = in_tp_order(cot).reshape(rows, width)
        middle = middle.reshape(rows, width)
        mean_two, inverse_two = [t.reshape(rows, 128) for t in (mean_two, inverse_two)]
        second_low = lows.reshape(rows, width)
        attended_all = attended_all.reshape(n_tp * cols, rows)
    else:
        x = gather(layer_in, "tp").astype(f32)
        mean_one, inverse_one = norm_stats(x)
        first_low = ((x - mean_one) * inverse_one * norm_gain[0] + norm_bias[0]).astype(bf16)
        projected = (
            jnp.einsum("dcf,rd->cfr", w_qkv, first_low, preferred_element_type=f32)
            + b_qkv[:, :, None]
        ).reshape(3, heads, HEAD, rows)
        w_part = gather(w_part, "tp").reshape(n_tp, part, width)
        w_out_all = lax.all_gather(w_part, "ctx", axis=1, tiled=True)
        cot = gather(cotangent, "tp")
        places, _ = row_places(ctx * rows, rows, table, seq_ids)
        qkv = jnp.concatenate([rotate(projected[0:2], places, 1.0), projected[2:3]], axis=0)
        queries, keys, values = [t.astype(bf16).transpose(2, 0, 1) for t in qkv]
        visit, offsets = gathered_setup(
            rows, table, seq_ids, keys.reshape(rows, cols), values.reshape(rows, cols)
        )
        out, logsum = gathered_forward(queries, visit, offsets)
        attended_all = gather(out.astype(bf16).reshape(rows, cols).T, "tp")
        middle = x + jnp.einsum(
            "fr,fd->rd",
            attended_all,
            w_out_all.reshape(n_tp * cols, width),
            preferred_element_type=f32,
        )
        mean_two, inverse_two = norm_stats(middle)
        normed_two = (middle - mean_two) * inverse_two
        second_low = (normed_two * norm_gain[1] + norm_bias[1]).astype(bf16)

    grad_hidden = lax.dot_general(cot, w_down, (((1,), (1,)), ((), ())), preferred_element_type=f32)
    gate_up = jnp.einsum("rd,dcf->rcf", second_low, w_gate_up, preferred_element_type=f32)
    gate, up = gate_up[:, 0], gate_up[:, 1]
    sigmoid = jax.nn.sigmoid(gate)
    activated = gate * sigmoid
    hidden = (activated * up).astype(bf16)
    grad_gate = grad_hidden * up * sigmoid * (1.0 + gate * (1.0 - sigmoid))
    grad_up = grad_hidden * activated
    grad_gu = jnp.stack([grad_gate, grad_up], axis=1).astype(bf16)
    grad_second = jnp.einsum("rcf,dcf->rd", grad_gu, w_gate_up, preferred_element_type=f32)

    if by_head:
        middle_term, sums = middle_backward(
            grad_second, middle, mean_two, inverse_two, norm_gain[1:2], cot, own
        )
        gain_two, bias_two = sums[0], sums[1]
    else:
        middle_norm, gain_two, bias_two = norm_backward(
            grad_second, normed_two, inverse_two, norm_gain[1]
        )
        is_own = (jnp.arange(rows, dtype=jnp.int32) // own == tp)[:, None]
        middle_term = (middle_norm + jnp.where(is_own, cot.astype(f32), 0.0)).astype(bf16)

    if by_head:
        grad_att, gate_grad, up_grad, out_grad, out_sent, down_grad, down_sent, *down = middle_sums(
            middle_term,
            w_out_all,
            second_low,
            grad_gate.astype(bf16),
            grad_up.astype(bf16),
            hidden,
            cot,
            attended_all.reshape(n_tp, cols, rows),
            w_down,
        )
        down = [down[0], down[-1]] + [
            lax.ppermute(down[s], "tp", [(i, (i - s) % n_tp) for i in range(n_tp)])
            for s in range(1, n_tp - 1)
        ]
    else:
        grad_att = lax.dot_general(
            w_out_all.reshape(n_tp * cols, width),
            middle_term,
            (((1,), (1,)), ((), ())),
            preferred_element_type=f32,
        ).astype(bf16)
        grad_att = scatter(grad_att, "tp")
        down = jnp.dot(hidden, w_down, preferred_element_type=f32).astype(bf16)
        down = [scatter(down, "tp")]

        def weight_grad(left, right):
            return lax.dot_general(
                left, right, (((0,), (0,)), ((), ())), preferred_element_type=f32
            ).astype(bf16)

        gu_grad = jnp.concatenate(
            [pair_sum(by_ctx(weight_grad(second_low, t.astype(bf16)))) for t in (grad_gate, grad_up)],
            axis=1,
        )
        gu_grad = spread_end(spread_start(gu_grad))
        out_grad = jnp.dot(attended_all, middle_term, preferred_element_type=f32).astype(bf16)
        out_grad = out_grad.reshape(n_tp, n_ctx, part, width).transpose(1, 0, 2, 3)
        other_grad = jnp.concatenate(
            [
                pair_sum(out_grad.reshape(n_ctx, n_tp * part, width)),
                pair_sum(by_ctx(weight_grad(hidden, cot))),
            ],
            axis=1,
        )
        other_grad = spread_end(spread_start(other_grad))
        gate_grad, up_grad = jnp.split(gu_grad, 2, axis=0)
        out_grad, down_grad = jnp.split(other_grad, [n_tp * part], axis=0)
    gate_grad, up_grad = gather(gate_grad, "ctx"), gather(up_grad, "ctx")
    grad_gate_up = interleave(gate_grad, up_grad)

    if by_head:
        grads = attention_backward(order, angles, packed, grad_att, out, logsum)
        out_sent = lax.ppermute(out_sent, "ctx", [(i, i ^ 4) for i in range(n_ctx)])
        down_sent = lax.ppermute(down_sent, "ctx", [(i, i ^ 2) for i in range(n_ctx)])
        grads, out_sent, down_sent, *down = lax.optimization_barrier(
            (grads, out_sent, down_sent, *down)
        )
        out_grad = (out_grad.astype(f32) + out_sent.astype(f32)).astype(bf16)
        down_grad = (down_grad.astype(f32) + down_sent.astype(f32)).astype(bf16)
        down_grad = gather(down_grad, "ctx")
        grad_input, out_grad, grad_qkv, small = final_sums(
            middle_term.reshape(n_tp, own, width),
            xs,
            mean_one,
            inverse_one,
            norm_gain[0:1],
            first_low,
            grads,
            w_qkv,
            out_grad,
            jnp.stack([gain_two, bias_two]).reshape(2, -1, 128),
        )
        grad_input, *down = lax.optimization_barrier((grad_input, *down))
        grad_qkv, down_grad, out_grad = widen(
            grad_qkv, down_grad.reshape(n_ctx, -1, width), out_grad
        )
        grad_qkv = grad_qkv.transpose(1, 0, 2)
        bias_qkv, norms = small[: 3 * cols // 128], small[3 * cols // 128 :]
    else:
        grads = gathered_backward(
            queries, visit, offsets, grad_att.T.reshape(rows, heads, HEAD), out, logsum
        )
        grads = jnp.stack([t.transpose(1, 2, 0) for t in grads])
        grads = jnp.concatenate([rotate(grads[0:2], places, -1.0), grads[2:3]], axis=0)
        grad_projected = grads.reshape(3 * cols, rows).astype(bf16)
        grad_first = jnp.einsum(
            "cfr,dcf->rd",
            grad_projected.reshape(3, cols, rows),
            w_qkv,
            preferred_element_type=f32,
        )
        input_norm, gain_one, bias_one = norm_backward(
            grad_first, (x - mean_one) * inverse_one, inverse_one, norm_gain[0]
        )
        grad_input = middle_term.astype(f32) + input_norm
        grad_input = exchange_sum(grad_input.astype(bf16).reshape(n_tp, own, width), "tp")
        grad_input = grad_input.astype(bf16)
        grad_qkv = lax.dot_general(
            first_low, grad_projected, (((0,), (1,)), ((), ())), preferred_element_type=f32
        ).astype(bf16)
        grad_qkv = spread_end(spread_start(pair_sum(by_ctx(grad_qkv))))
        out_grad = exchange_sum(out_grad.reshape(n_tp, part, width), "tp").astype(bf16)
        out_grad, grad_qkv = [gather(t, "ctx").astype(f32) for t in (out_grad, grad_qkv)]
        grad_qkv = grad_qkv.reshape(width, 3, cols)
        down_grad = gather(down_grad, "ctx").astype(f32)
        bias_qkv = lax.psum(jnp.sum(grad_projected.astype(f32), axis=1), "ctx")
        norms = jnp.stack([gain_one, gain_two, bias_one, bias_two])
        norms = lax.psum(norms, ("ctx", "tp"))
    own_middle = lax.dynamic_slice_in_dim(middle, tp * own, own, 0)
    layer_out = (own_middle + sum(t.astype(f32) for t in down)).astype(bf16)
    norms = norms.reshape(2, 2, width)
    return (
        layer_out,
        grad_input,
        norms[0],
        norms[1],
        grad_qkv,
        bias_qkv.reshape(3, cols),
        out_grad,
        grad_gate_up,
        down_grad,
    )


def solution(mesh):
    placed = (
        P(("ctx", "tp"), None),
        P(),
        P(),
        P(None, None, "tp"),
        P(None, "tp"),
        P("tp", None),
        P(None, None, "tp"),
        P("tp", None),
        P(("ctx", "tp"), None),
        P(),
        P(),
    )
    return jax.shard_map(
        shards,
        mesh=mesh,
        in_specs=placed,
        out_specs=(
            P(("ctx", "tp"), None),
            P(("ctx", "tp"), None),
            P(),
            P(),
            P(None, None, "tp"),
            P(None, "tp"),
            P("tp", None),
            P(None, None, "tp"),
            P("tp", None),
        ),
        check_vma=False,
    )
```
